32 devices in a mesh: parts: 2 (over y), gx: 4 (over z), gy: 2 (over x), gz: 2 (over core).
Axes of the slice: x: 2, y: 2, z: 4, core: 2. Of those that a mesh axis runs over, the one named last changes fastest.
Arguments:
- electric: float32 [4, 4, 2, 3, 65536], P(('parts', 'gy'), 'gx', 'gz'), parts along dimension 0, may hold values from -6 to 6
- magnetic: float32 [4, 4, 2, 3, 65536], P(('parts', 'gy'), 'gx', 'gz'), parts along dimension 0, may hold values from -6 to 6
- material: int32 [4, 4, 2, 65536], P(('parts', 'gy'), 'gx', 'gz'), parts along dimension 0, may hold values from 0 to 3
- permittivity: float32 [4], replicated, may hold values from 1 to 12
Outputs:
- electric_next: float32 [4, 4, 2, 3, 65536], P(('parts', 'gy'), 'gx', 'gz'), parts along dimension 0
- magnetic_next: float32 [4, 4, 2, 3, 65536], P(('parts', 'gy'), 'gx', 'gz'), parts along dimension 0
The draws below stay inside these ranges and needn't reach their ends.
There are 2 independent parts, one for each index of `parts`. The reference program is written for one: setup_inputs(seed, part) draws one part's arguments, and reference() takes and returns one part's arrays. A program takes and returns all parts, laid end to end along the dimension named above; an argument that names none is the same for every part. Nothing has to cross between parts.
All inputs are finite; a program needn't handle non-finite values.
Results may differ from the reference program's by a relative error of at most 0.0003.
Values sent between devices are 32-bit elements; how exact they have to be, the bound alone decides.
No kernel may reach another device: no remote copies, remote signals or barrier semaphores. Data moves between devices by JAX's collectives and lax.ppermute only.
A program may use at most 64 MiB of HBM per device.

```python
import math
import jax
import jax.numpy as jnp
from jax import lax

CZ = 4
CX = 32
CY = 512
MATS = 4
CELLS = 65536
N_GX = 4
N_GY = 2
N_GZ = 2


def with_ends(result, stream_key, least, top_value):
    index_at = [jax.random.randint(jax.random.fold_in(stream_key, axis), (), 0, length) for axis, length in enumerate(result.shape)]
    longest = result.shape.index(max(result.shape))
    neighbour = index_at[:longest] + [(index_at[longest] + 1) % result.shape[longest]] + index_at[longest + 1:]
    return result.at[tuple(index_at)].set(least).at[tuple(neighbour)].set(top_value)


def shard_levels(key, dims, shards, least, top_value):
    level, own = 1.0, jax.random.fold_in(key, 6)
    for position, shards_of in shards:
        heights = jnp.exp(jax.random.uniform(jax.random.fold_in(own, position), (shards_of,), jnp.float32, least / len(shards), top_value / len(shards)))
        level = level * jnp.repeat(heights, dims[position] // shards_of).reshape([-1 if axis == position else 1 for axis in range(len(dims))])
    return level


def normal_values(stream_key, shape, width, most, cuts=(), dtype=jnp.bfloat16):
    result = width * jax.random.normal(stream_key, shape, jnp.float32)
    if cuts:
        result = result * shard_levels(stream_key, shape, cuts, -0.22, 0.18)
    return jnp.clip(result, -most, most).astype(dtype)


def setup_inputs(seed: int = 0, part: int = 0) -> dict:
    seeds = jax.random.split(jax.random.key(seed), 5)
    part_keys = jax.random.split(jax.random.fold_in(seeds[4], part), 5)
    return {
        "electric": normal_values(part_keys[0], (N_GY, N_GX, N_GZ, 3, CELLS), 1.0, 6.0, ((0, 2), (1, 4), (2, 2)), jnp.float32),
        "magnetic": normal_values(part_keys[1], (N_GY, N_GX, N_GZ, 3, CELLS), 1.0, 6.0, ((0, 2), (1, 4), (2, 2)), jnp.float32),
        "material": with_ends(jax.random.randint(part_keys[2], (N_GY, N_GX, N_GZ, CELLS), 0, MATS), jax.random.fold_in(part_keys[2], 1), 0, MATS - 1).astype(jnp.int32),
        "permittivity": jnp.clip(jnp.exp(jax.random.uniform(seeds[3], (MATS,), jnp.float32, math.log(1.0), math.log(12.0))), 1.0, 12.0),
    }


courant = 0.5


def forward_diff(values, dim_axis, ghost_plane):
    shifted = jnp.concatenate([lax.slice_in_dim(values, 1, values.shape[dim_axis], axis=dim_axis), jnp.expand_dims(ghost_plane, dim_axis)], axis=dim_axis)
    return shifted - values


def backward_diff(values, dim_axis, ghost_plane):
    shifted = jnp.concatenate([jnp.expand_dims(ghost_plane, dim_axis), lax.slice_in_dim(values, 0, values.shape[dim_axis] - 1, axis=dim_axis)], axis=dim_axis)
    return values - shifted


def curl_with(differ, vectors, ghost_depth, ghost_width, ghost_height):
    ghosts = (ghost_depth, ghost_width, ghost_height)

    def along_axis(component, dim_axis):
        return differ(vectors[component], dim_axis, ghosts[dim_axis][component])

    curl_x = along_axis(2, 2) - along_axis(1, 0)
    curl_y = along_axis(0, 0) - along_axis(2, 1)
    curl_z = along_axis(1, 1) - along_axis(0, 2)
    return jnp.stack([curl_x, curl_y, curl_z])


def restrict(face_plane):
    quads = face_plane.reshape(3, face_plane.shape[1] // 2, 2, face_plane.shape[2] // 2, 2)
    return ((quads[:, :, 0, :, 0] + quads[:, :, 0, :, 1]) + (quads[:, :, 1, :, 0] + quads[:, :, 1, :, 1])) * 0.25


def enlarge(face_plane):
    return jnp.repeat(jnp.repeat(face_plane, 2, axis=1), 2, axis=2)


def lookup(material, permittivity):
    permit_sum = jnp.zeros(material.shape, jnp.float32)
    for material_id in range(MATS):
        permit_sum = permit_sum + jnp.where(material == material_id, permittivity[material_id], 0.0)
    return courant / permit_sum


def to_grids(blocks):
    half_rows = N_GY // 2
    components = blocks.shape[3]
    coarse = blocks[:half_rows].reshape(half_rows, N_GX, N_GZ, components, CZ, CX, CY)
    coarse = coarse.transpose(3, 2, 4, 1, 5, 0, 6).reshape(components, N_GZ * CZ, N_GX * CX, half_rows * CY)
    fine_grid = blocks[half_rows:].reshape(half_rows, N_GX, N_GZ, components, 2 * CZ, 2 * CX, CY // 4)
    fine_grid = fine_grid.transpose(3, 2, 4, 1, 5, 0, 6).reshape(components, N_GZ * 2 * CZ, N_GX * 2 * CX, half_rows * (CY // 4))
    return coarse, fine_grid


def to_blocks(coarse, fine_grid):
    half_rows = N_GY // 2
    components = coarse.shape[0]
    coarse_part = coarse.reshape(components, N_GZ, CZ, N_GX, CX, half_rows, CY)
    coarse_part = coarse_part.transpose(5, 3, 1, 0, 2, 4, 6).reshape(half_rows, N_GX, N_GZ, components, CZ * CX * CY)
    fine_part = fine_grid.reshape(components, N_GZ, 2 * CZ, N_GX, 2 * CX, half_rows, CY // 4)
    fine_part = fine_part.transpose(5, 3, 1, 0, 2, 4, 6).reshape(half_rows, N_GX, N_GZ, components, CZ * CX * CY)
    return jnp.concatenate([coarse_part, fine_part], axis=0)


def depth_zeros(grid):
    return jnp.zeros((3, grid.shape[2], grid.shape[3]), jnp.float32)


def height_zeros(grid):
    return jnp.zeros((3, grid.shape[1], grid.shape[2]), jnp.float32)


def reference(electric, magnetic, material, permittivity):
    e_coarse, e_fine = to_grids(electric)
    h_coarse, h_fine = to_grids(magnetic)
    m_coarse, m_fine = to_grids(material[:, :, :, None, :])
    c_coarse = lookup(m_coarse[0], permittivity)
    c_fine = lookup(m_fine[0], permittivity)
    h_coarse = h_coarse - courant * curl_with(forward_diff, e_coarse, depth_zeros(e_coarse), e_coarse[:, :, 0, :], restrict(e_fine[:, :, :, 0]))
    h_fine = h_fine - courant * curl_with(forward_diff, e_fine, depth_zeros(e_fine), e_fine[:, :, 0, :], height_zeros(e_fine))
    e_coarse = e_coarse + c_coarse * curl_with(backward_diff, h_coarse, depth_zeros(h_coarse), h_coarse[:, :, -1, :], height_zeros(h_coarse))
    interface = enlarge(h_coarse[:, :, :, -1])
    e_fine = e_fine + c_fine * curl_with(backward_diff, h_fine, depth_zeros(h_fine), h_fine[:, :, -1, :], interface)
    h_fine = h_fine - courant * curl_with(forward_diff, e_fine, depth_zeros(e_fine), e_fine[:, :, 0, :], height_zeros(e_fine))
    e_fine = e_fine + c_fine * curl_with(backward_diff, h_fine, depth_zeros(h_fine), h_fine[:, :, -1, :], interface)
    return to_blocks(e_coarse, e_fine), to_blocks(h_coarse, h_fine)
```

```python
from functools import partial

import jax
import jax.numpy as jnp
from jax import lax
from jax.experimental import pallas as pl
from jax.experimental.pallas import tpu as pltpu
from jax.sharding import PartitionSpec as P

CZ = 4
CX = 32
CY = 512
MATS = 4


courant = 0.5


def passed_along(x, axis, by):
    devices = lax.axis_size(axis)
    return lax.ppermute(x, axis, [(i, (i + by) % devices) for i in range(devices)])


def from_behind(x, axis, by):
    devices = lax.axis_size(axis)
    pairs = [(i, i + by) for i in range(devices) if 0 <= i + by < devices]
    return lax.ppermute(x, axis, pairs)


def forward_diff(values, dim_axis, ghost_plane):
    shifted = jnp.concatenate(
        [
            lax.slice_in_dim(values, 1, values.shape[dim_axis], axis=dim_axis),
            jnp.expand_dims(ghost_plane, dim_axis),
        ],
        axis=dim_axis,
    )
    return shifted - values


def backward_diff(values, dim_axis, ghost_plane):
    shifted = jnp.concatenate(
        [
            jnp.expand_dims(ghost_plane, dim_axis),
            lax.slice_in_dim(values, 0, values.shape[dim_axis] - 1, axis=dim_axis),
        ],
        axis=dim_axis,
    )
    return values - shifted


def curl_with(differ, vectors, ghost_depth, ghost_width, ghost_height):
    ghosts = (ghost_depth, ghost_width, ghost_height)

    def along_axis(component, dim_axis):
        return differ(vectors[component], dim_axis, ghosts[dim_axis][component])

    curl_x = along_axis(2, 2) - along_axis(1, 0)
    curl_y = along_axis(0, 0) - along_axis(2, 1)
    curl_z = along_axis(1, 1) - along_axis(0, 2)
    return jnp.stack([curl_x, curl_y, curl_z])


def restrict(face_plane):
    quads = face_plane.reshape(3, face_plane.shape[1] // 2, 2, face_plane.shape[2] // 2, 2)
    return (
        quads[:, :, 0, :, 0] + quads[:, :, 0, :, 1] + (quads[:, :, 1, :, 0] + quads[:, :, 1, :, 1])
    ) * 0.25


def enlarge(face_plane):
    return jnp.repeat(jnp.repeat(face_plane, 2, axis=1), 2, axis=2)


def lookup(material, permittivity):
    permit_sum = jnp.zeros(material.shape, jnp.float32)
    for material_id in range(MATS):
        permit_sum = permit_sum + jnp.where(material == material_id, permittivity[material_id], 0.0)
    return courant / permit_sum


def pack_face(face_plane, length):
    flat_face = face_plane.reshape(3, -1)
    if flat_face.shape[1] < length:
        flat_face = jnp.concatenate(
            [flat_face, jnp.zeros((3, length - flat_face.shape[1]), flat_face.dtype)], axis=1
        )
    return flat_face


def unpack_face(flat_face, row_count, col_count):
    return flat_face[:, : row_count * col_count].reshape(3, row_count, col_count)


def level_height(got_height, is_fine):
    return got_height if is_fine else restrict(got_height)


def low_faces(grid_shape, is_fine, flat_field):
    vectors = flat_field.reshape((3,) + grid_shape)
    face_plane = vectors[:, :, :, 0]
    if not is_fine:
        face_plane = enlarge(face_plane)
    return (
        pack_face(vectors[:, :, 0, :], CZ * CY),
        pack_face(vectors[:, 0, :, :], CX * CY),
        face_plane,
    )


def high_faces(grid_shape, is_fine, flat_field):
    vectors = flat_field.reshape((3,) + grid_shape)
    face_plane = vectors[:, :, :, -1]
    if not is_fine:
        face_plane = enlarge(face_plane)
    return (
        pack_face(vectors[:, :, -1, :], CZ * CY),
        pack_face(vectors[:, -1, :, :], CX * CY),
        face_plane,
    )


def advance_magnetic(
    grid_shape, is_fine, does_move, e_flat, h_flat, got_width, got_depth, got_height
):
    if not does_move:
        return h_flat
    deep_cells, wide_cells, tall_cells = grid_shape
    vectors = e_flat.reshape((3,) + grid_shape)
    curl_term = curl_with(
        forward_diff,
        vectors,
        unpack_face(got_depth, wide_cells, tall_cells),
        unpack_face(got_width, deep_cells, tall_cells),
        level_height(got_height, is_fine),
    )
    return (h_flat.reshape((3,) + grid_shape) - courant * curl_term).reshape(3, -1)


def advance_electric(
    grid_shape, is_fine, does_move, e_flat, h_flat, coefficient, got_width, got_depth, got_height
):
    if not does_move:
        return e_flat
    deep_cells, wide_cells, tall_cells = grid_shape
    magnetic = h_flat.reshape((3,) + grid_shape)
    curl_term = curl_with(
        backward_diff,
        magnetic,
        unpack_face(got_depth, wide_cells, tall_cells),
        unpack_face(got_width, deep_cells, tall_cells),
        level_height(got_height, is_fine),
    )
    return (
        e_flat.reshape((3,) + grid_shape) + coefficient.reshape(grid_shape) * curl_term
    ).reshape(3, -1)


def pass_width(face_plane, offset):
    return passed_along(face_plane, "gx", offset)


def pass_depth(face_plane, offset):
    return from_behind(face_plane, "gz", offset)


def pass_height(face_plane, offset):
    return from_behind(face_plane, "gy", offset)


def general_shards(electric, magnetic, material, permittivity):
    cell_count = electric.shape[-1]
    e_flat = electric.reshape(3, cell_count)
    h_flat = magnetic.reshape(3, cell_count)
    coefficient = lookup(material.reshape(cell_count), permittivity)
    is_fine = lax.axis_index("gy") >= lax.axis_size("gy") // 2
    coarse_shape = (CZ, CX, CY)
    fine_shape = (2 * CZ, 2 * CX, CY // 4)
    for substep in range(2):
        coarse_moves = substep == 0
        face_width, face_depth, face_height = lax.cond(
            is_fine,
            partial(low_faces, fine_shape, True),
            partial(low_faces, coarse_shape, False),
            e_flat,
        )
        got_depth = pass_depth(face_depth, -1)
        got_height = pass_height(face_height, -1)
        got_width = pass_width(face_width, -1)
        h_flat = lax.cond(
            is_fine,
            partial(advance_magnetic, fine_shape, True, True),
            partial(advance_magnetic, coarse_shape, False, coarse_moves),
            e_flat,
            h_flat,
            got_width,
            got_depth,
            got_height,
        )
        rim_width, rim_depth, rim_height = lax.cond(
            is_fine,
            partial(high_faces, fine_shape, True),
            partial(high_faces, coarse_shape, False),
            h_flat,
        )
        rim_depth = pass_depth(rim_depth, 1)
        rim_height = pass_height(rim_height, 1)
        rim_width = pass_width(rim_width, 1)
        e_flat = lax.cond(
            is_fine,
            partial(advance_electric, fine_shape, True, True),
            partial(advance_electric, coarse_shape, False, coarse_moves),
            e_flat,
            h_flat,
            coefficient,
            rim_width,
            rim_depth,
            rim_height,
        )
    return (e_flat.reshape(electric.shape), h_flat.reshape(magnetic.shape))


ROWS = 512
HALO = 128
BASE = 128
EXT = 1152
LIMIT = 40 * 1024 * 1024
F32 = jnp.float32
VM = pl.BlockSpec(memory_space=pltpu.VMEM)
HBM = pl.BlockSpec(memory_space=pl.ANY)


def vmem(*shape, dtype=F32):
    return pltpu.VMEM(shape, dtype)


def held(x):
    return pltpu.with_memory_space_constraint(x, pltpu.VMEM)


def kernel_call(body, out_shape, in_specs, out_specs, scratch=(), aliases=None):
    return pl.pallas_call(
        body,
        out_shape=out_shape,
        in_specs=in_specs,
        out_specs=out_specs,
        scratch_shapes=list(scratch),
        input_output_aliases=aliases or {},
        compiler_params=pltpu.CompilerParams(vmem_limit_bytes=LIMIT),
    )


def place():
    return lax.axis_index("gy") >= lax.axis_size("gy") // 2, lax.axis_index("gz")


def lanes_of(shape):
    return lax.broadcasted_iota(jnp.int32, shape, len(shape) - 1)


def rows_of(shape):
    return lax.broadcasted_iota(jnp.int32, shape, len(shape) - 2)


def roll_lanes(x, by):
    return pltpu.roll(x, by % 128, 1)


def roll_rows(x, by):
    return pltpu.roll(x, by % x.shape[0], 0)


def at_lane(tile, lane_from, lane_to, value):
    lane = lanes_of(value.shape)
    return jnp.where(lane == lane_to, roll_lanes(value, lane_to - lane_from), tile)


def average(ref, lead, row):
    quad = [ref[lead + (pl.ds(row + step, 32, stride=2), slice(None))] for step in (0, 1, 64, 65)]
    return ((quad[0] + quad[1]) + (quad[2] + quad[3])) * 0.25


def put_column(tile, lane_from, slot, column):
    for block in range(4):
        tile = at_lane(tile, lane_from, 32 * block + slot, column[8 * block : 8 * block + 8])
    return tile


def gather(e_hbm, h_hbm, m_hbm, e_own, h_own, m_own, zmsg_e, zmsg_h, zmsg_m, ytile, sems):
    is_fine, gz = place()
    first = (1 - gz) * (ROWS - HALO)
    order = (0, 2, 1)
    loads = {}
    for slot, comp in enumerate(order):
        loads["e", comp] = pltpu.make_async_copy(e_hbm.at[comp], e_own.at[comp], sems.at[slot])
    for slot, comp in enumerate(order):
        loads["h", comp] = pltpu.make_async_copy(h_hbm.at[comp], h_own.at[comp], sems.at[3 + slot])
    edge = pl.ds(first, HALO)
    loads["ze"] = pltpu.make_async_copy(e_hbm.at[:, edge], zmsg_e, sems.at[6])
    loads["zh"] = pltpu.make_async_copy(h_hbm.at[:, edge], zmsg_h, sems.at[7])
    loads["zm"] = pltpu.make_async_copy(m_hbm.at[edge], zmsg_m, sems.at[8])
    loads["m"] = pltpu.make_async_copy(m_hbm, m_own, sems.at[9])
    for load in loads.values():
        load.start()
    loads["e", 0].wait()
    loads["e", 2].wait()

    @pl.when(is_fine)
    def _():
        tile = jnp.zeros((8, 128), F32)
        for kind, comp in enumerate((0, 2)):
            for layer in range(4):
                tile = put_column(tile, 0, 8 * kind + layer, average(e_own, (comp,), 128 * layer))
        ytile[...] = jnp.where(gz == 1, roll_lanes(tile, 1), tile)

    loads["e", 1].wait()
    loads["h", 0].wait()
    loads["h", 2].wait()

    @pl.when(jnp.logical_not(is_fine))
    def _():
        tile = jnp.zeros((8, 128), F32)
        for layer in range(4):
            top = pl.ds(128 * layer + 3, 32, stride=4)
            ex, ey, ez = (e_own[comp, top, :] for comp in range(3))
            tile = put_column(tile, 127, layer, h_own[0, top, :] + 0.5 * ez)
            tile = put_column(tile, 127, 8 + layer, h_own[2, top, :] - 0.5 * ex)
            tile = put_column(tile, 127, 16 + layer, ey)
        ytile[...] = jnp.where(gz == 1, roll_lanes(tile, 1), tile)

    for name in (("h", 1), "ze", "zh", "zm", "m"):
        loads[name].wait()


def fine_up_x(f):
    return jnp.where(rows_of(f.shape) == 63, 0.0, roll_rows(f, -1))


def fine_down_x(f):
    return jnp.where(rows_of(f.shape) == 0, 0.0, roll_rows(f, 1))


def fine_up_y(f):
    return jnp.where(lanes_of(f.shape) == 127, 0.0, roll_lanes(f, -1))


def fine_down_y(f, ghost):
    return roll_lanes(jnp.where(lanes_of(f.shape) == 127, ghost, f), 1)


def coarse_up_x(f):
    return jnp.where(rows_of(f.shape) >= 124, 0.0, roll_rows(f, -4))


def coarse_down_x(f):
    return jnp.where(rows_of(f.shape) < 4, 0.0, roll_rows(f, 4))


def coarse_up_y(f):
    following = jnp.where(rows_of(f.shape) % 4 == 3, 0.0, roll_rows(f, -1))
    return roll_lanes(jnp.where(lanes_of(f.shape) == 0, following, f), -1)


def coarse_down_y(f):
    previous = jnp.where(rows_of(f.shape) % 4 == 0, 0.0, roll_rows(f, 1))
    return roll_lanes(jnp.where(lanes_of(f.shape) == 127, previous, f), 1)


def half_h(e_ref, h_from, h_to, row, depth, up_x, up_y):
    here, above = pl.ds(row, depth), pl.ds(row + depth, depth)
    ex, ey, ez = (e_ref[comp, here, :] for comp in range(3))
    ex_z, ey_z = e_ref[0, above, :], e_ref[1, above, :]
    h_to[0, here, :] = h_from[0, here, :] - 0.5 * ((up_y(ez) - ez) - (ey_z - ey))
    h_to[1, here, :] = h_from[1, here, :] - 0.5 * ((ex_z - ex) - (up_x(ez) - ez))
    h_to[2, here, :] = h_from[2, here, :] - 0.5 * ((up_x(ey) - ey) - (up_y(ex) - ex))


def half_e(h_ref, e_from, e_to, c_ref, row, depth, down_x, down_y_x, down_y_z):
    here, below = pl.ds(row, depth), pl.ds(row - depth, depth)
    hx, hy, hz = (h_ref[comp, here, :] for comp in range(3))
    hx_z, hy_z = h_ref[0, below, :], h_ref[1, below, :]
    c = c_ref[here, :]
    e_to[0, here, :] = e_from[0, here, :] + c * ((hz - down_y_z(hz)) - (hy - hy_z))
    e_to[1, here, :] = e_from[1, here, :] + c * ((hx - hx_z) - (hz - down_x(hz)))
    e_to[2, here, :] = e_from[2, here, :] + c * ((hy - down_x(hy)) - (hx - down_y_x(hx)))


def layers(count, depth, body):
    def step(index, carry):
        body(index, pl.multiple_of(BASE + index * depth, depth))
        return carry

    lax.fori_loop(0, count, step, 0)


def extend(
    e_own, h_own, m_own, in_e, in_h, in_m, permittivity, ytile, e_ext, h_ext, c_ext, rtile, h_raw
):
    is_fine, gz = place()
    own = pl.multiple_of(BASE + HALO * gz, 128)
    halo = pl.multiple_of(BASE + ROWS * (1 - gz), 128)
    zero = jnp.zeros((HALO, 128), F32)
    values = [0.5 / jnp.full((HALO, 128), permittivity[i], F32) for i in range(MATS)]

    def coef(material):
        found = values[MATS - 1]
        for i in range(MATS - 2, -1, -1):
            found = jnp.where(material == i, values[i], found)
        return found

    for comp in range(3):
        h_ext[comp, pl.ds(0, BASE), :] = zero
        e_ext[comp, pl.ds(BASE + ROWS + HALO, HALO), :] = zero
        e_ext[comp, pl.ds(halo, HALO), :] = in_e[comp]
        h_raw[comp, pl.ds(halo, HALO), :] = in_h[comp]
        for part in range(4):
            e_ext[comp, pl.ds(own + HALO * part, HALO), :] = e_own[comp, pl.ds(HALO * part, HALO), :]
            h_raw[comp, pl.ds(own + HALO * part, HALO), :] = h_own[comp, pl.ds(HALO * part, HALO), :]
    c_ext[pl.ds(halo, HALO), :] = coef(in_m[...])
    for part in range(4):
        c_ext[pl.ds(own + HALO * part, HALO), :] = coef(m_own[pl.ds(HALO * part, HALO), :])

    @pl.when(is_fine)
    def _():
        tile = jnp.zeros((8, 128), F32)
        for kind, comp in enumerate((0, 2)):
            tile = put_column(tile, 0, 8 * kind + 4, average(in_e, (comp,), 0))
        tile = jnp.where(gz == 1, roll_lanes(tile, -4), tile)
        rtile[...] = with_halo(ytile[...], tile, gz)
        layers(10, 64, lambda i, r: half_h(e_ext, h_raw, h_ext, r, 64, fine_up_x, fine_up_y))

    @pl.when(jnp.logical_not(is_fine))
    def _():
        rtile[...] = jnp.zeros((8, 128), F32)
        layers(5, 128, lambda i, r: half_h(e_ext, h_raw, h_ext, r, 128, coarse_up_x, coarse_up_y))


def with_halo(tile, halo_tile, gz):
    lane = lanes_of(tile.shape)
    return jnp.where(lane % 8 == 4 * (1 - gz), halo_tile, tile)


def joined(own, other, gz):
    return with_halo(own, jnp.where(gz == 0, roll_lanes(other, 3), roll_lanes(other, -3)), gz)


def column_of(tile, block, sub, slot, shape, per_layer):
    row = jnp.broadcast_to(tile[sub : sub + 1, :], shape)
    wanted = 32 * block + slot + rows_of(shape) // per_layer
    picked = jnp.where((lanes_of(shape) == wanted) & (rows_of(shape) < 5 * per_layer), row, 0.0)
    return jnp.broadcast_to(jnp.sum(picked, axis=1, keepdims=True), shape)


def column(read, x, is_fine):
    if is_fine:
        planes = [read(pl.ds(BASE + x, 16, stride=64))]
        used = 10
    else:
        planes = [read(pl.ds(BASE + 4 * x + part, 8, stride=128)) for part in range(4)]
        used = 5
    return [jnp.where(rows_of(p.shape) < used, p, 0.0) for p in planes]


def each(fn, *columns):
    return [fn(*parts) for parts in zip(*columns, strict=True)]


def plus_y(f, ghost=0.0):
    following = f[1:] + [ghost]
    return [
        roll_lanes(jnp.where(lanes_of(p.shape) == 0, nxt, p), -1) - p
        for p, nxt in zip(f, following, strict=True)
    ]


def minus_y(f, ghost=0.0):
    previous = [ghost] + f[:-1]
    return [
        p - roll_lanes(jnp.where(lanes_of(p.shape) == 127, prv, p), 1)
        for p, prv in zip(f, previous, strict=True)
    ]


def plus_z(f):
    return [roll_rows(p, -1) - p for p in f]


def minus_z(f):
    return [p - roll_rows(p, 1) for p in f]


def add(a, b):
    return each(lambda p, q: p + q, a, b)


def sub(a, b):
    return each(lambda p, q: p - q, a, b)


def mul(a, b):
    return each(lambda p, q: p * q, a, b)


def scale(by, a):
    return [by * p for p in a]


def halved(a):
    used = 10 if len(a) == 1 else 5
    return [jnp.where(rows_of(p.shape) < used, -0.5 * p, 0.0) for p in a]


def write_planes(ref, columns):
    row = 0
    for col in columns:
        used = 10 if len(col) == 1 else 5
        for p in col:
            ref[pl.ds(row, used), :] = p[:used]
            row += used


def read_planes(ref, count, is_fine):
    used, height, parts = (10, 16, 1) if is_fine else (5, 8, 4)
    columns, row = [], 0
    for _ in range(count):
        col = []
        for _ in range(parts):
            start = min(row, ref.shape[0] - height)
            p = ref[pl.ds(start, height), :]
            if start < row:
                p = roll_rows(p, start - row)
            col.append(jnp.where(rows_of(p.shape) < used, p, 0.0))
            row += used
        columns.append(col)
    return columns


def send_x(e_ext, h_ext, c_ext, yin, yzin, rtile, to_up, to_down, ptile):
    is_fine, gz = place()

    @pl.when(is_fine)
    def _():
        shape = (16, 128)
        top = joined(yin[...], yzin[...], gz)
        r = rtile[...]
        lane, row = lanes_of(top.shape), rows_of(top.shape)
        kind = (lane % 32) // 8
        px = top - 0.5 * roll_lanes(r, -8) + 0.5 * (roll_lanes(top, -17) - roll_lanes(top, -16))
        beside = roll_rows(top, -1)
        beside = jnp.where(row == 7, jnp.where(lane >= 96, 0.0, roll_lanes(beside, -32)), beside)
        pz = top + 0.5 * roll_lanes(r, 8) - 0.5 * (roll_lanes(beside, -8) - roll_lanes(top, -8))
        plane = jnp.where(kind == 0, px, jnp.where(kind == 1, pz, 0.0))
        ptile[...] = plane
        px0 = column_of(plane, 0, 0, 0, shape, 2)
        px63 = column_of(plane, 3, 7, 0, shape, 2)
        pz63 = column_of(plane, 3, 7, 8, shape, 2)
        ey_top = column_of(top, 0, 0, 16, shape, 2)

        def e(comp, x):
            return column(lambda rows: e_ext[comp, rows, :], x, True)

        def h(comp, x):
            return column(lambda rows: h_ext[comp, rows, :], x, True)

        def c(x):
            return column(lambda rows: c_ext[rows, :], x, True)

        ey0, ez0 = e(1, 0), e(2, 0)
        hx, hy, hz = h(0, 0), h(1, 0), h(2, 0)
        c0 = c(0)
        ey0_next = add(ey0, mul(c0, sub(minus_z(hx), hz)))
        ez0_next = add(ez0, mul(c0, sub(hy, minus_y(hx, px0))))
        write_planes(to_down, [ey0, ez0, ey0_next, ez0_next, c0, [ey_top]])
        hx, hy, hz = h(0, 63), h(1, 63), h(2, 63)
        hy62, hz62 = h(1, 62), h(2, 62)
        c63 = c(63)
        ex_next = add(e(0, 63), mul(c63, sub(minus_y(hz, pz63), minus_z(hy))))
        ey_next = add(e(1, 63), mul(c63, sub(minus_z(hx), sub(hz, hz62))))
        ez_next = add(e(2, 63), mul(c63, sub(sub(hy, hy62), minus_y(hx, px63))))
        write_planes(to_up, [hy, hz, ex_next, ey_next, ez_next, c63])

    @pl.when(jnp.logical_not(is_fine))
    def _():
        shape = (8, 128)
        top = joined(yin[...], yzin[...], gz)
        ptile[...] = top
        rx = column_of(top, 3, 7, 0, shape, 1)

        def e(comp, x):
            return column(lambda rows: e_ext[comp, rows, :], x, False)

        def h(comp, x):
            return column(lambda rows: h_ext[comp, rows, :], x, False)

        hz = h(2, 31)
        hz[3] = hz[3] + jnp.where(lanes_of(shape) == 127, 0.5 * rx, 0.0)
        write_planes(to_down, [e(1, 0), e(2, 0)])
        write_planes(to_up, [h(1, 31), hz])


def advance(
    e_ext, h_ext, c_ext, ptile, e_out, h_out, e_edge, h_edge, e_mid, h_mid, e_last, plane, sems
):
    is_fine, gz = place()
    own = pl.multiple_of(BASE + HALO * gz, 128)

    def write(source, target, layer, sem):
        rows = pl.ds(pl.multiple_of(own + 64 * layer, 64), 64)
        return pltpu.make_async_copy(source.at[:, rows], target.at[:, layer], sem)

    def keep_edges(source, target):
        for comp in range(3):
            for layer in range(8):
                for edge in range(2):
                    rows = pl.ds(pl.multiple_of(own + 64 * layer + 56 * edge, 8), 8)
                    target[edge, comp, pl.ds(8 * layer, 8), :] = source[comp, rows, :]

    @pl.when(is_fine)
    def _():
        tile = ptile[...]
        for kind in range(2):
            for layer in range(5):
                for block in range(4):
                    value = roll_lanes(tile, 127 - (32 * block + 8 * kind + layer))
                    for step in range(2):
                        plane[kind, pl.ds(BASE + 64 * layer + 16 * block + step, 8, stride=2), :] = value
        for comp in range(3):
            e_mid[comp, pl.ds(BASE + ROWS + HALO, HALO), :] = jnp.zeros((HALO, 128), F32)
            h_mid[comp, pl.ds(0, BASE), :] = jnp.zeros((BASE, 128), F32)

        def ghosts(index):
            rows = pl.ds(pl.multiple_of(BASE + 64 * (index // 2), 64), 64)
            return (
                lambda f: fine_down_y(f, plane[0, rows, :]),
                lambda f: fine_down_y(f, plane[1, rows, :]),
            )

        layers(
            10,
            64,
            lambda i, r: half_e(h_ext, e_ext, e_mid, c_ext, r, 64, fine_down_x, *ghosts(i)),
        )
        layers(10, 64, lambda i, r: half_h(e_mid, h_ext, h_mid, r, 64, fine_up_x, fine_up_y))
        for layer in range(8):
            write(h_mid, h_out, layer, sems.at[0]).start()

        def last(index, carry):
            row = pl.multiple_of(own + 64 * index, 64)
            layer = index + 2 * gz
            half_e(h_mid, e_mid, e_last, c_ext, row, 64, fine_down_x, *ghosts(layer))
            write(e_last, e_out, index, sems.at[1]).start()
            return carry

        lax.fori_loop(0, 8, last, 0)
        keep_edges(h_mid, h_edge)
        keep_edges(e_last, e_edge)
        for layer in range(8):
            write(h_mid, h_out, layer, sems.at[0]).wait()
            write(e_last, e_out, layer, sems.at[1]).wait()

    @pl.when(jnp.logical_not(is_fine))
    def _():
        tile = ptile[...]
        for comp in range(3):
            h_mid[comp, pl.ds(0, BASE), :] = jnp.zeros((BASE, 128), F32)
            for part in range(5):
                rows = pl.ds(BASE + HALO * part, HALO)
                h_mid[comp, rows, :] = h_ext[comp, rows, :]
        lane = lanes_of((8, 128))
        for layer in range(5):
            for block in range(4):
                rows = pl.ds(BASE + 128 * layer + 32 * block + 3, 8, stride=4)
                rx = roll_lanes(tile, 127 - (32 * block + layer))
                rz = roll_lanes(tile, 127 - (32 * block + 8 + layer))
                h_mid[0, rows, :] = h_mid[0, rows, :] - jnp.where(lane == 127, 0.5 * rz, 0.0)
                h_mid[2, rows, :] = h_mid[2, rows, :] + jnp.where(lane == 127, 0.5 * rx, 0.0)
        for layer in range(8):
            write(h_mid, h_out, layer, sems.at[0]).start()

        def last(index, carry):
            row = pl.multiple_of(own + 128 * index, 128)
            half_e(h_mid, e_ext, e_last, c_ext, row, 128, coarse_down_x, coarse_down_y, coarse_down_y)
            write(e_last, e_out, 2 * index, sems.at[1]).start()
            write(e_last, e_out, 2 * index + 1, sems.at[1]).start()
            return carry

        lax.fori_loop(0, 4, last, 0)
        keep_edges(h_mid, h_edge)
        keep_edges(e_last, e_edge)
        for layer in range(8):
            write(h_mid, h_out, layer, sems.at[0]).wait()
            write(e_last, e_out, layer, sems.at[1]).wait()


def correct(
    up_own, down_own, from_below, from_above, c_ext, e_edge, h_edge, e_in, h_in, e_out, h_out, e_tile, h_tile, sems
):
    is_fine, gz = place()
    for edge in range(2):
        for comp in range(3):
            e_tile[edge, comp] = e_edge[edge, comp]
            h_tile[edge, comp] = h_edge[edge, comp]

    def put(ref, edge, comp, x, change):
        if len(change) == 1:
            moved = pltpu.roll(change[0], 16 - 2 * gz, 0)[:8]
            rows = pl.ds(x % 8, 8, stride=8)
            ref[edge, comp, rows, :] = ref[edge, comp, rows, :] + moved
        else:
            for part in range(4):
                moved = pltpu.roll(change[part], 8 - gz, 0)[:4]
                rows = pl.ds(12 * edge + part, 4, stride=16)
                ref[edge, comp, rows, :] = ref[edge, comp, rows, :] + moved

    @pl.when(is_fine)
    def _():
        zero = [jnp.zeros((16, 128), F32)]

        def c(x):
            return column(lambda rows: c_ext[rows, :], x, True)

        ey64, ez64, ey64_part, ez64_part, c64, ey_top = read_planes(from_above, 6, True)
        hy63, hz63 = read_planes(up_own, 2, True)
        c62, c63 = c(62), c(63)
        ghost = -0.5 * ey_top[0]
        dhy, dhz = scale(0.5, ez64), scale(-0.5, ey64)
        dex = mul(c63, sub(minus_y(dhz, ghost), minus_z(dhy)))
        dey = scale(-1.0, mul(c63, dhz))
        dez = mul(c63, dhy)
        dex62 = mul(c62, minus_y(zero, ghost))
        ey64_next = add(ey64_part, mul(c64, add(hz63, dhz)))
        ez64_next = sub(ez64_part, mul(c64, add(hy63, dhy)))
        dhx2 = halved(sub(plus_y(dez), plus_z(dey)))
        dhy2 = add(dhy, halved(sub(plus_z(dex), sub(ez64_next, dez))))
        dhz2 = add(dhz, halved(sub(sub(ey64_next, dey), plus_y(dex))))
        dhy62 = halved(sub(plus_z(dex62), dez))
        dhz62 = halved(sub(dey, plus_y(dex62)))
        put(h_tile, 1, 0, 63, dhx2)
        put(h_tile, 1, 1, 63, dhy2)
        put(h_tile, 1, 2, 63, dhz2)
        put(h_tile, 1, 1, 62, dhy62)
        put(h_tile, 1, 2, 62, dhz62)
        put(e_tile, 1, 0, 63, add(dex, mul(c63, sub(minus_y(dhz2, ghost), minus_z(dhy2)))))
        put(e_tile, 1, 1, 63, add(dey, mul(c63, sub(minus_z(dhx2), sub(dhz2, dhz62)))))
        put(e_tile, 1, 2, 63, add(dez, mul(c63, sub(sub(dhy2, dhy62), minus_y(dhx2)))))
        put(e_tile, 1, 0, 62, add(dex62, mul(c62, sub(minus_y(dhz62, ghost), minus_z(dhy62)))))
        put(e_tile, 1, 1, 62, scale(-1.0, mul(c62, dhz62)))
        put(e_tile, 1, 2, 62, mul(c62, dhy62))

        hy_part, hz_part, ex_part, ey_part, ez_part, cm = read_planes(from_below, 6, True)
        ey0, ez0, ey0_part, ez0_part, c0, ey_top = read_planes(down_own, 6, True)
        c1 = c(1)
        ghost = -0.5 * ey_top[0]
        dhy, dhz = scale(0.5, ez0), scale(-0.5, ey0)
        hym, hzm = add(hy_part, dhy), add(hz_part, dhz)
        exm = add(ex_part, mul(cm, sub(minus_y(dhz, ghost), minus_z(dhy))))
        eym = sub(ey_part, mul(cm, dhz))
        ezm = add(ez_part, mul(cm, dhy))
        dey, dez = mul(c0, hzm), scale(-1.0, mul(c0, hym))
        dhx2 = halved(sub(plus_y(dez), plus_z(dey)))
        dhy2 = scale(-0.5, dez)
        dhz2 = scale(0.5, dey)
        hym2 = add(hym, halved(sub(plus_z(exm), sub(add(ez0_part, dez), ezm))))
        hzm2 = add(hzm, halved(sub(sub(add(ey0_part, dey), eym), plus_y(exm))))
        put(h_tile, 0, 0, 0, dhx2)
        put(h_tile, 0, 1, 0, dhy2)
        put(h_tile, 0, 2, 0, dhz2)
        put(e_tile, 0, 0, 0, mul(c0, sub(minus_y(dhz2), minus_z(dhy2))))
        put(e_tile, 0, 1, 0, add(dey, mul(c0, sub(minus_z(dhx2), sub(dhz2, hzm2)))))
        put(e_tile, 0, 2, 0, add(dez, mul(c0, sub(sub(dhy2, hym2), minus_y(dhx2)))))
        put(e_tile, 0, 1, 1, mul(c1, dhz2))
        put(e_tile, 0, 2, 1, scale(-1.0, mul(c1, dhy2)))

    @pl.when(jnp.logical_not(is_fine))
    def _():
        def c(x):
            return column(lambda rows: c_ext[rows, :], x, False)

        ey32, ez32 = read_planes(from_above, 2, False)
        c31 = c(31)
        dhy, dhz = scale(0.5, ez32), scale(-0.5, ey32)
        put(h_tile, 1, 1, 31, dhy)
        put(h_tile, 1, 2, 31, dhz)
        put(e_tile, 1, 0, 31, mul(c31, sub(minus_y(dhz), minus_z(dhy))))
        put(e_tile, 1, 1, 31, scale(-1.0, mul(c31, dhz)))
        put(e_tile, 1, 2, 31, mul(c31, dhy))
        hy_part, hz_part = read_planes(from_below, 2, False)
        ey0, ez0 = read_planes(down_own, 2, False)
        c0 = c(0)
        put(e_tile, 0, 1, 0, mul(c0, add(hz_part, scale(-0.5, ey0))))
        put(e_tile, 0, 2, 0, scale(-1.0, mul(c0, add(hy_part, scale(0.5, ez0)))))

    copies = []
    for edge in range(2):
        for slot, (tile, out) in enumerate(((h_tile, h_out), (e_tile, e_out))):
            copies.append(
                pltpu.make_async_copy(
                    tile.at[edge].reshape(3, 8, 8, 128),
                    out.at[:, :, pl.ds(56 * edge, 8), :],
                    sems.at[2 * edge + slot],
                )
            )
    for copy in copies:
        copy.start()
    for copy in copies:
        copy.wait()


def across(x, dx=0, dy=0, dz=0):
    nx, ny, nz = lax.axis_size("gx"), lax.axis_size("gy"), lax.axis_size("gz")
    pairs = [
        ((i * ny + j) * nz + k, ((i + dx) % nx * ny + (j + dy) % ny) * nz + (k + dz) % nz)
        for i in range(nx)
        for j in range(ny)
        for k in range(nz)
    ]
    return lax.ppermute(x, ("gx", "gy", "gz"), pairs)


def fast_shards(electric, magnetic, material, permittivity):
    e = electric.reshape(3, ROWS, 128)
    h = magnetic.reshape(3, ROWS, 128)
    m = material.reshape(ROWS, 128)
    dma = pltpu.SemaphoreType.DMA
    e_own, h_own, m_own, zmsg_e, zmsg_h, zmsg_m, ytile = kernel_call(
        gather,
        [
            vmem(3, ROWS, 128),
            vmem(3, ROWS, 128),
            vmem(ROWS, 128, dtype=jnp.int32),
            vmem(3, HALO, 128),
            vmem(3, HALO, 128),
            vmem(HALO, 128, dtype=jnp.int32),
            vmem(8, 128),
        ],
        [HBM] * 3,
        [VM] * 7,
        [dma((10,))],
    )(e, h, m)
    in_e, in_h, in_m = (across(part, dz=1) for part in (zmsg_e, zmsg_h, zmsg_m))
    yzin = across(ytile, dy=1, dz=1)
    yin = across(ytile, dy=1)
    e_ext, h_ext, c_ext, rtile = kernel_call(
        extend,
        [vmem(3, EXT, 128), vmem(3, EXT, 128), vmem(EXT, 128), vmem(8, 128)],
        [VM] * 6 + [pl.BlockSpec(memory_space=pltpu.SMEM), VM],
        [VM] * 4,
        [pltpu.VMEM((3, BASE + ROWS + HALO, 128), F32)],
    )(*(held(part) for part in (e_own, h_own, m_own, in_e, in_h, in_m)), permittivity, held(ytile))
    to_up, to_down, ptile = kernel_call(
        send_x,
        [vmem(64, 128), vmem(64, 128), vmem(8, 128)],
        [VM] * 6,
        [VM] * 3,
    )(*(held(part) for part in (e_ext, h_ext, c_ext, yin, yzin, rtile)))
    from_below = across(to_up, dx=1)
    from_above = across(to_down, dx=-1)
    whole = jax.ShapeDtypeStruct((3, 8, 64, 128), F32)
    e_out, h_out, e_edge, h_edge = kernel_call(
        advance,
        [whole, whole, vmem(2, 3, 64, 128), vmem(2, 3, 64, 128)],
        [VM] * 4,
        [HBM, HBM, VM, VM],
        [pltpu.VMEM((3, EXT, 128), F32)] * 3 + [pltpu.VMEM((2, EXT, 128), F32), dma((2,))],
    )(*(held(part) for part in (e_ext, h_ext, c_ext, ptile)))
    e_out, h_out = kernel_call(
        correct,
        [whole, whole],
        [VM] * 7 + [HBM] * 2,
        [HBM] * 2,
        [pltpu.VMEM((2, 3, 64, 128), F32)] * 2 + [dma((4,))],
        aliases={7: 0, 8: 1},
    )(
        *(held(part) for part in (to_up, to_down, from_below, from_above, c_ext, e_edge, h_edge)),
        e_out,
        h_out,
    )
    return e_out.reshape(electric.shape), h_out.reshape(magnetic.shape)


def solution(mesh):
    placed = (
        P(("parts", "gy"), "gx", "gz", None, None),
        P(("parts", "gy"), "gx", "gz", None, None),
        P(("parts", "gy"), "gx", "gz", None),
        P(),
    )
    fast = mesh.shape["gy"] == 2 and mesh.shape["gz"] == 2
    return jax.shard_map(
        fast_shards if fast else general_shards,
        mesh=mesh,
        in_specs=placed,
        out_specs=(
            P(("parts", "gy"), "gx", "gz", None, None),
            P(("parts", "gy"), "gx", "gz", None, None),
        ),
        check_vma=False,
    )
```

```python
from functools import partial

import jax
import jax.numpy as jnp
from jax import lax
from jax.experimental import pallas as pl
from jax.experimental.pallas import tpu as pltpu
from jax.sharding import PartitionSpec as P

CZ = 4
CX = 32
CY = 512
MATS = 4


courant = 0.5


def passed_along(x, axis, by):
    devices = lax.axis_size(axis)
    return lax.ppermute(x, axis, [(i, (i + by) % devices) for i in range(devices)])


def from_behind(x, axis, by):
    devices = lax.axis_size(axis)
    pairs = [(i, i + by) for i in range(devices) if 0 <= i + by < devices]
    return lax.ppermute(x, axis, pairs)


def forward_diff(values, dim_axis, ghost_plane):
    shifted = jnp.concatenate(
        [
            lax.slice_in_dim(values, 1, values.shape[dim_axis], axis=dim_axis),
            jnp.expand_dims(ghost_plane, dim_axis),
        ],
        axis=dim_axis,
    )
    return shifted - values


def backward_diff(values, dim_axis, ghost_plane):
    shifted = jnp.concatenate(
        [
            jnp.expand_dims(ghost_plane, dim_axis),
            lax.slice_in_dim(values, 0, values.shape[dim_axis] - 1, axis=dim_axis),
        ],
        axis=dim_axis,
    )
    return values - shifted


def curl_with(differ, vectors, ghost_depth, ghost_width, ghost_height):
    ghosts = (ghost_depth, ghost_width, ghost_height)

    def along_axis(component, dim_axis):
        return differ(vectors[component], dim_axis, ghosts[dim_axis][component])

    curl_x = along_axis(2, 2) - along_axis(1, 0)
    curl_y = along_axis(0, 0) - along_axis(2, 1)
    curl_z = along_axis(1, 1) - along_axis(0, 2)
    return jnp.stack([curl_x, curl_y, curl_z])


def restrict(face_plane):
    quads = face_plane.reshape(3, face_plane.shape[1] // 2, 2, face_plane.shape[2] // 2, 2)
    return (
        quads[:, :, 0, :, 0] + quads[:, :, 0, :, 1] + (quads[:, :, 1, :, 0] + quads[:, :, 1, :, 1])
    ) * 0.25


def enlarge(face_plane):
    return jnp.repeat(jnp.repeat(face_plane, 2, axis=1), 2, axis=2)


def lookup(material, permittivity):
    permit_sum = jnp.zeros(material.shape, jnp.float32)
    for material_id in range(MATS):
        permit_sum = permit_sum + jnp.where(material == material_id, permittivity[material_id], 0.0)
    return courant / permit_sum


def pack_face(face_plane, length):
    flat_face = face_plane.reshape(3, -1)
    if flat_face.shape[1] < length:
        flat_face = jnp.concatenate(
            [flat_face, jnp.zeros((3, length - flat_face.shape[1]), flat_face.dtype)], axis=1
        )
    return flat_face


def unpack_face(flat_face, row_count, col_count):
    return flat_face[:, : row_count * col_count].reshape(3, row_count, col_count)


def level_height(got_height, is_fine):
    return got_height if is_fine else restrict(got_height)


def low_faces(grid_shape, is_fine, flat_field):
    vectors = flat_field.reshape((3,) + grid_shape)
    face_plane = vectors[:, :, :, 0]
    if not is_fine:
        face_plane = enlarge(face_plane)
    return (
        pack_face(vectors[:, :, 0, :], CZ * CY),
        pack_face(vectors[:, 0, :, :], CX * CY),
        face_plane,
    )


def high_faces(grid_shape, is_fine, flat_field):
    vectors = flat_field.reshape((3,) + grid_shape)
    face_plane = vectors[:, :, :, -1]
    if not is_fine:
        face_plane = enlarge(face_plane)
    return (
        pack_face(vectors[:, :, -1, :], CZ * CY),
        pack_face(vectors[:, -1, :, :], CX * CY),
        face_plane,
    )


def advance_magnetic(
    grid_shape, is_fine, does_move, e_flat, h_flat, got_width, got_depth, got_height
):
    if not does_move:
        return h_flat
    deep_cells, wide_cells, tall_cells = grid_shape
    vectors = e_flat.reshape((3,) + grid_shape)
    curl_term = curl_with(
        forward_diff,
        vectors,
        unpack_face(got_depth, wide_cells, tall_cells),
        unpack_face(got_width, deep_cells, tall_cells),
        level_height(got_height, is_fine),
    )
    return (h_flat.reshape((3,) + grid_shape) - courant * curl_term).reshape(3, -1)


def advance_electric(
    grid_shape, is_fine, does_move, e_flat, h_flat, coefficient, got_width, got_depth, got_height
):
    if not does_move:
        return e_flat
    deep_cells, wide_cells, tall_cells = grid_shape
    magnetic = h_flat.reshape((3,) + grid_shape)
    curl_term = curl_with(
        backward_diff,
        magnetic,
        unpack_face(got_depth, wide_cells, tall_cells),
        unpack_face(got_width, deep_cells, tall_cells),
        level_height(got_height, is_fine),
    )
    return (
        e_flat.reshape((3,) + grid_shape) + coefficient.reshape(grid_shape) * curl_term
    ).reshape(3, -1)


def pass_width(face_plane, offset):
    return passed_along(face_plane, "gx", offset)


def pass_depth(face_plane, offset):
    return from_behind(face_plane, "gz", offset)


def pass_height(face_plane, offset):
    return from_behind(face_plane, "gy", offset)


def general_shards(electric, magnetic, material, permittivity):
    cell_count = electric.shape[-1]
    e_flat = electric.reshape(3, cell_count)
    h_flat = magnetic.reshape(3, cell_count)
    coefficient = lookup(material.reshape(cell_count), permittivity)
    is_fine = lax.axis_index("gy") >= lax.axis_size("gy") // 2
    coarse_shape = (CZ, CX, CY)
    fine_shape = (2 * CZ, 2 * CX, CY // 4)
    for substep in range(2):
        coarse_moves = substep == 0
        face_width, face_depth, face_height = lax.cond(
            is_fine,
            partial(low_faces, fine_shape, True),
            partial(low_faces, coarse_shape, False),
            e_flat,
        )
        got_depth = pass_depth(face_depth, -1)
        got_height = pass_height(face_height, -1)
        got_width = pass_width(face_width, -1)
        h_flat = lax.cond(
            is_fine,
            partial(advance_magnetic, fine_shape, True, True),
            partial(advance_magnetic, coarse_shape, False, coarse_moves),
            e_flat,
            h_flat,
            got_width,
            got_depth,
            got_height,
        )
        rim_width, rim_depth, rim_height = lax.cond(
            is_fine,
            partial(high_faces, fine_shape, True),
            partial(high_faces, coarse_shape, False),
            h_flat,
        )
        rim_depth = pass_depth(rim_depth, 1)
        rim_height = pass_height(rim_height, 1)
        rim_width = pass_width(rim_width, 1)
        e_flat = lax.cond(
            is_fine,
            partial(advance_electric, fine_shape, True, True),
            partial(advance_electric, coarse_shape, False, coarse_moves),
            e_flat,
            h_flat,
            coefficient,
            rim_width,
            rim_depth,
            rim_height,
        )
    return (e_flat.reshape(electric.shape), h_flat.reshape(magnetic.shape))


ROWS = 512
HALO = 128
EXT = 1296
LIMIT = 40 * 1024 * 1024
F32 = jnp.float32
VM = pl.BlockSpec(memory_space=pltpu.VMEM)
HBM = pl.BlockSpec(memory_space=pltpu.HBM)
CHUNK = 32


class Fine:
    depth, stride, count, own, step, used, height, parts, last = 64, 72, 10, 8, 1, 10, 16, 1, 63


class Coarse:
    depth, stride, count, own, step, used, height, parts, last = 128, 144, 5, 4, 4, 5, 8, 4, 31


def vmem(*shape, dtype=F32):
    return pltpu.VMEM(shape, dtype)


def held(x):
    return pltpu.with_memory_space_constraint(x, pltpu.VMEM)


def far(x):
    return pltpu.with_memory_space_constraint(x, pltpu.HBM)


def kernel_call(body, out_shape, in_specs, out_specs, scratch=(), aliases=None):
    return pl.pallas_call(
        body,
        out_shape=out_shape,
        in_specs=in_specs,
        out_specs=out_specs,
        scratch_shapes=list(scratch),
        input_output_aliases=aliases or {},
        compiler_params=pltpu.CompilerParams(vmem_limit_bytes=LIMIT),
    )


def by_level(body):
    is_fine = lax.axis_index("gy") >= lax.axis_size("gy") // 2
    gz = lax.axis_index("gz")
    pl.when(is_fine)(lambda: body(Fine, gz))
    pl.when(jnp.logical_not(is_fine))(lambda: body(Coarse, gz))


def lanes_of(shape):
    return lax.broadcasted_iota(jnp.int32, shape, len(shape) - 1)


def rows_of(shape):
    return lax.broadcasted_iota(jnp.int32, shape, len(shape) - 2)


def roll_lanes(x, by):
    return pltpu.roll(x, by % 128, 1)


def roll_rows(x, by):
    return pltpu.roll(x, by % x.shape[0], 0)


def layer_row(grid, index):
    return pl.multiple_of(grid.stride * (index + 1), 8)


def own_first(grid, gz):
    return (grid.count - grid.own) * gz


def halo_first(grid, gz):
    return grid.own * (1 - gz)


def clear_pads(grid, ref, *zero_layers):
    for comp in range(3):
        for index in range(grid.count + 2):
            start, size = grid.stride * index, grid.stride
            if index not in zero_layers:
                start, size = start + grid.depth, size - grid.depth
            ref[comp, pl.ds(start, size), :] = jnp.zeros((size, 128), F32)


def own_layers(grid, ref, gz):
    view = ref.reshape(3, EXT // grid.stride, grid.stride, 128)
    return view.at[:, pl.ds(1 + own_first(grid, gz), grid.own), pl.ds(0, grid.depth), :]


def block_layers(grid, ref):
    return ref.reshape(3, grid.own, grid.depth, 128)


def at_lane(tile, lane_from, lane_to, value):
    lane = lanes_of(value.shape)
    return jnp.where(lane == lane_to, roll_lanes(value, lane_to - lane_from), tile)


def average(ref, lead, row, stride):
    steps = (0, 1, stride, stride + 1)
    quad = [ref[lead, pl.ds(row + step, 32, stride=2), :] for step in steps]
    return ((quad[0] + quad[1]) + (quad[2] + quad[3])) * 0.25


def put_column(tile, lane_from, slot, column):
    for block in range(4):
        tile = at_lane(tile, lane_from, 32 * block + slot, column[8 * block : 8 * block + 8])
    return tile


def gather(e_hbm, h_hbm, m_hbm, e_ext, zmsg, ytile, h_top, m_edge, sems):
    def body(grid, gz):
        edge = pl.ds((1 - gz) * (ROWS - HALO), HALO)
        source, target = block_layers(grid, e_hbm), own_layers(grid, e_ext, gz)
        first = [0, 2] if grid is Fine else [0, 1, 2]
        e_loads = {
            comp: pltpu.make_async_copy(source.at[comp], target.at[comp], sems.at[comp])
            for comp in (0, 2, 1)
        }
        h_loads = [] if grid is Fine else [
            pltpu.make_async_copy(h_hbm.at[comp], h_top.at[comp], sems.at[3 + comp]) for comp in (0, 2)
        ]
        loads = [
            pltpu.make_async_copy(h_hbm.at[:, edge], zmsg.at[pl.ds(3, 3)], sems.at[6]),
            pltpu.make_async_copy(m_hbm.at[edge], m_edge, sems.at[7]),
        ]
        for load in list(e_loads.values()) + h_loads + loads:
            load.start()
        clear_pads(grid, e_ext, grid.count + 1)
        for comp in first:
            e_loads[comp].wait()
        for load in h_loads:
            load.wait()
        begin = layer_row(grid, own_first(grid, gz))
        tile = jnp.zeros((8, 128), F32)
        for layer in range(4):
            if grid is Fine:
                row = begin + 2 * grid.stride * layer
                tile = put_column(tile, 0, layer, average(e_ext, 0, row, grid.stride))
                tile = put_column(tile, 0, 8 + layer, average(e_ext, 2, row, grid.stride))
            else:
                top = pl.ds(begin + grid.stride * layer + 3, 32, stride=4)
                h_row = pl.ds(grid.depth * layer + 3, 32, stride=4)
                ex, ey, ez = (e_ext[comp, top, :] for comp in range(3))
                tile = put_column(tile, 127, layer, h_top[0, h_row, :] + 0.5 * ez)
                tile = put_column(tile, 127, 8 + layer, h_top[2, h_row, :] - 0.5 * ex)
                tile = put_column(tile, 127, 16 + layer, ey)
        ytile[...] = jnp.where(gz == 1, roll_lanes(tile, 1), tile)
        if grid is Fine:
            e_loads[1].wait()
        layers = HALO // grid.depth
        from_layer = own_first(grid, gz) + (grid.own - layers) * (1 - gz)
        for comp in range(3):
            for layer in range(layers):
                row = layer_row(grid, from_layer + layer)
                zmsg[comp, pl.ds(grid.depth * layer, grid.depth), :] = e_ext[comp, pl.ds(row, grid.depth), :]
        for load in loads:
            load.wait()
        zmsg[6] = m_edge[...].astype(F32)

    by_level(body)


def up_y(grid, ref, comp, row, f):
    lane = lanes_of(f.shape)
    if grid is Fine:
        return jnp.where(lane == 127, 0.0, roll_lanes(f, -1))
    following = ref[comp, pl.ds(row + 1, f.shape[0]), :]
    following = jnp.where(rows_of(f.shape) % 4 == 3, 0.0, following)
    return roll_lanes(jnp.where(lane == 0, following, f), -1)


def down_y(grid, ref, comp, row, f, ghost):
    lane = lanes_of(f.shape)
    if grid is Fine:
        return roll_lanes(jnp.where(lane == 127, ghost, f), 1)
    previous = ref[comp, pl.ds(row - 1, f.shape[0]), :]
    previous = jnp.where(rows_of(f.shape) % 4 == 0, 0.0, previous)
    return roll_lanes(jnp.where(lane == 127, previous, f), 1)


def half_h(grid, e, h_from, from_row, h_to, row):
    for start in range(0, grid.depth, CHUNK):
        r = row + start
        here = pl.ds(r, CHUNK)
        ex, ey, ez = (e[comp, here, :] for comp in range(3))
        above, beside = pl.ds(r + grid.stride, CHUNK), pl.ds(r + grid.step, CHUNK)
        h0 = [h_from(comp, pl.ds(from_row + start, CHUNK)) for comp in range(3)]
        ez_y, ex_y = up_y(grid, e, 2, r, ez), up_y(grid, e, 0, r, ex)
        h_to[0, here, :] = h0[0] - 0.5 * ((ez_y - ez) - (e[1, above, :] - ey))
        h_to[1, here, :] = h0[1] - 0.5 * ((e[0, above, :] - ex) - (e[2, beside, :] - ez))
        h_to[2, here, :] = h0[2] - 0.5 * ((e[1, beside, :] - ey) - (ex_y - ex))


def half_e(grid, h, e_from, e_to, c_ref, row, ghosts):
    for start in range(0, grid.depth, CHUNK):
        r = row + start
        here = pl.ds(r, CHUNK)
        hx, hy, hz = (h[comp, here, :] for comp in range(3))
        below, beside = pl.ds(r - grid.stride, CHUNK), pl.ds(r - grid.step, CHUNK)
        px, pz = ghosts(start)
        hx_y, hz_y = down_y(grid, h, 0, r, hx, px), down_y(grid, h, 2, r, hz, pz)
        c = c_ref[here, :]
        e_to[0, here, :] = e_from[0, here, :] + c * ((hz - hz_y) - (hy - h[1, below, :]))
        e_to[1, here, :] = e_from[1, here, :] + c * ((hx - h[0, below, :]) - (hz - h[2, beside, :]))
        e_to[2, here, :] = e_from[2, here, :] + c * ((hy - h[1, beside, :]) - (hx - hx_y))


def loop(first, count, body):
    def step(index, carry):
        body(index)
        return carry

    lax.fori_loop(first, first + count, step, 0)


def with_halo(tile, halo_tile, gz):
    lane = lanes_of(tile.shape)
    return jnp.where(lane % 8 == 4 * (1 - gz), halo_tile, tile)


def joined(own, other, gz):
    return with_halo(own, jnp.where(gz == 0, roll_lanes(other, 3), roll_lanes(other, -3)), gz)


def column_of(tile, block, sub, slot, shape, per_layer):
    row = jnp.broadcast_to(tile[sub : sub + 1, :], shape)
    wanted = 32 * block + slot + rows_of(shape) // per_layer
    picked = jnp.where((lanes_of(shape) == wanted) & (rows_of(shape) < 5 * per_layer), row, 0.0)
    return jnp.broadcast_to(jnp.sum(picked, axis=1, keepdims=True), shape)


def column(grid, read, x):
    begin = grid.stride + grid.step * x
    planes = [read(pl.ds(begin + part, grid.height, stride=grid.stride)) for part in range(grid.parts)]
    return [jnp.where(rows_of(p.shape) < grid.used, p, 0.0) for p in planes]


def each(fn, *columns):
    return [fn(*parts) for parts in zip(*columns, strict=True)]


def plus_y(f, ghost=0.0):
    following = f[1:] + [ghost]
    return [
        roll_lanes(jnp.where(lanes_of(p.shape) == 0, nxt, p), -1) - p
        for p, nxt in zip(f, following, strict=True)
    ]


def minus_y(f, ghost=0.0):
    previous = [ghost] + f[:-1]
    return [
        p - roll_lanes(jnp.where(lanes_of(p.shape) == 127, prv, p), 1)
        for p, prv in zip(f, previous, strict=True)
    ]


def plus_z(f):
    return [roll_rows(p, -1) - p for p in f]


def minus_z(f):
    return [p - roll_rows(p, 1) for p in f]


def add(a, b):
    return each(lambda p, q: p + q, a, b)


def sub(a, b):
    return each(lambda p, q: p - q, a, b)


def mul(a, b):
    return each(lambda p, q: p * q, a, b)


def scale(by, a):
    return [by * p for p in a]


def halved(a):
    used = 10 if len(a) == 1 else 5
    return [jnp.where(rows_of(p.shape) < used, -0.5 * p, 0.0) for p in a]


def write_planes(grid, ref, columns):
    row = 0
    for col in columns:
        for p in col:
            ref[pl.ds(row, grid.used), :] = p[: grid.used]
            row += grid.used


def read_plane(grid, ref, row):
    start = min(row, ref.shape[0] - grid.height)
    p = ref[pl.ds(start, grid.height), :]
    if start < row:
        p = roll_rows(p, start - row)
    return jnp.where(rows_of(p.shape) < grid.used, p, 0.0)


def read_planes(grid, ref, *wanted):
    used, parts = grid.used, grid.parts
    return [[read_plane(grid, ref, used * (parts * i + part)) for part in range(parts)] for i in wanted]


def extend(e_in, h_own, m_own, zmsg, permittivity, ytile, e_ext, h_ext, c_ext, rtile, up, down):
    def body(grid, gz):
        values = [0.5 / jnp.full((CHUNK, 128), permittivity[i], F32) for i in range(MATS)]

        def coef(is_material):
            found = values[MATS - 1]
            for i in range(MATS - 2, -1, -1):
                found = jnp.where(is_material(i), values[i], found)
            return found

        clear_pads(grid, h_ext, 0)
        halo = halo_first(grid, gz)
        for layer in range(grid.count - grid.own):
            for start in range(0, grid.depth, CHUNK):
                rows = pl.ds(layer_row(grid, halo + layer) + start, CHUNK)
                from_rows = pl.ds(grid.depth * layer + start, CHUNK)
                for comp in range(3):
                    e_ext[comp, rows, :] = zmsg[comp, from_rows, :]
                material = zmsg[6, from_rows, :]
                c_ext[rows, :] = coef(lambda i, m=material: m == float(i))
        for layer in range(grid.count - grid.own):
            row = layer_row(grid, halo + layer)
            half_h(
                grid, e_ext, lambda comp, rows: zmsg[3 + comp, rows, :], grid.depth * layer, h_ext, row
            )

        def own(index):
            row = layer_row(grid, own_first(grid, gz) + index)
            from_row = pl.multiple_of(grid.depth * index, 8)
            half_h(grid, e_ext, lambda comp, rows: h_own[comp, rows, :], from_row, h_ext, row)
            for start in range(0, grid.depth, CHUNK):
                material = m_own[pl.ds(from_row + start, CHUNK), :]
                c_ext[pl.ds(row + start, CHUNK), :] = coef(lambda i, m=material: m == i)

        loop(0, grid.own, own)

        def e(comp, x):
            return column(grid, lambda rows: e_ext[comp, rows, :], x)

        def h(comp, x):
            return column(grid, lambda rows: h_ext[comp, rows, :], x)

        def c(x):
            return column(grid, lambda rows: c_ext[rows, :], x)

        last = grid.last
        if grid is Coarse:
            rtile[...] = jnp.zeros((8, 128), F32)
            write_planes(grid, down, [e(1, 0), e(2, 0)])
            write_planes(grid, up, [h(1, last), h(2, last)])
            return
        tile = jnp.zeros((8, 128), F32)
        for kind, comp in enumerate((0, 2)):
            tile = put_column(tile, 0, 8 * kind + 4, average(zmsg, comp, 0, grid.depth))
        tile = jnp.where(gz == 1, roll_lanes(tile, -4), tile)
        rtile[...] = with_halo(ytile[...], tile, gz)
        ey, ez, hx, hy, hz, c0 = e(1, 0), e(2, 0), h(0, 0), h(1, 0), h(2, 0), c(0)
        ey_next = add(ey, mul(c0, sub(minus_z(hx), hz)))
        ez_next = add(ez, mul(c0, sub(hy, minus_y(hx))))
        write_planes(grid, down, [ey, ez, ey_next, ez_next, c0])
        hx, hy, hz, c63 = h(0, last), h(1, last), h(2, last), c(last)
        hy62, hz62 = h(1, last - 1), h(2, last - 1)
        ex_next = add(e(0, last), mul(c63, sub(minus_y(hz), minus_z(hy))))
        ey_next = add(e(1, last), mul(c63, sub(minus_z(hx), sub(hz, hz62))))
        ez_next = add(e(2, last), mul(c63, sub(sub(hy, hy62), minus_y(hx))))
        write_planes(grid, up, [hy, hz, ex_next, ey_next, ez_next, c63])

    by_level(body)


def join_y(up, down, yin, yzin, rtile, to_up, to_down, ptile):
    def body(grid, gz):
        top = joined(yin[...], yzin[...], gz)
        to_up[...] = up[...]
        to_down[...] = down[...]
        shape = (grid.height, 128)
        if grid is Coarse:
            ptile[...] = top
            at = 5 * 7
            change = jnp.where(lanes_of(shape) == 127, 0.5 * column_of(top, 3, 7, 0, shape, 1), 0.0)
            to_up[pl.ds(at, 5), :] = to_up[pl.ds(at, 5), :] + change[:5]
            return
        r = rtile[...]
        lane, row = lanes_of(top.shape), rows_of(top.shape)
        kind = (lane % 32) // 8
        px = top - 0.5 * roll_lanes(r, -8) + 0.5 * (roll_lanes(top, -17) - roll_lanes(top, -16))
        beside = roll_rows(top, -1)
        beside = jnp.where(row == 7, jnp.where(lane >= 96, 0.0, roll_lanes(beside, -32)), beside)
        pz = top + 0.5 * roll_lanes(r, 8) - 0.5 * (roll_lanes(beside, -8) - roll_lanes(top, -8))
        plane = jnp.where(kind == 0, px, jnp.where(kind == 1, pz, 0.0))
        ptile[...] = plane

        def change(ref, target, index, c, value):
            change = jnp.where(lanes_of(shape) == 0, c * value, 0.0)
            rows = pl.ds(10 * index, 10)
            target[rows, :] = ref[rows, :] + change[:10]

        ((c0,),) = read_planes(grid, down, 4)
        ((c63,),) = read_planes(grid, up, 5)
        change(down, to_down, 3, c0, column_of(plane, 0, 0, 0, shape, 2))
        change(up, to_up, 4, c63, column_of(plane, 3, 7, 0, shape, 2))
        change(up, to_up, 2, c63, -column_of(plane, 3, 7, 8, shape, 2))
        to_down[pl.ds(50, 10), :] = column_of(top, 0, 0, 16, shape, 2)[:10]

    by_level(body)


def advance(
    e_ext, h_ext, c_ext, ptile, e_out, h_out, e_edge, h_edge, e_mid, h_mid, e_last, plane, sems
):
    def body(grid, gz):
        first = own_first(grid, gz)
        tile = ptile[...]

        def write(source, target, sem, layer=None):
            source, target = own_layers(grid, source, gz), block_layers(grid, target)
            if layer is not None:
                source, target = source.at[:, layer], target.at[:, layer]
            return pltpu.make_async_copy(source, target, sem)

        def keep_edges(source, target):
            for comp in range(3):
                for layer in range(grid.own):
                    for edge in range(2):
                        row = layer_row(grid, first + layer) + (grid.depth - 8) * edge
                        target[edge, comp, pl.ds(8 * layer, 8), :] = source[comp, pl.ds(row, 8), :]

        clear_pads(grid, h_mid, 0)
        if grid is Fine:
            clear_pads(grid, e_mid, grid.count + 1)
            for kind in range(2):
                for layer in range(5):
                    for block in range(4):
                        value = roll_lanes(tile, 127 - (32 * block + 8 * kind + layer))
                        for step in range(2):
                            rows = pl.ds(64 * layer + 16 * block + step, 8, stride=2)
                            plane[kind, rows, :] = value

            def ghosts(index):
                begin = 64 * (index // 2)

                def of(start):
                    rows = pl.ds(pl.multiple_of(begin + start, 8), CHUNK)
                    return plane[0, rows, :], plane[1, rows, :]

                return of

            loop(
                0,
                grid.count,
                lambda i: half_e(grid, h_ext, e_ext, e_mid, c_ext, layer_row(grid, i), ghosts(i)),
            )
            loop(
                0,
                grid.count,
                lambda i: half_h(
                    grid,
                    e_mid,
                    lambda comp, rows: h_ext[comp, rows, :],
                    layer_row(grid, i),
                    h_mid,
                    layer_row(grid, i),
                ),
            )
            h_write = write(h_mid, h_out, sems.at[0])
            h_write.start()
            e_begin = e_mid
        else:
            for comp in range(3):
                for layer in range(grid.count):
                    rows = pl.ds(layer_row(grid, layer), grid.depth)
                    h_mid[comp, rows, :] = h_ext[comp, rows, :]
            lane = lanes_of((8, 128))
            for layer in range(grid.count):
                for block in range(4):
                    rows = pl.ds(layer_row(grid, layer) + 32 * block + 3, 8, stride=4)
                    rx = roll_lanes(tile, 127 - (32 * block + layer))
                    rz = roll_lanes(tile, 127 - (32 * block + 8 + layer))
                    h_mid[0, rows, :] = h_mid[0, rows, :] - jnp.where(lane == 127, 0.5 * rz, 0.0)
                    h_mid[2, rows, :] = h_mid[2, rows, :] + jnp.where(lane == 127, 0.5 * rx, 0.0)
            h_write = write(h_mid, h_out, sems.at[0])
            h_write.start()
            e_begin = e_ext

            def ghosts(index):
                return lambda start: (0.0, 0.0)

        def last(index):
            layer = first + index
            half_e(grid, h_mid, e_begin, e_last, c_ext, layer_row(grid, layer), ghosts(layer))
            write(e_last, e_out, sems.at[1], index).start()

        loop(0, grid.own, last)
        keep_edges(h_mid, h_edge)
        keep_edges(e_last, e_edge)
        h_write.wait()
        write(e_last, e_out, sems.at[1]).wait()

    by_level(body)


def correct(
    up_own, down_own, from_below, from_above, c_ext, e_edge, h_edge, e_in, h_in, e_out, h_out, e_tile, h_tile, sems
):
    def body(grid, gz):
        last = grid.last

        def put(ref, edge, comp, x, change):
            for part, p in enumerate(change):
                moved = pltpu.roll(p, grid.height - own_first(grid, gz), 0)[: grid.own]
                rows = pl.ds(grid.step * x % 8 + part, grid.own, stride=8)
                ref[edge, comp, rows, :] = ref[edge, comp, rows, :] + moved

        def c(x):
            return column(grid, lambda rows: c_ext[rows, :], x)

        def finish(edge):
            copies = []
            for slot, (tile, out) in enumerate(((h_tile, h_out), (e_tile, e_out))):
                source = tile.at[edge].reshape(3, 8, 8, 128).at[:, pl.ds(0, grid.own)]
                target = block_layers(grid, out).at[:, :, pl.ds((grid.depth - 8) * edge, 8), :]
                copies.append(pltpu.make_async_copy(source, target, sems.at[2 * edge + slot]))
            for copy in copies:
                copy.start()
            return copies

        for edge in range(2):
            for comp in range(3):
                rows = pl.ds(0, 8 * grid.own)
                e_tile[edge, comp, rows, :] = e_edge[edge, comp, rows, :]
                h_tile[edge, comp, rows, :] = h_edge[edge, comp, rows, :]

        if grid is Fine:
            zero = [jnp.zeros((16, 128), F32)]
            ey64, ez64, ey64_part, ez64_part, c64, ey_top = read_planes(grid, from_above, *range(6))
            hy63, hz63 = read_planes(grid, up_own, 0, 1)
            c62, c63 = c(62), c(63)
            ghost = -0.5 * ey_top[0]
            dhy, dhz = scale(0.5, ez64), scale(-0.5, ey64)
            dex = mul(c63, sub(minus_y(dhz, ghost), minus_z(dhy)))
            dey = scale(-1.0, mul(c63, dhz))
            dez = mul(c63, dhy)
            dex62 = mul(c62, minus_y(zero, ghost))
            ey64_next = add(ey64_part, mul(c64, add(hz63, dhz)))
            ez64_next = sub(ez64_part, mul(c64, add(hy63, dhy)))
            dhx2 = halved(sub(plus_y(dez), plus_z(dey)))
            dhy2 = add(dhy, halved(sub(plus_z(dex), sub(ez64_next, dez))))
            dhz2 = add(dhz, halved(sub(sub(ey64_next, dey), plus_y(dex))))
            dhy62 = halved(sub(plus_z(dex62), dez))
            dhz62 = halved(sub(dey, plus_y(dex62)))
            put(h_tile, 1, 0, 63, dhx2)
            put(h_tile, 1, 1, 63, dhy2)
            put(h_tile, 1, 2, 63, dhz2)
            put(h_tile, 1, 1, 62, dhy62)
            put(h_tile, 1, 2, 62, dhz62)
            put(e_tile, 1, 0, 63, add(dex, mul(c63, sub(minus_y(dhz2, ghost), minus_z(dhy2)))))
            put(e_tile, 1, 1, 63, add(dey, mul(c63, sub(minus_z(dhx2), sub(dhz2, dhz62)))))
            put(e_tile, 1, 2, 63, add(dez, mul(c63, sub(sub(dhy2, dhy62), minus_y(dhx2)))))
            put(e_tile, 1, 0, 62, add(dex62, mul(c62, sub(minus_y(dhz62, ghost), minus_z(dhy62)))))
            put(e_tile, 1, 1, 62, scale(-1.0, mul(c62, dhz62)))
            put(e_tile, 1, 2, 62, mul(c62, dhy62))
            copies = finish(1)

            hy_part, hz_part, ex_part, ey_part, ez_part, cm = read_planes(grid, from_below, *range(6))
            ey0, ez0, ey0_part, ez0_part, c0, ey_top = read_planes(grid, down_own, *range(6))
            c1 = c(1)
            ghost = -0.5 * ey_top[0]
            dhy, dhz = scale(0.5, ez0), scale(-0.5, ey0)
            hym, hzm = add(hy_part, dhy), add(hz_part, dhz)
            exm = add(ex_part, mul(cm, sub(minus_y(dhz, ghost), minus_z(dhy))))
            eym = sub(ey_part, mul(cm, dhz))
            ezm = add(ez_part, mul(cm, dhy))
            dey, dez = mul(c0, hzm), scale(-1.0, mul(c0, hym))
            dhx2 = halved(sub(plus_y(dez), plus_z(dey)))
            dhy2 = scale(-0.5, dez)
            dhz2 = scale(0.5, dey)
            hym2 = add(hym, halved(sub(plus_z(exm), sub(add(ez0_part, dez), ezm))))
            hzm2 = add(hzm, halved(sub(sub(add(ey0_part, dey), eym), plus_y(exm))))
            put(h_tile, 0, 0, 0, dhx2)
            put(h_tile, 0, 1, 0, dhy2)
            put(h_tile, 0, 2, 0, dhz2)
            put(e_tile, 0, 0, 0, mul(c0, sub(minus_y(dhz2), minus_z(dhy2))))
            put(e_tile, 0, 1, 0, add(dey, mul(c0, sub(minus_z(dhx2), sub(dhz2, hzm2)))))
            put(e_tile, 0, 2, 0, add(dez, mul(c0, sub(sub(dhy2, hym2), minus_y(dhx2)))))
            put(e_tile, 0, 1, 1, mul(c1, dhz2))
            put(e_tile, 0, 2, 1, scale(-1.0, mul(c1, dhy2)))
            copies += finish(0)
        else:
            ey32, ez32 = read_planes(grid, from_above, 0, 1)
            c31 = c(last)
            dhy, dhz = scale(0.5, ez32), scale(-0.5, ey32)
            put(h_tile, 1, 1, last, dhy)
            put(h_tile, 1, 2, last, dhz)
            put(e_tile, 1, 0, last, mul(c31, sub(minus_y(dhz), minus_z(dhy))))
            put(e_tile, 1, 1, last, scale(-1.0, mul(c31, dhz)))
            put(e_tile, 1, 2, last, mul(c31, dhy))
            copies = finish(1)
            hy_part, hz_part = read_planes(grid, from_below, 0, 1)
            ey0, ez0 = read_planes(grid, down_own, 0, 1)
            c0 = c(0)
            put(e_tile, 0, 1, 0, mul(c0, add(hz_part, scale(-0.5, ey0))))
            put(e_tile, 0, 2, 0, scale(-1.0, mul(c0, add(hy_part, scale(0.5, ez0)))))
            copies += finish(0)
        for copy in copies:
            copy.wait()

    by_level(body)


def across(x, dx=0, dy=0, dz=0):
    nx, ny, nz = lax.axis_size("gx"), lax.axis_size("gy"), lax.axis_size("gz")
    pairs = [
        ((i * ny + j) * nz + k, ((i + dx) % nx * ny + (j + dy) % ny) * nz + (k + dz) % nz)
        for i in range(nx)
        for j in range(ny)
        for k in range(nz)
    ]
    return lax.ppermute(x, ("gx", "gy", "gz"), pairs)


def fast_shards(electric, magnetic, material, permittivity):
    e = electric.reshape(3, ROWS, 128)
    h = magnetic.reshape(3, ROWS, 128)
    m = material.reshape(ROWS, 128)
    dma = pltpu.SemaphoreType.DMA
    e_ext, zmsg, ytile = kernel_call(
        gather,
        [vmem(3, EXT, 128), vmem(7, HALO, 128), vmem(8, 128)],
        [HBM] * 3,
        [VM] * 3,
        [pltpu.VMEM((3, ROWS, 128), F32), pltpu.VMEM((HALO, 128), jnp.int32), dma((8,))],
    )(far(e), far(h), far(m))
    zin = across(zmsg, dz=1)
    yzin = across(ytile, dy=1, dz=1)
    yin = across(ytile, dy=1)
    e_ext, h_ext, c_ext, rtile, up, down = kernel_call(
        extend,
        [
            vmem(3, EXT, 128),
            vmem(3, EXT, 128),
            vmem(EXT, 128),
            vmem(8, 128),
            vmem(64, 128),
            vmem(64, 128),
        ],
        [VM] * 4 + [pl.BlockSpec(memory_space=pltpu.SMEM), VM],
        [VM] * 6,
        aliases={0: 0},
    )(held(e_ext), held(h), held(m), held(zin), permittivity, held(ytile))
    to_up, to_down, ptile = kernel_call(
        join_y,
        [vmem(64, 128), vmem(64, 128), vmem(8, 128)],
        [VM] * 5,
        [VM] * 3,
    )(*(held(part) for part in (up, down, yin, yzin, rtile)))
    from_below = across(to_up, dx=1)
    from_above = across(to_down, dx=-1)
    whole = jax.ShapeDtypeStruct((3, ROWS, 128), F32)
    e_out, h_out, e_edge, h_edge = kernel_call(
        advance,
        [whole, whole, vmem(2, 3, 64, 128), vmem(2, 3, 64, 128)],
        [VM] * 4,
        [HBM, HBM, VM, VM],
        [pltpu.VMEM((3, EXT, 128), F32)] * 3 + [pltpu.VMEM((2, 320, 128), F32), dma((2,))],
    )(*(held(part) for part in (e_ext, h_ext, c_ext, ptile)))
    e_out, h_out = kernel_call(
        correct,
        [whole, whole],
        [VM] * 7 + [HBM] * 2,
        [HBM] * 2,
        [pltpu.VMEM((2, 3, 64, 128), F32)] * 2 + [dma((4,))],
        aliases={7: 0, 8: 1},
    )(
        *(held(part) for part in (to_up, to_down, from_below, from_above, c_ext, e_edge, h_edge)),
        e_out,
        h_out,
    )
    return e_out.reshape(electric.shape), h_out.reshape(magnetic.shape)


def solution(mesh):
    placed = (
        P(("parts", "gy"), "gx", "gz", None, None),
        P(("parts", "gy"), "gx", "gz", None, None),
        P(("parts", "gy"), "gx", "gz", None),
        P(),
    )
    fast = mesh.shape["gy"] == 2 and mesh.shape["gz"] == 2
    return jax.shard_map(
        fast_shards if fast else general_shards,
        mesh=mesh,
        in_specs=placed,
        out_specs=(
            P(("parts", "gy"), "gx", "gz", None, None),
            P(("parts", "gy"), "gx", "gz", None, None),
        ),
        check_vma=False,
    )
```

```python
from functools import partial

import jax
import jax.numpy as jnp
from jax import lax
from jax.experimental import pallas as pl
from jax.experimental.pallas import tpu as pltpu
from jax.sharding import PartitionSpec as P

CZ = 4
CX = 32
CY = 512
MATS = 4


courant = 0.5


def passed_along(x, axis, by):
    devices = lax.axis_size(axis)
    return lax.ppermute(x, axis, [(i, (i + by) % devices) for i in range(devices)])


def from_behind(x, axis, by):
    devices = lax.axis_size(axis)
    pairs = [(i, i + by) for i in range(devices) if 0 <= i + by < devices]
    return lax.ppermute(x, axis, pairs)


def forward_diff(values, dim_axis, ghost_plane):
    shifted = jnp.concatenate(
        [
            lax.slice_in_dim(values, 1, values.shape[dim_axis], axis=dim_axis),
            jnp.expand_dims(ghost_plane, dim_axis),
        ],
        axis=dim_axis,
    )
    return shifted - values


def backward_diff(values, dim_axis, ghost_plane):
    shifted = jnp.concatenate(
        [
            jnp.expand_dims(ghost_plane, dim_axis),
            lax.slice_in_dim(values, 0, values.shape[dim_axis] - 1, axis=dim_axis),
        ],
        axis=dim_axis,
    )
    return values - shifted


def curl_with(differ, vectors, ghost_depth, ghost_width, ghost_height):
    ghosts = (ghost_depth, ghost_width, ghost_height)

    def along_axis(component, dim_axis):
        return differ(vectors[component], dim_axis, ghosts[dim_axis][component])

    curl_x = along_axis(2, 2) - along_axis(1, 0)
    curl_y = along_axis(0, 0) - along_axis(2, 1)
    curl_z = along_axis(1, 1) - along_axis(0, 2)
    return jnp.stack([curl_x, curl_y, curl_z])


def restrict(face_plane):
    quads = face_plane.reshape(3, face_plane.shape[1] // 2, 2, face_plane.shape[2] // 2, 2)
    return (
        quads[:, :, 0, :, 0] + quads[:, :, 0, :, 1] + (quads[:, :, 1, :, 0] + quads[:, :, 1, :, 1])
    ) * 0.25


def enlarge(face_plane):
    return jnp.repeat(jnp.repeat(face_plane, 2, axis=1), 2, axis=2)


def lookup(material, permittivity):
    permit_sum = jnp.zeros(material.shape, jnp.float32)
    for material_id in range(MATS):
        permit_sum = permit_sum + jnp.where(material == material_id, permittivity[material_id], 0.0)
    return courant / permit_sum


def pack_face(face_plane, length):
    flat_face = face_plane.reshape(3, -1)
    if flat_face.shape[1] < length:
        flat_face = jnp.concatenate(
            [flat_face, jnp.zeros((3, length - flat_face.shape[1]), flat_face.dtype)], axis=1
        )
    return flat_face


def unpack_face(flat_face, row_count, col_count):
    return flat_face[:, : row_count * col_count].reshape(3, row_count, col_count)


def level_height(got_height, is_fine):
    return got_height if is_fine else restrict(got_height)


def low_faces(grid_shape, is_fine, flat_field):
    vectors = flat_field.reshape((3,) + grid_shape)
    face_plane = vectors[:, :, :, 0]
    if not is_fine:
        face_plane = enlarge(face_plane)
    return (
        pack_face(vectors[:, :, 0, :], CZ * CY),
        pack_face(vectors[:, 0, :, :], CX * CY),
        face_plane,
    )


def high_faces(grid_shape, is_fine, flat_field):
    vectors = flat_field.reshape((3,) + grid_shape)
    face_plane = vectors[:, :, :, -1]
    if not is_fine:
        face_plane = enlarge(face_plane)
    return (
        pack_face(vectors[:, :, -1, :], CZ * CY),
        pack_face(vectors[:, -1, :, :], CX * CY),
        face_plane,
    )


def advance_magnetic(
    grid_shape, is_fine, does_move, e_flat, h_flat, got_width, got_depth, got_height
):
    if not does_move:
        return h_flat
    deep_cells, wide_cells, tall_cells = grid_shape
    vectors = e_flat.reshape((3,) + grid_shape)
    curl_term = curl_with(
        forward_diff,
        vectors,
        unpack_face(got_depth, wide_cells, tall_cells),
        unpack_face(got_width, deep_cells, tall_cells),
        level_height(got_height, is_fine),
    )
    return (h_flat.reshape((3,) + grid_shape) - courant * curl_term).reshape(3, -1)


def advance_electric(
    grid_shape, is_fine, does_move, e_flat, h_flat, coefficient, got_width, got_depth, got_height
):
    if not does_move:
        return e_flat
    deep_cells, wide_cells, tall_cells = grid_shape
    magnetic = h_flat.reshape((3,) + grid_shape)
    curl_term = curl_with(
        backward_diff,
        magnetic,
        unpack_face(got_depth, wide_cells, tall_cells),
        unpack_face(got_width, deep_cells, tall_cells),
        level_height(got_height, is_fine),
    )
    return (
        e_flat.reshape((3,) + grid_shape) + coefficient.reshape(grid_shape) * curl_term
    ).reshape(3, -1)


def pass_width(face_plane, offset):
    return passed_along(face_plane, "gx", offset)


def pass_depth(face_plane, offset):
    return from_behind(face_plane, "gz", offset)


def pass_height(face_plane, offset):
    return from_behind(face_plane, "gy", offset)


def general_shards(electric, magnetic, material, permittivity):
    cell_count = electric.shape[-1]
    e_flat = electric.reshape(3, cell_count)
    h_flat = magnetic.reshape(3, cell_count)
    coefficient = lookup(material.reshape(cell_count), permittivity)
    is_fine = lax.axis_index("gy") >= lax.axis_size("gy") // 2
    coarse_shape = (CZ, CX, CY)
    fine_shape = (2 * CZ, 2 * CX, CY // 4)
    for substep in range(2):
        coarse_moves = substep == 0
        face_width, face_depth, face_height = lax.cond(
            is_fine,
            partial(low_faces, fine_shape, True),
            partial(low_faces, coarse_shape, False),
            e_flat,
        )
        got_depth = pass_depth(face_depth, -1)
        got_height = pass_height(face_height, -1)
        got_width = pass_width(face_width, -1)
        h_flat = lax.cond(
            is_fine,
            partial(advance_magnetic, fine_shape, True, True),
            partial(advance_magnetic, coarse_shape, False, coarse_moves),
            e_flat,
            h_flat,
            got_width,
            got_depth,
            got_height,
        )
        rim_width, rim_depth, rim_height = lax.cond(
            is_fine,
            partial(high_faces, fine_shape, True),
            partial(high_faces, coarse_shape, False),
            h_flat,
        )
        rim_depth = pass_depth(rim_depth, 1)
        rim_height = pass_height(rim_height, 1)
        rim_width = pass_width(rim_width, 1)
        e_flat = lax.cond(
            is_fine,
            partial(advance_electric, fine_shape, True, True),
            partial(advance_electric, coarse_shape, False, coarse_moves),
            e_flat,
            h_flat,
            coefficient,
            rim_width,
            rim_depth,
            rim_height,
        )
    return (e_flat.reshape(electric.shape), h_flat.reshape(magnetic.shape))


ROWS = 512
HALO = 128
EXT = 1296
LIMIT = 40 * 1024 * 1024
F32 = jnp.float32
VM = pl.BlockSpec(memory_space=pltpu.VMEM)
HBM = pl.BlockSpec(memory_space=pltpu.HBM)
CHUNK = 32


class Fine:
    depth, stride, count, own, step, used, height, parts, last = 64, 72, 10, 8, 1, 10, 16, 1, 63


class Coarse:
    depth, stride, count, own, step, used, height, parts, last = 128, 144, 5, 4, 4, 5, 8, 4, 31


def vmem(*shape, dtype=F32):
    return pltpu.VMEM(shape, dtype)


def held(x):
    return pltpu.with_memory_space_constraint(x, pltpu.VMEM)


def far(x):
    return pltpu.with_memory_space_constraint(x, pltpu.HBM)


def kernel_call(body, out_shape, in_specs, out_specs, scratch=(), aliases=None):
    return pl.pallas_call(
        body,
        out_shape=out_shape,
        in_specs=in_specs,
        out_specs=out_specs,
        scratch_shapes=list(scratch),
        input_output_aliases=aliases or {},
        compiler_params=pltpu.CompilerParams(vmem_limit_bytes=LIMIT),
    )


def by_level(body):
    is_fine = lax.axis_index("gy") >= lax.axis_size("gy") // 2
    gz = lax.axis_index("gz")
    pl.when(is_fine)(lambda: body(Fine, gz))
    pl.when(jnp.logical_not(is_fine))(lambda: body(Coarse, gz))


def lanes_of(shape):
    return lax.broadcasted_iota(jnp.int32, shape, len(shape) - 1)


def rows_of(shape):
    return lax.broadcasted_iota(jnp.int32, shape, len(shape) - 2)


def roll_lanes(x, by):
    return pltpu.roll(x, by % 128, 1)


def roll_rows(x, by):
    return pltpu.roll(x, by % x.shape[0], 0)


def layer_row(grid, index):
    return pl.multiple_of(grid.stride * (index + 1), 8)


def own_first(grid, gz):
    return (grid.count - grid.own) * gz


def halo_first(grid, gz):
    return grid.own * (1 - gz)


def clear_pads(grid, ref, *zero_layers):
    for comp in range(3):
        for index in range(grid.count + 2):
            start, size = grid.stride * index, grid.stride
            if index not in zero_layers:
                start, size = start + grid.depth, size - grid.depth
            ref[comp, pl.ds(start, size), :] = jnp.zeros((size, 128), F32)


def own_layers(grid, ref, gz):
    view = ref.reshape(3, EXT // grid.stride, grid.stride, 128)
    return view.at[:, pl.ds(1 + own_first(grid, gz), grid.own), pl.ds(0, grid.depth), :]


def block_layers(grid, ref):
    return ref.reshape(3, grid.own, grid.depth, 128)


def at_lane(tile, lane_from, lane_to, value):
    lane = lanes_of(value.shape)
    return jnp.where(lane == lane_to, roll_lanes(value, lane_to - lane_from), tile)


def average(ref, lead, row, stride):
    steps = (0, 1, stride, stride + 1)
    quad = [ref[lead, pl.ds(row + step, 32, stride=2), :] for step in steps]
    return ((quad[0] + quad[1]) + (quad[2] + quad[3])) * 0.25


def put_column(tile, lane_from, slot, column):
    for block in range(4):
        tile = at_lane(tile, lane_from, 32 * block + slot, column[8 * block : 8 * block + 8])
    return tile


def gather(e_hbm, h_hbm, m_hbm, e_ext, zmsg, ytile, h_top, m_edge, sems):
    def body(grid, gz):
        edge = pl.ds((1 - gz) * (ROWS - HALO), HALO)
        source, target = block_layers(grid, e_hbm), own_layers(grid, e_ext, gz)
        first = [0, 2] if grid is Fine else [0, 1, 2]
        e_loads = {
            comp: pltpu.make_async_copy(source.at[comp], target.at[comp], sems.at[comp])
            for comp in (0, 2, 1)
        }
        h_loads = [] if grid is Fine else [
            pltpu.make_async_copy(h_hbm.at[comp], h_top.at[comp], sems.at[3 + comp]) for comp in (0, 2)
        ]
        loads = [
            pltpu.make_async_copy(h_hbm.at[:, edge], zmsg.at[pl.ds(3, 3)], sems.at[6]),
            pltpu.make_async_copy(m_hbm.at[edge], m_edge, sems.at[7]),
        ]
        for load in list(e_loads.values()) + h_loads + loads:
            load.start()
        clear_pads(grid, e_ext, grid.count + 1)
        for comp in first:
            e_loads[comp].wait()
        for load in h_loads:
            load.wait()
        begin = layer_row(grid, own_first(grid, gz))
        tile = jnp.zeros((8, 128), F32)
        for layer in range(4):
            if grid is Fine:
                row = begin + 2 * grid.stride * layer
                tile = put_column(tile, 0, layer, average(e_ext, 0, row, grid.stride))
                tile = put_column(tile, 0, 8 + layer, average(e_ext, 2, row, grid.stride))
            else:
                top = pl.ds(begin + grid.stride * layer + 3, 32, stride=4)
                h_row = pl.ds(grid.depth * layer + 3, 32, stride=4)
                ex, ey, ez = (e_ext[comp, top, :] for comp in range(3))
                tile = put_column(tile, 127, layer, h_top[0, h_row, :] + 0.5 * ez)
                tile = put_column(tile, 127, 8 + layer, h_top[2, h_row, :] - 0.5 * ex)
                tile = put_column(tile, 127, 16 + layer, ey)
        ytile[...] = jnp.where(gz == 1, roll_lanes(tile, 1), tile)
        if grid is Fine:
            e_loads[1].wait()
        layers = HALO // grid.depth
        from_layer = own_first(grid, gz) + (grid.own - layers) * (1 - gz)
        for comp in range(3):
            for layer in range(layers):
                row = layer_row(grid, from_layer + layer)
                zmsg[comp, pl.ds(grid.depth * layer, grid.depth), :] = e_ext[comp, pl.ds(row, grid.depth), :]
        for load in loads:
            load.wait()
        zmsg[6] = m_edge[...].astype(F32)

    by_level(body)


def up_y(grid, ref, comp, row, f):
    lane = lanes_of(f.shape)
    if grid is Fine:
        return jnp.where(lane == 127, 0.0, roll_lanes(f, -1))
    following = ref[comp, pl.ds(row + 1, f.shape[0]), :]
    following = jnp.where(rows_of(f.shape) % 4 == 3, 0.0, following)
    return roll_lanes(jnp.where(lane == 0, following, f), -1)


def down_y(grid, ref, comp, row, f, ghost):
    lane = lanes_of(f.shape)
    if grid is Fine:
        return roll_lanes(jnp.where(lane == 127, ghost, f), 1)
    previous = ref[comp, pl.ds(row - 1, f.shape[0]), :]
    previous = jnp.where(rows_of(f.shape) % 4 == 0, 0.0, previous)
    return roll_lanes(jnp.where(lane == 127, previous, f), 1)


def half_h(grid, e, h_from, from_row, h_to, row):
    for start in range(0, grid.depth, CHUNK):
        r = row + start
        here = pl.ds(r, CHUNK)
        ex, ey, ez = (e[comp, here, :] for comp in range(3))
        above, beside = pl.ds(r + grid.stride, CHUNK), pl.ds(r + grid.step, CHUNK)
        h0 = [h_from(comp, pl.ds(from_row + start, CHUNK)) for comp in range(3)]
        ez_y, ex_y = up_y(grid, e, 2, r, ez), up_y(grid, e, 0, r, ex)
        h_to[0, here, :] = h0[0] - 0.5 * ((ez_y - ez) - (e[1, above, :] - ey))
        h_to[1, here, :] = h0[1] - 0.5 * ((e[0, above, :] - ex) - (e[2, beside, :] - ez))
        h_to[2, here, :] = h0[2] - 0.5 * ((e[1, beside, :] - ey) - (ex_y - ex))


def half_e(grid, h, e_from, e_to, c_ref, row, ghosts):
    for start in range(0, grid.depth, CHUNK):
        r = row + start
        here = pl.ds(r, CHUNK)
        hx, hy, hz = (h[comp, here, :] for comp in range(3))
        below, beside = pl.ds(r - grid.stride, CHUNK), pl.ds(r - grid.step, CHUNK)
        px, pz = ghosts(start)
        hx_y, hz_y = down_y(grid, h, 0, r, hx, px), down_y(grid, h, 2, r, hz, pz)
        c = c_ref[here, :]
        e_to[0, here, :] = e_from[0, here, :] + c * ((hz - hz_y) - (hy - h[1, below, :]))
        e_to[1, here, :] = e_from[1, here, :] + c * ((hx - h[0, below, :]) - (hz - h[2, beside, :]))
        e_to[2, here, :] = e_from[2, here, :] + c * ((hy - h[1, beside, :]) - (hx - hx_y))


def with_halo(tile, halo_tile, gz):
    lane = lanes_of(tile.shape)
    return jnp.where(lane % 8 == 4 * (1 - gz), halo_tile, tile)


def joined(own, other, gz):
    return with_halo(own, jnp.where(gz == 0, roll_lanes(other, 3), roll_lanes(other, -3)), gz)


def column_of(tile, block, sub, slot, shape, per_layer):
    row = jnp.broadcast_to(tile[sub : sub + 1, :], shape)
    wanted = 32 * block + slot + rows_of(shape) // per_layer
    picked = jnp.where((lanes_of(shape) == wanted) & (rows_of(shape) < 5 * per_layer), row, 0.0)
    return jnp.broadcast_to(jnp.sum(picked, axis=1, keepdims=True), shape)


def column(grid, read, x):
    begin = grid.stride + grid.step * x
    planes = [read(pl.ds(begin + part, grid.height, stride=grid.stride)) for part in range(grid.parts)]
    return [jnp.where(rows_of(p.shape) < grid.used, p, 0.0) for p in planes]


def each(fn, *columns):
    return [fn(*parts) for parts in zip(*columns, strict=True)]


def plus_y(f, ghost=0.0):
    following = f[1:] + [ghost]
    return [
        roll_lanes(jnp.where(lanes_of(p.shape) == 0, nxt, p), -1) - p
        for p, nxt in zip(f, following, strict=True)
    ]


def minus_y(f, ghost=0.0):
    previous = [ghost] + f[:-1]
    return [
        p - roll_lanes(jnp.where(lanes_of(p.shape) == 127, prv, p), 1)
        for p, prv in zip(f, previous, strict=True)
    ]


def plus_z(f):
    return [roll_rows(p, -1) - p for p in f]


def minus_z(f):
    return [p - roll_rows(p, 1) for p in f]


def add(a, b):
    return each(lambda p, q: p + q, a, b)


def sub(a, b):
    return each(lambda p, q: p - q, a, b)


def mul(a, b):
    return each(lambda p, q: p * q, a, b)


def scale(by, a):
    return [by * p for p in a]


def halved(a):
    used = 10 if len(a) == 1 else 5
    return [jnp.where(rows_of(p.shape) < used, -0.5 * p, 0.0) for p in a]


def write_planes(grid, ref, columns):
    row = 0
    for col in columns:
        for p in col:
            ref[pl.ds(row, grid.used), :] = p[: grid.used]
            row += grid.used


def read_plane(grid, ref, row):
    start = min(row, ref.shape[0] - grid.height)
    p = ref[pl.ds(start, grid.height), :]
    if start < row:
        p = roll_rows(p, start - row)
    return jnp.where(rows_of(p.shape) < grid.used, p, 0.0)


def read_planes(grid, ref, *wanted):
    used, parts = grid.used, grid.parts
    return [[read_plane(grid, ref, used * (parts * i + part)) for part in range(parts)] for i in wanted]


def extend(
    e_in, h_own, m_own, zmsg, permittivity, ytile, e_ext, h_ext, c_ext, rtile, up, down, table, sems
):
    def body(grid, gz):
        load = pltpu.make_async_copy(permittivity, table, sems.at[0])
        load.start()
        clear_pads(grid, h_ext, 0)
        halo = halo_first(grid, gz)
        for layer in range(grid.count - grid.own):
            for start in range(0, grid.depth, CHUNK):
                rows = pl.ds(layer_row(grid, halo + layer) + start, CHUNK)
                from_rows = pl.ds(grid.depth * layer + start, CHUNK)
                for comp in range(3):
                    e_ext[comp, rows, :] = zmsg[comp, from_rows, :]
        for layer in range(grid.count - grid.own):
            row = layer_row(grid, halo + layer)
            half_h(
                grid, e_ext, lambda comp, rows: zmsg[3 + comp, rows, :], grid.depth * layer, h_ext, row
            )

        for layer in range(grid.own):
            row = layer_row(grid, own_first(grid, gz) + layer)
            half_h(grid, e_ext, lambda comp, rows: h_own[comp, rows, :], grid.depth * layer, h_ext, row)
        load.wait()
        values = [0.5 / jnp.full((CHUNK, 128), table[i], F32) for i in range(MATS)]

        def coef(is_material):
            found = values[MATS - 1]
            for i in range(MATS - 2, -1, -1):
                found = jnp.where(is_material(i), values[i], found)
            return found

        for start in range(0, HALO, CHUNK):
            layer, rest = divmod(start, grid.depth)
            material = zmsg[6, pl.ds(start, CHUNK), :]
            row = layer_row(grid, halo + layer) + rest
            c_ext[pl.ds(row, CHUNK), :] = coef(lambda i, m=material: m == float(i))
        for start in range(0, ROWS, CHUNK):
            layer, rest = divmod(start, grid.depth)
            material = m_own[pl.ds(start, CHUNK), :]
            row = layer_row(grid, own_first(grid, gz) + layer) + rest
            c_ext[pl.ds(row, CHUNK), :] = coef(lambda i, m=material: m == i)

        def e(comp, x):
            return column(grid, lambda rows: e_ext[comp, rows, :], x)

        def h(comp, x):
            return column(grid, lambda rows: h_ext[comp, rows, :], x)

        def c(x):
            return column(grid, lambda rows: c_ext[rows, :], x)

        last = grid.last
        if grid is Coarse:
            rtile[...] = jnp.zeros((8, 128), F32)
            write_planes(grid, down, [e(1, 0), e(2, 0)])
            write_planes(grid, up, [h(1, last), h(2, last)])
            return
        tile = jnp.zeros((8, 128), F32)
        for kind, comp in enumerate((0, 2)):
            tile = put_column(tile, 0, 8 * kind + 4, average(zmsg, comp, 0, grid.depth))
        tile = jnp.where(gz == 1, roll_lanes(tile, -4), tile)
        rtile[...] = with_halo(ytile[...], tile, gz)
        ey, ez, hx, hy, hz, c0 = e(1, 0), e(2, 0), h(0, 0), h(1, 0), h(2, 0), c(0)
        ey_next = add(ey, mul(c0, sub(minus_z(hx), hz)))
        ez_next = add(ez, mul(c0, sub(hy, minus_y(hx))))
        write_planes(grid, down, [ey, ez, ey_next, ez_next, c0])
        hx, hy, hz, c63 = h(0, last), h(1, last), h(2, last), c(last)
        hy62, hz62 = h(1, last - 1), h(2, last - 1)
        ex_next = add(e(0, last), mul(c63, sub(minus_y(hz), minus_z(hy))))
        ey_next = add(e(1, last), mul(c63, sub(minus_z(hx), sub(hz, hz62))))
        ez_next = add(e(2, last), mul(c63, sub(sub(hy, hy62), minus_y(hx))))
        write_planes(grid, up, [hy, hz, ex_next, ey_next, ez_next, c63])

    by_level(body)


def join_y(up, down, yin, yzin, rtile, to_up, to_down, ptile):
    def body(grid, gz):
        top = joined(yin[...], yzin[...], gz)
        to_up[...] = up[...]
        to_down[...] = down[...]
        shape = (grid.height, 128)
        if grid is Coarse:
            ptile[...] = top
            at = 5 * 7
            change = jnp.where(lanes_of(shape) == 127, 0.5 * column_of(top, 3, 7, 0, shape, 1), 0.0)
            to_up[pl.ds(at, 5), :] = to_up[pl.ds(at, 5), :] + change[:5]
            return
        r = rtile[...]
        lane, row = lanes_of(top.shape), rows_of(top.shape)
        kind = (lane % 32) // 8
        px = top - 0.5 * roll_lanes(r, -8) + 0.5 * (roll_lanes(top, -17) - roll_lanes(top, -16))
        beside = roll_rows(top, -1)
        beside = jnp.where(row == 7, jnp.where(lane >= 96, 0.0, roll_lanes(beside, -32)), beside)
        pz = top + 0.5 * roll_lanes(r, 8) - 0.5 * (roll_lanes(beside, -8) - roll_lanes(top, -8))
        plane = jnp.where(kind == 0, px, jnp.where(kind == 1, pz, 0.0))
        ptile[...] = plane

        def change(ref, target, index, c, value):
            change = jnp.where(lanes_of(shape) == 0, c * value, 0.0)
            rows = pl.ds(10 * index, 10)
            target[rows, :] = ref[rows, :] + change[:10]

        ((c0,),) = read_planes(grid, down, 4)
        ((c63,),) = read_planes(grid, up, 5)
        change(down, to_down, 3, c0, column_of(plane, 0, 0, 0, shape, 2))
        change(up, to_up, 4, c63, column_of(plane, 3, 7, 0, shape, 2))
        change(up, to_up, 2, c63, -column_of(plane, 3, 7, 8, shape, 2))
        to_down[pl.ds(50, 10), :] = column_of(top, 0, 0, 16, shape, 2)[:10]

    by_level(body)


def advance(
    e_ext, h_ext, c_ext, ptile, e_out, h_out, e_edge, h_edge, e_mid, h_mid, e_last, plane, sems
):
    def body(grid, gz):
        first = own_first(grid, gz)
        tile = ptile[...]

        def write(source, target, sem, layer=None):
            source, target = own_layers(grid, source, gz), block_layers(grid, target)
            if layer is not None:
                source, target = source.at[:, layer], target.at[:, layer]
            return pltpu.make_async_copy(source, target, sem)

        def keep_edges(source, target):
            for comp in range(3):
                for layer in range(grid.own):
                    for edge in range(2):
                        row = layer_row(grid, first + layer) + (grid.depth - 8) * edge
                        target[edge, comp, pl.ds(8 * layer, 8), :] = source[comp, pl.ds(row, 8), :]

        clear_pads(grid, h_mid, 0)
        if grid is Fine:
            clear_pads(grid, e_mid, grid.count + 1)
            for kind in range(2):
                for layer in range(5):
                    for block in range(4):
                        value = roll_lanes(tile, 127 - (32 * block + 8 * kind + layer))
                        for step in range(2):
                            rows = pl.ds(64 * layer + 16 * block + step, 8, stride=2)
                            plane[kind, rows, :] = value

            def ghosts(index):
                begin = 64 * (index // 2)

                def of(start):
                    rows = pl.ds(pl.multiple_of(begin + start, 8), CHUNK)
                    return plane[0, rows, :], plane[1, rows, :]

                return of

            for layer in range(grid.count):
                row = grid.stride * (layer + 1)
                half_e(grid, h_ext, e_ext, e_mid, c_ext, row, ghosts(layer))
            for layer in range(grid.count):
                row = grid.stride * (layer + 1)
                half_h(grid, e_mid, lambda comp, rows: h_ext[comp, rows, :], row, h_mid, row)
            h_write = write(h_mid, h_out, sems.at[0])
            h_write.start()
            e_begin = e_mid
        else:
            for comp in range(3):
                for layer in range(grid.count):
                    rows = pl.ds(layer_row(grid, layer), grid.depth)
                    h_mid[comp, rows, :] = h_ext[comp, rows, :]
            lane = lanes_of((8, 128))
            for layer in range(grid.count):
                for block in range(4):
                    rows = pl.ds(layer_row(grid, layer) + 32 * block + 3, 8, stride=4)
                    rx = roll_lanes(tile, 127 - (32 * block + layer))
                    rz = roll_lanes(tile, 127 - (32 * block + 8 + layer))
                    h_mid[0, rows, :] = h_mid[0, rows, :] - jnp.where(lane == 127, 0.5 * rz, 0.0)
                    h_mid[2, rows, :] = h_mid[2, rows, :] + jnp.where(lane == 127, 0.5 * rx, 0.0)
            h_write = write(h_mid, h_out, sems.at[0])
            h_write.start()
            e_begin = e_ext

            def ghosts(index):
                return lambda start: (0.0, 0.0)

        for layer in range(grid.own):
            row = layer_row(grid, first + layer)
            half_e(grid, h_mid, e_begin, e_last, c_ext, row, ghosts(first + layer))
            write(e_last, e_out, sems.at[1], layer).start()
        keep_edges(h_mid, h_edge)
        keep_edges(e_last, e_edge)
        h_write.wait()
        write(e_last, e_out, sems.at[1]).wait()

    by_level(body)


def correct(
    up_own, down_own, from_below, from_above, c_ext, e_edge, h_edge, e_in, h_in, e_out, h_out, e_tile, h_tile, sems
):
    def body(grid, gz):
        last = grid.last

        def put(ref, edge, comp, x, change):
            for part, p in enumerate(change):
                moved = pltpu.roll(p, grid.height - own_first(grid, gz), 0)[: grid.own]
                rows = pl.ds(grid.step * x % 8 + part, grid.own, stride=8)
                ref[edge, comp, rows, :] = ref[edge, comp, rows, :] + moved

        def c(x):
            return column(grid, lambda rows: c_ext[rows, :], x)

        def finish(edge):
            copies = []
            for slot, (tile, out) in enumerate(((h_tile, h_out), (e_tile, e_out))):
                source = tile.at[edge].reshape(3, 8, 8, 128).at[:, pl.ds(0, grid.own)]
                target = block_layers(grid, out).at[:, :, pl.ds((grid.depth - 8) * edge, 8), :]
                copies.append(pltpu.make_async_copy(source, target, sems.at[2 * edge + slot]))
            for copy in copies:
                copy.start()
            return copies

        if grid is Fine:
            zero = [jnp.zeros((16, 128), F32)]
            ey64, ez64, ey64_part, ez64_part, c64, ey_top = read_planes(grid, from_above, *range(6))
            hy63, hz63 = read_planes(grid, up_own, 0, 1)
            c62, c63 = c(62), c(63)
            ghost = -0.5 * ey_top[0]
            dhy, dhz = scale(0.5, ez64), scale(-0.5, ey64)
            dex = mul(c63, sub(minus_y(dhz, ghost), minus_z(dhy)))
            dey = scale(-1.0, mul(c63, dhz))
            dez = mul(c63, dhy)
            dex62 = mul(c62, minus_y(zero, ghost))
            ey64_next = add(ey64_part, mul(c64, add(hz63, dhz)))
            ez64_next = sub(ez64_part, mul(c64, add(hy63, dhy)))
            dhx2 = halved(sub(plus_y(dez), plus_z(dey)))
            dhy2 = add(dhy, halved(sub(plus_z(dex), sub(ez64_next, dez))))
            dhz2 = add(dhz, halved(sub(sub(ey64_next, dey), plus_y(dex))))
            dhy62 = halved(sub(plus_z(dex62), dez))
            dhz62 = halved(sub(dey, plus_y(dex62)))
            put(h_tile, 1, 0, 63, dhx2)
            put(h_tile, 1, 1, 63, dhy2)
            put(h_tile, 1, 2, 63, dhz2)
            put(h_tile, 1, 1, 62, dhy62)
            put(h_tile, 1, 2, 62, dhz62)
            put(e_tile, 1, 0, 63, add(dex, mul(c63, sub(minus_y(dhz2, ghost), minus_z(dhy2)))))
            put(e_tile, 1, 1, 63, add(dey, mul(c63, sub(minus_z(dhx2), sub(dhz2, dhz62)))))
            put(e_tile, 1, 2, 63, add(dez, mul(c63, sub(sub(dhy2, dhy62), minus_y(dhx2)))))
            put(e_tile, 1, 0, 62, add(dex62, mul(c62, sub(minus_y(dhz62, ghost), minus_z(dhy62)))))
            put(e_tile, 1, 1, 62, scale(-1.0, mul(c62, dhz62)))
            put(e_tile, 1, 2, 62, mul(c62, dhy62))
            copies = finish(1)

            hy_part, hz_part, ex_part, ey_part, ez_part, cm = read_planes(grid, from_below, *range(6))
            ey0, ez0, ey0_part, ez0_part, c0, ey_top = read_planes(grid, down_own, *range(6))
            c1 = c(1)
            ghost = -0.5 * ey_top[0]
            dhy, dhz = scale(0.5, ez0), scale(-0.5, ey0)
            hym, hzm = add(hy_part, dhy), add(hz_part, dhz)
            exm = add(ex_part, mul(cm, sub(minus_y(dhz, ghost), minus_z(dhy))))
            eym = sub(ey_part, mul(cm, dhz))
            ezm = add(ez_part, mul(cm, dhy))
            dey, dez = mul(c0, hzm), scale(-1.0, mul(c0, hym))
            dhx2 = halved(sub(plus_y(dez), plus_z(dey)))
            dhy2 = scale(-0.5, dez)
            dhz2 = scale(0.5, dey)
            hym2 = add(hym, halved(sub(plus_z(exm), sub(add(ez0_part, dez), ezm))))
            hzm2 = add(hzm, halved(sub(sub(add(ey0_part, dey), eym), plus_y(exm))))
            put(h_tile, 0, 0, 0, dhx2)
            put(h_tile, 0, 1, 0, dhy2)
            put(h_tile, 0, 2, 0, dhz2)
            put(e_tile, 0, 0, 0, mul(c0, sub(minus_y(dhz2), minus_z(dhy2))))
            put(e_tile, 0, 1, 0, add(dey, mul(c0, sub(minus_z(dhx2), sub(dhz2, hzm2)))))
            put(e_tile, 0, 2, 0, add(dez, mul(c0, sub(sub(dhy2, hym2), minus_y(dhx2)))))
            put(e_tile, 0, 1, 1, mul(c1, dhz2))
            put(e_tile, 0, 2, 1, scale(-1.0, mul(c1, dhy2)))
            copies += finish(0)
        else:
            ey32, ez32 = read_planes(grid, from_above, 0, 1)
            c31 = c(last)
            dhy, dhz = scale(0.5, ez32), scale(-0.5, ey32)
            put(h_tile, 1, 1, last, dhy)
            put(h_tile, 1, 2, last, dhz)
            put(e_tile, 1, 0, last, mul(c31, sub(minus_y(dhz), minus_z(dhy))))
            put(e_tile, 1, 1, last, scale(-1.0, mul(c31, dhz)))
            put(e_tile, 1, 2, last, mul(c31, dhy))
            copies = finish(1)
            hy_part, hz_part = read_planes(grid, from_below, 0, 1)
            ey0, ez0 = read_planes(grid, down_own, 0, 1)
            c0 = c(0)
            put(e_tile, 0, 1, 0, mul(c0, add(hz_part, scale(-0.5, ey0))))
            put(e_tile, 0, 2, 0, scale(-1.0, mul(c0, add(hy_part, scale(0.5, ez0)))))
            copies += finish(0)
        for copy in copies:
            copy.wait()

    by_level(body)


def across(x, dx=0, dy=0, dz=0):
    nx, ny, nz = lax.axis_size("gx"), lax.axis_size("gy"), lax.axis_size("gz")
    pairs = [
        ((i * ny + j) * nz + k, ((i + dx) % nx * ny + (j + dy) % ny) * nz + (k + dz) % nz)
        for i in range(nx)
        for j in range(ny)
        for k in range(nz)
    ]
    return lax.ppermute(x, ("gx", "gy", "gz"), pairs)


def fast_shards(electric, magnetic, material, permittivity):
    e = electric.reshape(3, ROWS, 128)
    h = magnetic.reshape(3, ROWS, 128)
    m = material.reshape(ROWS, 128)
    dma = pltpu.SemaphoreType.DMA
    e_ext, zmsg, ytile = kernel_call(
        gather,
        [vmem(3, EXT, 128), vmem(7, HALO, 128), vmem(8, 128)],
        [HBM] * 3,
        [VM] * 3,
        [pltpu.VMEM((3, ROWS, 128), F32), pltpu.VMEM((HALO, 128), jnp.int32), dma((8,))],
    )(far(e), far(h), far(m))
    h, m, ytile = lax.optimization_barrier((h, m, ytile))
    zin = across(zmsg, dz=1)
    yzin = across(ytile, dy=1, dz=1)
    yin = across(ytile, dy=1)
    e_ext, h_ext, c_ext, rtile, up, down = kernel_call(
        extend,
        [
            vmem(3, EXT, 128),
            vmem(3, EXT, 128),
            vmem(EXT, 128),
            vmem(8, 128),
            vmem(64, 128),
            vmem(64, 128),
        ],
        [VM] * 4 + [HBM, VM],
        [VM] * 6,
        [pltpu.SMEM((MATS,), F32), dma((1,))],
        aliases={0: 0},
    )(held(e_ext), held(h), held(m), held(zin), far(permittivity), held(ytile))
    to_up, to_down, ptile = kernel_call(
        join_y,
        [vmem(64, 128), vmem(64, 128), vmem(8, 128)],
        [VM] * 5,
        [VM] * 3,
    )(*(held(part) for part in (up, down, yin, yzin, rtile)))
    from_below = across(to_up, dx=1)
    from_above = across(to_down, dx=-1)
    whole = jax.ShapeDtypeStruct((3, ROWS, 128), F32)
    e_out, h_out, e_edge, h_edge = kernel_call(
        advance,
        [whole, whole, vmem(2, 3, 64, 128), vmem(2, 3, 64, 128)],
        [VM] * 4,
        [HBM, HBM, VM, VM],
        [pltpu.VMEM((3, EXT, 128), F32)] * 3 + [pltpu.VMEM((2, 320, 128), F32), dma((2,))],
    )(*(held(part) for part in (e_ext, h_ext, c_ext, ptile)))
    e_out, h_out, _, _ = kernel_call(
        correct,
        [whole, whole, vmem(2, 3, 64, 128), vmem(2, 3, 64, 128)],
        [VM] * 7 + [HBM] * 2,
        [HBM] * 2 + [VM] * 2,
        [dma((4,))],
        aliases={7: 0, 8: 1, 5: 2, 6: 3},
    )(
        *(held(part) for part in (to_up, to_down, from_below, from_above, c_ext, e_edge, h_edge)),
        e_out,
        h_out,
    )
    return e_out.reshape(electric.shape), h_out.reshape(magnetic.shape)


def solution(mesh):
    placed = (
        P(("parts", "gy"), "gx", "gz", None, None),
        P(("parts", "gy"), "gx", "gz", None, None),
        P(("parts", "gy"), "gx", "gz", None),
        P(),
    )
    fast = mesh.shape["gy"] == 2 and mesh.shape["gz"] == 2
    return jax.shard_map(
        fast_shards if fast else general_shards,
        mesh=mesh,
        in_specs=placed,
        out_specs=(
            P(("parts", "gy"), "gx", "gz", None, None),
            P(("parts", "gy"), "gx", "gz", None, None),
        ),
        check_vma=False,
    )
```

```python
from functools import partial

import jax
import jax.numpy as jnp
from jax import lax
from jax.experimental import pallas as pl
from jax.experimental.pallas import tpu as pltpu
from jax.sharding import PartitionSpec as P

CZ = 4
CX = 32
CY = 512
MATS = 4


courant = 0.5


def passed_along(x, axis, by):
    devices = lax.axis_size(axis)
    return lax.ppermute(x, axis, [(i, (i + by) % devices) for i in range(devices)])


def from_behind(x, axis, by):
    devices = lax.axis_size(axis)
    pairs = [(i, i + by) for i in range(devices) if 0 <= i + by < devices]
    return lax.ppermute(x, axis, pairs)


def forward_diff(values, dim_axis, ghost_plane):
    shifted = jnp.concatenate(
        [
            lax.slice_in_dim(values, 1, values.shape[dim_axis], axis=dim_axis),
            jnp.expand_dims(ghost_plane, dim_axis),
        ],
        axis=dim_axis,
    )
    return shifted - values


def backward_diff(values, dim_axis, ghost_plane):
    shifted = jnp.concatenate(
        [
            jnp.expand_dims(ghost_plane, dim_axis),
            lax.slice_in_dim(values, 0, values.shape[dim_axis] - 1, axis=dim_axis),
        ],
        axis=dim_axis,
    )
    return values - shifted


def curl_with(differ, vectors, ghost_depth, ghost_width, ghost_height):
    ghosts = (ghost_depth, ghost_width, ghost_height)

    def along_axis(component, dim_axis):
        return differ(vectors[component], dim_axis, ghosts[dim_axis][component])

    curl_x = along_axis(2, 2) - along_axis(1, 0)
    curl_y = along_axis(0, 0) - along_axis(2, 1)
    curl_z = along_axis(1, 1) - along_axis(0, 2)
    return jnp.stack([curl_x, curl_y, curl_z])


def restrict(face_plane):
    quads = face_plane.reshape(3, face_plane.shape[1] // 2, 2, face_plane.shape[2] // 2, 2)
    return (
        quads[:, :, 0, :, 0] + quads[:, :, 0, :, 1] + (quads[:, :, 1, :, 0] + quads[:, :, 1, :, 1])
    ) * 0.25


def enlarge(face_plane):
    return jnp.repeat(jnp.repeat(face_plane, 2, axis=1), 2, axis=2)


def lookup(material, permittivity):
    permit_sum = jnp.zeros(material.shape, jnp.float32)
    for material_id in range(MATS):
        permit_sum = permit_sum + jnp.where(material == material_id, permittivity[material_id], 0.0)
    return courant / permit_sum


def pack_face(face_plane, length):
    flat_face = face_plane.reshape(3, -1)
    if flat_face.shape[1] < length:
        flat_face = jnp.concatenate(
            [flat_face, jnp.zeros((3, length - flat_face.shape[1]), flat_face.dtype)], axis=1
        )
    return flat_face


def unpack_face(flat_face, row_count, col_count):
    return flat_face[:, : row_count * col_count].reshape(3, row_count, col_count)


def level_height(got_height, is_fine):
    return got_height if is_fine else restrict(got_height)


def low_faces(grid_shape, is_fine, flat_field):
    vectors = flat_field.reshape((3,) + grid_shape)
    face_plane = vectors[:, :, :, 0]
    if not is_fine:
        face_plane = enlarge(face_plane)
    return (
        pack_face(vectors[:, :, 0, :], CZ * CY),
        pack_face(vectors[:, 0, :, :], CX * CY),
        face_plane,
    )


def high_faces(grid_shape, is_fine, flat_field):
    vectors = flat_field.reshape((3,) + grid_shape)
    face_plane = vectors[:, :, :, -1]
    if not is_fine:
        face_plane = enlarge(face_plane)
    return (
        pack_face(vectors[:, :, -1, :], CZ * CY),
        pack_face(vectors[:, -1, :, :], CX * CY),
        face_plane,
    )


def advance_magnetic(
    grid_shape, is_fine, does_move, e_flat, h_flat, got_width, got_depth, got_height
):
    if not does_move:
        return h_flat
    deep_cells, wide_cells, tall_cells = grid_shape
    vectors = e_flat.reshape((3,) + grid_shape)
    curl_term = curl_with(
        forward_diff,
        vectors,
        unpack_face(got_depth, wide_cells, tall_cells),
        unpack_face(got_width, deep_cells, tall_cells),
        level_height(got_height, is_fine),
    )
    return (h_flat.reshape((3,) + grid_shape) - courant * curl_term).reshape(3, -1)


def advance_electric(
    grid_shape, is_fine, does_move, e_flat, h_flat, coefficient, got_width, got_depth, got_height
):
    if not does_move:
        return e_flat
    deep_cells, wide_cells, tall_cells = grid_shape
    magnetic = h_flat.reshape((3,) + grid_shape)
    curl_term = curl_with(
        backward_diff,
        magnetic,
        unpack_face(got_depth, wide_cells, tall_cells),
        unpack_face(got_width, deep_cells, tall_cells),
        level_height(got_height, is_fine),
    )
    return (
        e_flat.reshape((3,) + grid_shape) + coefficient.reshape(grid_shape) * curl_term
    ).reshape(3, -1)


def pass_width(face_plane, offset):
    return passed_along(face_plane, "gx", offset)


def pass_depth(face_plane, offset):
    return from_behind(face_plane, "gz", offset)


def pass_height(face_plane, offset):
    return from_behind(face_plane, "gy", offset)


def general_shards(electric, magnetic, material, permittivity):
    cell_count = electric.shape[-1]
    e_flat = electric.reshape(3, cell_count)
    h_flat = magnetic.reshape(3, cell_count)
    coefficient = lookup(material.reshape(cell_count), permittivity)
    is_fine = lax.axis_index("gy") >= lax.axis_size("gy") // 2
    coarse_shape = (CZ, CX, CY)
    fine_shape = (2 * CZ, 2 * CX, CY // 4)
    for substep in range(2):
        coarse_moves = substep == 0
        face_width, face_depth, face_height = lax.cond(
            is_fine,
            partial(low_faces, fine_shape, True),
            partial(low_faces, coarse_shape, False),
            e_flat,
        )
        got_depth = pass_depth(face_depth, -1)
        got_height = pass_height(face_height, -1)
        got_width = pass_width(face_width, -1)
        h_flat = lax.cond(
            is_fine,
            partial(advance_magnetic, fine_shape, True, True),
            partial(advance_magnetic, coarse_shape, False, coarse_moves),
            e_flat,
            h_flat,
            got_width,
            got_depth,
            got_height,
        )
        rim_width, rim_depth, rim_height = lax.cond(
            is_fine,
            partial(high_faces, fine_shape, True),
            partial(high_faces, coarse_shape, False),
            h_flat,
        )
        rim_depth = pass_depth(rim_depth, 1)
        rim_height = pass_height(rim_height, 1)
        rim_width = pass_width(rim_width, 1)
        e_flat = lax.cond(
            is_fine,
            partial(advance_electric, fine_shape, True, True),
            partial(advance_electric, coarse_shape, False, coarse_moves),
            e_flat,
            h_flat,
            coefficient,
            rim_width,
            rim_depth,
            rim_height,
        )
    return (e_flat.reshape(electric.shape), h_flat.reshape(magnetic.shape))


ROWS = 512
HALO = 128
EXT = 1296
LIMIT = 40 * 1024 * 1024
F32 = jnp.float32
VM = pl.BlockSpec(memory_space=pltpu.VMEM)
HBM = pl.BlockSpec(memory_space=pltpu.HBM)
CHUNK = 32


class Fine:
    depth, stride, count, own, step, parts, last = 64, 72, 10, 8, 1, 1, 63


class Coarse:
    depth, stride, count, own, step, parts, last = 128, 144, 5, 4, 4, 4, 31


def vmem(*shape, dtype=F32):
    return pltpu.VMEM(shape, dtype)


def held(x):
    return pltpu.with_memory_space_constraint(x, pltpu.VMEM)


def far(x):
    return pltpu.with_memory_space_constraint(x, pltpu.HBM)


def kernel_call(body, out_shape, in_specs, out_specs, scratch=(), aliases=None):
    return pl.pallas_call(
        body,
        out_shape=out_shape,
        in_specs=in_specs,
        out_specs=out_specs,
        scratch_shapes=list(scratch),
        input_output_aliases=aliases or {},
        compiler_params=pltpu.CompilerParams(vmem_limit_bytes=LIMIT),
    )


def by_level(body):
    is_fine = lax.axis_index("gy") >= lax.axis_size("gy") // 2
    gz = lax.axis_index("gz")
    pl.when(is_fine)(lambda: body(Fine, gz))
    pl.when(jnp.logical_not(is_fine))(lambda: body(Coarse, gz))


def lanes_of(shape):
    return lax.broadcasted_iota(jnp.int32, shape, len(shape) - 1)


def rows_of(shape):
    return lax.broadcasted_iota(jnp.int32, shape, len(shape) - 2)


def roll_lanes(x, by):
    return pltpu.roll(x, by % 128, 1)


def roll_rows(x, by):
    return pltpu.roll(x, by % x.shape[0], 0)


def layer_row(grid, index):
    return pl.multiple_of(grid.stride * (index + 1), 8)


def own_first(grid, gz):
    return (grid.count - grid.own) * gz


def halo_first(grid, gz):
    return grid.own * (1 - gz)


def clear_pads(grid, ref, *zero_layers):
    for comp in range(3):
        for index in range(grid.count + 2):
            start, size = grid.stride * index, grid.stride
            if index not in zero_layers:
                start, size = start + grid.depth, size - grid.depth
            ref[comp, pl.ds(start, size), :] = jnp.zeros((size, 128), F32)


def own_layers(grid, ref, gz):
    view = ref.reshape(3, EXT // grid.stride, grid.stride, 128)
    return view.at[:, pl.ds(1 + own_first(grid, gz), grid.own), pl.ds(0, grid.depth), :]


def block_layers(grid, ref):
    return ref.reshape(3, grid.own, grid.depth, 128)


def at_lane(tile, lane_from, lane_to, value):
    lane = lanes_of(value.shape)
    return jnp.where(lane == lane_to, roll_lanes(value, lane_to - lane_from), tile)


def average(ref, lead, row, stride):
    steps = (0, 1, stride, stride + 1)
    quad = [ref[lead, pl.ds(row + step, 32, stride=2), :] for step in steps]
    return ((quad[0] + quad[1]) + (quad[2] + quad[3])) * 0.25


def put_column(tile, lane_from, slot, column):
    for block in range(4):
        tile = at_lane(tile, lane_from, 32 * block + slot, column[8 * block : 8 * block + 8])
    return tile


def edge_tiles(grid, ref):
    view = ref.reshape(*ref.shape[:-2], grid.own, grid.depth, 128)
    lead = (slice(None),) * (len(ref.shape) - 1)
    return [view.at[lead + (pl.ds((grid.depth - 8) * end, 8),)] for end in range(2)]


FINE_E = [(0, comp) for comp in range(3)] + [(1, 1), (1, 2)] + [(x, comp) for x in (62, 63) for comp in range(3)]
FINE_H = [(0, comp) for comp in range(3)] + [(62, 1), (62, 2)] + [(63, comp) for comp in range(3)]
FINE_M = [0, 1, 62, 63]
COARSE_E = [(0, 1), (0, 2)] + [(31, comp) for comp in range(3)]
COARSE_H = [(31, 1), (31, 2)]
COARSE_M = [0, 31]
COLUMNS = 192
R_ROW = COLUMNS - 8
FACE = 7 * HALO


def wanted(grid):
    return (FINE_E, FINE_H, FINE_M) if grid is Fine else (COARSE_E, COARSE_H, COARSE_M)


def gather(e_hbm, h_hbm, m_hbm, e_ext, zmsg, ytile, columns, h_top, m_edge, h_ends, m_ends, sems):
    def body(grid, gz):
        edge = pl.ds((1 - gz) * (ROWS - HALO), HALO)
        source, target = block_layers(grid, e_hbm), own_layers(grid, e_ext, gz)
        first = [0, 2] if grid is Fine else [0, 1, 2]
        e_loads = {
            comp: pltpu.make_async_copy(source.at[comp], target.at[comp], sems.at[comp])
            for comp in (0, 2, 1)
        }
        h_loads = [] if grid is Fine else [
            pltpu.make_async_copy(h_hbm.at[comp], h_top.at[comp], sems.at[3 + comp]) for comp in (0, 2)
        ]
        loads = [
            pltpu.make_async_copy(h_hbm.at[:, edge], zmsg.at[pl.ds(0, 3 * HALO)].reshape(3, HALO, 128), sems.at[6]),
            pltpu.make_async_copy(m_hbm.at[edge], m_edge, sems.at[7]),
        ]
        for end in range(2):
            for slot, (array, ends) in enumerate(((h_hbm, h_ends), (m_hbm, m_ends))):
                place = ends.at[end].reshape(*ends.shape[1:-2], 8, 8, 128)
                place = place.at[(slice(None),) * (len(ends.shape) - 3) + (pl.ds(0, grid.own),)]
                tiles = edge_tiles(grid, array)[end]
                loads.append(pltpu.make_async_copy(tiles, place, sems.at[8 + 2 * end + slot]))
        for load in list(e_loads.values()) + h_loads + loads:
            load.start()
        clear_pads(grid, e_ext, grid.count + 1)
        for comp in first:
            e_loads[comp].wait()
        for load in h_loads:
            load.wait()
        begin = layer_row(grid, own_first(grid, gz))
        tile = jnp.zeros((8, 128), F32)
        for layer in range(4):
            if grid is Fine:
                row = begin + 2 * grid.stride * layer
                tile = put_column(tile, 0, layer, average(e_ext, 0, row, grid.stride))
                tile = put_column(tile, 0, 8 + layer, average(e_ext, 2, row, grid.stride))
            else:
                top = pl.ds(begin + grid.stride * layer + 3, 32, stride=4)
                h_row = pl.ds(grid.depth * layer + 3, 32, stride=4)
                ex, ey, ez = (e_ext[comp, top, :] for comp in range(3))
                tile = put_column(tile, 127, layer, h_top[0, h_row, :] + 0.5 * ez)
                tile = put_column(tile, 127, 8 + layer, h_top[2, h_row, :] - 0.5 * ex)
                tile = put_column(tile, 127, 16 + layer, ey)
        tile = jnp.where(gz == 1, roll_lanes(tile, 4), tile)
        ytile[...] = tile
        columns[pl.ds(R_ROW, 8), :] = tile
        if grid is Fine:
            e_loads[1].wait()
        layers = HALO // grid.depth
        from_layer = own_first(grid, gz) + (grid.own - layers) * (1 - gz)
        for comp in range(3):
            for layer in range(layers):
                row = layer_row(grid, from_layer + layer)
                to = HALO * (3 + comp) + grid.depth * layer
                zmsg[pl.ds(to, grid.depth), :] = e_ext[comp, pl.ds(row, grid.depth), :]
        want_e, want_h, want_m = wanted(grid)
        slot = 0
        for x, comp in want_e:
            for part in range(grid.parts):
                rows = pl.ds(begin + grid.step * x + part, grid.own, stride=grid.stride)
                columns[pl.ds(slot, grid.own), :] = e_ext[comp, rows, :]
                slot += grid.own
        for load in loads:
            load.wait()
        for x, comp in want_h:
            for part in range(grid.parts):
                rows = pl.ds(grid.step * x % 8 + part, grid.own, stride=8)
                columns[pl.ds(slot, grid.own), :] = h_ends[int(x > 1), comp, rows, :]
                slot += grid.own
        for x in want_m:
            for part in range(grid.parts):
                rows = pl.ds(grid.step * x % 8 + part, grid.own, stride=8)
                columns[pl.ds(slot, grid.own), :] = m_ends[int(x > 1), rows, :].astype(F32)
                slot += grid.own
        zmsg[pl.ds(6 * HALO, HALO), :] = m_edge[...].astype(F32)
        zmsg[pl.ds(FACE, COLUMNS), :] = columns[...]

    by_level(body)


def up_y(grid, ref, comp, row, f):
    lane = lanes_of(f.shape)
    if grid is Fine:
        return jnp.where(lane == 127, 0.0, roll_lanes(f, -1))
    following = ref[comp, pl.ds(row + 1, f.shape[0]), :]
    following = jnp.where(rows_of(f.shape) % 4 == 3, 0.0, following)
    return roll_lanes(jnp.where(lane == 0, following, f), -1)


def down_y(grid, ref, comp, row, f, ghost):
    lane = lanes_of(f.shape)
    if grid is Fine:
        return roll_lanes(jnp.where(lane == 127, ghost, f), 1)
    previous = ref[comp, pl.ds(row - 1, f.shape[0]), :]
    previous = jnp.where(rows_of(f.shape) % 4 == 0, 0.0, previous)
    return roll_lanes(jnp.where(lane == 127, previous, f), 1)


def half_h(grid, e, h_from, from_row, h_to, row):
    for start in range(0, grid.depth, CHUNK):
        r = row + start
        here = pl.ds(r, CHUNK)
        ex, ey, ez = (e[comp, here, :] for comp in range(3))
        above, beside = pl.ds(r + grid.stride, CHUNK), pl.ds(r + grid.step, CHUNK)
        h0 = [h_from(comp, pl.ds(from_row + start, CHUNK)) for comp in range(3)]
        ez_y, ex_y = up_y(grid, e, 2, r, ez), up_y(grid, e, 0, r, ex)
        h_to[0, here, :] = h0[0] - 0.5 * ((ez_y - ez) - (e[1, above, :] - ey))
        h_to[1, here, :] = h0[1] - 0.5 * ((e[0, above, :] - ex) - (e[2, beside, :] - ez))
        h_to[2, here, :] = h0[2] - 0.5 * ((e[1, beside, :] - ey) - (ex_y - ex))


def half_e(grid, h, e_from, e_to, c_ref, row, ghosts):
    for start in range(0, grid.depth, CHUNK):
        r = row + start
        here = pl.ds(r, CHUNK)
        hx, hy, hz = (h[comp, here, :] for comp in range(3))
        below, beside = pl.ds(r - grid.stride, CHUNK), pl.ds(r - grid.step, CHUNK)
        px, pz = ghosts(start)
        hx_y, hz_y = down_y(grid, h, 0, r, hx, px), down_y(grid, h, 2, r, hz, pz)
        c = c_ref[here, :]
        e_to[0, here, :] = e_from[0, here, :] + c * ((hz - hz_y) - (hy - h[1, below, :]))
        e_to[1, here, :] = e_from[1, here, :] + c * ((hx - h[0, below, :]) - (hz - h[2, beside, :]))
        e_to[2, here, :] = e_from[2, here, :] + c * ((hy - h[1, beside, :]) - (hx - hx_y))


def column_of(tile, block, sub, slot, grid):
    shape = (2 * grid.own, 128)
    row = jnp.broadcast_to(tile[sub : sub + 1, :], shape)
    lane = 32 * block + slot + rows_of(shape) // (2 * grid.own // 8)
    picked = jnp.where(lanes_of(shape) == lane, row, 0.0)
    return jnp.broadcast_to(jnp.sum(picked, axis=1, keepdims=True), shape)


def each(fn, *columns):
    return [fn(*parts) for parts in zip(*columns, strict=True)]


def plus_y(f, ghost=0.0):
    following = f[1:] + [ghost]
    return [
        roll_lanes(jnp.where(lanes_of(p.shape) == 0, nxt, p), -1) - p
        for p, nxt in zip(f, following, strict=True)
    ]


def minus_y(f, ghost=0.0):
    previous = [ghost] + f[:-1]
    return [
        p - roll_lanes(jnp.where(lanes_of(p.shape) == 127, prv, p), 1)
        for p, prv in zip(f, previous, strict=True)
    ]


def plus_z(f):
    return [
        jnp.where(rows_of(p.shape) == p.shape[0] - 1, 0.0, roll_rows(p, -1)) - p for p in f
    ]


def minus_z(f):
    return [p - jnp.where(rows_of(p.shape) == 0, 0.0, roll_rows(p, 1)) for p in f]


def add(a, b):
    return each(lambda p, q: p + q, a, b)


def sub(a, b):
    return each(lambda p, q: p - q, a, b)


def mul(a, b):
    return each(lambda p, q: p * q, a, b)


def scale(by, a):
    return [by * p for p in a]


def read_columns(grid, own, other, gz):
    want_e, want_h, want_m = wanted(grid)
    found, slot = [], 0
    for _ in range(len(want_e) + len(want_h) + len(want_m)):
        col = []
        for _ in range(grid.parts):
            rows = pl.ds(slot, grid.own)
            mine, theirs = own[rows, :], other[pl.ds(FACE + slot, grid.own), :]
            low, high = jnp.where(gz == 0, mine, theirs), jnp.where(gz == 0, theirs, mine)
            col.append(jnp.concatenate([low, high], axis=0))
            slot += grid.own
        found.append(col)
    e_found, found = found[: len(want_e)], found[len(want_e) :]
    h_found, m_found = found[: len(want_h)], found[len(want_h) :]
    return (
        dict(zip(want_e, e_found, strict=True)),
        dict(zip(want_h, h_found, strict=True)),
        dict(zip(want_m, m_found, strict=True)),
    )


def write_planes(ref, columns):
    row = 0
    for col in columns:
        for p in col:
            ref[pl.ds(row, p.shape[0]), :] = p
            row += p.shape[0]


def read_planes(grid, ref, *indices):
    height, parts = 2 * grid.own, grid.parts
    return [
        [ref[pl.ds(height * (parts * i + part), height), :] for part in range(parts)] for i in indices
    ]


def sent_rows(plane, gz):
    return jnp.where(gz == 0, roll_rows(plane, -6), plane)[:10]


def write_message(grid, ref, columns, gz):
    row = 0
    for col in columns:
        for p in col:
            rows = p if grid is Coarse else sent_rows(p, gz)
            ref[pl.ds(row, rows.shape[0]), :] = rows
            row += rows.shape[0]


def read_message(grid, ref, count, gz):
    if grid is Coarse:
        return read_planes(grid, ref, *range(count))
    planes = []
    for i in range(count):
        start = min(10 * i, ref.shape[0] - 16)
        p = ref[pl.ds(start, 16), :]
        planes.append([pltpu.roll(p, 16 + start - 10 * i + 6 * gz, 0)])
    return planes


def extend(
    e_in,
    h_own,
    m_own,
    zmsg,
    permittivity,
    columns,
    e_ext,
    h_ext,
    c_ext,
    up,
    down,
    to_up,
    to_down,
    c_planes,
    table,
    sems,
):
    def body(grid, gz):
        load = pltpu.make_async_copy(permittivity, table, sems.at[0])
        load.start()
        clear_pads(grid, h_ext, 0)
        halo = halo_first(grid, gz)
        for layer in range(grid.count - grid.own):
            for start in range(0, grid.depth, CHUNK):
                rows = pl.ds(layer_row(grid, halo + layer) + start, CHUNK)
                for comp in range(3):
                    from_rows = pl.ds(HALO * (3 + comp) + grid.depth * layer + start, CHUNK)
                    e_ext[comp, rows, :] = zmsg[from_rows, :]

        def h_halo(comp, rows):
            return zmsg[pl.ds(HALO * comp + rows.start, rows.size), :]

        for layer in range(grid.count - grid.own):
            row = layer_row(grid, halo + layer)
            half_h(grid, e_ext, h_halo, grid.depth * layer, h_ext, row)
        for layer in range(grid.own):
            row = layer_row(grid, own_first(grid, gz) + layer)
            half_h(grid, e_ext, lambda comp, rows: h_own[comp, rows, :], grid.depth * layer, h_ext, row)
        load.wait()
        values = [0.5 / jnp.full((8, 128), table[i], F32) for i in range(MATS)]

        def coef(is_material, rows):
            parts = [jnp.concatenate([value] * (rows // 8), axis=0) for value in values]
            found = parts[MATS - 1]
            for i in range(MATS - 2, -1, -1):
                found = jnp.where(is_material(i), parts[i], found)
            return found

        for start in range(0, HALO, CHUNK):
            layer, rest = divmod(start, grid.depth)
            material = zmsg[pl.ds(6 * HALO + start, CHUNK), :]
            row = layer_row(grid, halo + layer) + rest
            c_ext[pl.ds(row, CHUNK), :] = coef(lambda i, m=material: m == float(i), CHUNK)
        for start in range(0, ROWS, CHUNK):
            layer, rest = divmod(start, grid.depth)
            material = m_own[pl.ds(start, CHUNK), :]
            row = layer_row(grid, own_first(grid, gz) + layer) + rest
            c_ext[pl.ds(row, CHUNK), :] = coef(lambda i, m=material: m == i, CHUNK)

        e, h, m = read_columns(grid, columns, zmsg, gz)
        c = {
            x: [coef(lambda i, q=part: q == float(i), part.shape[0]) for part in col] for x, col in m.items()
        }
        write_planes(c_planes, list(c.values()))
        if grid is Coarse:
            ex, ey, ez = (e[31, comp] for comp in range(3))
            hy = sub(h[31, 1], scale(0.5, add(plus_z(ex), ez)))
            hz = add(h[31, 2], scale(0.5, add(ey, plus_y(ex))))
            sent_up, sent_down = [hy, hz], [e[0, 1], e[0, 2]]
        else:
            ex, ey, ez = (e[0, comp] for comp in range(3))
            hx = sub(h[0, 0], scale(0.5, sub(plus_y(ez), plus_z(ey))))
            hy = sub(h[0, 1], scale(0.5, sub(plus_z(ex), sub(e[1, 2], ez))))
            hz = sub(h[0, 2], scale(0.5, sub(sub(e[1, 1], ey), plus_y(ex))))
            ey_next = add(ey, mul(c[0], sub(minus_z(hx), hz)))
            ez_next = add(ez, mul(c[0], sub(hy, minus_y(hx))))
            sent_down = [ey, ez, ey_next, ez_next, c[0]]
            ex, ey, ez = (e[62, comp] for comp in range(3))
            hy62 = sub(h[62, 1], scale(0.5, sub(plus_z(ex), sub(e[63, 2], ez))))
            hz62 = sub(h[62, 2], scale(0.5, sub(sub(e[63, 1], ey), plus_y(ex))))
            ex, ey, ez = (e[63, comp] for comp in range(3))
            hx = sub(h[63, 0], scale(0.5, sub(plus_y(ez), plus_z(ey))))
            hy = sub(h[63, 1], scale(0.5, add(plus_z(ex), ez)))
            hz = add(h[63, 2], scale(0.5, add(ey, plus_y(ex))))
            ex_next = add(ex, mul(c[63], sub(minus_y(hz), minus_z(hy))))
            ey_next = add(ey, mul(c[63], sub(minus_z(hx), sub(hz, hz62))))
            ez_next = add(ez, mul(c[63], sub(sub(hy, hy62), minus_y(hx))))
            sent_up = [hy, hz, ex_next, ey_next, ez_next, c[63]]
        write_planes(up, sent_up)
        write_planes(down, sent_down)
        write_message(grid, to_up, sent_up, gz)
        write_message(grid, to_down, sent_down, gz)

    by_level(body)


def join_y(up_in, down_in, c_planes, yin, yzin, r_own, r_other, to_up, to_down, ptile, patched):
    def body(grid, gz):
        top = yin[...] + yzin[...]
        lane, row = lanes_of(top.shape), rows_of(top.shape)
        to_up[...] = up_in[...]
        to_down[...] = down_in[...]
        shape = (2 * grid.own, 128)
        if grid is Coarse:
            ptile[...] = top
            rows = pl.ds(8 * 7, 8)
            change = jnp.where(lanes_of(shape) == 127, 0.5 * column_of(top, 3, 7, 0, grid), 0.0)
            to_up[rows, :] = to_up[rows, :] + change
            return
        r = r_own[pl.ds(R_ROW, 8), :] + r_other[pl.ds(FACE + R_ROW, 8), :]
        kind = (lane % 32) // 8
        above = jnp.where(lane % 8 == 7, 0.0, roll_lanes(top, -1))
        px = top - 0.5 * roll_lanes(r, -8) + 0.5 * roll_lanes(above - top, -16)
        beside = roll_rows(top, -1)
        beside = jnp.where(row == 7, jnp.where(lane >= 96, 0.0, roll_lanes(beside, -32)), beside)
        pz = top + 0.5 * roll_lanes(r, 8) - 0.5 * roll_lanes(beside - top, -8)
        plane = jnp.where(kind == 0, px, jnp.where(kind == 1, pz, 0.0))
        ptile[...] = plane
        bottom = lanes_of(shape) == 0
        (c0,), (c63,) = read_planes(grid, c_planes, 0, 3)
        low = jnp.where(bottom, c0 * column_of(plane, 0, 0, 0, grid), 0.0)
        high_z = jnp.where(bottom, c63 * column_of(plane, 3, 7, 0, grid), 0.0)
        high_x = jnp.where(bottom, -c63 * column_of(plane, 3, 7, 8, grid), 0.0)
        ey_top = column_of(top, 0, 0, 16, grid)
        patched[pl.ds(0, 16), :] = low
        patched[pl.ds(16, 16), :] = ey_top

        def change(ref, index, value):
            rows = pl.ds(10 * index, 10)
            ref[rows, :] = ref[rows, :] + sent_rows(value, gz)

        change(to_down, 3, low)
        change(to_up, 4, high_z)
        change(to_up, 2, high_x)
        to_down[pl.ds(50, 10), :] = sent_rows(ey_top, gz)

    by_level(body)


def advance(
    e_ext, h_ext, c_ext, ptile, e_out, h_out, e_edge, h_edge, e_mid, h_mid, e_last, plane, sems
):
    def body(grid, gz):
        first = own_first(grid, gz)
        tile = jnp.where(gz == 0, ptile[...], roll_lanes(ptile[...], -3))

        def write(source, target, sem, layer=None):
            source, target = own_layers(grid, source, gz), block_layers(grid, target)
            if layer is not None:
                source, target = source.at[:, layer], target.at[:, layer]
            return pltpu.make_async_copy(source, target, sem)

        def keep_edges(source, target):
            for comp in range(3):
                for layer in range(grid.own):
                    for edge in range(2):
                        row = layer_row(grid, first + layer) + (grid.depth - 8) * edge
                        target[edge, comp, pl.ds(8 * layer, 8), :] = source[comp, pl.ds(row, 8), :]

        clear_pads(grid, h_mid, 0)
        if grid is Fine:
            clear_pads(grid, e_mid, grid.count + 1)
            for kind in range(2):
                for layer in range(5):
                    for block in range(4):
                        value = roll_lanes(tile, 127 - (32 * block + 8 * kind + layer))
                        for step in range(2):
                            rows = pl.ds(64 * layer + 16 * block + step, 8, stride=2)
                            plane[kind, rows, :] = value

            def ghosts(index):
                begin = 64 * (index // 2)

                def of(start):
                    rows = pl.ds(pl.multiple_of(begin + start, 8), CHUNK)
                    return plane[0, rows, :], plane[1, rows, :]

                return of

            for layer in range(grid.count):
                row = grid.stride * (layer + 1)
                half_e(grid, h_ext, e_ext, e_mid, c_ext, row, ghosts(layer))
            for layer in range(grid.count):
                row = grid.stride * (layer + 1)
                half_h(grid, e_mid, lambda comp, rows: h_ext[comp, rows, :], row, h_mid, row)
            h_write = write(h_mid, h_out, sems.at[0])
            h_write.start()
            e_begin = e_mid
        else:
            for comp in range(3):
                for layer in range(grid.count):
                    rows = pl.ds(layer_row(grid, layer), grid.depth)
                    h_mid[comp, rows, :] = h_ext[comp, rows, :]
            lane = lanes_of((8, 128))
            for layer in range(grid.count):
                for block in range(4):
                    rows = pl.ds(layer_row(grid, layer) + 32 * block + 3, 8, stride=4)
                    rx = roll_lanes(tile, 127 - (32 * block + layer))
                    rz = roll_lanes(tile, 127 - (32 * block + 8 + layer))
                    h_mid[0, rows, :] = h_mid[0, rows, :] - jnp.where(lane == 127, 0.5 * rz, 0.0)
                    h_mid[2, rows, :] = h_mid[2, rows, :] + jnp.where(lane == 127, 0.5 * rx, 0.0)
            h_write = write(h_mid, h_out, sems.at[0])
            h_write.start()
            e_begin = e_ext

            def ghosts(index):
                return lambda start: (0.0, 0.0)

        for layer in range(grid.own):
            row = layer_row(grid, first + layer)
            half_e(grid, h_mid, e_begin, e_last, c_ext, row, ghosts(first + layer))
            write(e_last, e_out, sems.at[1], layer).start()
        keep_edges(h_mid, h_edge)
        keep_edges(e_last, e_edge)
        h_write.wait()
        write(e_last, e_out, sems.at[1]).wait()

    by_level(body)


def correct(
    up,
    down,
    c_planes,
    patched,
    from_below,
    from_above,
    e_edge,
    h_edge,
    e_in,
    h_in,
    e_out,
    h_out,
    e_tile,
    h_tile,
    sems,
):
    def body(grid, gz):
        last = grid.last

        def put(ref, edge, comp, x, change):
            for part, p in enumerate(change):
                own = jnp.where(gz == 0, p[: grid.own], p[grid.own :])
                rows = pl.ds(grid.step * x % 8 + part, grid.own, stride=8)
                ref[edge, comp, rows, :] = ref[edge, comp, rows, :] + own

        def finish(edge):
            copies = []
            for slot, (tile, out) in enumerate(((h_tile, h_out), (e_tile, e_out))):
                source = tile.at[edge].reshape(3, 8, 8, 128).at[:, pl.ds(0, grid.own)]
                target = block_layers(grid, out).at[:, :, pl.ds((grid.depth - 8) * edge, 8), :]
                copies.append(pltpu.make_async_copy(source, target, sems.at[2 * edge + slot]))
            for copy in copies:
                copy.start()
            return copies

        if grid is Fine:
            zero = [jnp.zeros((16, 128), F32)]
            ey64, ez64, ey64_part, ez64_part, c64, ey_top = read_message(grid, from_above, 6, gz)
            hy63, hz63 = read_planes(grid, up, 0, 1)
            c0, c1, c62, c63 = read_planes(grid, c_planes, *range(4))
            ghost = -0.5 * ey_top[0]
            dhy, dhz = scale(0.5, ez64), scale(-0.5, ey64)
            dex = mul(c63, sub(minus_y(dhz, ghost), minus_z(dhy)))
            dey = scale(-1.0, mul(c63, dhz))
            dez = mul(c63, dhy)
            dex62 = mul(c62, minus_y(zero, ghost))
            ey64_next = add(ey64_part, mul(c64, add(hz63, dhz)))
            ez64_next = sub(ez64_part, mul(c64, add(hy63, dhy)))
            dhx2 = scale(-0.5, sub(plus_y(dez), plus_z(dey)))
            dhy2 = add(dhy, scale(-0.5, sub(plus_z(dex), sub(ez64_next, dez))))
            dhz2 = add(dhz, scale(-0.5, sub(sub(ey64_next, dey), plus_y(dex))))
            dhy62 = scale(-0.5, sub(plus_z(dex62), dez))
            dhz62 = scale(-0.5, sub(dey, plus_y(dex62)))
            put(h_tile, 1, 0, 63, dhx2)
            put(h_tile, 1, 1, 63, dhy2)
            put(h_tile, 1, 2, 63, dhz2)
            put(h_tile, 1, 1, 62, dhy62)
            put(h_tile, 1, 2, 62, dhz62)
            put(e_tile, 1, 0, 63, add(dex, mul(c63, sub(minus_y(dhz2, ghost), minus_z(dhy2)))))
            put(e_tile, 1, 1, 63, add(dey, mul(c63, sub(minus_z(dhx2), sub(dhz2, dhz62)))))
            put(e_tile, 1, 2, 63, add(dez, mul(c63, sub(sub(dhy2, dhy62), minus_y(dhx2)))))
            put(e_tile, 1, 0, 62, add(dex62, mul(c62, sub(minus_y(dhz62, ghost), minus_z(dhy62)))))
            put(e_tile, 1, 1, 62, scale(-1.0, mul(c62, dhz62)))
            put(e_tile, 1, 2, 62, mul(c62, dhy62))
            copies = finish(1)

            hy_part, hz_part, ex_part, ey_part, ez_part, cm = read_message(grid, from_below, 6, gz)
            ey0, ez0, ey0_part, ez0_part = read_planes(grid, down, *range(4))
            ez0_change, ey_top = read_planes(grid, patched, 0, 1)
            ez0_part = add(ez0_part, ez0_change)
            ghost = -0.5 * ey_top[0]
            dhy, dhz = scale(0.5, ez0), scale(-0.5, ey0)
            hym, hzm = add(hy_part, dhy), add(hz_part, dhz)
            exm = add(ex_part, mul(cm, sub(minus_y(dhz, ghost), minus_z(dhy))))
            eym = sub(ey_part, mul(cm, dhz))
            ezm = add(ez_part, mul(cm, dhy))
            dey, dez = mul(c0, hzm), scale(-1.0, mul(c0, hym))
            dhx2 = scale(-0.5, sub(plus_y(dez), plus_z(dey)))
            dhy2 = scale(-0.5, dez)
            dhz2 = scale(0.5, dey)
            hym2 = add(hym, scale(-0.5, sub(plus_z(exm), sub(add(ez0_part, dez), ezm))))
            hzm2 = add(hzm, scale(-0.5, sub(sub(add(ey0_part, dey), eym), plus_y(exm))))
            put(h_tile, 0, 0, 0, dhx2)
            put(h_tile, 0, 1, 0, dhy2)
            put(h_tile, 0, 2, 0, dhz2)
            put(e_tile, 0, 0, 0, mul(c0, sub(minus_y(dhz2), minus_z(dhy2))))
            put(e_tile, 0, 1, 0, add(dey, mul(c0, sub(minus_z(dhx2), sub(dhz2, hzm2)))))
            put(e_tile, 0, 2, 0, add(dez, mul(c0, sub(sub(dhy2, hym2), minus_y(dhx2)))))
            put(e_tile, 0, 1, 1, mul(c1, dhz2))
            put(e_tile, 0, 2, 1, scale(-1.0, mul(c1, dhy2)))
            copies += finish(0)
        else:
            ey32, ez32 = read_message(grid, from_above, 2, gz)
            c0, c31 = read_planes(grid, c_planes, 0, 1)
            dhy, dhz = scale(0.5, ez32), scale(-0.5, ey32)
            put(h_tile, 1, 1, last, dhy)
            put(h_tile, 1, 2, last, dhz)
            put(e_tile, 1, 0, last, mul(c31, sub(minus_y(dhz), minus_z(dhy))))
            put(e_tile, 1, 1, last, scale(-1.0, mul(c31, dhz)))
            put(e_tile, 1, 2, last, mul(c31, dhy))
            copies = finish(1)
            hy_part, hz_part = read_message(grid, from_below, 2, gz)
            ey0, ez0 = read_planes(grid, down, 0, 1)
            put(e_tile, 0, 1, 0, mul(c0, add(hz_part, scale(-0.5, ey0))))
            put(e_tile, 0, 2, 0, scale(-1.0, mul(c0, add(hy_part, scale(0.5, ez0)))))
            copies += finish(0)
        for copy in copies:
            copy.wait()

    by_level(body)


def across(x, dx=0, dy=0, dz=0):
    nx, ny, nz = lax.axis_size("gx"), lax.axis_size("gy"), lax.axis_size("gz")
    pairs = [
        ((i * ny + j) * nz + k, ((i + dx) % nx * ny + (j + dy) % ny) * nz + (k + dz) % nz)
        for i in range(nx)
        for j in range(ny)
        for k in range(nz)
    ]
    return lax.ppermute(x, ("gx", "gy", "gz"), pairs)


def fast_shards(electric, magnetic, material, permittivity):
    e = electric.reshape(3, ROWS, 128)
    h = magnetic.reshape(3, ROWS, 128)
    m = material.reshape(ROWS, 128)
    dma = pltpu.SemaphoreType.DMA
    e_ext, zmsg, ytile, columns = kernel_call(
        gather,
        [vmem(3, EXT, 128), vmem(FACE + COLUMNS, 128), vmem(8, 128), vmem(COLUMNS, 128)],
        [HBM] * 3,
        [VM] * 4,
        [
            pltpu.VMEM((3, ROWS, 128), F32),
            pltpu.VMEM((HALO, 128), jnp.int32),
            pltpu.VMEM((2, 3, 64, 128), F32),
            pltpu.VMEM((2, 64, 128), jnp.int32),
            dma((12,)),
        ],
    )(far(e), far(h), far(m))
    zin = across(zmsg, dz=1)
    yzin = across(ytile, dy=1, dz=1)
    yin = across(ytile, dy=1)
    e_ext, h_ext, c_ext, up, down, up_part, down_part, c_planes = kernel_call(
        extend,
        [
            vmem(3, EXT, 128),
            vmem(3, EXT, 128),
            vmem(EXT, 128),
            vmem(96, 128),
            vmem(96, 128),
            vmem(64, 128),
            vmem(64, 128),
            vmem(64, 128),
        ],
        [VM] * 4 + [HBM, VM],
        [VM] * 8,
        [pltpu.SMEM((MATS,), F32), dma((1,))],
        aliases={0: 0},
    )(held(e_ext), held(h), held(m), held(zin), far(permittivity), held(columns))
    to_up, to_down, ptile, patched = kernel_call(
        join_y,
        [vmem(64, 128), vmem(64, 128), vmem(8, 128), vmem(32, 128)],
        [VM] * 7,
        [VM] * 4,
    )(*(held(part) for part in (up_part, down_part, c_planes, yin, yzin, columns, zin)))
    from_below = across(to_up, dx=1, dz=1)
    from_above = across(to_down, dx=-1, dz=1)
    whole = jax.ShapeDtypeStruct((3, ROWS, 128), F32)
    e_out, h_out, e_edge, h_edge = kernel_call(
        advance,
        [whole, whole, vmem(2, 3, 64, 128), vmem(2, 3, 64, 128)],
        [VM] * 4,
        [HBM, HBM, VM, VM],
        [pltpu.VMEM((3, EXT, 128), F32)] * 3 + [pltpu.VMEM((2, 320, 128), F32), dma((2,))],
    )(*(held(part) for part in (e_ext, h_ext, c_ext, ptile)))
    e_out, h_out, _, _ = kernel_call(
        correct,
        [whole, whole, vmem(2, 3, 64, 128), vmem(2, 3, 64, 128)],
        [VM] * 8 + [HBM] * 2,
        [HBM] * 2 + [VM] * 2,
        [dma((4,))],
        aliases={8: 0, 9: 1, 6: 2, 7: 3},
    )(
        *(held(part) for part in (up, down, c_planes, patched, from_below, from_above, e_edge, h_edge)),
        e_out,
        h_out,
    )
    return e_out.reshape(electric.shape), h_out.reshape(magnetic.shape)


def solution(mesh):
    placed = (
        P(("parts", "gy"), "gx", "gz", None, None),
        P(("parts", "gy"), "gx", "gz", None, None),
        P(("parts", "gy"), "gx", "gz", None),
        P(),
    )
    fast = mesh.shape["gy"] == 2 and mesh.shape["gz"] == 2
    return jax.shard_map(
        fast_shards if fast else general_shards,
        mesh=mesh,
        in_specs=placed,
        out_specs=(
            P(("parts", "gy"), "gx", "gz", None, None),
            P(("parts", "gy"), "gx", "gz", None, None),
        ),
        check_vma=False,
    )
```

```python
from functools import partial

import jax
import jax.numpy as jnp
from jax import lax
from jax.experimental import pallas as pl
from jax.experimental.pallas import tpu as pltpu
from jax.sharding import PartitionSpec as P

CZ = 4
CX = 32
CY = 512
MATS = 4


courant = 0.5


def passed_along(x, axis, by):
    devices = lax.axis_size(axis)
    return lax.ppermute(x, axis, [(i, (i + by) % devices) for i in range(devices)])


def from_behind(x, axis, by):
    devices = lax.axis_size(axis)
    pairs = [(i, i + by) for i in range(devices) if 0 <= i + by < devices]
    return lax.ppermute(x, axis, pairs)


def forward_diff(values, dim_axis, ghost_plane):
    shifted = jnp.concatenate(
        [
            lax.slice_in_dim(values, 1, values.shape[dim_axis], axis=dim_axis),
            jnp.expand_dims(ghost_plane, dim_axis),
        ],
        axis=dim_axis,
    )
    return shifted - values


def backward_diff(values, dim_axis, ghost_plane):
    shifted = jnp.concatenate(
        [
            jnp.expand_dims(ghost_plane, dim_axis),
            lax.slice_in_dim(values, 0, values.shape[dim_axis] - 1, axis=dim_axis),
        ],
        axis=dim_axis,
    )
    return values - shifted


def curl_with(differ, vectors, ghost_depth, ghost_width, ghost_height):
    ghosts = (ghost_depth, ghost_width, ghost_height)

    def along_axis(component, dim_axis):
        return differ(vectors[component], dim_axis, ghosts[dim_axis][component])

    curl_x = along_axis(2, 2) - along_axis(1, 0)
    curl_y = along_axis(0, 0) - along_axis(2, 1)
    curl_z = along_axis(1, 1) - along_axis(0, 2)
    return jnp.stack([curl_x, curl_y, curl_z])


def restrict(face_plane):
    quads = face_plane.reshape(3, face_plane.shape[1] // 2, 2, face_plane.shape[2] // 2, 2)
    return (
        quads[:, :, 0, :, 0] + quads[:, :, 0, :, 1] + (quads[:, :, 1, :, 0] + quads[:, :, 1, :, 1])
    ) * 0.25


def enlarge(face_plane):
    return jnp.repeat(jnp.repeat(face_plane, 2, axis=1), 2, axis=2)


def lookup(material, permittivity):
    permit_sum = jnp.zeros(material.shape, jnp.float32)
    for material_id in range(MATS):
        permit_sum = permit_sum + jnp.where(material == material_id, permittivity[material_id], 0.0)
    return courant / permit_sum


def pack_face(face_plane, length):
    flat_face = face_plane.reshape(3, -1)
    if flat_face.shape[1] < length:
        flat_face = jnp.concatenate(
            [flat_face, jnp.zeros((3, length - flat_face.shape[1]), flat_face.dtype)], axis=1
        )
    return flat_face


def unpack_face(flat_face, row_count, col_count):
    return flat_face[:, : row_count * col_count].reshape(3, row_count, col_count)


def level_height(got_height, is_fine):
    return got_height if is_fine else restrict(got_height)


def low_faces(grid_shape, is_fine, flat_field):
    vectors = flat_field.reshape((3,) + grid_shape)
    face_plane = vectors[:, :, :, 0]
    if not is_fine:
        face_plane = enlarge(face_plane)
    return (
        pack_face(vectors[:, :, 0, :], CZ * CY),
        pack_face(vectors[:, 0, :, :], CX * CY),
        face_plane,
    )


def high_faces(grid_shape, is_fine, flat_field):
    vectors = flat_field.reshape((3,) + grid_shape)
    face_plane = vectors[:, :, :, -1]
    if not is_fine:
        face_plane = enlarge(face_plane)
    return (
        pack_face(vectors[:, :, -1, :], CZ * CY),
        pack_face(vectors[:, -1, :, :], CX * CY),
        face_plane,
    )


def advance_magnetic(
    grid_shape, is_fine, does_move, e_flat, h_flat, got_width, got_depth, got_height
):
    if not does_move:
        return h_flat
    deep_cells, wide_cells, tall_cells = grid_shape
    vectors = e_flat.reshape((3,) + grid_shape)
    curl_term = curl_with(
        forward_diff,
        vectors,
        unpack_face(got_depth, wide_cells, tall_cells),
        unpack_face(got_width, deep_cells, tall_cells),
        level_height(got_height, is_fine),
    )
    return (h_flat.reshape((3,) + grid_shape) - courant * curl_term).reshape(3, -1)


def advance_electric(
    grid_shape, is_fine, does_move, e_flat, h_flat, coefficient, got_width, got_depth, got_height
):
    if not does_move:
        return e_flat
    deep_cells, wide_cells, tall_cells = grid_shape
    magnetic = h_flat.reshape((3,) + grid_shape)
    curl_term = curl_with(
        backward_diff,
        magnetic,
        unpack_face(got_depth, wide_cells, tall_cells),
        unpack_face(got_width, deep_cells, tall_cells),
        level_height(got_height, is_fine),
    )
    return (
        e_flat.reshape((3,) + grid_shape) + coefficient.reshape(grid_shape) * curl_term
    ).reshape(3, -1)


def pass_width(face_plane, offset):
    return passed_along(face_plane, "gx", offset)


def pass_depth(face_plane, offset):
    return from_behind(face_plane, "gz", offset)


def pass_height(face_plane, offset):
    return from_behind(face_plane, "gy", offset)


def general_shards(electric, magnetic, material, permittivity):
    cell_count = electric.shape[-1]
    e_flat = electric.reshape(3, cell_count)
    h_flat = magnetic.reshape(3, cell_count)
    coefficient = lookup(material.reshape(cell_count), permittivity)
    is_fine = lax.axis_index("gy") >= lax.axis_size("gy") // 2
    coarse_shape = (CZ, CX, CY)
    fine_shape = (2 * CZ, 2 * CX, CY // 4)
    for substep in range(2):
        coarse_moves = substep == 0
        face_width, face_depth, face_height = lax.cond(
            is_fine,
            partial(low_faces, fine_shape, True),
            partial(low_faces, coarse_shape, False),
            e_flat,
        )
        got_depth = pass_depth(face_depth, -1)
        got_height = pass_height(face_height, -1)
        got_width = pass_width(face_width, -1)
        h_flat = lax.cond(
            is_fine,
            partial(advance_magnetic, fine_shape, True, True),
            partial(advance_magnetic, coarse_shape, False, coarse_moves),
            e_flat,
            h_flat,
            got_width,
            got_depth,
            got_height,
        )
        rim_width, rim_depth, rim_height = lax.cond(
            is_fine,
            partial(high_faces, fine_shape, True),
            partial(high_faces, coarse_shape, False),
            h_flat,
        )
        rim_depth = pass_depth(rim_depth, 1)
        rim_height = pass_height(rim_height, 1)
        rim_width = pass_width(rim_width, 1)
        e_flat = lax.cond(
            is_fine,
            partial(advance_electric, fine_shape, True, True),
            partial(advance_electric, coarse_shape, False, coarse_moves),
            e_flat,
            h_flat,
            coefficient,
            rim_width,
            rim_depth,
            rim_height,
        )
    return (e_flat.reshape(electric.shape), h_flat.reshape(magnetic.shape))


ROWS = 512
HALO = 128
EXT = 1296
LIMIT = 40 * 1024 * 1024
F32 = jnp.float32
VM = pl.BlockSpec(memory_space=pltpu.VMEM)
HBM = pl.BlockSpec(memory_space=pltpu.HBM)
CHUNK = 32


class Fine:
    depth, stride, count, own, step, parts, last = 64, 72, 10, 8, 1, 1, 63


class Coarse:
    depth, stride, count, own, step, parts, last = 128, 144, 5, 4, 4, 4, 31


def vmem(*shape, dtype=F32):
    return pltpu.VMEM(shape, dtype)


def held(x):
    return pltpu.with_memory_space_constraint(x, pltpu.VMEM)


def far(x):
    return pltpu.with_memory_space_constraint(x, pltpu.HBM)


def kernel_call(body, out_shape, in_specs, out_specs, scratch=(), aliases=None, cost=None):
    return pl.pallas_call(
        body,
        cost_estimate=cost,
        out_shape=out_shape,
        in_specs=in_specs,
        out_specs=out_specs,
        scratch_shapes=list(scratch),
        input_output_aliases=aliases or {},
        compiler_params=pltpu.CompilerParams(vmem_limit_bytes=LIMIT),
    )


def by_level(body):
    is_fine = lax.axis_index("gy") >= lax.axis_size("gy") // 2
    gz = lax.axis_index("gz")
    pl.when(is_fine)(lambda: body(Fine, gz))
    pl.when(jnp.logical_not(is_fine))(lambda: body(Coarse, gz))


def lanes_of(shape):
    return lax.broadcasted_iota(jnp.int32, shape, len(shape) - 1)


def rows_of(shape):
    return lax.broadcasted_iota(jnp.int32, shape, len(shape) - 2)


def roll_lanes(x, by):
    return pltpu.roll(x, by % 128, 1)


def roll_rows(x, by):
    return pltpu.roll(x, by % x.shape[0], 0)


def layer_row(grid, index):
    return pl.multiple_of(grid.stride * (index + 1), 8)


def own_first(grid, gz):
    return (grid.count - grid.own) * gz


def halo_first(grid, gz):
    return grid.own * (1 - gz)


def clear_pads(grid, ref, *zero_layers):
    for comp in range(3):
        for index in range(grid.count + 2):
            start, size = grid.stride * index, grid.stride
            if index not in zero_layers:
                start, size = start + grid.depth, size - grid.depth
            ref[comp, pl.ds(start, size), :] = jnp.zeros((size, 128), F32)


def own_layers(grid, ref, gz):
    view = ref.reshape(3, EXT // grid.stride, grid.stride, 128)
    return view.at[:, pl.ds(1 + own_first(grid, gz), grid.own), pl.ds(0, grid.depth), :]


def block_layers(grid, ref):
    return ref.reshape(3, grid.own, grid.depth, 128)


def at_lane(tile, lane_from, lane_to, value):
    lane = lanes_of(value.shape)
    return jnp.where(lane == lane_to, roll_lanes(value, lane_to - lane_from), tile)


def average(ref, lead, row, stride):
    steps = (0, 1, stride, stride + 1)
    quad = [ref[lead, pl.ds(row + step, 32, stride=2), :] for step in steps]
    return ((quad[0] + quad[1]) + (quad[2] + quad[3])) * 0.25


def put_column(tile, lane_from, slot, column):
    for block in range(4):
        tile = at_lane(tile, lane_from, 32 * block + slot, column[8 * block : 8 * block + 8])
    return tile


FINE_E = [(0, comp) for comp in range(3)] + [(1, 1), (1, 2)] + [(x, comp) for x in (62, 63) for comp in range(3)]
FINE_H = [(0, comp) for comp in range(3)] + [(62, 1), (62, 2)] + [(63, comp) for comp in range(3)]
FINE_M = [0, 1, 62, 63]
COARSE_E = [(0, 1), (0, 2)] + [(31, comp) for comp in range(3)]
COARSE_H = [(31, 1), (31, 2)]
COARSE_M = [0, 31]
COLUMNS = 192
R_ROW = COLUMNS - 8
FACE = 7 * HALO


def wanted(grid):
    return (FINE_E, FINE_H, FINE_M) if grid is Fine else (COARSE_E, COARSE_H, COARSE_M)


def top_tile(tile, layer, ex, ey, ez, hx, hz):
    tile = put_column(tile, 127, layer, hx + 0.5 * ez)
    tile = put_column(tile, 127, 8 + layer, hz - 0.5 * ex)
    return put_column(tile, 127, 16 + layer, ey)


def edge_tiles(grid, ref):
    view = ref.reshape(grid.own, grid.depth, 128)
    return [view.at[:, pl.ds((grid.depth - 8) * end, 8), :] for end in range(2)]


def peek(e_hbm, h_hbm, edge_tile, e_ends, h_ends, sems):
    def body(grid, gz):
        if grid is Fine:
            edge_tile[...] = jnp.zeros((8, 128), F32)
            return
        loads = []
        for end in range(2):
            rows = pl.ds((1 - gz) * (ROWS - HALO) + (HALO - 8) * end, 8)
            loads.append(pltpu.make_async_copy(e_hbm.at[:, rows], e_ends.at[end], sems.at[2 * end]))
            loads.append(pltpu.make_async_copy(h_hbm.at[:, rows], h_ends.at[end], sems.at[2 * end + 1]))
        for load in loads:
            load.start()
        for load in loads:
            load.wait()
        tile = jnp.zeros((8, 128), F32)
        for end in range(2):
            ex, ey, ez = (e_ends[end, comp] for comp in range(3))
            hx, hz = h_ends[end, 0], h_ends[end, 2]
            for kind, value in enumerate((hx + 0.5 * ez, hz - 0.5 * ex, ey)):
                value = value if end else roll_rows(value, -3)
                tile = at_lane(tile, 127, 96 * end + 8 * kind + 3, value)
        edge_tile[...] = jnp.where(gz == 1, roll_lanes(tile, 1), tile)

    by_level(body)


def take_material(m_hbm, after, m_face, m_ends, sems):
    def body(grid, gz):
        layer = pl.ds((1 - gz) * (ROWS - HALO), HALO)
        loads = [pltpu.make_async_copy(m_hbm.at[layer], m_face, sems.at[0])]
        for end, tiles in enumerate(edge_tiles(grid, m_hbm)):
            place = m_ends.at[end].reshape(8, 8, 128).at[pl.ds(0, grid.own)]
            loads.append(pltpu.make_async_copy(tiles, place, sems.at[1 + end]))
        for load in loads:
            load.start()
        for load in loads:
            load.wait()

    by_level(body)


def gather(e_own, h_own, m_face, m_ends, zmsg, ytile, columns):
    def body(grid, gz):
        tile = jnp.zeros((8, 128), F32)
        for layer in range(4):
            if grid is Fine:
                row = 2 * grid.depth * layer
                tile = put_column(tile, 0, layer, average(e_own, 0, row, grid.depth))
                tile = put_column(tile, 0, 8 + layer, average(e_own, 2, row, grid.depth))
            else:
                top = pl.ds(grid.depth * layer + 3, 32, stride=4)
                ex, ey, ez = (e_own[comp, top, :] for comp in range(3))
                tile = top_tile(tile, layer, ex, ey, ez, h_own[0, top, :], h_own[2, top, :])
        tile = jnp.where(gz == 1, roll_lanes(tile, 4), tile)
        ytile[...] = tile
        columns[pl.ds(R_ROW, 8), :] = tile
        want_e, want_h, want_m = wanted(grid)
        slot = 0

        def column_rows(x, part):
            return pl.ds(grid.step * x + part, grid.own, stride=grid.depth)

        def put(value):
            nonlocal slot
            columns[pl.ds(slot, grid.own), :] = value
            slot += grid.own

        for x, comp in want_e:
            for part in range(grid.parts):
                put(e_own[comp, column_rows(x, part), :])
        for x, comp in want_h:
            for part in range(grid.parts):
                put(h_own[comp, column_rows(x, part), :])
        for x in want_m:
            for part in range(grid.parts):
                rows = pl.ds(grid.step * x % 8 + part, grid.own, stride=8)
                put(m_ends[int(x > 1), rows, :].astype(F32))
        edge = pl.ds(pl.multiple_of((1 - gz) * (ROWS - HALO), HALO), HALO)
        for comp in range(3):
            zmsg[pl.ds(HALO * comp, HALO), :] = h_own[comp, edge, :]
            zmsg[pl.ds(HALO * (3 + comp), HALO), :] = e_own[comp, edge, :]
        zmsg[pl.ds(6 * HALO, HALO), :] = m_face[...].astype(F32)
        zmsg[pl.ds(FACE, COLUMNS), :] = columns[...]

    by_level(body)


def join_z(ytile, edge_tile, z_in, joined, z_out):
    joined[...] = ytile[...] + edge_tile[...]


def up_y(grid, ref, comp, row, f):
    lane = lanes_of(f.shape)
    if grid is Fine:
        return jnp.where(lane == 127, 0.0, roll_lanes(f, -1))
    following = ref[comp, pl.ds(row + 1, f.shape[0]), :]
    following = jnp.where(rows_of(f.shape) % 4 == 3, 0.0, following)
    return roll_lanes(jnp.where(lane == 0, following, f), -1)


def down_y(grid, ref, comp, row, f, ghost):
    lane = lanes_of(f.shape)
    if grid is Fine:
        return roll_lanes(jnp.where(lane == 127, ghost, f), 1)
    previous = ref[comp, pl.ds(row - 1, f.shape[0]), :]
    previous = jnp.where(rows_of(f.shape) % 4 == 0, 0.0, previous)
    return roll_lanes(jnp.where(lane == 127, previous, f), 1)


def half_h(grid, e, h_from, from_row, h_to, row):
    for start in range(0, grid.depth, CHUNK):
        r = row + start
        here = pl.ds(r, CHUNK)
        ex, ey, ez = (e[comp, here, :] for comp in range(3))
        above, beside = pl.ds(r + grid.stride, CHUNK), pl.ds(r + grid.step, CHUNK)
        h0 = [h_from(comp, pl.ds(from_row + start, CHUNK)) for comp in range(3)]
        ez_y, ex_y = up_y(grid, e, 2, r, ez), up_y(grid, e, 0, r, ex)
        h_to[0, here, :] = h0[0] - 0.5 * ((ez_y - ez) - (e[1, above, :] - ey))
        h_to[1, here, :] = h0[1] - 0.5 * ((e[0, above, :] - ex) - (e[2, beside, :] - ez))
        h_to[2, here, :] = h0[2] - 0.5 * ((e[1, beside, :] - ey) - (ex_y - ex))


def half_e(grid, h, e_from, e_to, c_ref, row, ghosts):
    for start in range(0, grid.depth, CHUNK):
        r = row + start
        here = pl.ds(r, CHUNK)
        hx, hy, hz = (h[comp, here, :] for comp in range(3))
        below, beside = pl.ds(r - grid.stride, CHUNK), pl.ds(r - grid.step, CHUNK)
        px, pz = ghosts(start)
        hx_y, hz_y = down_y(grid, h, 0, r, hx, px), down_y(grid, h, 2, r, hz, pz)
        c = c_ref[here, :]
        e_to[0, here, :] = e_from[0, here, :] + c * ((hz - hz_y) - (hy - h[1, below, :]))
        e_to[1, here, :] = e_from[1, here, :] + c * ((hx - h[0, below, :]) - (hz - h[2, beside, :]))
        e_to[2, here, :] = e_from[2, here, :] + c * ((hy - h[1, beside, :]) - (hx - hx_y))


def column_of(tile, block, sub, slot, grid):
    shape = (2 * grid.own, 128)
    row = jnp.broadcast_to(tile[sub : sub + 1, :], shape)
    lane = 32 * block + slot + rows_of(shape) // (2 * grid.own // 8)
    picked = jnp.where(lanes_of(shape) == lane, row, 0.0)
    return jnp.broadcast_to(jnp.sum(picked, axis=1, keepdims=True), shape)


def each(fn, *columns):
    return [fn(*parts) for parts in zip(*columns, strict=True)]


def plus_y(f, ghost=0.0):
    following = f[1:] + [ghost]
    return [
        roll_lanes(jnp.where(lanes_of(p.shape) == 0, nxt, p), -1) - p
        for p, nxt in zip(f, following, strict=True)
    ]


def minus_y(f, ghost=0.0):
    previous = [ghost] + f[:-1]
    return [
        p - roll_lanes(jnp.where(lanes_of(p.shape) == 127, prv, p), 1)
        for p, prv in zip(f, previous, strict=True)
    ]


def plus_z(f):
    return [
        jnp.where(rows_of(p.shape) == p.shape[0] - 1, 0.0, roll_rows(p, -1)) - p for p in f
    ]


def minus_z(f):
    return [p - jnp.where(rows_of(p.shape) == 0, 0.0, roll_rows(p, 1)) for p in f]


def add(a, b):
    return each(lambda p, q: p + q, a, b)


def sub(a, b):
    return each(lambda p, q: p - q, a, b)


def mul(a, b):
    return each(lambda p, q: p * q, a, b)


def scale(by, a):
    return [by * p for p in a]


def read_columns(grid, own, other, gz):
    want_e, want_h, want_m = wanted(grid)
    found, slot = [], 0
    for _ in range(len(want_e) + len(want_h) + len(want_m)):
        col = []
        for _ in range(grid.parts):
            rows = pl.ds(slot, grid.own)
            mine, theirs = own[rows, :], other[pl.ds(FACE + slot, grid.own), :]
            low, high = jnp.where(gz == 0, mine, theirs), jnp.where(gz == 0, theirs, mine)
            col.append(jnp.concatenate([low, high], axis=0))
            slot += grid.own
        found.append(col)
    e_found, found = found[: len(want_e)], found[len(want_e) :]
    h_found, m_found = found[: len(want_h)], found[len(want_h) :]
    return (
        dict(zip(want_e, e_found, strict=True)),
        dict(zip(want_h, h_found, strict=True)),
        dict(zip(want_m, m_found, strict=True)),
    )


def write_planes(ref, columns):
    row = 0
    for col in columns:
        for p in col:
            ref[pl.ds(row, p.shape[0]), :] = p
            row += p.shape[0]


def read_planes(grid, ref, *indices):
    height, parts = 2 * grid.own, grid.parts
    return [
        [ref[pl.ds(height * (parts * i + part), height), :] for part in range(parts)] for i in indices
    ]


def sent_rows(plane, gz):
    return jnp.where(gz == 0, roll_rows(plane, -6), plane)[:10]


def write_message(grid, ref, columns, gz):
    row = 0
    for col in columns:
        for p in col:
            rows = p if grid is Coarse else sent_rows(p, gz)
            ref[pl.ds(row, rows.shape[0]), :] = rows
            row += rows.shape[0]


def read_message(grid, ref, count, gz):
    if grid is Coarse:
        return read_planes(grid, ref, *range(count))
    planes = []
    for i in range(count):
        start = min(10 * i, ref.shape[0] - 16)
        p = ref[pl.ds(start, 16), :]
        planes.append([pltpu.roll(p, 16 + start - 10 * i + 6 * gz, 0)])
    return planes


def extend(
    e_own,
    h_own,
    m_own,
    zmsg,
    permittivity,
    columns,
    e_ext,
    h_ext,
    c_ext,
    up,
    down,
    to_up,
    to_down,
    c_planes,
    table,
    sems,
):
    def body(grid, gz):
        load = pltpu.make_async_copy(permittivity, table, sems.at[0])
        load.start()
        clear_pads(grid, h_ext, 0)
        clear_pads(grid, e_ext, grid.count + 1)
        for layer in range(grid.own):
            for start in range(0, grid.depth, CHUNK):
                rows = pl.ds(layer_row(grid, own_first(grid, gz) + layer) + start, CHUNK)
                from_rows = pl.ds(grid.depth * layer + start, CHUNK)
                for comp in range(3):
                    e_ext[comp, rows, :] = e_own[comp, from_rows, :]
        halo = halo_first(grid, gz)
        for layer in range(grid.count - grid.own):
            for start in range(0, grid.depth, CHUNK):
                rows = pl.ds(layer_row(grid, halo + layer) + start, CHUNK)
                for comp in range(3):
                    from_rows = pl.ds(HALO * (3 + comp) + grid.depth * layer + start, CHUNK)
                    e_ext[comp, rows, :] = zmsg[from_rows, :]

        def h_halo(comp, rows):
            return zmsg[pl.ds(HALO * comp + rows.start, rows.size), :]

        for layer in range(grid.count - grid.own):
            row = layer_row(grid, halo + layer)
            half_h(grid, e_ext, h_halo, grid.depth * layer, h_ext, row)
        for layer in range(grid.own):
            row = layer_row(grid, own_first(grid, gz) + layer)
            half_h(grid, e_ext, lambda comp, rows: h_own[comp, rows, :], grid.depth * layer, h_ext, row)
        load.wait()
        values = [0.5 / jnp.full((8, 128), table[i], F32) for i in range(MATS)]

        def coef(is_material, rows):
            parts = [jnp.concatenate([value] * (rows // 8), axis=0) for value in values]
            found = parts[MATS - 1]
            for i in range(MATS - 2, -1, -1):
                found = jnp.where(is_material(i), parts[i], found)
            return found

        for start in range(0, HALO, CHUNK):
            layer, rest = divmod(start, grid.depth)
            material = zmsg[pl.ds(6 * HALO + start, CHUNK), :]
            row = layer_row(grid, halo + layer) + rest
            c_ext[pl.ds(row, CHUNK), :] = coef(lambda i, m=material: m == float(i), CHUNK)
        for start in range(0, ROWS, CHUNK):
            layer, rest = divmod(start, grid.depth)
            material = m_own[pl.ds(start, CHUNK), :]
            row = layer_row(grid, own_first(grid, gz) + layer) + rest
            c_ext[pl.ds(row, CHUNK), :] = coef(lambda i, m=material: m == i, CHUNK)

        e, h, m = read_columns(grid, columns, zmsg, gz)
        c = {
            x: [coef(lambda i, q=part: q == float(i), part.shape[0]) for part in col] for x, col in m.items()
        }
        write_planes(c_planes, list(c.values()))
        if grid is Coarse:
            ex, ey, ez = (e[31, comp] for comp in range(3))
            hy = sub(h[31, 1], scale(0.5, add(plus_z(ex), ez)))
            hz = add(h[31, 2], scale(0.5, add(ey, plus_y(ex))))
            sent_up, sent_down = [hy, hz], [e[0, 1], e[0, 2]]
        else:
            ex, ey, ez = (e[0, comp] for comp in range(3))
            hx = sub(h[0, 0], scale(0.5, sub(plus_y(ez), plus_z(ey))))
            hy = sub(h[0, 1], scale(0.5, sub(plus_z(ex), sub(e[1, 2], ez))))
            hz = sub(h[0, 2], scale(0.5, sub(sub(e[1, 1], ey), plus_y(ex))))
            ey_next = add(ey, mul(c[0], sub(minus_z(hx), hz)))
            ez_next = add(ez, mul(c[0], sub(hy, minus_y(hx))))
            sent_down = [ey, ez, ey_next, ez_next, c[0]]
            ex, ey, ez = (e[62, comp] for comp in range(3))
            hy62 = sub(h[62, 1], scale(0.5, sub(plus_z(ex), sub(e[63, 2], ez))))
            hz62 = sub(h[62, 2], scale(0.5, sub(sub(e[63, 1], ey), plus_y(ex))))
            ex, ey, ez = (e[63, comp] for comp in range(3))
            hx = sub(h[63, 0], scale(0.5, sub(plus_y(ez), plus_z(ey))))
            hy = sub(h[63, 1], scale(0.5, add(plus_z(ex), ez)))
            hz = add(h[63, 2], scale(0.5, add(ey, plus_y(ex))))
            ex_next = add(ex, mul(c[63], sub(minus_y(hz), minus_z(hy))))
            ey_next = add(ey, mul(c[63], sub(minus_z(hx), sub(hz, hz62))))
            ez_next = add(ez, mul(c[63], sub(sub(hy, hy62), minus_y(hx))))
            sent_up = [hy, hz, ex_next, ey_next, ez_next, c[63]]
        write_planes(up, sent_up)
        write_planes(down, sent_down)
        write_message(grid, to_up, sent_up, gz)
        write_message(grid, to_down, sent_down, gz)

    by_level(body)


def between(top, r):
    lane, row = lanes_of(top.shape), rows_of(top.shape)
    kind = (lane % 32) // 8
    above = jnp.where(lane % 8 == 7, 0.0, roll_lanes(top, -1))
    px = top - 0.5 * roll_lanes(r, -8) + 0.5 * roll_lanes(above - top, -16)
    beside = roll_rows(top, -1)
    beside = jnp.where(row == 7, jnp.where(lane >= 96, 0.0, roll_lanes(beside, -32)), beside)
    pz = top + 0.5 * roll_lanes(r, 8) - 0.5 * roll_lanes(beside - top, -8)
    return jnp.where(kind == 0, px, jnp.where(kind == 1, pz, 0.0))


def join_y(up_in, down_in, c_planes, yzin, r_own, r_other, to_up, to_down):
    def body(grid, gz):
        top = yzin[...]
        to_up[...] = up_in[...]
        to_down[...] = down_in[...]
        shape = (2 * grid.own, 128)
        if grid is Coarse:
            rows = pl.ds(8 * 7, 8)
            change = jnp.where(lanes_of(shape) == 127, 0.5 * column_of(top, 3, 7, 0, grid), 0.0)
            to_up[rows, :] = to_up[rows, :] + change
            return
        plane = between(top, r_own[pl.ds(R_ROW, 8), :] + r_other[pl.ds(FACE + R_ROW, 8), :])
        bottom = lanes_of(shape) == 0
        (c0,), (c63,) = read_planes(grid, c_planes, 0, 3)

        def change(ref, index, value):
            rows = pl.ds(10 * index, 10)
            ref[rows, :] = ref[rows, :] + sent_rows(value, gz)

        change(to_down, 3, jnp.where(bottom, c0 * column_of(plane, 0, 0, 0, grid), 0.0))
        change(to_up, 4, jnp.where(bottom, c63 * column_of(plane, 3, 7, 0, grid), 0.0))
        change(to_up, 2, jnp.where(bottom, -c63 * column_of(plane, 3, 7, 8, grid), 0.0))
        to_down[pl.ds(50, 10), :] = sent_rows(column_of(top, 0, 0, 16, grid), gz)

    by_level(body)


def advance(
    e_ext,
    h_ext,
    c_ext,
    c_planes,
    yin,
    yzin,
    r_own,
    r_other,
    e_out,
    h_out,
    e_edge,
    h_edge,
    patched,
    e_mid,
    h_mid,
    e_last,
    plane,
    sems,
):
    def body(grid, gz):
        first = own_first(grid, gz)
        upper = lanes_of((8, 128)) % 8 >= 4
        tile = jnp.where(upper == (gz == 0), yzin[...], yin[...])
        if grid is Fine:
            top = tile
            tile = between(top, r_own[pl.ds(R_ROW, 8), :] + r_other[pl.ds(FACE + R_ROW, 8), :])
            ((c0,),) = read_planes(grid, c_planes, 0)
            change = jnp.where(lanes_of((16, 128)) == 0, c0 * column_of(tile, 0, 0, 0, grid), 0.0)
            patched[pl.ds(0, 16), :] = change
            patched[pl.ds(16, 16), :] = column_of(top, 0, 0, 16, grid)
        tile = jnp.where(gz == 0, tile, roll_lanes(tile, -3))

        def write(source, target, sem, layer=None):
            source, target = own_layers(grid, source, gz), block_layers(grid, target)
            if layer is not None:
                source, target = source.at[:, layer], target.at[:, layer]
            return pltpu.make_async_copy(source, target, sem)

        def keep_edges(source, target):
            for comp in range(3):
                for layer in range(grid.own):
                    for edge in range(2):
                        row = layer_row(grid, first + layer) + (grid.depth - 8) * edge
                        target[edge, comp, pl.ds(8 * layer, 8), :] = source[comp, pl.ds(row, 8), :]

        clear_pads(grid, h_mid, 0)
        if grid is Fine:
            clear_pads(grid, e_mid, grid.count + 1)
            for kind in range(2):
                for layer in range(5):
                    for block in range(4):
                        value = roll_lanes(tile, 127 - (32 * block + 8 * kind + layer))
                        for step in range(2):
                            rows = pl.ds(64 * layer + 16 * block + step, 8, stride=2)
                            plane[kind, rows, :] = value

            def ghosts(index):
                begin = 64 * (index // 2)

                def of(start):
                    rows = pl.ds(pl.multiple_of(begin + start, 8), CHUNK)
                    return plane[0, rows, :], plane[1, rows, :]

                return of

            for layer in range(grid.count):
                row = grid.stride * (layer + 1)
                half_e(grid, h_ext, e_ext, e_mid, c_ext, row, ghosts(layer))
            for layer in range(grid.count):
                row = grid.stride * (layer + 1)
                half_h(grid, e_mid, lambda comp, rows: h_ext[comp, rows, :], row, h_mid, row)
            h_write = write(h_mid, h_out, sems.at[0])
            h_write.start()
            e_begin = e_mid
        else:
            for comp in range(3):
                for layer in range(grid.count):
                    rows = pl.ds(layer_row(grid, layer), grid.depth)
                    h_mid[comp, rows, :] = h_ext[comp, rows, :]
            lane = lanes_of((8, 128))
            for layer in range(grid.count):
                for block in range(4):
                    rows = pl.ds(layer_row(grid, layer) + 32 * block + 3, 8, stride=4)
                    rx = roll_lanes(tile, 127 - (32 * block + layer))
                    rz = roll_lanes(tile, 127 - (32 * block + 8 + layer))
                    h_mid[0, rows, :] = h_mid[0, rows, :] - jnp.where(lane == 127, 0.5 * rz, 0.0)
                    h_mid[2, rows, :] = h_mid[2, rows, :] + jnp.where(lane == 127, 0.5 * rx, 0.0)
            h_write = write(h_mid, h_out, sems.at[0])
            h_write.start()
            e_begin = e_ext

            def ghosts(index):
                return lambda start: (0.0, 0.0)

        for layer in range(grid.own):
            row = layer_row(grid, first + layer)
            half_e(grid, h_mid, e_begin, e_last, c_ext, row, ghosts(first + layer))
            write(e_last, e_out, sems.at[1], layer).start()
        keep_edges(h_mid, h_edge)
        keep_edges(e_last, e_edge)
        h_write.wait()
        write(e_last, e_out, sems.at[1]).wait()

    by_level(body)


def correct(
    up,
    down,
    c_planes,
    patched,
    from_below,
    from_above,
    e_edge,
    h_edge,
    e_in,
    h_in,
    e_out,
    h_out,
    e_tile,
    h_tile,
    sems,
):
    def body(grid, gz):
        last = grid.last

        def put(ref, edge, comp, x, change):
            for part, p in enumerate(change):
                own = jnp.where(gz == 0, p[: grid.own], p[grid.own :])
                rows = pl.ds(grid.step * x % 8 + part, grid.own, stride=8)
                ref[edge, comp, rows, :] = ref[edge, comp, rows, :] + own

        def finish(edge):
            copies = []
            for slot, (tile, out) in enumerate(((h_tile, h_out), (e_tile, e_out))):
                source = tile.at[edge].reshape(3, 8, 8, 128).at[:, pl.ds(0, grid.own)]
                target = block_layers(grid, out).at[:, :, pl.ds((grid.depth - 8) * edge, 8), :]
                copies.append(pltpu.make_async_copy(source, target, sems.at[2 * edge + slot]))
            for copy in copies:
                copy.start()
            return copies

        if grid is Fine:
            zero = [jnp.zeros((16, 128), F32)]
            ey64, ez64, ey64_part, ez64_part, c64, ey_top = read_message(grid, from_above, 6, gz)
            hy63, hz63 = read_planes(grid, up, 0, 1)
            c0, c1, c62, c63 = read_planes(grid, c_planes, *range(4))
            ghost = -0.5 * ey_top[0]
            dhy, dhz = scale(0.5, ez64), scale(-0.5, ey64)
            dex = mul(c63, sub(minus_y(dhz, ghost), minus_z(dhy)))
            dey = scale(-1.0, mul(c63, dhz))
            dez = mul(c63, dhy)
            dex62 = mul(c62, minus_y(zero, ghost))
            ey64_next = add(ey64_part, mul(c64, add(hz63, dhz)))
            ez64_next = sub(ez64_part, mul(c64, add(hy63, dhy)))
            dhx2 = scale(-0.5, sub(plus_y(dez), plus_z(dey)))
            dhy2 = add(dhy, scale(-0.5, sub(plus_z(dex), sub(ez64_next, dez))))
            dhz2 = add(dhz, scale(-0.5, sub(sub(ey64_next, dey), plus_y(dex))))
            dhy62 = scale(-0.5, sub(plus_z(dex62), dez))
            dhz62 = scale(-0.5, sub(dey, plus_y(dex62)))
            put(h_tile, 1, 0, 63, dhx2)
            put(h_tile, 1, 1, 63, dhy2)
            put(h_tile, 1, 2, 63, dhz2)
            put(h_tile, 1, 1, 62, dhy62)
            put(h_tile, 1, 2, 62, dhz62)
            put(e_tile, 1, 0, 63, add(dex, mul(c63, sub(minus_y(dhz2, ghost), minus_z(dhy2)))))
            put(e_tile, 1, 1, 63, add(dey, mul(c63, sub(minus_z(dhx2), sub(dhz2, dhz62)))))
            put(e_tile, 1, 2, 63, add(dez, mul(c63, sub(sub(dhy2, dhy62), minus_y(dhx2)))))
            put(e_tile, 1, 0, 62, add(dex62, mul(c62, sub(minus_y(dhz62, ghost), minus_z(dhy62)))))
            put(e_tile, 1, 1, 62, scale(-1.0, mul(c62, dhz62)))
            put(e_tile, 1, 2, 62, mul(c62, dhy62))
            copies = finish(1)

            hy_part, hz_part, ex_part, ey_part, ez_part, cm = read_message(grid, from_below, 6, gz)
            ey0, ez0, ey0_part, ez0_part = read_planes(grid, down, *range(4))
            ez0_change, ey_top = read_planes(grid, patched, 0, 1)
            ez0_part = add(ez0_part, ez0_change)
            ghost = -0.5 * ey_top[0]
            dhy, dhz = scale(0.5, ez0), scale(-0.5, ey0)
            hym, hzm = add(hy_part, dhy), add(hz_part, dhz)
            exm = add(ex_part, mul(cm, sub(minus_y(dhz, ghost), minus_z(dhy))))
            eym = sub(ey_part, mul(cm, dhz))
            ezm = add(ez_part, mul(cm, dhy))
            dey, dez = mul(c0, hzm), scale(-1.0, mul(c0, hym))
            dhx2 = scale(-0.5, sub(plus_y(dez), plus_z(dey)))
            dhy2 = scale(-0.5, dez)
            dhz2 = scale(0.5, dey)
            hym2 = add(hym, scale(-0.5, sub(plus_z(exm), sub(add(ez0_part, dez), ezm))))
            hzm2 = add(hzm, scale(-0.5, sub(sub(add(ey0_part, dey), eym), plus_y(exm))))
            put(h_tile, 0, 0, 0, dhx2)
            put(h_tile, 0, 1, 0, dhy2)
            put(h_tile, 0, 2, 0, dhz2)
            put(e_tile, 0, 0, 0, mul(c0, sub(minus_y(dhz2), minus_z(dhy2))))
            put(e_tile, 0, 1, 0, add(dey, mul(c0, sub(minus_z(dhx2), sub(dhz2, hzm2)))))
            put(e_tile, 0, 2, 0, add(dez, mul(c0, sub(sub(dhy2, hym2), minus_y(dhx2)))))
            put(e_tile, 0, 1, 1, mul(c1, dhz2))
            put(e_tile, 0, 2, 1, scale(-1.0, mul(c1, dhy2)))
            copies += finish(0)
        else:
            ey32, ez32 = read_message(grid, from_above, 2, gz)
            c0, c31 = read_planes(grid, c_planes, 0, 1)
            dhy, dhz = scale(0.5, ez32), scale(-0.5, ey32)
            put(h_tile, 1, 1, last, dhy)
            put(h_tile, 1, 2, last, dhz)
            put(e_tile, 1, 0, last, mul(c31, sub(minus_y(dhz), minus_z(dhy))))
            put(e_tile, 1, 1, last, scale(-1.0, mul(c31, dhz)))
            put(e_tile, 1, 2, last, mul(c31, dhy))
            copies = finish(1)
            hy_part, hz_part = read_message(grid, from_below, 2, gz)
            ey0, ez0 = read_planes(grid, down, 0, 1)
            put(e_tile, 0, 1, 0, mul(c0, add(hz_part, scale(-0.5, ey0))))
            put(e_tile, 0, 2, 0, scale(-1.0, mul(c0, add(hy_part, scale(0.5, ez0)))))
            copies += finish(0)
        for copy in copies:
            copy.wait()

    by_level(body)


def across(x, dx=0, dy=0, dz=0):
    nx, ny, nz = lax.axis_size("gx"), lax.axis_size("gy"), lax.axis_size("gz")
    pairs = [
        ((i * ny + j) * nz + k, ((i + dx) % nx * ny + (j + dy) % ny) * nz + (k + dz) % nz)
        for i in range(nx)
        for j in range(ny)
        for k in range(nz)
    ]
    return lax.ppermute(x, ("gx", "gy", "gz"), pairs)


def fast_shards(electric, magnetic, material, permittivity):
    e = electric.reshape(3, ROWS, 128)
    h = magnetic.reshape(3, ROWS, 128)
    m = material.reshape(ROWS, 128)
    dma = pltpu.SemaphoreType.DMA
    edge_tile = kernel_call(
        peek,
        vmem(8, 128),
        [HBM] * 2,
        VM,
        [pltpu.VMEM((2, 3, 8, 128), F32)] * 2 + [dma((4,))],
    )(far(e), far(h))
    m_face, m_ends = kernel_call(
        take_material,
        [vmem(HALO, 128, dtype=jnp.int32), vmem(2, 64, 128, dtype=jnp.int32)],
        [HBM, VM],
        [VM] * 2,
        [dma((3,))],
    )(far(m), held(edge_tile))
    edge_tile = across(edge_tile, dz=1)
    zmsg, ytile, columns = kernel_call(
        gather,
        [vmem(FACE + COLUMNS, 128), vmem(8, 128), vmem(COLUMNS, 128)],
        [VM] * 4,
        [VM] * 3,
    )(held(e), held(h), held(m_face), held(m_ends))
    ytile, zmsg = kernel_call(
        join_z,
        [vmem(8, 128), vmem(FACE + COLUMNS, 128)],
        [VM] * 3,
        [VM] * 2,
        aliases={2: 1},
    )(held(ytile), held(edge_tile), held(zmsg))
    zin = across(zmsg, dz=1)
    yin = across(ytile, dy=1)
    yzin = across(ytile, dy=1, dz=1)
    e_ext, h_ext, c_ext, up, down, up_part, down_part, c_planes = kernel_call(
        extend,
        [
            vmem(3, EXT, 128),
            vmem(3, EXT, 128),
            vmem(EXT, 128),
            vmem(96, 128),
            vmem(96, 128),
            vmem(64, 128),
            vmem(64, 128),
            vmem(64, 128),
        ],
        [VM] * 4 + [HBM, VM],
        [VM] * 8,
        [pltpu.SMEM((MATS,), F32), dma((1,))],
    )(held(e), held(h), held(m), held(zin), far(permittivity), held(columns))
    to_up, to_down = kernel_call(
        join_y,
        [vmem(64, 128), vmem(64, 128)],
        [VM] * 6,
        [VM] * 2,
    )(*(held(part) for part in (up_part, down_part, c_planes, yzin, columns, zin)))
    from_below = across(to_up, dx=1, dz=1)
    from_above = across(to_down, dx=-1, dz=1)
    whole = jax.ShapeDtypeStruct((3, ROWS, 128), F32)
    e_out, h_out, e_edge, h_edge, patched = kernel_call(
        advance,
        [whole, whole, vmem(2, 3, 64, 128), vmem(2, 3, 64, 128), vmem(32, 128)],
        [VM] * 8,
        [HBM, HBM, VM, VM, VM],
        [pltpu.VMEM((3, EXT, 128), F32)] * 3 + [pltpu.VMEM((2, 320, 128), F32), dma((2,))],
        cost=pl.CostEstimate(flops=10**10, bytes_accessed=10**8, transcendentals=0),
    )(*(held(part) for part in (e_ext, h_ext, c_ext, c_planes, yin, yzin, columns, zin)))
    e_out, h_out, _, _ = kernel_call(
        correct,
        [whole, whole, vmem(2, 3, 64, 128), vmem(2, 3, 64, 128)],
        [VM] * 8 + [HBM] * 2,
        [HBM] * 2 + [VM] * 2,
        [dma((4,))],
        aliases={8: 0, 9: 1, 6: 2, 7: 3},
    )(
        *(held(part) for part in (up, down, c_planes, patched, from_below, from_above, e_edge, h_edge)),
        e_out,
        h_out,
    )
    return e_out.reshape(electric.shape), h_out.reshape(magnetic.shape)


def solution(mesh):
    placed = (
        P(("parts", "gy"), "gx", "gz", None, None),
        P(("parts", "gy"), "gx", "gz", None, None),
        P(("parts", "gy"), "gx", "gz", None),
        P(),
    )
    fast = mesh.shape["gy"] == 2 and mesh.shape["gz"] == 2
    return jax.shard_map(
        fast_shards if fast else general_shards,
        mesh=mesh,
        in_specs=placed,
        out_specs=(
            P(("parts", "gy"), "gx", "gz", None, None),
            P(("parts", "gy"), "gx", "gz", None, None),
        ),
        check_vma=False,
    )
```

```python
from functools import partial

import jax
import jax.numpy as jnp
from jax import lax
from jax.experimental import pallas as pl
from jax.experimental.pallas import tpu as pltpu
from jax.sharding import PartitionSpec as P

CZ = 4
CX = 32
CY = 512
MATS = 4


courant = 0.5


def passed_along(x, axis, by):
    devices = lax.axis_size(axis)
    return lax.ppermute(x, axis, [(i, (i + by) % devices) for i in range(devices)])


def from_behind(x, axis, by):
    devices = lax.axis_size(axis)
    pairs = [(i, i + by) for i in range(devices) if 0 <= i + by < devices]
    return lax.ppermute(x, axis, pairs)


def forward_diff(values, dim_axis, ghost_plane):
    shifted = jnp.concatenate(
        [
            lax.slice_in_dim(values, 1, values.shape[dim_axis], axis=dim_axis),
            jnp.expand_dims(ghost_plane, dim_axis),
        ],
        axis=dim_axis,
    )
    return shifted - values


def backward_diff(values, dim_axis, ghost_plane):
    shifted = jnp.concatenate(
        [
            jnp.expand_dims(ghost_plane, dim_axis),
            lax.slice_in_dim(values, 0, values.shape[dim_axis] - 1, axis=dim_axis),
        ],
        axis=dim_axis,
    )
    return values - shifted


def curl_with(differ, vectors, ghost_depth, ghost_width, ghost_height):
    ghosts = (ghost_depth, ghost_width, ghost_height)

    def along_axis(component, dim_axis):
        return differ(vectors[component], dim_axis, ghosts[dim_axis][component])

    curl_x = along_axis(2, 2) - along_axis(1, 0)
    curl_y = along_axis(0, 0) - along_axis(2, 1)
    curl_z = along_axis(1, 1) - along_axis(0, 2)
    return jnp.stack([curl_x, curl_y, curl_z])


def restrict(face_plane):
    quads = face_plane.reshape(3, face_plane.shape[1] // 2, 2, face_plane.shape[2] // 2, 2)
    return (
        quads[:, :, 0, :, 0] + quads[:, :, 0, :, 1] + (quads[:, :, 1, :, 0] + quads[:, :, 1, :, 1])
    ) * 0.25


def enlarge(face_plane):
    return jnp.repeat(jnp.repeat(face_plane, 2, axis=1), 2, axis=2)


def lookup(material, permittivity):
    permit_sum = jnp.zeros(material.shape, jnp.float32)
    for material_id in range(MATS):
        permit_sum = permit_sum + jnp.where(material == material_id, permittivity[material_id], 0.0)
    return courant / permit_sum


def pack_face(face_plane, length):
    flat_face = face_plane.reshape(3, -1)
    if flat_face.shape[1] < length:
        flat_face = jnp.concatenate(
            [flat_face, jnp.zeros((3, length - flat_face.shape[1]), flat_face.dtype)], axis=1
        )
    return flat_face


def unpack_face(flat_face, row_count, col_count):
    return flat_face[:, : row_count * col_count].reshape(3, row_count, col_count)


def level_height(got_height, is_fine):
    return got_height if is_fine else restrict(got_height)


def low_faces(grid_shape, is_fine, flat_field):
    vectors = flat_field.reshape((3,) + grid_shape)
    face_plane = vectors[:, :, :, 0]
    if not is_fine:
        face_plane = enlarge(face_plane)
    return (
        pack_face(vectors[:, :, 0, :], CZ * CY),
        pack_face(vectors[:, 0, :, :], CX * CY),
        face_plane,
    )


def high_faces(grid_shape, is_fine, flat_field):
    vectors = flat_field.reshape((3,) + grid_shape)
    face_plane = vectors[:, :, :, -1]
    if not is_fine:
        face_plane = enlarge(face_plane)
    return (
        pack_face(vectors[:, :, -1, :], CZ * CY),
        pack_face(vectors[:, -1, :, :], CX * CY),
        face_plane,
    )


def advance_magnetic(
    grid_shape, is_fine, does_move, e_flat, h_flat, got_width, got_depth, got_height
):
    if not does_move:
        return h_flat
    deep_cells, wide_cells, tall_cells = grid_shape
    vectors = e_flat.reshape((3,) + grid_shape)
    curl_term = curl_with(
        forward_diff,
        vectors,
        unpack_face(got_depth, wide_cells, tall_cells),
        unpack_face(got_width, deep_cells, tall_cells),
        level_height(got_height, is_fine),
    )
    return (h_flat.reshape((3,) + grid_shape) - courant * curl_term).reshape(3, -1)


def advance_electric(
    grid_shape, is_fine, does_move, e_flat, h_flat, coefficient, got_width, got_depth, got_height
):
    if not does_move:
        return e_flat
    deep_cells, wide_cells, tall_cells = grid_shape
    magnetic = h_flat.reshape((3,) + grid_shape)
    curl_term = curl_with(
        backward_diff,
        magnetic,
        unpack_face(got_depth, wide_cells, tall_cells),
        unpack_face(got_width, deep_cells, tall_cells),
        level_height(got_height, is_fine),
    )
    return (
        e_flat.reshape((3,) + grid_shape) + coefficient.reshape(grid_shape) * curl_term
    ).reshape(3, -1)


def pass_width(face_plane, offset):
    return passed_along(face_plane, "gx", offset)


def pass_depth(face_plane, offset):
    return from_behind(face_plane, "gz", offset)


def pass_height(face_plane, offset):
    return from_behind(face_plane, "gy", offset)


def general_shards(electric, magnetic, material, permittivity):
    cell_count = electric.shape[-1]
    e_flat = electric.reshape(3, cell_count)
    h_flat = magnetic.reshape(3, cell_count)
    coefficient = lookup(material.reshape(cell_count), permittivity)
    is_fine = lax.axis_index("gy") >= lax.axis_size("gy") // 2
    coarse_shape = (CZ, CX, CY)
    fine_shape = (2 * CZ, 2 * CX, CY // 4)
    for substep in range(2):
        coarse_moves = substep == 0
        face_width, face_depth, face_height = lax.cond(
            is_fine,
            partial(low_faces, fine_shape, True),
            partial(low_faces, coarse_shape, False),
            e_flat,
        )
        got_depth = pass_depth(face_depth, -1)
        got_height = pass_height(face_height, -1)
        got_width = pass_width(face_width, -1)
        h_flat = lax.cond(
            is_fine,
            partial(advance_magnetic, fine_shape, True, True),
            partial(advance_magnetic, coarse_shape, False, coarse_moves),
            e_flat,
            h_flat,
            got_width,
            got_depth,
            got_height,
        )
        rim_width, rim_depth, rim_height = lax.cond(
            is_fine,
            partial(high_faces, fine_shape, True),
            partial(high_faces, coarse_shape, False),
            h_flat,
        )
        rim_depth = pass_depth(rim_depth, 1)
        rim_height = pass_height(rim_height, 1)
        rim_width = pass_width(rim_width, 1)
        e_flat = lax.cond(
            is_fine,
            partial(advance_electric, fine_shape, True, True),
            partial(advance_electric, coarse_shape, False, coarse_moves),
            e_flat,
            h_flat,
            coefficient,
            rim_width,
            rim_depth,
            rim_height,
        )
    return (e_flat.reshape(electric.shape), h_flat.reshape(magnetic.shape))


ROWS = 512
HALO = 128
EXT = 1296
LIMIT = 40 * 1024 * 1024
F32 = jnp.float32
VM = pl.BlockSpec(memory_space=pltpu.VMEM)
HBM = pl.BlockSpec(memory_space=pltpu.HBM)
CHUNK = 32


class Fine:
    depth, stride, count, own, step, parts, last = 64, 72, 10, 8, 1, 1, 63


class Coarse:
    depth, stride, count, own, step, parts, last = 128, 144, 5, 4, 4, 4, 31


def vmem(*shape, dtype=F32):
    return pltpu.VMEM(shape, dtype)


def held(x):
    return pltpu.with_memory_space_constraint(x, pltpu.VMEM)


def far(x):
    return pltpu.with_memory_space_constraint(x, pltpu.HBM)


def kernel_call(body, out_shape, in_specs, out_specs, scratch=(), aliases=None, cost=None):
    return pl.pallas_call(
        body,
        cost_estimate=cost,
        out_shape=out_shape,
        in_specs=in_specs,
        out_specs=out_specs,
        scratch_shapes=list(scratch),
        input_output_aliases=aliases or {},
        compiler_params=pltpu.CompilerParams(vmem_limit_bytes=LIMIT),
    )


def by_level(body):
    is_fine = lax.axis_index("gy") >= lax.axis_size("gy") // 2
    gz = lax.axis_index("gz")
    pl.when(is_fine)(lambda: body(Fine, gz))
    pl.when(jnp.logical_not(is_fine))(lambda: body(Coarse, gz))


def lanes_of(shape):
    return lax.broadcasted_iota(jnp.int32, shape, len(shape) - 1)


def rows_of(shape):
    return lax.broadcasted_iota(jnp.int32, shape, len(shape) - 2)


def roll_lanes(x, by):
    return pltpu.roll(x, by % 128, 1)


def roll_rows(x, by):
    return pltpu.roll(x, by % x.shape[0], 0)


def layer_row(grid, index):
    return pl.multiple_of(grid.stride * (index + 1), 8)


def own_first(grid, gz):
    return (grid.count - grid.own) * gz


def halo_first(grid, gz):
    return grid.own * (1 - gz)


def clear_pads(grid, ref, *zero_layers):
    for comp in range(3):
        for index in range(grid.count + 2):
            start, size = grid.stride * index, grid.stride
            if index not in zero_layers:
                start, size = start + grid.depth, size - grid.depth
            ref[comp, pl.ds(start, size), :] = jnp.zeros((size, 128), F32)


def own_layers(grid, ref, gz):
    view = ref.reshape(3, EXT // grid.stride, grid.stride, 128)
    return view.at[:, pl.ds(1 + own_first(grid, gz), grid.own), pl.ds(0, grid.depth), :]


def block_layers(grid, ref):
    return ref.reshape(3, grid.own, grid.depth, 128)


def at_lane(tile, lane_from, lane_to, value):
    lane = lanes_of(value.shape)
    return jnp.where(lane == lane_to, roll_lanes(value, lane_to - lane_from), tile)


def average(ref, lead, row, stride):
    steps = (0, 1, stride, stride + 1)
    quad = [ref[lead, pl.ds(row + step, 32, stride=2), :] for step in steps]
    return ((quad[0] + quad[1]) + (quad[2] + quad[3])) * 0.25


def put_column(tile, lane_from, slot, column):
    for block in range(4):
        tile = at_lane(tile, lane_from, 32 * block + slot, column[8 * block : 8 * block + 8])
    return tile


FINE_E = [(0, comp) for comp in range(3)] + [(1, 1), (1, 2)] + [(x, comp) for x in (62, 63) for comp in range(3)]
FINE_H = [(0, comp) for comp in range(3)] + [(62, 1), (62, 2)] + [(63, comp) for comp in range(3)]
FINE_M = [0, 1, 62, 63]
COARSE_E = [(0, 1), (0, 2)] + [(31, comp) for comp in range(3)]
COARSE_H = [(31, 1), (31, 2)]
COARSE_M = [0, 31]
COLUMNS = 192
R_ROW = COLUMNS - 8
FACE = 7 * HALO


def wanted(grid):
    return (FINE_E, FINE_H, FINE_M) if grid is Fine else (COARSE_E, COARSE_H, COARSE_M)


def top_tile(tile, layer, ex, ey, ez, hx, hz):
    tile = put_column(tile, 127, layer, hx + 0.5 * ez)
    tile = put_column(tile, 127, 8 + layer, hz - 0.5 * ex)
    return put_column(tile, 127, 16 + layer, ey)


def edge_tiles(grid, ref):
    view = ref.reshape(grid.own, grid.depth, 128)
    return [view.at[:, pl.ds((grid.depth - 8) * end, 8), :] for end in range(2)]


def material_loads(grid, gz, m_hbm, m_face, m_ends, sems):
    face = pl.ds((1 - gz) * (ROWS - HALO), HALO)
    loads = [pltpu.make_async_copy(m_hbm.at[face], m_face, sems.at[0])]
    for end, tiles in enumerate(edge_tiles(grid, m_hbm)):
        place = m_ends.at[end].reshape(8, 8, 128).at[pl.ds(0, grid.own)]
        loads.append(pltpu.make_async_copy(tiles, place, sems.at[1 + end]))
    return loads


def peek(e_hbm, h_hbm, m_hbm, edge_tile, m_face, m_ends, e_ends, h_ends, sems, m_sems):
    def body(grid, gz):
        if grid is Fine:
            edge_tile[...] = jnp.zeros((8, 128), F32)
            return
        m_loads = material_loads(grid, gz, m_hbm, m_face, m_ends, m_sems)
        loads = []
        for end in range(2):
            rows = pl.ds((1 - gz) * (ROWS - HALO) + (HALO - 8) * end, 8)
            place = pl.ds(0, 8)
            loads.append(pltpu.make_async_copy(e_hbm.at[:, rows], e_ends.at[end, :, place], sems.at[2 * end]))
            loads.append(pltpu.make_async_copy(h_hbm.at[:, rows], h_ends.at[end, :, place], sems.at[2 * end + 1]))
        for load in loads + m_loads:
            load.start()
        for load in loads:
            load.wait()
        tile = jnp.zeros((8, 128), F32)
        lane = lanes_of((8, 128))
        for end in range(2):
            rows = pl.ds(0 if end else 3, 8)
            ex, ey, ez = (e_ends[end, comp, rows, :] for comp in range(3))
            hx, hz = h_ends[end, 0, rows, :], h_ends[end, 2, rows, :]
            for kind, value in enumerate((hx + 0.5 * ez, hz - 0.5 * ex, ey)):
                to = 96 * end + 8 * kind + 3 + gz
                tile = jnp.where(lane == to, pltpu.roll(value, to + 1, 1), tile)
        edge_tile[...] = tile
        for load in m_loads:
            load.wait()

    by_level(body)


def fine_material(m_hbm, face_in, ends_in, m_face, m_ends, sems):
    def body(grid, gz):
        if grid is Coarse:
            return
        loads = material_loads(grid, gz, m_hbm, m_face, m_ends, sems)
        for load in loads:
            load.start()
        for load in loads:
            load.wait()

    by_level(body)


def gather(e_own, h_own, m_face, m_ends, zmsg, ytile, columns):
    def body(grid, gz):
        tile = jnp.zeros((8, 128), F32)
        for layer in range(4):
            if grid is Fine:
                row = 2 * grid.depth * layer
                tile = put_column(tile, 0, layer, average(e_own, 0, row, grid.depth))
                tile = put_column(tile, 0, 8 + layer, average(e_own, 2, row, grid.depth))
            else:
                top = pl.ds(grid.depth * layer + 3, 32, stride=4)
                ex, ey, ez = (e_own[comp, top, :] for comp in range(3))
                tile = top_tile(tile, layer, ex, ey, ez, h_own[0, top, :], h_own[2, top, :])
        tile = jnp.where(gz == 1, roll_lanes(tile, 4), tile)
        ytile[...] = tile
        columns[pl.ds(R_ROW, 8), :] = tile
        want_e, want_h, want_m = wanted(grid)
        slot = 0

        def column_rows(x, part):
            return pl.ds(grid.step * x + part, grid.own, stride=grid.depth)

        def put(value):
            nonlocal slot
            columns[pl.ds(slot, grid.own), :] = value
            slot += grid.own

        for x, comp in want_e:
            for part in range(grid.parts):
                put(e_own[comp, column_rows(x, part), :])
        for x, comp in want_h:
            for part in range(grid.parts):
                put(h_own[comp, column_rows(x, part), :])
        for x in want_m:
            for part in range(grid.parts):
                rows = pl.ds(grid.step * x % 8 + part, grid.own, stride=8)
                put(m_ends[int(x > 1), rows, :].astype(F32))
        edge = pl.ds(pl.multiple_of((1 - gz) * (ROWS - HALO), HALO), HALO)
        for comp in range(3):
            zmsg[pl.ds(HALO * comp, HALO), :] = h_own[comp, edge, :]
            zmsg[pl.ds(HALO * (3 + comp), HALO), :] = e_own[comp, edge, :]
        zmsg[pl.ds(6 * HALO, HALO), :] = m_face[...].astype(F32)
        zmsg[pl.ds(FACE, COLUMNS), :] = columns[...]

    by_level(body)


def join_z(ytile, edge_tile, joined):
    joined[...] = ytile[...] + edge_tile[...]


def up_y(grid, ref, comp, row, f):
    lane = lanes_of(f.shape)
    if grid is Fine:
        return jnp.where(lane == 127, 0.0, roll_lanes(f, -1))
    following = ref[comp, pl.ds(row + 1, f.shape[0]), :]
    following = jnp.where(rows_of(f.shape) % 4 == 3, 0.0, following)
    return roll_lanes(jnp.where(lane == 0, following, f), -1)


def down_y(grid, ref, comp, row, f, ghost):
    lane = lanes_of(f.shape)
    if grid is Fine:
        return roll_lanes(jnp.where(lane == 127, ghost, f), 1)
    previous = ref[comp, pl.ds(row - 1, f.shape[0]), :]
    previous = jnp.where(rows_of(f.shape) % 4 == 0, 0.0, previous)
    return roll_lanes(jnp.where(lane == 127, previous, f), 1)


def half_h(grid, e, h_from, from_row, h_to, row):
    for start in range(0, grid.depth, CHUNK):
        r = row + start
        here = pl.ds(r, CHUNK)
        ex, ey, ez = (e[comp, here, :] for comp in range(3))
        above, beside = pl.ds(r + grid.stride, CHUNK), pl.ds(r + grid.step, CHUNK)
        h0 = [h_from(comp, pl.ds(from_row + start, CHUNK)) for comp in range(3)]
        ez_y, ex_y = up_y(grid, e, 2, r, ez), up_y(grid, e, 0, r, ex)
        h_to[0, here, :] = h0[0] - 0.5 * ((ez_y - ez) - (e[1, above, :] - ey))
        h_to[1, here, :] = h0[1] - 0.5 * ((e[0, above, :] - ex) - (e[2, beside, :] - ez))
        h_to[2, here, :] = h0[2] - 0.5 * ((e[1, beside, :] - ey) - (ex_y - ex))


def half_e(grid, h, e_from, e_to, c_ref, row, ghosts):
    for start in range(0, grid.depth, CHUNK):
        r = row + start
        here = pl.ds(r, CHUNK)
        hx, hy, hz = (h[comp, here, :] for comp in range(3))
        below, beside = pl.ds(r - grid.stride, CHUNK), pl.ds(r - grid.step, CHUNK)
        px, pz = ghosts(start)
        hx_y, hz_y = down_y(grid, h, 0, r, hx, px), down_y(grid, h, 2, r, hz, pz)
        c = c_ref[here, :]
        e_to[0, here, :] = e_from[0, here, :] + c * ((hz - hz_y) - (hy - h[1, below, :]))
        e_to[1, here, :] = e_from[1, here, :] + c * ((hx - h[0, below, :]) - (hz - h[2, beside, :]))
        e_to[2, here, :] = e_from[2, here, :] + c * ((hy - h[1, beside, :]) - (hx - hx_y))


def column_of(tile, block, sub, slot, grid):
    shape = (2 * grid.own, 128)
    row = jnp.broadcast_to(tile[sub : sub + 1, :], shape)
    lane = 32 * block + slot + rows_of(shape) // (2 * grid.own // 8)
    picked = jnp.where(lanes_of(shape) == lane, row, 0.0)
    return jnp.broadcast_to(jnp.sum(picked, axis=1, keepdims=True), shape)


def each(fn, *columns):
    return [fn(*parts) for parts in zip(*columns, strict=True)]


def plus_y(f, ghost=0.0):
    following = f[1:] + [ghost]
    return [
        roll_lanes(jnp.where(lanes_of(p.shape) == 0, nxt, p), -1) - p
        for p, nxt in zip(f, following, strict=True)
    ]


def minus_y(f, ghost=0.0):
    previous = [ghost] + f[:-1]
    return [
        p - roll_lanes(jnp.where(lanes_of(p.shape) == 127, prv, p), 1)
        for p, prv in zip(f, previous, strict=True)
    ]


def plus_z(f):
    return [
        jnp.where(rows_of(p.shape) == p.shape[0] - 1, 0.0, roll_rows(p, -1)) - p for p in f
    ]


def minus_z(f):
    return [p - jnp.where(rows_of(p.shape) == 0, 0.0, roll_rows(p, 1)) for p in f]


def add(a, b):
    return each(lambda p, q: p + q, a, b)


def sub(a, b):
    return each(lambda p, q: p - q, a, b)


def mul(a, b):
    return each(lambda p, q: p * q, a, b)


def scale(by, a):
    return [by * p for p in a]


def read_columns(grid, own, other, gz):
    want_e, want_h, want_m = wanted(grid)
    found, slot = [], 0
    for _ in range(len(want_e) + len(want_h) + len(want_m)):
        col = []
        for _ in range(grid.parts):
            rows = pl.ds(slot, grid.own)
            mine, theirs = own[rows, :], other[pl.ds(FACE + slot, grid.own), :]
            low, high = jnp.where(gz == 0, mine, theirs), jnp.where(gz == 0, theirs, mine)
            col.append(jnp.concatenate([low, high], axis=0))
            slot += grid.own
        found.append(col)
    e_found, found = found[: len(want_e)], found[len(want_e) :]
    h_found, m_found = found[: len(want_h)], found[len(want_h) :]
    return (
        dict(zip(want_e, e_found, strict=True)),
        dict(zip(want_h, h_found, strict=True)),
        dict(zip(want_m, m_found, strict=True)),
    )


def write_planes(ref, columns):
    row = 0
    for col in columns:
        for p in col:
            ref[pl.ds(row, p.shape[0]), :] = p
            row += p.shape[0]


def read_planes(grid, ref, *indices):
    height, parts = 2 * grid.own, grid.parts
    return [
        [ref[pl.ds(height * (parts * i + part), height), :] for part in range(parts)] for i in indices
    ]


def sent_rows(plane, gz):
    return jnp.where(gz == 0, roll_rows(plane, -6), plane)[:10]


def write_message(grid, ref, columns, gz):
    row = 0
    for col in columns:
        for p in col:
            rows = p if grid is Coarse else sent_rows(p, gz)
            ref[pl.ds(row, rows.shape[0]), :] = rows
            row += rows.shape[0]


def read_message(grid, ref, count, gz):
    if grid is Coarse:
        return read_planes(grid, ref, *range(count))
    planes = []
    for i in range(count):
        start = min(10 * i, ref.shape[0] - 16)
        p = ref[pl.ds(start, 16), :]
        planes.append([pltpu.roll(p, 16 + start - 10 * i + 6 * gz, 0)])
    return planes


def extend(
    e_own,
    h_own,
    m_own,
    zmsg,
    permittivity,
    columns,
    e_ext,
    h_ext,
    c_ext,
    up,
    down,
    to_up,
    to_down,
    c_planes,
    table,
    sems,
):
    def body(grid, gz):
        load = pltpu.make_async_copy(permittivity, table, sems.at[0])
        load.start()
        clear_pads(grid, h_ext, 0)
        clear_pads(grid, e_ext, grid.count + 1)
        for layer in range(grid.own):
            for start in range(0, grid.depth, CHUNK):
                rows = pl.ds(layer_row(grid, own_first(grid, gz) + layer) + start, CHUNK)
                from_rows = pl.ds(grid.depth * layer + start, CHUNK)
                for comp in range(3):
                    e_ext[comp, rows, :] = e_own[comp, from_rows, :]
        halo = halo_first(grid, gz)
        for layer in range(grid.count - grid.own):
            for start in range(0, grid.depth, CHUNK):
                rows = pl.ds(layer_row(grid, halo + layer) + start, CHUNK)
                for comp in range(3):
                    from_rows = pl.ds(HALO * (3 + comp) + grid.depth * layer + start, CHUNK)
                    e_ext[comp, rows, :] = zmsg[from_rows, :]

        def h_halo(comp, rows):
            return zmsg[pl.ds(HALO * comp + rows.start, rows.size), :]

        for layer in range(grid.count - grid.own):
            row = layer_row(grid, halo + layer)
            half_h(grid, e_ext, h_halo, grid.depth * layer, h_ext, row)
        for layer in range(grid.own):
            row = layer_row(grid, own_first(grid, gz) + layer)
            half_h(grid, e_ext, lambda comp, rows: h_own[comp, rows, :], grid.depth * layer, h_ext, row)
        load.wait()
        values = [0.5 / jnp.full((8, 128), table[i], F32) for i in range(MATS)]

        def coef(is_material, rows):
            parts = [jnp.concatenate([value] * (rows // 8), axis=0) for value in values]
            found = parts[MATS - 1]
            for i in range(MATS - 2, -1, -1):
                found = jnp.where(is_material(i), parts[i], found)
            return found

        for start in range(0, HALO, CHUNK):
            layer, rest = divmod(start, grid.depth)
            material = zmsg[pl.ds(6 * HALO + start, CHUNK), :]
            row = layer_row(grid, halo + layer) + rest
            c_ext[pl.ds(row, CHUNK), :] = coef(lambda i, m=material: m == float(i), CHUNK)
        for start in range(0, ROWS, CHUNK):
            layer, rest = divmod(start, grid.depth)
            material = m_own[pl.ds(start, CHUNK), :]
            row = layer_row(grid, own_first(grid, gz) + layer) + rest
            c_ext[pl.ds(row, CHUNK), :] = coef(lambda i, m=material: m == i, CHUNK)

        e, h, m = read_columns(grid, columns, zmsg, gz)
        c = {
            x: [coef(lambda i, q=part: q == float(i), part.shape[0]) for part in col] for x, col in m.items()
        }
        write_planes(c_planes, list(c.values()))
        if grid is Coarse:
            ex, ey, ez = (e[31, comp] for comp in range(3))
            hy = sub(h[31, 1], scale(0.5, add(plus_z(ex), ez)))
            hz = add(h[31, 2], scale(0.5, add(ey, plus_y(ex))))
            sent_up, sent_down = [hy, hz], [e[0, 1], e[0, 2]]
        else:
            ex, ey, ez = (e[0, comp] for comp in range(3))
            hx = sub(h[0, 0], scale(0.5, sub(plus_y(ez), plus_z(ey))))
            hy = sub(h[0, 1], scale(0.5, sub(plus_z(ex), sub(e[1, 2], ez))))
            hz = sub(h[0, 2], scale(0.5, sub(sub(e[1, 1], ey), plus_y(ex))))
            ey_next = add(ey, mul(c[0], sub(minus_z(hx), hz)))
            ez_next = add(ez, mul(c[0], sub(hy, minus_y(hx))))
            sent_down = [ey, ez, ey_next, ez_next, c[0]]
            ex, ey, ez = (e[62, comp] for comp in range(3))
            hy62 = sub(h[62, 1], scale(0.5, sub(plus_z(ex), sub(e[63, 2], ez))))
            hz62 = sub(h[62, 2], scale(0.5, sub(sub(e[63, 1], ey), plus_y(ex))))
            ex, ey, ez = (e[63, comp] for comp in range(3))
            hx = sub(h[63, 0], scale(0.5, sub(plus_y(ez), plus_z(ey))))
            hy = sub(h[63, 1], scale(0.5, add(plus_z(ex), ez)))
            hz = add(h[63, 2], scale(0.5, add(ey, plus_y(ex))))
            ex_next = add(ex, mul(c[63], sub(minus_y(hz), minus_z(hy))))
            ey_next = add(ey, mul(c[63], sub(minus_z(hx), sub(hz, hz62))))
            ez_next = add(ez, mul(c[63], sub(sub(hy, hy62), minus_y(hx))))
            sent_up = [hy, hz, ex_next, ey_next, ez_next, c[63]]
        write_planes(up, sent_up)
        write_planes(down, sent_down)
        write_message(grid, to_up, sent_up, gz)
        write_message(grid, to_down, sent_down, gz)

    by_level(body)


def between(top, r):
    lane, row = lanes_of(top.shape), rows_of(top.shape)
    kind = (lane % 32) // 8
    above = jnp.where(lane % 8 == 7, 0.0, roll_lanes(top, -1))
    px = top - 0.5 * roll_lanes(r, -8) + 0.5 * roll_lanes(above - top, -16)
    beside = roll_rows(top, -1)
    beside = jnp.where(row == 7, jnp.where(lane >= 96, 0.0, roll_lanes(beside, -32)), beside)
    pz = top + 0.5 * roll_lanes(r, 8) - 0.5 * roll_lanes(beside - top, -8)
    return jnp.where(kind == 0, px, jnp.where(kind == 1, pz, 0.0))


def join_y(up_in, down_in, c_planes, yzin, r_own, r_other, to_up, to_down):
    def body(grid, gz):
        top = yzin[...]
        to_up[...] = up_in[...]
        to_down[...] = down_in[...]
        shape = (2 * grid.own, 128)
        if grid is Coarse:
            rows = pl.ds(8 * 7, 8)
            change = jnp.where(lanes_of(shape) == 127, 0.5 * column_of(top, 3, 7, 0, grid), 0.0)
            to_up[rows, :] = to_up[rows, :] + change
            return
        plane = between(top, r_own[pl.ds(R_ROW, 8), :] + r_other[pl.ds(FACE + R_ROW, 8), :])
        bottom = lanes_of(shape) == 0
        (c0,), (c63,) = read_planes(grid, c_planes, 0, 3)

        def change(ref, index, value):
            rows = pl.ds(10 * index, 10)
            ref[rows, :] = ref[rows, :] + sent_rows(value, gz)

        change(to_down, 3, jnp.where(bottom, c0 * column_of(plane, 0, 0, 0, grid), 0.0))
        change(to_up, 4, jnp.where(bottom, c63 * column_of(plane, 3, 7, 0, grid), 0.0))
        change(to_up, 2, jnp.where(bottom, -c63 * column_of(plane, 3, 7, 8, grid), 0.0))
        to_down[pl.ds(50, 10), :] = sent_rows(column_of(top, 0, 0, 16, grid), gz)

    by_level(body)


def advance(
    e_ext,
    h_ext,
    c_ext,
    c_planes,
    yin,
    yzin,
    r_own,
    r_other,
    e_out,
    h_out,
    e_edge,
    h_edge,
    patched,
    e_mid,
    h_mid,
    e_last,
    plane,
    sems,
):
    def body(grid, gz):
        first = own_first(grid, gz)
        upper = lanes_of((8, 128)) % 8 >= 4
        tile = jnp.where(upper == (gz == 0), yzin[...], yin[...])
        if grid is Fine:
            top = tile
            tile = between(top, r_own[pl.ds(R_ROW, 8), :] + r_other[pl.ds(FACE + R_ROW, 8), :])
            ((c0,),) = read_planes(grid, c_planes, 0)
            change = jnp.where(lanes_of((16, 128)) == 0, c0 * column_of(tile, 0, 0, 0, grid), 0.0)
            patched[pl.ds(0, 16), :] = change
            patched[pl.ds(16, 16), :] = column_of(top, 0, 0, 16, grid)
        tile = jnp.where(gz == 0, tile, roll_lanes(tile, -3))

        def write(source, target, sem, layer=None):
            source, target = own_layers(grid, source, gz), block_layers(grid, target)
            if layer is not None:
                source, target = source.at[:, layer], target.at[:, layer]
            return pltpu.make_async_copy(source, target, sem)

        def keep_edges(source, target):
            for comp in range(3):
                for layer in range(grid.own):
                    for edge in range(2):
                        row = layer_row(grid, first + layer) + (grid.depth - 8) * edge
                        target[edge, comp, pl.ds(8 * layer, 8), :] = source[comp, pl.ds(row, 8), :]

        clear_pads(grid, h_mid, 0)
        if grid is Fine:
            clear_pads(grid, e_mid, grid.count + 1)
            for kind in range(2):
                for layer in range(5):
                    for block in range(4):
                        value = roll_lanes(tile, 127 - (32 * block + 8 * kind + layer))
                        for step in range(2):
                            rows = pl.ds(64 * layer + 16 * block + step, 8, stride=2)
                            plane[kind, rows, :] = value

            def ghosts(index):
                begin = 64 * (index // 2)

                def of(start):
                    rows = pl.ds(pl.multiple_of(begin + start, 8), CHUNK)
                    return plane[0, rows, :], plane[1, rows, :]

                return of

            for layer in range(grid.count):
                row = grid.stride * (layer + 1)
                half_e(grid, h_ext, e_ext, e_mid, c_ext, row, ghosts(layer))
            for layer in range(grid.count):
                row = grid.stride * (layer + 1)
                half_h(grid, e_mid, lambda comp, rows: h_ext[comp, rows, :], row, h_mid, row)
            h_write = write(h_mid, h_out, sems.at[0])
            h_write.start()
            e_begin = e_mid
        else:
            for comp in range(3):
                for layer in range(grid.count):
                    rows = pl.ds(layer_row(grid, layer), grid.depth)
                    h_mid[comp, rows, :] = h_ext[comp, rows, :]
            lane = lanes_of((8, 128))
            for layer in range(grid.count):
                for block in range(4):
                    rows = pl.ds(layer_row(grid, layer) + 32 * block + 3, 8, stride=4)
                    rx = roll_lanes(tile, 127 - (32 * block + layer))
                    rz = roll_lanes(tile, 127 - (32 * block + 8 + layer))
                    h_mid[0, rows, :] = h_mid[0, rows, :] - jnp.where(lane == 127, 0.5 * rz, 0.0)
                    h_mid[2, rows, :] = h_mid[2, rows, :] + jnp.where(lane == 127, 0.5 * rx, 0.0)
            h_write = write(h_mid, h_out, sems.at[0])
            h_write.start()
            e_begin = e_ext

            def ghosts(index):
                return lambda start: (0.0, 0.0)

        for layer in range(grid.own):
            row = layer_row(grid, first + layer)
            half_e(grid, h_mid, e_begin, e_last, c_ext, row, ghosts(first + layer))
            write(e_last, e_out, sems.at[1], layer).start()
        keep_edges(h_mid, h_edge)
        keep_edges(e_last, e_edge)
        h_write.wait()
        write(e_last, e_out, sems.at[1]).wait()

    by_level(body)


def correct(
    up,
    down,
    c_planes,
    patched,
    from_below,
    from_above,
    e_edge,
    h_edge,
    e_in,
    h_in,
    e_out,
    h_out,
    e_tile,
    h_tile,
    sems,
):
    def body(grid, gz):
        last = grid.last

        def put(ref, edge, comp, x, change):
            for part, p in enumerate(change):
                own = jnp.where(gz == 0, p[: grid.own], p[grid.own :])
                rows = pl.ds(grid.step * x % 8 + part, grid.own, stride=8)
                ref[edge, comp, rows, :] = ref[edge, comp, rows, :] + own

        def finish(edge):
            copies = []
            for slot, (tile, out) in enumerate(((h_tile, h_out), (e_tile, e_out))):
                source = tile.at[edge].reshape(3, 8, 8, 128).at[:, pl.ds(0, grid.own)]
                target = block_layers(grid, out).at[:, :, pl.ds((grid.depth - 8) * edge, 8), :]
                copies.append(pltpu.make_async_copy(source, target, sems.at[2 * edge + slot]))
            for copy in copies:
                copy.start()
            return copies

        if grid is Fine:
            zero = [jnp.zeros((16, 128), F32)]
            ey64, ez64, ey64_part, ez64_part, c64, ey_top = read_message(grid, from_above, 6, gz)
            hy63, hz63 = read_planes(grid, up, 0, 1)
            c0, c1, c62, c63 = read_planes(grid, c_planes, *range(4))
            ghost = -0.5 * ey_top[0]
            dhy, dhz = scale(0.5, ez64), scale(-0.5, ey64)
            dex = mul(c63, sub(minus_y(dhz, ghost), minus_z(dhy)))
            dey = scale(-1.0, mul(c63, dhz))
            dez = mul(c63, dhy)
            dex62 = mul(c62, minus_y(zero, ghost))
            ey64_next = add(ey64_part, mul(c64, add(hz63, dhz)))
            ez64_next = sub(ez64_part, mul(c64, add(hy63, dhy)))
            dhx2 = scale(-0.5, sub(plus_y(dez), plus_z(dey)))
            dhy2 = add(dhy, scale(-0.5, sub(plus_z(dex), sub(ez64_next, dez))))
            dhz2 = add(dhz, scale(-0.5, sub(sub(ey64_next, dey), plus_y(dex))))
            dhy62 = scale(-0.5, sub(plus_z(dex62), dez))
            dhz62 = scale(-0.5, sub(dey, plus_y(dex62)))
            put(h_tile, 1, 0, 63, dhx2)
            put(h_tile, 1, 1, 63, dhy2)
            put(h_tile, 1, 2, 63, dhz2)
            put(h_tile, 1, 1, 62, dhy62)
            put(h_tile, 1, 2, 62, dhz62)
            put(e_tile, 1, 0, 63, add(dex, mul(c63, sub(minus_y(dhz2, ghost), minus_z(dhy2)))))
            put(e_tile, 1, 1, 63, add(dey, mul(c63, sub(minus_z(dhx2), sub(dhz2, dhz62)))))
            put(e_tile, 1, 2, 63, add(dez, mul(c63, sub(sub(dhy2, dhy62), minus_y(dhx2)))))
            put(e_tile, 1, 0, 62, add(dex62, mul(c62, sub(minus_y(dhz62, ghost), minus_z(dhy62)))))
            put(e_tile, 1, 1, 62, scale(-1.0, mul(c62, dhz62)))
            put(e_tile, 1, 2, 62, mul(c62, dhy62))
            copies = finish(1)

            hy_part, hz_part, ex_part, ey_part, ez_part, cm = read_message(grid, from_below, 6, gz)
            ey0, ez0, ey0_part, ez0_part = read_planes(grid, down, *range(4))
            ez0_change, ey_top = read_planes(grid, patched, 0, 1)
            ez0_part = add(ez0_part, ez0_change)
            ghost = -0.5 * ey_top[0]
            dhy, dhz = scale(0.5, ez0), scale(-0.5, ey0)
            hym, hzm = add(hy_part, dhy), add(hz_part, dhz)
            exm = add(ex_part, mul(cm, sub(minus_y(dhz, ghost), minus_z(dhy))))
            eym = sub(ey_part, mul(cm, dhz))
            ezm = add(ez_part, mul(cm, dhy))
            dey, dez = mul(c0, hzm), scale(-1.0, mul(c0, hym))
            dhx2 = scale(-0.5, sub(plus_y(dez), plus_z(dey)))
            dhy2 = scale(-0.5, dez)
            dhz2 = scale(0.5, dey)
            hym2 = add(hym, scale(-0.5, sub(plus_z(exm), sub(add(ez0_part, dez), ezm))))
            hzm2 = add(hzm, scale(-0.5, sub(sub(add(ey0_part, dey), eym), plus_y(exm))))
            put(h_tile, 0, 0, 0, dhx2)
            put(h_tile, 0, 1, 0, dhy2)
            put(h_tile, 0, 2, 0, dhz2)
            put(e_tile, 0, 0, 0, mul(c0, sub(minus_y(dhz2), minus_z(dhy2))))
            put(e_tile, 0, 1, 0, add(dey, mul(c0, sub(minus_z(dhx2), sub(dhz2, hzm2)))))
            put(e_tile, 0, 2, 0, add(dez, mul(c0, sub(sub(dhy2, hym2), minus_y(dhx2)))))
            put(e_tile, 0, 1, 1, mul(c1, dhz2))
            put(e_tile, 0, 2, 1, scale(-1.0, mul(c1, dhy2)))
            copies += finish(0)
        else:
            ey32, ez32 = read_message(grid, from_above, 2, gz)
            c0, c31 = read_planes(grid, c_planes, 0, 1)
            dhy, dhz = scale(0.5, ez32), scale(-0.5, ey32)
            put(h_tile, 1, 1, last, dhy)
            put(h_tile, 1, 2, last, dhz)
            put(e_tile, 1, 0, last, mul(c31, sub(minus_y(dhz), minus_z(dhy))))
            put(e_tile, 1, 1, last, scale(-1.0, mul(c31, dhz)))
            put(e_tile, 1, 2, last, mul(c31, dhy))
            copies = finish(1)
            hy_part, hz_part = read_message(grid, from_below, 2, gz)
            ey0, ez0 = read_planes(grid, down, 0, 1)
            put(e_tile, 0, 1, 0, mul(c0, add(hz_part, scale(-0.5, ey0))))
            put(e_tile, 0, 2, 0, scale(-1.0, mul(c0, add(hy_part, scale(0.5, ez0)))))
            copies += finish(0)
        for copy in copies:
            copy.wait()

    by_level(body)


def across(x, dx=0, dy=0, dz=0):
    nx, ny, nz = lax.axis_size("gx"), lax.axis_size("gy"), lax.axis_size("gz")
    pairs = [
        ((i * ny + j) * nz + k, ((i + dx) % nx * ny + (j + dy) % ny) * nz + (k + dz) % nz)
        for i in range(nx)
        for j in range(ny)
        for k in range(nz)
    ]
    return lax.ppermute(x, ("gx", "gy", "gz"), pairs)


def fast_shards(electric, magnetic, material, permittivity):
    e = electric.reshape(3, ROWS, 128)
    h = magnetic.reshape(3, ROWS, 128)
    m = material.reshape(ROWS, 128)
    dma = pltpu.SemaphoreType.DMA
    edge_tile, m_face, m_ends = kernel_call(
        peek,
        [vmem(8, 128), vmem(HALO, 128, dtype=jnp.int32), vmem(2, 64, 128, dtype=jnp.int32)],
        [HBM] * 3,
        [VM] * 3,
        [pltpu.VMEM((2, 3, 16, 128), F32)] * 2 + [dma((4,)), dma((3,))],
    )(far(e), far(h), far(m))
    m_face, m_ends = kernel_call(
        fine_material,
        [vmem(HALO, 128, dtype=jnp.int32), vmem(2, 64, 128, dtype=jnp.int32)],
        [HBM, VM, VM],
        [VM] * 2,
        [dma((3,))],
        aliases={1: 0, 2: 1},
    )(far(m), held(m_face), held(m_ends))
    edge_tile = across(edge_tile, dz=1)
    zmsg, ytile, columns = kernel_call(
        gather,
        [vmem(FACE + COLUMNS, 128), vmem(8, 128), vmem(COLUMNS, 128)],
        [VM] * 4,
        [VM] * 3,
    )(held(e), held(h), held(m_face), held(m_ends))
    ytile = kernel_call(
        join_z,
        vmem(8, 128),
        [VM] * 2,
        VM,
        cost=pl.CostEstimate(flops=10**10, bytes_accessed=10**8, transcendentals=0),
    )(held(ytile), held(edge_tile))
    zin = across(zmsg, dz=1)
    yin = across(ytile, dy=1)
    yzin = across(ytile, dy=1, dz=1)
    e_ext, h_ext, c_ext, up, down, up_part, down_part, c_planes = kernel_call(
        extend,
        [
            vmem(3, EXT, 128),
            vmem(3, EXT, 128),
            vmem(EXT, 128),
            vmem(96, 128),
            vmem(96, 128),
            vmem(64, 128),
            vmem(64, 128),
            vmem(64, 128),
        ],
        [VM] * 4 + [HBM, VM],
        [VM] * 8,
        [pltpu.SMEM((MATS,), F32), dma((1,))],
    )(held(e), held(h), held(m), held(zin), far(permittivity), held(columns))
    to_up, to_down = kernel_call(
        join_y,
        [vmem(64, 128), vmem(64, 128)],
        [VM] * 6,
        [VM] * 2,
    )(*(held(part) for part in (up_part, down_part, c_planes, yzin, columns, zin)))
    from_below = across(to_up, dx=1, dz=1)
    from_above = across(to_down, dx=-1, dz=1)
    whole = jax.ShapeDtypeStruct((3, ROWS, 128), F32)
    e_out, h_out, e_edge, h_edge, patched = kernel_call(
        advance,
        [whole, whole, vmem(2, 3, 64, 128), vmem(2, 3, 64, 128), vmem(32, 128)],
        [VM] * 8,
        [HBM, HBM, VM, VM, VM],
        [pltpu.VMEM((3, EXT, 128), F32)] * 3 + [pltpu.VMEM((2, 320, 128), F32), dma((2,))],
        cost=pl.CostEstimate(flops=10**10, bytes_accessed=10**8, transcendentals=0),
    )(*(held(part) for part in (e_ext, h_ext, c_ext, c_planes, yin, yzin, columns, zin)))
    e_out, h_out, _, _ = kernel_call(
        correct,
        [whole, whole, vmem(2, 3, 64, 128), vmem(2, 3, 64, 128)],
        [VM] * 8 + [HBM] * 2,
        [HBM] * 2 + [VM] * 2,
        [dma((4,))],
        aliases={8: 0, 9: 1, 6: 2, 7: 3},
    )(
        *(held(part) for part in (up, down, c_planes, patched, from_below, from_above, e_edge, h_edge)),
        e_out,
        h_out,
    )
    return e_out.reshape(electric.shape), h_out.reshape(magnetic.shape)


def solution(mesh):
    placed = (
        P(("parts", "gy"), "gx", "gz", None, None),
        P(("parts", "gy"), "gx", "gz", None, None),
        P(("parts", "gy"), "gx", "gz", None),
        P(),
    )
    fast = mesh.shape["gy"] == 2 and mesh.shape["gz"] == 2
    return jax.shard_map(
        fast_shards if fast else general_shards,
        mesh=mesh,
        in_specs=placed,
        out_specs=(
            P(("parts", "gy"), "gx", "gz", None, None),
            P(("parts", "gy"), "gx", "gz", None, None),
        ),
        check_vma=False,
    )
```

```python
from functools import partial

import jax
import jax.numpy as jnp
from jax import lax
from jax.experimental import pallas as pl
from jax.experimental.pallas import tpu as pltpu
from jax.sharding import PartitionSpec as P

CZ = 4
CX = 32
CY = 512
MATS = 4


courant = 0.5


def passed_along(x, axis, by):
    devices = lax.axis_size(axis)
    return lax.ppermute(x, axis, [(i, (i + by) % devices) for i in range(devices)])


def from_behind(x, axis, by):
    devices = lax.axis_size(axis)
    pairs = [(i, i + by) for i in range(devices) if 0 <= i + by < devices]
    return lax.ppermute(x, axis, pairs)


def forward_diff(values, dim_axis, ghost_plane):
    shifted = jnp.concatenate(
        [
            lax.slice_in_dim(values, 1, values.shape[dim_axis], axis=dim_axis),
            jnp.expand_dims(ghost_plane, dim_axis),
        ],
        axis=dim_axis,
    )
    return shifted - values


def backward_diff(values, dim_axis, ghost_plane):
    shifted = jnp.concatenate(
        [
            jnp.expand_dims(ghost_plane, dim_axis),
            lax.slice_in_dim(values, 0, values.shape[dim_axis] - 1, axis=dim_axis),
        ],
        axis=dim_axis,
    )
    return values - shifted


def curl_with(differ, vectors, ghost_depth, ghost_width, ghost_height):
    ghosts = (ghost_depth, ghost_width, ghost_height)

    def along_axis(component, dim_axis):
        return differ(vectors[component], dim_axis, ghosts[dim_axis][component])

    curl_x = along_axis(2, 2) - along_axis(1, 0)
    curl_y = along_axis(0, 0) - along_axis(2, 1)
    curl_z = along_axis(1, 1) - along_axis(0, 2)
    return jnp.stack([curl_x, curl_y, curl_z])


def restrict(face_plane):
    quads = face_plane.reshape(3, face_plane.shape[1] // 2, 2, face_plane.shape[2] // 2, 2)
    return (
        quads[:, :, 0, :, 0] + quads[:, :, 0, :, 1] + (quads[:, :, 1, :, 0] + quads[:, :, 1, :, 1])
    ) * 0.25


def enlarge(face_plane):
    return jnp.repeat(jnp.repeat(face_plane, 2, axis=1), 2, axis=2)


def lookup(material, permittivity):
    permit_sum = jnp.zeros(material.shape, jnp.float32)
    for material_id in range(MATS):
        permit_sum = permit_sum + jnp.where(material == material_id, permittivity[material_id], 0.0)
    return courant / permit_sum


def pack_face(face_plane, length):
    flat_face = face_plane.reshape(3, -1)
    if flat_face.shape[1] < length:
        flat_face = jnp.concatenate(
            [flat_face, jnp.zeros((3, length - flat_face.shape[1]), flat_face.dtype)], axis=1
        )
    return flat_face


def unpack_face(flat_face, row_count, col_count):
    return flat_face[:, : row_count * col_count].reshape(3, row_count, col_count)


def level_height(got_height, is_fine):
    return got_height if is_fine else restrict(got_height)


def low_faces(grid_shape, is_fine, flat_field):
    vectors = flat_field.reshape((3,) + grid_shape)
    face_plane = vectors[:, :, :, 0]
    if not is_fine:
        face_plane = enlarge(face_plane)
    return (
        pack_face(vectors[:, :, 0, :], CZ * CY),
        pack_face(vectors[:, 0, :, :], CX * CY),
        face_plane,
    )


def high_faces(grid_shape, is_fine, flat_field):
    vectors = flat_field.reshape((3,) + grid_shape)
    face_plane = vectors[:, :, :, -1]
    if not is_fine:
        face_plane = enlarge(face_plane)
    return (
        pack_face(vectors[:, :, -1, :], CZ * CY),
        pack_face(vectors[:, -1, :, :], CX * CY),
        face_plane,
    )


def advance_magnetic(
    grid_shape, is_fine, does_move, e_flat, h_flat, got_width, got_depth, got_height
):
    if not does_move:
        return h_flat
    deep_cells, wide_cells, tall_cells = grid_shape
    vectors = e_flat.reshape((3,) + grid_shape)
    curl_term = curl_with(
        forward_diff,
        vectors,
        unpack_face(got_depth, wide_cells, tall_cells),
        unpack_face(got_width, deep_cells, tall_cells),
        level_height(got_height, is_fine),
    )
    return (h_flat.reshape((3,) + grid_shape) - courant * curl_term).reshape(3, -1)


def advance_electric(
    grid_shape, is_fine, does_move, e_flat, h_flat, coefficient, got_width, got_depth, got_height
):
    if not does_move:
        return e_flat
    deep_cells, wide_cells, tall_cells = grid_shape
    magnetic = h_flat.reshape((3,) + grid_shape)
    curl_term = curl_with(
        backward_diff,
        magnetic,
        unpack_face(got_depth, wide_cells, tall_cells),
        unpack_face(got_width, deep_cells, tall_cells),
        level_height(got_height, is_fine),
    )
    return (
        e_flat.reshape((3,) + grid_shape) + coefficient.reshape(grid_shape) * curl_term
    ).reshape(3, -1)


def pass_width(face_plane, offset):
    return passed_along(face_plane, "gx", offset)


def pass_depth(face_plane, offset):
    return from_behind(face_plane, "gz", offset)


def pass_height(face_plane, offset):
    return from_behind(face_plane, "gy", offset)


def general_shards(electric, magnetic, material, permittivity):
    cell_count = electric.shape[-1]
    e_flat = electric.reshape(3, cell_count)
    h_flat = magnetic.reshape(3, cell_count)
    coefficient = lookup(material.reshape(cell_count), permittivity)
    is_fine = lax.axis_index("gy") >= lax.axis_size("gy") // 2
    coarse_shape = (CZ, CX, CY)
    fine_shape = (2 * CZ, 2 * CX, CY // 4)
    for substep in range(2):
        coarse_moves = substep == 0
        face_width, face_depth, face_height = lax.cond(
            is_fine,
            partial(low_faces, fine_shape, True),
            partial(low_faces, coarse_shape, False),
            e_flat,
        )
        got_depth = pass_depth(face_depth, -1)
        got_height = pass_height(face_height, -1)
        got_width = pass_width(face_width, -1)
        h_flat = lax.cond(
            is_fine,
            partial(advance_magnetic, fine_shape, True, True),
            partial(advance_magnetic, coarse_shape, False, coarse_moves),
            e_flat,
            h_flat,
            got_width,
            got_depth,
            got_height,
        )
        rim_width, rim_depth, rim_height = lax.cond(
            is_fine,
            partial(high_faces, fine_shape, True),
            partial(high_faces, coarse_shape, False),
            h_flat,
        )
        rim_depth = pass_depth(rim_depth, 1)
        rim_height = pass_height(rim_height, 1)
        rim_width = pass_width(rim_width, 1)
        e_flat = lax.cond(
            is_fine,
            partial(advance_electric, fine_shape, True, True),
            partial(advance_electric, coarse_shape, False, coarse_moves),
            e_flat,
            h_flat,
            coefficient,
            rim_width,
            rim_depth,
            rim_height,
        )
    return (e_flat.reshape(electric.shape), h_flat.reshape(magnetic.shape))


ROWS = 512
HALO = 128
EXT = 1296
LIMIT = 40 * 1024 * 1024
F32 = jnp.float32
VM = pl.BlockSpec(memory_space=pltpu.VMEM)
HBM = pl.BlockSpec(memory_space=pltpu.HBM)
CHUNK = 32
SKEW = 2


class Fine:
    depth, stride, count, own, step, parts, last = 64, 72, 10, 8, 1, 1, 63


class Coarse:
    depth, stride, count, own, step, parts, last = 128, 144, 5, 4, 4, 4, 31


def vmem(*shape, dtype=F32):
    return pltpu.VMEM(shape, dtype)


def held(x):
    return pltpu.with_memory_space_constraint(x, pltpu.VMEM)


def far(x):
    return pltpu.with_memory_space_constraint(x, pltpu.HBM)


def kernel_call(body, out_shape, in_specs, out_specs, scratch=(), aliases=None, cost=None):
    return pl.pallas_call(
        body,
        cost_estimate=cost,
        out_shape=out_shape,
        in_specs=in_specs,
        out_specs=out_specs,
        scratch_shapes=list(scratch),
        input_output_aliases=aliases or {},
        compiler_params=pltpu.CompilerParams(vmem_limit_bytes=LIMIT),
    )


def by_level(body):
    is_fine = lax.axis_index("gy") >= lax.axis_size("gy") // 2
    gz = lax.axis_index("gz")
    pl.when(is_fine)(lambda: body(Fine, gz))
    pl.when(jnp.logical_not(is_fine))(lambda: body(Coarse, gz))


def lanes_of(shape):
    return lax.broadcasted_iota(jnp.int32, shape, len(shape) - 1)


def rows_of(shape):
    return lax.broadcasted_iota(jnp.int32, shape, len(shape) - 2)


def roll_lanes(x, by):
    return pltpu.roll(x, by % 128, 1)


def roll_rows(x, by):
    return pltpu.roll(x, by % x.shape[0], 0)


def layer_row(grid, index):
    return pl.multiple_of(grid.stride * (index + 1), 8)


def own_first(grid, gz):
    return (grid.count - grid.own) * gz


def halo_first(grid, gz):
    return grid.own * (1 - gz)


def clear_pads(grid, ref, *zero_layers):
    for comp in range(3):
        for index in range(grid.count + 2):
            start, size = grid.stride * index, grid.stride
            if index not in zero_layers:
                start, size = start + grid.depth, size - grid.depth
            ref[comp, pl.ds(start, size), :] = jnp.zeros((size, 128), F32)


def own_layers(grid, ref, gz):
    view = ref.reshape(3, EXT // grid.stride, grid.stride, 128)
    return view.at[:, pl.ds(1 + own_first(grid, gz), grid.own), pl.ds(0, grid.depth), :]


def block_layers(grid, ref):
    return ref.reshape(3, grid.own, grid.depth, 128)


def at_lane(tile, lane_from, lane_to, value):
    lane = lanes_of(value.shape)
    return jnp.where(lane == lane_to, roll_lanes(value, lane_to - lane_from), tile)


def average(ref, lead, row, stride):
    steps = (0, 1, stride, stride + 1)
    quad = [ref[lead, pl.ds(row + step, 32, stride=2), :] for step in steps]
    return ((quad[0] + quad[1]) + (quad[2] + quad[3])) * 0.25


def put_column(tile, lane_from, slot, column):
    for block in range(4):
        tile = at_lane(tile, lane_from, 32 * block + slot, column[8 * block : 8 * block + 8])
    return tile


FINE_E = [(0, comp) for comp in range(3)] + [(1, 1), (1, 2)] + [(x, comp) for x in (62, 63) for comp in range(3)]
FINE_H = [(0, comp) for comp in range(3)] + [(62, 1), (62, 2)] + [(63, comp) for comp in range(3)]
FINE_M = [0, 1, 62, 63]
COARSE_E = [(0, 1), (0, 2)] + [(31, comp) for comp in range(3)]
COARSE_H = [(31, 1), (31, 2)]
COARSE_M = [0, 31]
COLUMNS = 192
R_ROW = COLUMNS - 8
FACE = 7 * HALO


def wanted(grid):
    return (FINE_E, FINE_H, FINE_M) if grid is Fine else (COARSE_E, COARSE_H, COARSE_M)


def top_tile(tile, layer, ex, ey, ez, hx, hz):
    tile = put_column(tile, 127, layer, hx + 0.5 * ez)
    tile = put_column(tile, 127, 8 + layer, hz - 0.5 * ex)
    return put_column(tile, 127, 16 + layer, ey)


def edge_tiles(grid, ref):
    view = ref.reshape(grid.own, grid.depth, 128)
    return [view.at[:, pl.ds((grid.depth - 8) * end, 8), :] for end in range(2)]


def material_loads(grid, gz, m_hbm, m_face, m_ends, sems):
    face = pl.ds((1 - gz) * (ROWS - HALO), HALO)
    loads = [pltpu.make_async_copy(m_hbm.at[face], m_face, sems.at[0])]
    for end, tiles in enumerate(edge_tiles(grid, m_hbm)):
        place = m_ends.at[end].reshape(8, 8, 128).at[pl.ds(0, grid.own)]
        loads.append(pltpu.make_async_copy(tiles, place, sems.at[1 + end]))
    return loads


def peek(e_hbm, h_hbm, m_hbm, edge_tile, m_face, m_ends, e_ends, h_ends, sems, m_sems):
    def body(grid, gz):
        if grid is Fine:
            edge_tile[...] = jnp.zeros((8, 128), F32)
            return
        m_loads = material_loads(grid, gz, m_hbm, m_face, m_ends, m_sems)
        loads = []
        for end in range(2):
            rows = pl.ds((1 - gz) * (ROWS - HALO) + (HALO - 8) * end, 8)
            place = pl.ds(0, 8)
            loads.append(pltpu.make_async_copy(e_hbm.at[:, rows], e_ends.at[end, :, place], sems.at[2 * end]))
            loads.append(pltpu.make_async_copy(h_hbm.at[:, rows], h_ends.at[end, :, place], sems.at[2 * end + 1]))
        for load in loads + m_loads:
            load.start()
        for load in loads:
            load.wait()
        tile = jnp.zeros((8, 128), F32)
        lane = lanes_of((8, 128))
        for end in range(2):
            rows = pl.ds(0 if end else 3, 8)
            ex, ey, ez = (e_ends[end, comp, rows, :] for comp in range(3))
            hx, hz = h_ends[end, 0, rows, :], h_ends[end, 2, rows, :]
            for kind, value in enumerate((hx + 0.5 * ez, hz - 0.5 * ex, ey)):
                to = 96 * end + 8 * kind + 3 + gz
                tile = jnp.where(lane == to, pltpu.roll(value, to + 1, 1), tile)
        edge_tile[...] = tile
        for load in m_loads:
            load.wait()

    by_level(body)


def fine_material(m_hbm, face_in, ends_in, m_face, m_ends, sems):
    def body(grid, gz):
        if grid is Coarse:
            return
        loads = material_loads(grid, gz, m_hbm, m_face, m_ends, sems)
        for load in loads:
            load.start()
        for load in loads:
            load.wait()

    by_level(body)


def gather(e_own, h_own, m_face, m_ends, zmsg, ytile, columns):
    def body(grid, gz):
        tile = jnp.zeros((8, 128), F32)
        for layer in range(4):
            if grid is Fine:
                row = 2 * grid.depth * layer
                tile = put_column(tile, 0, layer, average(e_own, 0, row, grid.depth))
                tile = put_column(tile, 0, 8 + layer, average(e_own, 2, row, grid.depth))
            else:
                top = pl.ds(grid.depth * layer + 3, 32, stride=4)
                ex, ey, ez = (e_own[comp, top, :] for comp in range(3))
                tile = top_tile(tile, layer, ex, ey, ez, h_own[0, top, :], h_own[2, top, :])
        tile = jnp.where(gz == 1, roll_lanes(tile, 4), tile)
        ytile[...] = tile
        columns[pl.ds(R_ROW, 8), :] = tile
        want_e, want_h, want_m = wanted(grid)
        slot = 0

        def column_rows(x, part):
            return pl.ds(grid.step * x + part, grid.own, stride=grid.depth)

        def put(value):
            nonlocal slot
            columns[pl.ds(slot, grid.own), :] = value
            slot += grid.own

        for x, comp in want_e:
            for part in range(grid.parts):
                put(e_own[comp, column_rows(x, part), :])
        for x, comp in want_h:
            for part in range(grid.parts):
                put(h_own[comp, column_rows(x, part), :])
        for x in want_m:
            for part in range(grid.parts):
                rows = pl.ds(grid.step * x % 8 + part, grid.own, stride=8)
                put(m_ends[int(x > 1), rows, :].astype(F32))
        edge = pl.ds(pl.multiple_of((1 - gz) * (ROWS - HALO), HALO), HALO)
        for comp in range(3):
            zmsg[pl.ds(HALO * comp, HALO), :] = h_own[comp, edge, :]
            zmsg[pl.ds(HALO * (3 + comp), HALO), :] = e_own[comp, edge, :]
        zmsg[pl.ds(6 * HALO, HALO), :] = m_face[...].astype(F32)
        zmsg[pl.ds(FACE, COLUMNS), :] = columns[...]

    by_level(body)


def join_z(ytile, edge_tile, joined):
    joined[...] = ytile[...] + edge_tile[...]


def up_y(grid, ref, comp, row, f):
    lane = lanes_of(f.shape)
    if grid is Fine:
        return jnp.where(lane == 127, 0.0, roll_lanes(f, -1))
    following = ref[comp, pl.ds(row + 1, f.shape[0]), :]
    following = jnp.where(rows_of(f.shape) % 4 == 3, 0.0, following)
    return roll_lanes(jnp.where(lane == 0, following, f), -1)


def down_y(grid, ref, comp, row, f, ghost):
    lane = lanes_of(f.shape)
    if grid is Fine:
        return roll_lanes(jnp.where(lane == 127, ghost, f), 1)
    previous = ref[comp, pl.ds(row - 1, f.shape[0]), :]
    previous = jnp.where(rows_of(f.shape) % 4 == 0, 0.0, previous)
    return roll_lanes(jnp.where(lane == 127, previous, f), 1)


def half_h(grid, e, h_from, from_row, h_to, row):
    for start in range(0, grid.depth, CHUNK):
        r = row + start
        here = pl.ds(r, CHUNK)
        ex, ey, ez = (e[comp, here, :] for comp in range(3))
        above, beside = pl.ds(r + grid.stride, CHUNK), pl.ds(r + grid.step, CHUNK)
        h0 = [h_from(comp, pl.ds(from_row + start, CHUNK)) for comp in range(3)]
        ez_y, ex_y = up_y(grid, e, 2, r, ez), up_y(grid, e, 0, r, ex)
        h_to[0, here, :] = h0[0] - 0.5 * ((ez_y - ez) - (e[1, above, :] - ey))
        h_to[1, here, :] = h0[1] - 0.5 * ((e[0, above, :] - ex) - (e[2, beside, :] - ez))
        h_to[2, here, :] = h0[2] - 0.5 * ((e[1, beside, :] - ey) - (ex_y - ex))


def half_e(grid, h, e_from, e_to, c_ref, row, ghosts):
    for start in range(0, grid.depth, CHUNK):
        r = row + start
        here = pl.ds(r, CHUNK)
        hx, hy, hz = (h[comp, here, :] for comp in range(3))
        below, beside = pl.ds(r - grid.stride, CHUNK), pl.ds(r - grid.step, CHUNK)
        px, pz = ghosts(start)
        hx_y, hz_y = down_y(grid, h, 0, r, hx, px), down_y(grid, h, 2, r, hz, pz)
        c = c_ref[here, :]
        e_to[0, here, :] = e_from[0, here, :] + c * ((hz - hz_y) - (hy - h[1, below, :]))
        e_to[1, here, :] = e_from[1, here, :] + c * ((hx - h[0, below, :]) - (hz - h[2, beside, :]))
        e_to[2, here, :] = e_from[2, here, :] + c * ((hy - h[1, beside, :]) - (hx - hx_y))


def column_of(tile, block, sub, slot, grid):
    shape = (2 * grid.own, 128)
    row = jnp.broadcast_to(tile[sub : sub + 1, :], shape)
    lane = 32 * block + slot + rows_of(shape) // (2 * grid.own // 8)
    picked = jnp.where(lanes_of(shape) == lane, row, 0.0)
    return jnp.broadcast_to(jnp.sum(picked, axis=1, keepdims=True), shape)


def each(fn, *columns):
    return [fn(*parts) for parts in zip(*columns, strict=True)]


def plus_y(f, ghost=0.0):
    following = f[1:] + [ghost]
    return [
        roll_lanes(jnp.where(lanes_of(p.shape) == 0, nxt, p), -1) - p
        for p, nxt in zip(f, following, strict=True)
    ]


def minus_y(f, ghost=0.0):
    previous = [ghost] + f[:-1]
    return [
        p - roll_lanes(jnp.where(lanes_of(p.shape) == 127, prv, p), 1)
        for p, prv in zip(f, previous, strict=True)
    ]


def plus_z(f):
    return [
        jnp.where(rows_of(p.shape) == p.shape[0] - 1, 0.0, roll_rows(p, -1)) - p for p in f
    ]


def minus_z(f):
    return [p - jnp.where(rows_of(p.shape) == 0, 0.0, roll_rows(p, 1)) for p in f]


def add(a, b):
    return each(lambda p, q: p + q, a, b)


def sub(a, b):
    return each(lambda p, q: p - q, a, b)


def mul(a, b):
    return each(lambda p, q: p * q, a, b)


def scale(by, a):
    return [by * p for p in a]


def read_columns(grid, own, other, gz):
    want_e, want_h, want_m = wanted(grid)
    found, slot = [], 0
    for _ in range(len(want_e) + len(want_h) + len(want_m)):
        col = []
        for _ in range(grid.parts):
            rows = pl.ds(slot, grid.own)
            mine, theirs = own[rows, :], other[pl.ds(FACE + slot, grid.own), :]
            low, high = jnp.where(gz == 0, mine, theirs), jnp.where(gz == 0, theirs, mine)
            col.append(jnp.concatenate([low, high], axis=0))
            slot += grid.own
        found.append(col)
    e_found, found = found[: len(want_e)], found[len(want_e) :]
    h_found, m_found = found[: len(want_h)], found[len(want_h) :]
    return (
        dict(zip(want_e, e_found, strict=True)),
        dict(zip(want_h, h_found, strict=True)),
        dict(zip(want_m, m_found, strict=True)),
    )


def write_planes(ref, columns):
    row = 0
    for col in columns:
        for p in col:
            ref[pl.ds(row, p.shape[0]), :] = p
            row += p.shape[0]


def read_planes(grid, ref, *indices):
    height, parts = 2 * grid.own, grid.parts
    return [
        [ref[pl.ds(height * (parts * i + part), height), :] for part in range(parts)] for i in indices
    ]


MESSAGE = 48
UP = {Fine: [(9, 7)] * 5, Coarse: [(4, 4)] * 2}
DOWN = {Fine: [(10, 6)] + [(9, 7)] * 4, Coarse: [(5, 3)] * 2}


def sent_rows(plane, entry, gz):
    count, begin = entry
    return jnp.where(gz == 0, roll_rows(plane, -begin), plane)[:count]


def places(grid, entries):
    row = 0
    for entry in entries:
        for _ in range(grid.parts):
            yield row, entry
            row += entry[0]


def write_message(grid, ref, entries, columns, gz):
    planes = [p for col in columns for p in col]
    for (row, entry), p in zip(places(grid, entries), planes, strict=True):
        ref[pl.ds(row, entry[0]), :] = sent_rows(p, entry, gz)


def read_message(grid, ref, entries, gz):
    height, planes = 2 * grid.own, []
    for row, (_, begin) in places(grid, entries):
        start = min(row, MESSAGE - height)
        p = ref[pl.ds(start, height), :]
        planes.append(pltpu.roll(p, height + start - row + begin * gz, 0))
    return [planes[i : i + grid.parts] for i in range(0, len(planes), grid.parts)]


def extend(
    e_own,
    h_own,
    m_own,
    zmsg,
    permittivity,
    columns,
    e_ext,
    h_ext,
    c_ext,
    up,
    down,
    to_up,
    to_down,
    c_planes,
    table,
    sems,
):
    def body(grid, gz):
        load = pltpu.make_async_copy(permittivity, table, sems.at[0])
        load.start()
        clear_pads(grid, h_ext, 0)
        clear_pads(grid, e_ext, grid.count + 1)
        for layer in range(grid.own):
            for start in range(0, grid.depth, CHUNK):
                rows = pl.ds(layer_row(grid, own_first(grid, gz) + layer) + start, CHUNK)
                from_rows = pl.ds(grid.depth * layer + start, CHUNK)
                for comp in range(3):
                    e_ext[comp, rows, :] = e_own[comp, from_rows, :]
        halo = halo_first(grid, gz)
        for layer in range(grid.count - grid.own):
            for start in range(0, grid.depth, CHUNK):
                rows = pl.ds(layer_row(grid, halo + layer) + start, CHUNK)
                for comp in range(3):
                    from_rows = pl.ds(HALO * (3 + comp) + grid.depth * layer + start, CHUNK)
                    e_ext[comp, rows, :] = zmsg[from_rows, :]

        def h_halo(comp, rows):
            return zmsg[pl.ds(HALO * comp + rows.start, rows.size), :]

        for layer in range(grid.count - grid.own):
            row = layer_row(grid, halo + layer)
            half_h(grid, e_ext, h_halo, grid.depth * layer, h_ext, row)
        for layer in range(grid.own):
            row = layer_row(grid, own_first(grid, gz) + layer)
            half_h(grid, e_ext, lambda comp, rows: h_own[comp, rows, :], grid.depth * layer, h_ext, row)
        load.wait()
        values = [0.5 / jnp.full((8, 128), table[i], F32) for i in range(MATS)]

        def coef(is_material, rows):
            parts = [jnp.concatenate([value] * (rows // 8), axis=0) for value in values]
            found = parts[MATS - 1]
            for i in range(MATS - 2, -1, -1):
                found = jnp.where(is_material(i), parts[i], found)
            return found

        for start in range(0, HALO, CHUNK):
            layer, rest = divmod(start, grid.depth)
            material = zmsg[pl.ds(6 * HALO + start, CHUNK), :]
            row = layer_row(grid, halo + layer) + rest
            c_ext[pl.ds(row, CHUNK), :] = coef(lambda i, m=material: m == float(i), CHUNK)
        for start in range(0, ROWS, CHUNK):
            layer, rest = divmod(start, grid.depth)
            material = m_own[pl.ds(start, CHUNK), :]
            row = layer_row(grid, own_first(grid, gz) + layer) + rest
            c_ext[pl.ds(row, CHUNK), :] = coef(lambda i, m=material: m == i, CHUNK)

        e, h, m = read_columns(grid, columns, zmsg, gz)
        c = {
            x: [coef(lambda i, q=part: q == float(i), part.shape[0]) for part in col] for x, col in m.items()
        }
        write_planes(c_planes, list(c.values()))
        if grid is Coarse:
            ex, ey, ez = (e[31, comp] for comp in range(3))
            hy = sub(h[31, 1], scale(0.5, add(plus_z(ex), ez)))
            hz = add(h[31, 2], scale(0.5, add(ey, plus_y(ex))))
            sent_up, sent_down = [hy, hz], [e[0, 2], e[0, 1]]
        else:
            ex, ey, ez = (e[0, comp] for comp in range(3))
            hx = sub(h[0, 0], scale(0.5, sub(plus_y(ez), plus_z(ey))))
            hy = sub(h[0, 1], scale(0.5, sub(plus_z(ex), sub(e[1, 2], ez))))
            hz = sub(h[0, 2], scale(0.5, sub(sub(e[1, 1], ey), plus_y(ex))))
            ey_next = add(ey, mul(c[0], sub(minus_z(hx), hz)))
            ez_next = add(ez, mul(c[0], sub(hy, minus_y(hx))))
            sent_down = [ez, ey, ey_next, ez_next, c[0]]
            ex, ey, ez = (e[62, comp] for comp in range(3))
            hy62 = sub(h[62, 1], scale(0.5, sub(plus_z(ex), sub(e[63, 2], ez))))
            hz62 = sub(h[62, 2], scale(0.5, sub(sub(e[63, 1], ey), plus_y(ex))))
            ex, ey, ez = (e[63, comp] for comp in range(3))
            hx = sub(h[63, 0], scale(0.5, sub(plus_y(ez), plus_z(ey))))
            hy = sub(h[63, 1], scale(0.5, add(plus_z(ex), ez)))
            hz = add(h[63, 2], scale(0.5, add(ey, plus_y(ex))))
            ex_next = add(ex, mul(c[63], sub(minus_y(hz), minus_z(hy))))
            ey_next = add(ey, mul(c[63], sub(minus_z(hx), sub(hz, hz62))))
            ez_next = add(ez, mul(c[63], sub(sub(hy, hy62), minus_y(hx))))
            next_y = sub(hy, scale(0.5, add(plus_z(ex_next), ez_next)))
            next_z = add(hz, scale(0.5, add(ey_next, plus_y(ex_next))))
            sent_up = [hy, hz, next_y, next_z, c[63]]
        write_planes(up, sent_up)
        write_planes(down, sent_down)
        write_message(grid, to_up, UP[grid], sent_up, gz)
        write_message(grid, to_down, DOWN[grid], sent_down, gz)

    by_level(body)


def between(top, r):
    lane, row = lanes_of(top.shape), rows_of(top.shape)
    kind = (lane % 32) // 8
    above = jnp.where(lane % 8 == 7, 0.0, roll_lanes(top, -1))
    px = top - 0.5 * roll_lanes(r, -8) + 0.5 * roll_lanes(above - top, -16)
    beside = roll_rows(top, -1)
    beside = jnp.where(row == 7, jnp.where(lane >= 96, 0.0, roll_lanes(beside, -32)), beside)
    pz = top + 0.5 * roll_lanes(r, 8) - 0.5 * roll_lanes(beside - top, -8)
    return jnp.where(kind == 0, px, jnp.where(kind == 1, pz, 0.0))


def join_y(up_in, down_in, c_planes, yzin, r_own, r_other, to_up, to_down):
    def body(grid, gz):
        def patch(ref, entries, index, value):
            row, entry = list(places(grid, entries))[index]
            rows = pl.ds(row, entry[0])
            ref[rows, :] = ref[rows, :] + sent_rows(value, entry, gz)

        top = yzin[...]
        to_up[...] = up_in[...]
        to_down[...] = down_in[...]
        shape = (2 * grid.own, 128)
        if grid is Coarse:
            change = jnp.where(lanes_of(shape) == 127, 0.5 * column_of(top, 3, 7, 0, grid), 0.0)
            patch(to_up, UP[grid], 7, change)
            return
        plane = between(top, r_own[pl.ds(R_ROW, 8), :] + r_other[pl.ds(FACE + R_ROW, 8), :])
        bottom = lanes_of(shape) == 0
        (c0,), (c63,) = read_planes(grid, c_planes, 0, 3)

        patch(to_down, DOWN[grid], 3, jnp.where(bottom, c0 * column_of(plane, 0, 0, 0, grid), 0.0))
        ez_change = jnp.where(bottom, c63 * column_of(plane, 3, 7, 0, grid), 0.0)
        ex_change = jnp.where(bottom, -c63 * column_of(plane, 3, 7, 8, grid), 0.0)
        patch(to_up, UP[grid], 2, -0.5 * (plus_z([ex_change])[0] + ez_change))
        patch(to_up, UP[grid], 3, -0.5 * ex_change)
        to_down[pl.ds(MESSAGE - 1, 1), :] = top[:1]

    by_level(body)


def advance(
    e_ext,
    h_ext,
    c_ext,
    c_planes,
    yin,
    yzin,
    r_own,
    r_other,
    e_out,
    h_out,
    e_edge,
    h_edge,
    patched,
    e_mid,
    h_mid,
    e_last,
    plane,
    sems,
):
    def body(grid, gz):
        first = own_first(grid, gz)
        upper = lanes_of((8, 128)) % 8 >= 4
        tile = jnp.where(upper == (gz == 0), yzin[...], yin[...])
        if grid is Fine:
            top = tile
            tile = between(top, r_own[pl.ds(R_ROW, 8), :] + r_other[pl.ds(FACE + R_ROW, 8), :])
            ((c0,),) = read_planes(grid, c_planes, 0)
            change = jnp.where(lanes_of((16, 128)) == 0, c0 * column_of(tile, 0, 0, 0, grid), 0.0)
            patched[pl.ds(0, 16), :] = change
            patched[pl.ds(16, 16), :] = column_of(top, 0, 0, 16, grid)
        tile = jnp.where(gz == 0, tile, roll_lanes(tile, -3))

        def write(source, target, sem, layer=None):
            source, target = own_layers(grid, source, gz), block_layers(grid, target)
            if layer is not None:
                source, target = source.at[:, layer], target.at[:, layer]
            return pltpu.make_async_copy(source, target, sem)

        def keep_edges(source, target):
            for comp in range(3):
                for layer in range(grid.own):
                    for edge in range(2):
                        row = layer_row(grid, first + layer) + (grid.depth - 8) * edge
                        target[edge, comp, pl.ds(8 * layer, 8), :] = source[comp, pl.ds(row, 8), :]

        clear_pads(grid, h_mid, 0)
        if grid is Fine:
            clear_pads(grid, e_mid, grid.count + 1)
            for kind in range(2):
                for layer in range(5):
                    for block in range(4):
                        value = roll_lanes(tile, 127 - (32 * block + 8 * kind + layer))
                        for step in range(2):
                            rows = pl.ds(64 * layer + 16 * block + step, 8, stride=2)
                            plane[kind, rows, :] = value

            def ghosts(index):
                begin = 64 * (index // 2)

                def of(start):
                    rows = pl.ds(pl.multiple_of(begin + start, 8), CHUNK)
                    return plane[0, rows, :], plane[1, rows, :]

                return of

            def own_write(source, target, sem, layer):
                def start():
                    rows = pl.ds(layer_row(grid, layer), grid.depth)
                    to = block_layers(grid, target).at[:, layer - first]
                    pltpu.make_async_copy(source.at[:, rows], to, sem).start()

                if 2 <= layer < 8:
                    start()
                else:
                    pl.when((layer < 8) == (gz == 0))(start)

            def h1(comp, rows):
                return h_ext[comp, rows, :]

            for step in range(grid.count + 2 * SKEW):
                if step < grid.count:
                    half_e(grid, h_ext, e_ext, e_mid, c_ext, grid.stride * (step + 1), ghosts(step))
                layer = step - SKEW
                if 0 <= layer < grid.count:
                    row = grid.stride * (layer + 1)
                    half_h(grid, e_mid, h1, row, h_mid, row)
                    own_write(h_mid, h_out, sems.at[0], layer)
                layer = step - 2 * SKEW
                if 0 <= layer < grid.count:
                    row = grid.stride * (layer + 1)
                    half_e(grid, h_mid, e_mid, e_last, c_ext, row, ghosts(layer))
                    own_write(e_last, e_out, sems.at[1], layer)
        else:
            for comp in range(3):
                for layer in range(grid.count):
                    rows = pl.ds(layer_row(grid, layer), grid.depth)
                    h_mid[comp, rows, :] = h_ext[comp, rows, :]
            lane = lanes_of((8, 128))
            for layer in range(grid.count):
                for block in range(4):
                    rows = pl.ds(layer_row(grid, layer) + 32 * block + 3, 8, stride=4)
                    rx = roll_lanes(tile, 127 - (32 * block + layer))
                    rz = roll_lanes(tile, 127 - (32 * block + 8 + layer))
                    h_mid[0, rows, :] = h_mid[0, rows, :] - jnp.where(lane == 127, 0.5 * rz, 0.0)
                    h_mid[2, rows, :] = h_mid[2, rows, :] + jnp.where(lane == 127, 0.5 * rx, 0.0)
            write(h_mid, h_out, sems.at[0]).start()
            for layer in range(grid.own):
                row = layer_row(grid, first + layer)
                half_e(grid, h_mid, e_ext, e_last, c_ext, row, lambda start: (0.0, 0.0))
                write(e_last, e_out, sems.at[1], layer).start()
        keep_edges(h_mid, h_edge)
        keep_edges(e_last, e_edge)
        write(h_mid, h_out, sems.at[0]).wait()
        write(e_last, e_out, sems.at[1]).wait()

    by_level(body)


def correct(
    up,
    down,
    c_planes,
    patched,
    from_below,
    from_above,
    e_edge,
    h_edge,
    e_in,
    h_in,
    e_out,
    h_out,
    e_tile,
    h_tile,
    sems,
):
    def body(grid, gz):
        last = grid.last

        def put(ref, edge, comp, x, change):
            for part, p in enumerate(change):
                own = jnp.where(gz == 0, p[: grid.own], p[grid.own :])
                rows = pl.ds(grid.step * x % 8 + part, grid.own, stride=8)
                ref[edge, comp, rows, :] = ref[edge, comp, rows, :] + own

        def finish(edge):
            copies = []
            for slot, (tile, out) in enumerate(((h_tile, h_out), (e_tile, e_out))):
                source = tile.at[edge].reshape(3, 8, 8, 128).at[:, pl.ds(0, grid.own)]
                target = block_layers(grid, out).at[:, :, pl.ds((grid.depth - 8) * edge, 8), :]
                copies.append(pltpu.make_async_copy(source, target, sems.at[2 * edge + slot]))
            for copy in copies:
                copy.start()
            return copies

        if grid is Fine:
            zero = [jnp.zeros((16, 128), F32)]
            ez64, ey64, ey64_part, ez64_part, c64 = read_message(grid, from_above, DOWN[grid], gz)
            ey_top = column_of(from_above[pl.ds(MESSAGE - 8, 8), :], 0, 7, 16, grid)
            hy63, hz63 = read_planes(grid, up, 0, 1)
            c0, c1, c62, c63 = read_planes(grid, c_planes, *range(4))
            ghost = -0.5 * ey_top
            dhy, dhz = scale(0.5, ez64), scale(-0.5, ey64)
            dex = mul(c63, sub(minus_y(dhz, ghost), minus_z(dhy)))
            dey = scale(-1.0, mul(c63, dhz))
            dez = mul(c63, dhy)
            dex62 = mul(c62, minus_y(zero, ghost))
            ey64_next = add(ey64_part, mul(c64, add(hz63, dhz)))
            ez64_next = sub(ez64_part, mul(c64, add(hy63, dhy)))
            dhx2 = scale(-0.5, sub(plus_y(dez), plus_z(dey)))
            dhy2 = add(dhy, scale(-0.5, sub(plus_z(dex), sub(ez64_next, dez))))
            dhz2 = add(dhz, scale(-0.5, sub(sub(ey64_next, dey), plus_y(dex))))
            dhy62 = scale(-0.5, sub(plus_z(dex62), dez))
            dhz62 = scale(-0.5, sub(dey, plus_y(dex62)))
            put(h_tile, 1, 0, 63, dhx2)
            put(h_tile, 1, 1, 63, dhy2)
            put(h_tile, 1, 2, 63, dhz2)
            put(h_tile, 1, 1, 62, dhy62)
            put(h_tile, 1, 2, 62, dhz62)
            put(e_tile, 1, 0, 63, add(dex, mul(c63, sub(minus_y(dhz2, ghost), minus_z(dhy2)))))
            put(e_tile, 1, 1, 63, add(dey, mul(c63, sub(minus_z(dhx2), sub(dhz2, dhz62)))))
            put(e_tile, 1, 2, 63, add(dez, mul(c63, sub(sub(dhy2, dhy62), minus_y(dhx2)))))
            put(e_tile, 1, 0, 62, add(dex62, mul(c62, sub(minus_y(dhz62, ghost), minus_z(dhy62)))))
            put(e_tile, 1, 1, 62, scale(-1.0, mul(c62, dhz62)))
            put(e_tile, 1, 2, 62, mul(c62, dhy62))
            copies = finish(1)

            hy_part, hz_part, next_y, next_z, cm = read_message(grid, from_below, UP[grid], gz)
            ez0, ey0, ey0_part, ez0_part = read_planes(grid, down, *range(4))
            ez0_change, ey_top = read_planes(grid, patched, 0, 1)
            ez0_part = add(ez0_part, ez0_change)
            ghost = -0.5 * ey_top[0]
            dhy, dhz = scale(0.5, ez0), scale(-0.5, ey0)
            hym, hzm = add(hy_part, dhy), add(hz_part, dhz)
            dexm = mul(cm, sub(minus_y(dhz, ghost), minus_z(dhy)))
            dey, dez = mul(c0, hzm), scale(-1.0, mul(c0, hym))
            dhx2 = scale(-0.5, sub(plus_y(dez), plus_z(dey)))
            dhy2 = scale(-0.5, dez)
            dhz2 = scale(0.5, dey)
            change = sub(sub(add(ez0_part, dez), plus_z(dexm)), mul(cm, dhy))
            hym2 = add(add(next_y, dhy), scale(0.5, change))
            change = sub(sub(plus_y(dexm), add(ey0_part, dey)), mul(cm, dhz))
            hzm2 = add(add(next_z, dhz), scale(0.5, change))
            put(h_tile, 0, 0, 0, dhx2)
            put(h_tile, 0, 1, 0, dhy2)
            put(h_tile, 0, 2, 0, dhz2)
            put(e_tile, 0, 0, 0, mul(c0, sub(minus_y(dhz2), minus_z(dhy2))))
            put(e_tile, 0, 1, 0, add(dey, mul(c0, sub(minus_z(dhx2), sub(dhz2, hzm2)))))
            put(e_tile, 0, 2, 0, add(dez, mul(c0, sub(sub(dhy2, hym2), minus_y(dhx2)))))
            put(e_tile, 0, 1, 1, mul(c1, dhz2))
            put(e_tile, 0, 2, 1, scale(-1.0, mul(c1, dhy2)))
            copies += finish(0)
        else:
            ez32, ey32 = read_message(grid, from_above, DOWN[grid], gz)
            c0, c31 = read_planes(grid, c_planes, 0, 1)
            dhy, dhz = scale(0.5, ez32), scale(-0.5, ey32)
            put(h_tile, 1, 1, last, dhy)
            put(h_tile, 1, 2, last, dhz)
            put(e_tile, 1, 0, last, mul(c31, sub(minus_y(dhz), minus_z(dhy))))
            put(e_tile, 1, 1, last, scale(-1.0, mul(c31, dhz)))
            put(e_tile, 1, 2, last, mul(c31, dhy))
            copies = finish(1)
            hy_part, hz_part = read_message(grid, from_below, UP[grid], gz)
            ez0, ey0 = read_planes(grid, down, 0, 1)
            put(e_tile, 0, 1, 0, mul(c0, add(hz_part, scale(-0.5, ey0))))
            put(e_tile, 0, 2, 0, scale(-1.0, mul(c0, add(hy_part, scale(0.5, ez0)))))
            copies += finish(0)
        for copy in copies:
            copy.wait()

    by_level(body)


def across(x, dx=0, dy=0, dz=0):
    nx, ny, nz = lax.axis_size("gx"), lax.axis_size("gy"), lax.axis_size("gz")
    pairs = [
        ((i * ny + j) * nz + k, ((i + dx) % nx * ny + (j + dy) % ny) * nz + (k + dz) % nz)
        for i in range(nx)
        for j in range(ny)
        for k in range(nz)
    ]
    return lax.ppermute(x, ("gx", "gy", "gz"), pairs)


def fast_shards(electric, magnetic, material, permittivity):
    e = electric.reshape(3, ROWS, 128)
    h = magnetic.reshape(3, ROWS, 128)
    m = material.reshape(ROWS, 128)
    dma = pltpu.SemaphoreType.DMA
    edge_tile, m_face, m_ends = kernel_call(
        peek,
        [vmem(8, 128), vmem(HALO, 128, dtype=jnp.int32), vmem(2, 64, 128, dtype=jnp.int32)],
        [HBM] * 3,
        [VM] * 3,
        [pltpu.VMEM((2, 3, 16, 128), F32)] * 2 + [dma((4,)), dma((3,))],
    )(far(e), far(h), far(m))
    m_face, m_ends = kernel_call(
        fine_material,
        [vmem(HALO, 128, dtype=jnp.int32), vmem(2, 64, 128, dtype=jnp.int32)],
        [HBM, VM, VM],
        [VM] * 2,
        [dma((3,))],
        aliases={1: 0, 2: 1},
    )(far(m), held(m_face), held(m_ends))
    edge_tile = across(edge_tile, dz=1)
    zmsg, ytile, columns = kernel_call(
        gather,
        [vmem(FACE + COLUMNS, 128), vmem(8, 128), vmem(COLUMNS, 128)],
        [VM] * 4,
        [VM] * 3,
    )(held(e), held(h), held(m_face), held(m_ends))
    ytile = kernel_call(
        join_z,
        vmem(8, 128),
        [VM] * 2,
        VM,
        cost=pl.CostEstimate(flops=10**10, bytes_accessed=10**8, transcendentals=0),
    )(held(ytile), held(edge_tile))
    zin = across(zmsg, dz=1)
    yin = across(ytile, dy=1)
    yzin = across(ytile, dy=1, dz=1)
    e_ext, h_ext, c_ext, up, down, up_part, down_part, c_planes = kernel_call(
        extend,
        [
            vmem(3, EXT, 128),
            vmem(3, EXT, 128),
            vmem(EXT, 128),
            vmem(96, 128),
            vmem(96, 128),
            vmem(MESSAGE, 128),
            vmem(MESSAGE, 128),
            vmem(64, 128),
        ],
        [VM] * 4 + [HBM, VM],
        [VM] * 8,
        [pltpu.SMEM((MATS,), F32), dma((1,))],
    )(held(e), held(h), held(m), held(zin), far(permittivity), held(columns))
    to_up, to_down = kernel_call(
        join_y,
        [vmem(MESSAGE, 128), vmem(MESSAGE, 128)],
        [VM] * 6,
        [VM] * 2,
    )(*(held(part) for part in (up_part, down_part, c_planes, yzin, columns, zin)))
    from_below = across(to_up, dx=1, dz=1)
    from_above = across(to_down, dx=-1, dz=1)
    whole = jax.ShapeDtypeStruct((3, ROWS, 128), F32)
    e_out, h_out, e_edge, h_edge, patched = kernel_call(
        advance,
        [whole, whole, vmem(2, 3, 64, 128), vmem(2, 3, 64, 128), vmem(32, 128)],
        [VM] * 8,
        [HBM, HBM, VM, VM, VM],
        [pltpu.VMEM((3, EXT, 128), F32)] * 3 + [pltpu.VMEM((2, 320, 128), F32), dma((2,))],
        cost=pl.CostEstimate(flops=10**10, bytes_accessed=10**8, transcendentals=0),
    )(*(held(part) for part in (e_ext, h_ext, c_ext, c_planes, yin, yzin, columns, zin)))
    e_out, h_out, _, _ = kernel_call(
        correct,
        [whole, whole, vmem(2, 3, 64, 128), vmem(2, 3, 64, 128)],
        [VM] * 8 + [HBM] * 2,
        [HBM] * 2 + [VM] * 2,
        [dma((4,))],
        aliases={8: 0, 9: 1, 6: 2, 7: 3},
    )(
        *(held(part) for part in (up, down, c_planes, patched, from_below, from_above, e_edge, h_edge)),
        e_out,
        h_out,
    )
    return e_out.reshape(electric.shape), h_out.reshape(magnetic.shape)


def solution(mesh):
    placed = (
        P(("parts", "gy"), "gx", "gz", None, None),
        P(("parts", "gy"), "gx", "gz", None, None),
        P(("parts", "gy"), "gx", "gz", None),
        P(),
    )
    fast = mesh.shape["gy"] == 2 and mesh.shape["gz"] == 2
    return jax.shard_map(
        fast_shards if fast else general_shards,
        mesh=mesh,
        in_specs=placed,
        out_specs=(
            P(("parts", "gy"), "gx", "gz", None, None),
            P(("parts", "gy"), "gx", "gz", None, None),
        ),
        check_vma=False,
    )
```

```python
from functools import partial

import jax
import jax.numpy as jnp
from jax import lax
from jax.experimental import pallas as pl
from jax.experimental.pallas import tpu as pltpu
from jax.sharding import PartitionSpec as P

CZ = 4
CX = 32
CY = 512
MATS = 4


courant = 0.5


def passed_along(x, axis, by):
    devices = lax.axis_size(axis)
    return lax.ppermute(x, axis, [(i, (i + by) % devices) for i in range(devices)])


def from_behind(x, axis, by):
    devices = lax.axis_size(axis)
    pairs = [(i, i + by) for i in range(devices) if 0 <= i + by < devices]
    return lax.ppermute(x, axis, pairs)


def forward_diff(values, dim_axis, ghost_plane):
    shifted = jnp.concatenate(
        [
            lax.slice_in_dim(values, 1, values.shape[dim_axis], axis=dim_axis),
            jnp.expand_dims(ghost_plane, dim_axis),
        ],
        axis=dim_axis,
    )
    return shifted - values


def backward_diff(values, dim_axis, ghost_plane):
    shifted = jnp.concatenate(
        [
            jnp.expand_dims(ghost_plane, dim_axis),
            lax.slice_in_dim(values, 0, values.shape[dim_axis] - 1, axis=dim_axis),
        ],
        axis=dim_axis,
    )
    return values - shifted


def curl_with(differ, vectors, ghost_depth, ghost_width, ghost_height):
    ghosts = (ghost_depth, ghost_width, ghost_height)

    def along_axis(component, dim_axis):
        return differ(vectors[component], dim_axis, ghosts[dim_axis][component])

    curl_x = along_axis(2, 2) - along_axis(1, 0)
    curl_y = along_axis(0, 0) - along_axis(2, 1)
    curl_z = along_axis(1, 1) - along_axis(0, 2)
    return jnp.stack([curl_x, curl_y, curl_z])


def restrict(face_plane):
    quads = face_plane.reshape(3, face_plane.shape[1] // 2, 2, face_plane.shape[2] // 2, 2)
    return (
        quads[:, :, 0, :, 0] + quads[:, :, 0, :, 1] + (quads[:, :, 1, :, 0] + quads[:, :, 1, :, 1])
    ) * 0.25


def enlarge(face_plane):
    return jnp.repeat(jnp.repeat(face_plane, 2, axis=1), 2, axis=2)


def lookup(material, permittivity):
    permit_sum = jnp.zeros(material.shape, jnp.float32)
    for material_id in range(MATS):
        permit_sum = permit_sum + jnp.where(material == material_id, permittivity[material_id], 0.0)
    return courant / permit_sum


def pack_face(face_plane, length):
    flat_face = face_plane.reshape(3, -1)
    if flat_face.shape[1] < length:
        flat_face = jnp.concatenate(
            [flat_face, jnp.zeros((3, length - flat_face.shape[1]), flat_face.dtype)], axis=1
        )
    return flat_face


def unpack_face(flat_face, row_count, col_count):
    return flat_face[:, : row_count * col_count].reshape(3, row_count, col_count)


def level_height(got_height, is_fine):
    return got_height if is_fine else restrict(got_height)


def low_faces(grid_shape, is_fine, flat_field):
    vectors = flat_field.reshape((3,) + grid_shape)
    face_plane = vectors[:, :, :, 0]
    if not is_fine:
        face_plane = enlarge(face_plane)
    return (
        pack_face(vectors[:, :, 0, :], CZ * CY),
        pack_face(vectors[:, 0, :, :], CX * CY),
        face_plane,
    )


def high_faces(grid_shape, is_fine, flat_field):
    vectors = flat_field.reshape((3,) + grid_shape)
    face_plane = vectors[:, :, :, -1]
    if not is_fine:
        face_plane = enlarge(face_plane)
    return (
        pack_face(vectors[:, :, -1, :], CZ * CY),
        pack_face(vectors[:, -1, :, :], CX * CY),
        face_plane,
    )


def advance_magnetic(
    grid_shape, is_fine, does_move, e_flat, h_flat, got_width, got_depth, got_height
):
    if not does_move:
        return h_flat
    deep_cells, wide_cells, tall_cells = grid_shape
    vectors = e_flat.reshape((3,) + grid_shape)
    curl_term = curl_with(
        forward_diff,
        vectors,
        unpack_face(got_depth, wide_cells, tall_cells),
        unpack_face(got_width, deep_cells, tall_cells),
        level_height(got_height, is_fine),
    )
    return (h_flat.reshape((3,) + grid_shape) - courant * curl_term).reshape(3, -1)


def advance_electric(
    grid_shape, is_fine, does_move, e_flat, h_flat, coefficient, got_width, got_depth, got_height
):
    if not does_move:
        return e_flat
    deep_cells, wide_cells, tall_cells = grid_shape
    magnetic = h_flat.reshape((3,) + grid_shape)
    curl_term = curl_with(
        backward_diff,
        magnetic,
        unpack_face(got_depth, wide_cells, tall_cells),
        unpack_face(got_width, deep_cells, tall_cells),
        level_height(got_height, is_fine),
    )
    return (
        e_flat.reshape((3,) + grid_shape) + coefficient.reshape(grid_shape) * curl_term
    ).reshape(3, -1)


def pass_width(face_plane, offset):
    return passed_along(face_plane, "gx", offset)


def pass_depth(face_plane, offset):
    return from_behind(face_plane, "gz", offset)


def pass_height(face_plane, offset):
    return from_behind(face_plane, "gy", offset)


def general_shards(electric, magnetic, material, permittivity):
    cell_count = electric.shape[-1]
    e_flat = electric.reshape(3, cell_count)
    h_flat = magnetic.reshape(3, cell_count)
    coefficient = lookup(material.reshape(cell_count), permittivity)
    is_fine = lax.axis_index("gy") >= lax.axis_size("gy") // 2
    coarse_shape = (CZ, CX, CY)
    fine_shape = (2 * CZ, 2 * CX, CY // 4)
    for substep in range(2):
        coarse_moves = substep == 0
        face_width, face_depth, face_height = lax.cond(
            is_fine,
            partial(low_faces, fine_shape, True),
            partial(low_faces, coarse_shape, False),
            e_flat,
        )
        got_depth = pass_depth(face_depth, -1)
        got_height = pass_height(face_height, -1)
        got_width = pass_width(face_width, -1)
        h_flat = lax.cond(
            is_fine,
            partial(advance_magnetic, fine_shape, True, True),
            partial(advance_magnetic, coarse_shape, False, coarse_moves),
            e_flat,
            h_flat,
            got_width,
            got_depth,
            got_height,
        )
        rim_width, rim_depth, rim_height = lax.cond(
            is_fine,
            partial(high_faces, fine_shape, True),
            partial(high_faces, coarse_shape, False),
            h_flat,
        )
        rim_depth = pass_depth(rim_depth, 1)
        rim_height = pass_height(rim_height, 1)
        rim_width = pass_width(rim_width, 1)
        e_flat = lax.cond(
            is_fine,
            partial(advance_electric, fine_shape, True, True),
            partial(advance_electric, coarse_shape, False, coarse_moves),
            e_flat,
            h_flat,
            coefficient,
            rim_width,
            rim_depth,
            rim_height,
        )
    return (e_flat.reshape(electric.shape), h_flat.reshape(magnetic.shape))


ROWS = 512
HALO = 128
EXT = 1296
LIMIT = 40 * 1024 * 1024
F32 = jnp.float32
VM = pl.BlockSpec(memory_space=pltpu.VMEM)
HBM = pl.BlockSpec(memory_space=pltpu.HBM)
CHUNK = 32
SKEW = 2


class Fine:
    depth, stride, count, own, step, parts, last = 64, 72, 10, 8, 1, 1, 63


class Coarse:
    depth, stride, count, own, step, parts, last = 128, 144, 5, 4, 4, 4, 31


def vmem(*shape, dtype=F32):
    return pltpu.VMEM(shape, dtype)


def held(x):
    return pltpu.with_memory_space_constraint(x, pltpu.VMEM)


def far(x):
    return pltpu.with_memory_space_constraint(x, pltpu.HBM)


def kernel_call(body, out_shape, in_specs, out_specs, scratch=(), aliases=None, cost=None):
    return pl.pallas_call(
        body,
        cost_estimate=cost,
        out_shape=out_shape,
        in_specs=in_specs,
        out_specs=out_specs,
        scratch_shapes=list(scratch),
        input_output_aliases=aliases or {},
        compiler_params=pltpu.CompilerParams(vmem_limit_bytes=LIMIT),
    )


def by_level(body):
    is_fine = lax.axis_index("gy") >= lax.axis_size("gy") // 2
    gz = lax.axis_index("gz")
    pl.when(is_fine)(lambda: body(Fine, gz))
    pl.when(jnp.logical_not(is_fine))(lambda: body(Coarse, gz))


def lanes_of(shape):
    return lax.broadcasted_iota(jnp.int32, shape, len(shape) - 1)


def rows_of(shape):
    return lax.broadcasted_iota(jnp.int32, shape, len(shape) - 2)


def roll_lanes(x, by):
    return pltpu.roll(x, by % 128, 1)


def roll_rows(x, by):
    return pltpu.roll(x, by % x.shape[0], 0)


def layer_row(grid, index):
    return pl.multiple_of(grid.stride * (index + 1), 8)


def own_first(grid, gz):
    return (grid.count - grid.own) * gz


def halo_first(grid, gz):
    return grid.own * (1 - gz)


def clear_pads(grid, ref, *zero_layers):
    for comp in range(3):
        for index in range(grid.count + 2):
            start, size = grid.stride * index, grid.stride
            if index not in zero_layers:
                start, size = start + grid.depth, size - grid.depth
            ref[comp, pl.ds(start, size), :] = jnp.zeros((size, 128), F32)


def own_layers(grid, ref, gz):
    view = ref.reshape(3, EXT // grid.stride, grid.stride, 128)
    return view.at[:, pl.ds(1 + own_first(grid, gz), grid.own), pl.ds(0, grid.depth), :]


def block_layers(grid, ref):
    return ref.reshape(3, grid.own, grid.depth, 128)


def at_lane(tile, lane_from, lane_to, value):
    lane = lanes_of(value.shape)
    return jnp.where(lane == lane_to, roll_lanes(value, lane_to - lane_from), tile)


def average(ref, lead, row, stride):
    steps = (0, 1, stride, stride + 1)
    quad = [ref[lead, pl.ds(row + step, 32, stride=2), :] for step in steps]
    return ((quad[0] + quad[1]) + (quad[2] + quad[3])) * 0.25


def put_column(tile, lane_from, slot, column):
    for block in range(4):
        tile = at_lane(tile, lane_from, 32 * block + slot, column[8 * block : 8 * block + 8])
    return tile


FINE_E = [(0, comp) for comp in range(3)] + [(1, 1), (1, 2)] + [(x, comp) for x in (62, 63) for comp in range(3)]
FINE_H = [(0, comp) for comp in range(3)] + [(62, 1), (62, 2)] + [(63, comp) for comp in range(3)]
FINE_M = [0, 1, 62, 63]
COARSE_E = [(0, 1), (0, 2)] + [(31, comp) for comp in range(3)]
COARSE_H = [(31, 1), (31, 2)]
COARSE_M = [0, 31]
COLUMNS = 192
R_ROW = COLUMNS - 8
FACE = 7 * HALO


def wanted(grid):
    return (FINE_E, FINE_H, FINE_M) if grid is Fine else (COARSE_E, COARSE_H, COARSE_M)


def top_tile(tile, layer, ex, ey, ez, hx, hz):
    tile = put_column(tile, 127, layer, hx + 0.5 * ez)
    tile = put_column(tile, 127, 8 + layer, hz - 0.5 * ex)
    return put_column(tile, 127, 16 + layer, ey)


def edge_tiles(grid, ref):
    view = ref.reshape(grid.own, grid.depth, 128)
    return [view.at[:, pl.ds((grid.depth - 8) * end, 8), :] for end in range(2)]


def material_loads(grid, gz, m_hbm, m_face, m_ends, sems):
    face = pl.ds((1 - gz) * (ROWS - HALO), HALO)
    loads = [pltpu.make_async_copy(m_hbm.at[face], m_face, sems.at[0])]
    for end, tiles in enumerate(edge_tiles(grid, m_hbm)):
        place = m_ends.at[end].reshape(8, 8, 128).at[pl.ds(0, grid.own)]
        loads.append(pltpu.make_async_copy(tiles, place, sems.at[1 + end]))
    return loads


def peek(e_hbm, h_hbm, edge_tile, e_ends, h_ends, sems):
    def body(grid, gz):
        if grid is Fine:
            edge_tile[...] = jnp.zeros((8, 128), F32)
            return
        loads = []
        for end in range(2):
            rows = pl.ds((1 - gz) * (ROWS - HALO) + (HALO - 8) * end, 8)
            place = pl.ds(0, 8)
            loads.append(pltpu.make_async_copy(e_hbm.at[:, rows], e_ends.at[end, :, place], sems.at[2 * end]))
            for slot, comp in enumerate((0, 2)):
                into = h_ends.at[end, comp, place]
                loads.append(pltpu.make_async_copy(h_hbm.at[comp, rows], into, sems.at[4 + 2 * end + slot]))
        for load in loads:
            load.start()
        for load in loads:
            load.wait()
        tile = jnp.zeros((8, 128), F32)
        lane = lanes_of((8, 128))
        for end in range(2):
            rows = pl.ds(0 if end else 3, 8)
            ex, ey, ez = (e_ends[end, comp, rows, :] for comp in range(3))
            hx, hz = h_ends[end, 0, rows, :], h_ends[end, 2, rows, :]
            for kind, value in enumerate((hx + 0.5 * ez, hz - 0.5 * ex, ey)):
                to = 96 * end + 8 * kind + 3 + gz
                tile = jnp.where(lane == to, pltpu.roll(value, to + 1, 1), tile)
        edge_tile[...] = tile

    by_level(body)


def fine_material(m_hbm, after, m_face, m_ends, sems):
    def body(grid, gz):
        if grid is Coarse:
            return
        loads = material_loads(grid, gz, m_hbm, m_face, m_ends, sems)
        for load in loads:
            load.start()
        for load in loads:
            load.wait()

    by_level(body)


def gather(e_own, h_own, m_face, m_ends, zmsg, ytile, columns):
    def body(grid, gz):
        tile = jnp.zeros((8, 128), F32)
        for layer in range(4):
            if grid is Fine:
                row = 2 * grid.depth * layer
                tile = put_column(tile, 0, layer, average(e_own, 0, row, grid.depth))
                tile = put_column(tile, 0, 8 + layer, average(e_own, 2, row, grid.depth))
            else:
                top = pl.ds(grid.depth * layer + 3, 32, stride=4)
                ex, ey, ez = (e_own[comp, top, :] for comp in range(3))
                tile = top_tile(tile, layer, ex, ey, ez, h_own[0, top, :], h_own[2, top, :])
        tile = jnp.where(gz == 1, roll_lanes(tile, 4), tile)
        ytile[...] = tile
        columns[pl.ds(R_ROW, 8), :] = tile
        want_e, want_h, want_m = wanted(grid)
        slot = 0

        def column_rows(x, part):
            return pl.ds(grid.step * x + part, grid.own, stride=grid.depth)

        def put(value):
            nonlocal slot
            columns[pl.ds(slot, grid.own), :] = value
            slot += grid.own

        for x, comp in want_e:
            for part in range(grid.parts):
                put(e_own[comp, column_rows(x, part), :])
        for x, comp in want_h:
            for part in range(grid.parts):
                put(h_own[comp, column_rows(x, part), :])
        for x in want_m if grid is Fine else []:
            for part in range(grid.parts):
                rows = pl.ds(grid.step * x % 8 + part, grid.own, stride=8)
                put(m_ends[int(x > 1), rows, :].astype(F32))
        edge = pl.ds(pl.multiple_of((1 - gz) * (ROWS - HALO), HALO), HALO)
        for comp in range(3):
            zmsg[pl.ds(HALO * comp, HALO), :] = h_own[comp, edge, :]
            zmsg[pl.ds(HALO * (3 + comp), HALO), :] = e_own[comp, edge, :]
        if grid is Fine:
            zmsg[pl.ds(6 * HALO, HALO), :] = m_face[...].astype(F32)
        zmsg[pl.ds(FACE, COLUMNS), :] = columns[...]

    by_level(body)


def join_z(ytile, edge_tile, joined):
    joined[...] = ytile[...] + edge_tile[...]


def up_y(grid, ref, comp, row, f):
    lane = lanes_of(f.shape)
    if grid is Fine:
        return jnp.where(lane == 127, 0.0, roll_lanes(f, -1))
    following = ref[comp, pl.ds(row + 1, f.shape[0]), :]
    following = jnp.where(rows_of(f.shape) % 4 == 3, 0.0, following)
    return roll_lanes(jnp.where(lane == 0, following, f), -1)


def down_y(grid, ref, comp, row, f, ghost):
    lane = lanes_of(f.shape)
    if grid is Fine:
        return roll_lanes(jnp.where(lane == 127, ghost, f), 1)
    previous = ref[comp, pl.ds(row - 1, f.shape[0]), :]
    previous = jnp.where(rows_of(f.shape) % 4 == 0, 0.0, previous)
    return roll_lanes(jnp.where(lane == 127, previous, f), 1)


def half_h(grid, e, h_from, from_row, h_to, row):
    for start in range(0, grid.depth, CHUNK):
        r = row + start
        here = pl.ds(r, CHUNK)
        ex, ey, ez = (e[comp, here, :] for comp in range(3))
        above, beside = pl.ds(r + grid.stride, CHUNK), pl.ds(r + grid.step, CHUNK)
        h0 = [h_from(comp, pl.ds(from_row + start, CHUNK)) for comp in range(3)]
        ez_y, ex_y = up_y(grid, e, 2, r, ez), up_y(grid, e, 0, r, ex)
        h_to[0, here, :] = h0[0] - 0.5 * ((ez_y - ez) - (e[1, above, :] - ey))
        h_to[1, here, :] = h0[1] - 0.5 * ((e[0, above, :] - ex) - (e[2, beside, :] - ez))
        h_to[2, here, :] = h0[2] - 0.5 * ((e[1, beside, :] - ey) - (ex_y - ex))


def half_e(grid, h, e_from, e_to, c_ref, row, ghosts):
    for start in range(0, grid.depth, CHUNK):
        r = row + start
        here = pl.ds(r, CHUNK)
        hx, hy, hz = (h[comp, here, :] for comp in range(3))
        below, beside = pl.ds(r - grid.stride, CHUNK), pl.ds(r - grid.step, CHUNK)
        px, pz = ghosts(start)
        hx_y, hz_y = down_y(grid, h, 0, r, hx, px), down_y(grid, h, 2, r, hz, pz)
        c = c_ref[here, :]
        e_to[0, here, :] = e_from[0, here, :] + c * ((hz - hz_y) - (hy - h[1, below, :]))
        e_to[1, here, :] = e_from[1, here, :] + c * ((hx - h[0, below, :]) - (hz - h[2, beside, :]))
        e_to[2, here, :] = e_from[2, here, :] + c * ((hy - h[1, beside, :]) - (hx - hx_y))


def column_of(tile, block, sub, slot, grid):
    shape = (2 * grid.own, 128)
    row = jnp.broadcast_to(tile[sub : sub + 1, :], shape)
    lane = 32 * block + slot + rows_of(shape) // (2 * grid.own // 8)
    picked = jnp.where(lanes_of(shape) == lane, row, 0.0)
    return jnp.broadcast_to(jnp.sum(picked, axis=1, keepdims=True), shape)


def each(fn, *columns):
    return [fn(*parts) for parts in zip(*columns, strict=True)]


def plus_y(f, ghost=0.0):
    following = f[1:] + [ghost]
    return [
        roll_lanes(jnp.where(lanes_of(p.shape) == 0, nxt, p), -1) - p
        for p, nxt in zip(f, following, strict=True)
    ]


def minus_y(f, ghost=0.0):
    previous = [ghost] + f[:-1]
    return [
        p - roll_lanes(jnp.where(lanes_of(p.shape) == 127, prv, p), 1)
        for p, prv in zip(f, previous, strict=True)
    ]


def plus_z(f):
    return [
        jnp.where(rows_of(p.shape) == p.shape[0] - 1, 0.0, roll_rows(p, -1)) - p for p in f
    ]


def minus_z(f):
    return [p - jnp.where(rows_of(p.shape) == 0, 0.0, roll_rows(p, 1)) for p in f]


def add(a, b):
    return each(lambda p, q: p + q, a, b)


def sub(a, b):
    return each(lambda p, q: p - q, a, b)


def mul(a, b):
    return each(lambda p, q: p * q, a, b)


def scale(by, a):
    return [by * p for p in a]


def read_columns(grid, own, other, gz):
    want_e, want_h, want_m = wanted(grid)
    found, slot = [], 0
    for _ in range(len(want_e) + len(want_h) + len(want_m)):
        col = []
        for _ in range(grid.parts):
            rows = pl.ds(slot, grid.own)
            mine, theirs = own[rows, :], other[pl.ds(FACE + slot, grid.own), :]
            low, high = jnp.where(gz == 0, mine, theirs), jnp.where(gz == 0, theirs, mine)
            col.append(jnp.concatenate([low, high], axis=0))
            slot += grid.own
        found.append(col)
    e_found, found = found[: len(want_e)], found[len(want_e) :]
    h_found, m_found = found[: len(want_h)], found[len(want_h) :]
    return (
        dict(zip(want_e, e_found, strict=True)),
        dict(zip(want_h, h_found, strict=True)),
        dict(zip(want_m, m_found, strict=True)),
    )


def write_planes(ref, columns):
    row = 0
    for col in columns:
        for p in col:
            ref[pl.ds(row, p.shape[0]), :] = p
            row += p.shape[0]


def read_planes(grid, ref, *indices):
    height, parts = 2 * grid.own, grid.parts
    return [
        [ref[pl.ds(height * (parts * i + part), height), :] for part in range(parts)] for i in indices
    ]


MESSAGE = 48
UP = {Fine: [(9, 7)] * 5, Coarse: [(4, 4)] * 2}
DOWN = {Fine: [(10, 6)] + [(9, 7)] * 4, Coarse: [(5, 3)] * 2}


def sent_rows(plane, entry, gz):
    count, begin = entry
    return jnp.where(gz == 0, roll_rows(plane, -begin), plane)[:count]


def places(grid, entries):
    row = 0
    for entry in entries:
        for _ in range(grid.parts):
            yield row, entry
            row += entry[0]


def write_message(grid, ref, entries, columns, gz):
    planes = [p for col in columns for p in col]
    for (row, entry), p in zip(places(grid, entries), planes, strict=True):
        ref[pl.ds(row, entry[0]), :] = sent_rows(p, entry, gz)


def read_message(grid, ref, entries, gz):
    height, planes = 2 * grid.own, []
    for row, (_, begin) in places(grid, entries):
        start = min(row, MESSAGE - height)
        p = ref[pl.ds(start, height), :]
        planes.append(pltpu.roll(p, height + start - row + begin * gz, 0))
    return [planes[i : i + grid.parts] for i in range(0, len(planes), grid.parts)]


def extend(
    e_own,
    h_own,
    m_own,
    zmsg,
    permittivity,
    columns,
    e_ext,
    h_ext,
    c_ext,
    up,
    down,
    to_up,
    to_down,
    c_planes,
    table,
    sems,
):
    def body(grid, gz):
        load = pltpu.make_async_copy(permittivity, table, sems.at[0])
        load.start()
        clear_pads(grid, h_ext, 0)
        clear_pads(grid, e_ext, grid.count + 1)
        for layer in range(grid.own):
            for start in range(0, grid.depth, CHUNK):
                rows = pl.ds(layer_row(grid, own_first(grid, gz) + layer) + start, CHUNK)
                from_rows = pl.ds(grid.depth * layer + start, CHUNK)
                for comp in range(3):
                    e_ext[comp, rows, :] = e_own[comp, from_rows, :]
        halo = halo_first(grid, gz)
        for layer in range(grid.count - grid.own):
            for start in range(0, grid.depth, CHUNK):
                rows = pl.ds(layer_row(grid, halo + layer) + start, CHUNK)
                for comp in range(3):
                    from_rows = pl.ds(HALO * (3 + comp) + grid.depth * layer + start, CHUNK)
                    e_ext[comp, rows, :] = zmsg[from_rows, :]

        def h_halo(comp, rows):
            return zmsg[pl.ds(HALO * comp + rows.start, rows.size), :]

        for layer in range(grid.count - grid.own):
            row = layer_row(grid, halo + layer)
            half_h(grid, e_ext, h_halo, grid.depth * layer, h_ext, row)
        for layer in range(grid.own):
            row = layer_row(grid, own_first(grid, gz) + layer)
            half_h(grid, e_ext, lambda comp, rows: h_own[comp, rows, :], grid.depth * layer, h_ext, row)
        load.wait()
        values = [0.5 / jnp.full((8, 128), table[i], F32) for i in range(MATS)]

        def coef(is_material, rows):
            parts = [jnp.concatenate([value] * (rows // 8), axis=0) for value in values]
            found = parts[MATS - 1]
            for i in range(MATS - 2, -1, -1):
                found = jnp.where(is_material(i), parts[i], found)
            return found

        for start in range(0, HALO if grid is Fine else 0, CHUNK):
            layer, rest = divmod(start, grid.depth)
            material = zmsg[pl.ds(6 * HALO + start, CHUNK), :]
            row = layer_row(grid, halo + layer) + rest
            c_ext[pl.ds(row, CHUNK), :] = coef(lambda i, m=material: m == float(i), CHUNK)
        for start in range(0, ROWS, CHUNK):
            layer, rest = divmod(start, grid.depth)
            material = m_own[pl.ds(start, CHUNK), :]
            row = layer_row(grid, own_first(grid, gz) + layer) + rest
            c_ext[pl.ds(row, CHUNK), :] = coef(lambda i, m=material: m == i, CHUNK)

        e, h, m = read_columns(grid, columns, zmsg, gz)
        if grid is Coarse:
            for x in m:
                rows = [pl.ds(4 * x + part, 4, stride=grid.depth) for part in range(4)]
                own = [m_own[part, :].astype(F32) for part in rows]
                m[x] = [jnp.concatenate([part, part], axis=0) for part in own]
        c = {
            x: [coef(lambda i, q=part: q == float(i), part.shape[0]) for part in col] for x, col in m.items()
        }
        write_planes(c_planes, list(c.values()))
        if grid is Coarse:
            ex, ey, ez = (e[31, comp] for comp in range(3))
            hy = sub(h[31, 1], scale(0.5, add(plus_z(ex), ez)))
            hz = add(h[31, 2], scale(0.5, add(ey, plus_y(ex))))
            sent_up, sent_down = [hy, hz], [e[0, 2], e[0, 1]]
        else:
            ex, ey, ez = (e[0, comp] for comp in range(3))
            hx = sub(h[0, 0], scale(0.5, sub(plus_y(ez), plus_z(ey))))
            hy = sub(h[0, 1], scale(0.5, sub(plus_z(ex), sub(e[1, 2], ez))))
            hz = sub(h[0, 2], scale(0.5, sub(sub(e[1, 1], ey), plus_y(ex))))
            ey_next = add(ey, mul(c[0], sub(minus_z(hx), hz)))
            ez_next = add(ez, mul(c[0], sub(hy, minus_y(hx))))
            sent_down = [ez, ey, ey_next, ez_next, c[0]]
            ex, ey, ez = (e[62, comp] for comp in range(3))
            hy62 = sub(h[62, 1], scale(0.5, sub(plus_z(ex), sub(e[63, 2], ez))))
            hz62 = sub(h[62, 2], scale(0.5, sub(sub(e[63, 1], ey), plus_y(ex))))
            ex, ey, ez = (e[63, comp] for comp in range(3))
            hx = sub(h[63, 0], scale(0.5, sub(plus_y(ez), plus_z(ey))))
            hy = sub(h[63, 1], scale(0.5, add(plus_z(ex), ez)))
            hz = add(h[63, 2], scale(0.5, add(ey, plus_y(ex))))
            ex_next = add(ex, mul(c[63], sub(minus_y(hz), minus_z(hy))))
            ey_next = add(ey, mul(c[63], sub(minus_z(hx), sub(hz, hz62))))
            ez_next = add(ez, mul(c[63], sub(sub(hy, hy62), minus_y(hx))))
            next_y = sub(hy, scale(0.5, add(plus_z(ex_next), ez_next)))
            next_z = add(hz, scale(0.5, add(ey_next, plus_y(ex_next))))
            sent_up = [hy, hz, next_y, next_z, c[63]]
        write_planes(up, sent_up)
        write_planes(down, sent_down)
        write_message(grid, to_up, UP[grid], sent_up, gz)
        write_message(grid, to_down, DOWN[grid], sent_down, gz)

    by_level(body)


def between(top, r):
    lane, row = lanes_of(top.shape), rows_of(top.shape)
    kind = (lane % 32) // 8
    above = jnp.where(lane % 8 == 7, 0.0, roll_lanes(top, -1))
    px = top - 0.5 * roll_lanes(r, -8) + 0.5 * roll_lanes(above - top, -16)
    beside = roll_rows(top, -1)
    beside = jnp.where(row == 7, jnp.where(lane >= 96, 0.0, roll_lanes(beside, -32)), beside)
    pz = top + 0.5 * roll_lanes(r, 8) - 0.5 * roll_lanes(beside - top, -8)
    return jnp.where(kind == 0, px, jnp.where(kind == 1, pz, 0.0))


def join_y(up_in, down_in, c_planes, yzin, r_own, r_other, to_up, to_down):
    def body(grid, gz):
        def patch(ref, entries, index, value):
            row, entry = list(places(grid, entries))[index]
            rows = pl.ds(row, entry[0])
            ref[rows, :] = ref[rows, :] + sent_rows(value, entry, gz)

        top = yzin[...]
        to_up[...] = up_in[...]
        to_down[...] = down_in[...]
        shape = (2 * grid.own, 128)
        if grid is Coarse:
            change = jnp.where(lanes_of(shape) == 127, 0.5 * column_of(top, 3, 7, 0, grid), 0.0)
            patch(to_up, UP[grid], 7, change)
            return
        plane = between(top, r_own[pl.ds(R_ROW, 8), :] + r_other[pl.ds(FACE + R_ROW, 8), :])
        bottom = lanes_of(shape) == 0
        (c0,), (c63,) = read_planes(grid, c_planes, 0, 3)

        patch(to_down, DOWN[grid], 3, jnp.where(bottom, c0 * column_of(plane, 0, 0, 0, grid), 0.0))
        ez_change = jnp.where(bottom, c63 * column_of(plane, 3, 7, 0, grid), 0.0)
        ex_change = jnp.where(bottom, -c63 * column_of(plane, 3, 7, 8, grid), 0.0)
        patch(to_up, UP[grid], 2, -0.5 * (plus_z([ex_change])[0] + ez_change))
        patch(to_up, UP[grid], 3, -0.5 * ex_change)
        to_down[pl.ds(MESSAGE - 1, 1), :] = top[:1]

    by_level(body)


def advance(
    e_ext,
    h_ext,
    c_ext,
    c_planes,
    yin,
    yzin,
    r_own,
    r_other,
    e_out,
    h_out,
    e_edge,
    h_edge,
    patched,
    e_mid,
    h_mid,
    e_last,
    plane,
    sems,
):
    def body(grid, gz):
        first = own_first(grid, gz)
        upper = lanes_of((8, 128)) % 8 >= 4
        tile = jnp.where(upper == (gz == 0), yzin[...], yin[...])
        if grid is Fine:
            top = tile
            tile = between(top, r_own[pl.ds(R_ROW, 8), :] + r_other[pl.ds(FACE + R_ROW, 8), :])
            ((c0,),) = read_planes(grid, c_planes, 0)
            change = jnp.where(lanes_of((16, 128)) == 0, c0 * column_of(tile, 0, 0, 0, grid), 0.0)
            patched[pl.ds(0, 16), :] = change
            patched[pl.ds(16, 16), :] = column_of(top, 0, 0, 16, grid)
        tile = jnp.where(gz == 0, tile, roll_lanes(tile, -3))

        def write(source, target, sem, layer=None):
            source, target = own_layers(grid, source, gz), block_layers(grid, target)
            if layer is not None:
                source, target = source.at[:, layer], target.at[:, layer]
            return pltpu.make_async_copy(source, target, sem)

        def keep_edges(source, target):
            for comp in range(3):
                for layer in range(grid.own):
                    for edge in range(2):
                        row = layer_row(grid, first + layer) + (grid.depth - 8) * edge
                        target[edge, comp, pl.ds(8 * layer, 8), :] = source[comp, pl.ds(row, 8), :]

        clear_pads(grid, h_mid, 0)
        if grid is Fine:
            clear_pads(grid, e_mid, grid.count + 1)
            for kind in range(2):
                for layer in range(5):
                    for block in range(4):
                        value = roll_lanes(tile, 127 - (32 * block + 8 * kind + layer))
                        for step in range(2):
                            rows = pl.ds(64 * layer + 16 * block + step, 8, stride=2)
                            plane[kind, rows, :] = value

            def ghosts(index):
                begin = 64 * (index // 2)

                def of(start):
                    rows = pl.ds(pl.multiple_of(begin + start, 8), CHUNK)
                    return plane[0, rows, :], plane[1, rows, :]

                return of

            def own_write(source, target, sem, layer):
                def start():
                    rows = pl.ds(layer_row(grid, layer), grid.depth)
                    to = block_layers(grid, target).at[:, layer - first]
                    pltpu.make_async_copy(source.at[:, rows], to, sem).start()

                if 2 <= layer < 8:
                    start()
                else:
                    pl.when((layer < 8) == (gz == 0))(start)

            def h1(comp, rows):
                return h_ext[comp, rows, :]

            for step in range(grid.count + 2 * SKEW):
                if step < grid.count:
                    half_e(grid, h_ext, e_ext, e_mid, c_ext, grid.stride * (step + 1), ghosts(step))
                layer = step - SKEW
                if 0 <= layer < grid.count:
                    row = grid.stride * (layer + 1)
                    half_h(grid, e_mid, h1, row, h_mid, row)
                    own_write(h_mid, h_out, sems.at[0], layer)
                layer = step - 2 * SKEW
                if 0 <= layer < grid.count:
                    row = grid.stride * (layer + 1)
                    half_e(grid, h_mid, e_mid, e_last, c_ext, row, ghosts(layer))
                    own_write(e_last, e_out, sems.at[1], layer)
        else:
            for comp in range(3):
                for layer in range(grid.count):
                    rows = pl.ds(layer_row(grid, layer), grid.depth)
                    h_mid[comp, rows, :] = h_ext[comp, rows, :]
            lane = lanes_of((8, 128))
            for layer in range(grid.count):
                for block in range(4):
                    rows = pl.ds(layer_row(grid, layer) + 32 * block + 3, 8, stride=4)
                    rx = roll_lanes(tile, 127 - (32 * block + layer))
                    rz = roll_lanes(tile, 127 - (32 * block + 8 + layer))
                    h_mid[0, rows, :] = h_mid[0, rows, :] - jnp.where(lane == 127, 0.5 * rz, 0.0)
                    h_mid[2, rows, :] = h_mid[2, rows, :] + jnp.where(lane == 127, 0.5 * rx, 0.0)
            write(h_mid, h_out, sems.at[0]).start()
            for layer in range(grid.own):
                row = layer_row(grid, first + layer)
                half_e(grid, h_mid, e_ext, e_last, c_ext, row, lambda start: (0.0, 0.0))
                write(e_last, e_out, sems.at[1], layer).start()
        keep_edges(h_mid, h_edge)
        keep_edges(e_last, e_edge)
        write(h_mid, h_out, sems.at[0]).wait()
        write(e_last, e_out, sems.at[1]).wait()

    by_level(body)


def correct(
    up,
    down,
    c_planes,
    patched,
    from_below,
    from_above,
    e_edge,
    h_edge,
    e_in,
    h_in,
    e_out,
    h_out,
    e_tile,
    h_tile,
    sems,
):
    def body(grid, gz):
        last = grid.last

        def put(ref, edge, comp, x, change):
            for part, p in enumerate(change):
                own = jnp.where(gz == 0, p[: grid.own], p[grid.own :])
                rows = pl.ds(grid.step * x % 8 + part, grid.own, stride=8)
                ref[edge, comp, rows, :] = ref[edge, comp, rows, :] + own

        def finish(edge):
            copies = []
            for slot, (tile, out) in enumerate(((h_tile, h_out), (e_tile, e_out))):
                if grid is Coarse and edge == 0 and slot == 0:
                    continue
                source = tile.at[edge].reshape(3, 8, 8, 128).at[:, pl.ds(0, grid.own)]
                target = block_layers(grid, out).at[:, :, pl.ds((grid.depth - 8) * edge, 8), :]
                copies.append(pltpu.make_async_copy(source, target, sems.at[2 * edge + slot]))
            for copy in copies:
                copy.start()
            return copies

        if grid is Fine:
            zero = [jnp.zeros((16, 128), F32)]
            ez64, ey64, ey64_part, ez64_part, c64 = read_message(grid, from_above, DOWN[grid], gz)
            ey_top = column_of(from_above[pl.ds(MESSAGE - 8, 8), :], 0, 7, 16, grid)
            hy63, hz63 = read_planes(grid, up, 0, 1)
            c0, c1, c62, c63 = read_planes(grid, c_planes, *range(4))
            ghost = -0.5 * ey_top
            dhy, dhz = scale(0.5, ez64), scale(-0.5, ey64)
            dex = mul(c63, sub(minus_y(dhz, ghost), minus_z(dhy)))
            dey = scale(-1.0, mul(c63, dhz))
            dez = mul(c63, dhy)
            dex62 = mul(c62, minus_y(zero, ghost))
            ey64_next = add(ey64_part, mul(c64, add(hz63, dhz)))
            ez64_next = sub(ez64_part, mul(c64, add(hy63, dhy)))
            dhx2 = scale(-0.5, sub(plus_y(dez), plus_z(dey)))
            dhy2 = add(dhy, scale(-0.5, sub(plus_z(dex), sub(ez64_next, dez))))
            dhz2 = add(dhz, scale(-0.5, sub(sub(ey64_next, dey), plus_y(dex))))
            dhy62 = scale(-0.5, sub(plus_z(dex62), dez))
            dhz62 = scale(-0.5, sub(dey, plus_y(dex62)))
            put(h_tile, 1, 0, 63, dhx2)
            put(h_tile, 1, 1, 63, dhy2)
            put(h_tile, 1, 2, 63, dhz2)
            put(h_tile, 1, 1, 62, dhy62)
            put(h_tile, 1, 2, 62, dhz62)
            put(e_tile, 1, 0, 63, add(dex, mul(c63, sub(minus_y(dhz2, ghost), minus_z(dhy2)))))
            put(e_tile, 1, 1, 63, add(dey, mul(c63, sub(minus_z(dhx2), sub(dhz2, dhz62)))))
            put(e_tile, 1, 2, 63, add(dez, mul(c63, sub(sub(dhy2, dhy62), minus_y(dhx2)))))
            put(e_tile, 1, 0, 62, add(dex62, mul(c62, sub(minus_y(dhz62, ghost), minus_z(dhy62)))))
            put(e_tile, 1, 1, 62, scale(-1.0, mul(c62, dhz62)))
            put(e_tile, 1, 2, 62, mul(c62, dhy62))
            copies = finish(1)

            hy_part, hz_part, next_y, next_z, cm = read_message(grid, from_below, UP[grid], gz)
            ez0, ey0, ey0_part, ez0_part = read_planes(grid, down, *range(4))
            ez0_change, ey_top = read_planes(grid, patched, 0, 1)
            ez0_part = add(ez0_part, ez0_change)
            ghost = -0.5 * ey_top[0]
            dhy, dhz = scale(0.5, ez0), scale(-0.5, ey0)
            hym, hzm = add(hy_part, dhy), add(hz_part, dhz)
            dexm = mul(cm, sub(minus_y(dhz, ghost), minus_z(dhy)))
            dey, dez = mul(c0, hzm), scale(-1.0, mul(c0, hym))
            dhx2 = scale(-0.5, sub(plus_y(dez), plus_z(dey)))
            dhy2 = scale(-0.5, dez)
            dhz2 = scale(0.5, dey)
            change = sub(sub(add(ez0_part, dez), plus_z(dexm)), mul(cm, dhy))
            hym2 = add(add(next_y, dhy), scale(0.5, change))
            change = sub(sub(plus_y(dexm), add(ey0_part, dey)), mul(cm, dhz))
            hzm2 = add(add(next_z, dhz), scale(0.5, change))
            put(h_tile, 0, 0, 0, dhx2)
            put(h_tile, 0, 1, 0, dhy2)
            put(h_tile, 0, 2, 0, dhz2)
            put(e_tile, 0, 0, 0, mul(c0, sub(minus_y(dhz2), minus_z(dhy2))))
            put(e_tile, 0, 1, 0, add(dey, mul(c0, sub(minus_z(dhx2), sub(dhz2, hzm2)))))
            put(e_tile, 0, 2, 0, add(dez, mul(c0, sub(sub(dhy2, hym2), minus_y(dhx2)))))
            put(e_tile, 0, 1, 1, mul(c1, dhz2))
            put(e_tile, 0, 2, 1, scale(-1.0, mul(c1, dhy2)))
            copies += finish(0)
        else:
            ez32, ey32 = read_message(grid, from_above, DOWN[grid], gz)
            c0, c31 = read_planes(grid, c_planes, 0, 1)
            dhy, dhz = scale(0.5, ez32), scale(-0.5, ey32)
            put(h_tile, 1, 1, last, dhy)
            put(h_tile, 1, 2, last, dhz)
            put(e_tile, 1, 0, last, mul(c31, sub(minus_y(dhz), minus_z(dhy))))
            put(e_tile, 1, 1, last, scale(-1.0, mul(c31, dhz)))
            put(e_tile, 1, 2, last, mul(c31, dhy))
            copies = finish(1)
            hy_part, hz_part = read_message(grid, from_below, UP[grid], gz)
            ez0, ey0 = read_planes(grid, down, 0, 1)
            put(e_tile, 0, 1, 0, mul(c0, add(hz_part, scale(-0.5, ey0))))
            put(e_tile, 0, 2, 0, scale(-1.0, mul(c0, add(hy_part, scale(0.5, ez0)))))
            copies += finish(0)
        for copy in copies:
            copy.wait()

    by_level(body)


def across(x, dx=0, dy=0, dz=0):
    nx, ny, nz = lax.axis_size("gx"), lax.axis_size("gy"), lax.axis_size("gz")
    pairs = [
        ((i * ny + j) * nz + k, ((i + dx) % nx * ny + (j + dy) % ny) * nz + (k + dz) % nz)
        for i in range(nx)
        for j in range(ny)
        for k in range(nz)
    ]
    return lax.ppermute(x, ("gx", "gy", "gz"), pairs)


def fast_shards(electric, magnetic, material, permittivity):
    e = electric.reshape(3, ROWS, 128)
    h = magnetic.reshape(3, ROWS, 128)
    m = material.reshape(ROWS, 128)
    dma = pltpu.SemaphoreType.DMA
    edge_tile = kernel_call(
        peek,
        vmem(8, 128),
        [HBM] * 2,
        VM,
        [pltpu.VMEM((2, 3, 16, 128), F32)] * 2 + [dma((8,))],
    )(far(e), far(h))
    m_face, m_ends = kernel_call(
        fine_material,
        [vmem(HALO, 128, dtype=jnp.int32), vmem(2, 64, 128, dtype=jnp.int32)],
        [HBM, VM],
        [VM] * 2,
        [dma((3,))],
    )(far(m), held(edge_tile))
    edge_tile = across(edge_tile, dz=1)
    zmsg, ytile, columns = kernel_call(
        gather,
        [vmem(FACE + COLUMNS, 128), vmem(8, 128), vmem(COLUMNS, 128)],
        [VM] * 4,
        [VM] * 3,
    )(held(e), held(h), held(m_face), held(m_ends))
    ytile = kernel_call(
        join_z,
        vmem(8, 128),
        [VM] * 2,
        VM,
        cost=pl.CostEstimate(flops=10**10, bytes_accessed=10**8, transcendentals=0),
    )(held(ytile), held(edge_tile))
    zin = across(zmsg, dz=1)
    yin = across(ytile, dy=1)
    yzin = across(ytile, dy=1, dz=1)
    e_ext, h_ext, c_ext, up, down, up_part, down_part, c_planes = kernel_call(
        extend,
        [
            vmem(3, EXT, 128),
            vmem(3, EXT, 128),
            vmem(EXT, 128),
            vmem(96, 128),
            vmem(96, 128),
            vmem(MESSAGE, 128),
            vmem(MESSAGE, 128),
            vmem(64, 128),
        ],
        [VM] * 4 + [HBM, VM],
        [VM] * 8,
        [pltpu.SMEM((MATS,), F32), dma((1,))],
    )(held(e), held(h), held(m), held(zin), far(permittivity), held(columns))
    to_up, to_down = kernel_call(
        join_y,
        [vmem(MESSAGE, 128), vmem(MESSAGE, 128)],
        [VM] * 6,
        [VM] * 2,
    )(*(held(part) for part in (up_part, down_part, c_planes, yzin, columns, zin)))
    from_below = across(to_up, dx=1, dz=1)
    from_above = across(to_down, dx=-1, dz=1)
    whole = jax.ShapeDtypeStruct((3, ROWS, 128), F32)
    e_out, h_out, e_edge, h_edge, patched = kernel_call(
        advance,
        [whole, whole, vmem(2, 3, 64, 128), vmem(2, 3, 64, 128), vmem(32, 128)],
        [VM] * 8,
        [HBM, HBM, VM, VM, VM],
        [pltpu.VMEM((3, EXT, 128), F32)] * 3 + [pltpu.VMEM((2, 320, 128), F32), dma((2,))],
        cost=pl.CostEstimate(flops=10**10, bytes_accessed=10**8, transcendentals=0),
    )(*(held(part) for part in (e_ext, h_ext, c_ext, c_planes, yin, yzin, columns, zin)))
    e_out, h_out, _, _ = kernel_call(
        correct,
        [whole, whole, vmem(2, 3, 64, 128), vmem(2, 3, 64, 128)],
        [VM] * 8 + [HBM] * 2,
        [HBM] * 2 + [VM] * 2,
        [dma((4,))],
        aliases={8: 0, 9: 1, 6: 2, 7: 3},
    )(
        *(held(part) for part in (up, down, c_planes, patched, from_below, from_above, e_edge, h_edge)),
        e_out,
        h_out,
    )
    return e_out.reshape(electric.shape), h_out.reshape(magnetic.shape)


def solution(mesh):
    placed = (
        P(("parts", "gy"), "gx", "gz", None, None),
        P(("parts", "gy"), "gx", "gz", None, None),
        P(("parts", "gy"), "gx", "gz", None),
        P(),
    )
    fast = mesh.shape["gy"] == 2 and mesh.shape["gz"] == 2
    return jax.shard_map(
        fast_shards if fast else general_shards,
        mesh=mesh,
        in_specs=placed,
        out_specs=(
            P(("parts", "gy"), "gx", "gz", None, None),
            P(("parts", "gy"), "gx", "gz", None, None),
        ),
        check_vma=False,
    )
```

```python
from functools import partial

import jax
import jax.numpy as jnp
from jax import lax
from jax.experimental import pallas as pl
from jax.experimental.pallas import tpu as pltpu
from jax.sharding import PartitionSpec as P

CZ = 4
CX = 32
CY = 512
MATS = 4


courant = 0.5


def passed_along(x, axis, by):
    devices = lax.axis_size(axis)
    return lax.ppermute(x, axis, [(i, (i + by) % devices) for i in range(devices)])


def from_behind(x, axis, by):
    devices = lax.axis_size(axis)
    pairs = [(i, i + by) for i in range(devices) if 0 <= i + by < devices]
    return lax.ppermute(x, axis, pairs)


def forward_diff(values, dim_axis, ghost_plane):
    shifted = jnp.concatenate(
        [
            lax.slice_in_dim(values, 1, values.shape[dim_axis], axis=dim_axis),
            jnp.expand_dims(ghost_plane, dim_axis),
        ],
        axis=dim_axis,
    )
    return shifted - values


def backward_diff(values, dim_axis, ghost_plane):
    shifted = jnp.concatenate(
        [
            jnp.expand_dims(ghost_plane, dim_axis),
            lax.slice_in_dim(values, 0, values.shape[dim_axis] - 1, axis=dim_axis),
        ],
        axis=dim_axis,
    )
    return values - shifted


def curl_with(differ, vectors, ghost_depth, ghost_width, ghost_height):
    ghosts = (ghost_depth, ghost_width, ghost_height)

    def along_axis(component, dim_axis):
        return differ(vectors[component], dim_axis, ghosts[dim_axis][component])

    curl_x = along_axis(2, 2) - along_axis(1, 0)
    curl_y = along_axis(0, 0) - along_axis(2, 1)
    curl_z = along_axis(1, 1) - along_axis(0, 2)
    return jnp.stack([curl_x, curl_y, curl_z])


def restrict(face_plane):
    quads = face_plane.reshape(3, face_plane.shape[1] // 2, 2, face_plane.shape[2] // 2, 2)
    return (
        quads[:, :, 0, :, 0] + quads[:, :, 0, :, 1] + (quads[:, :, 1, :, 0] + quads[:, :, 1, :, 1])
    ) * 0.25


def enlarge(face_plane):
    return jnp.repeat(jnp.repeat(face_plane, 2, axis=1), 2, axis=2)


def lookup(material, permittivity):
    permit_sum = jnp.zeros(material.shape, jnp.float32)
    for material_id in range(MATS):
        permit_sum = permit_sum + jnp.where(material == material_id, permittivity[material_id], 0.0)
    return courant / permit_sum


def pack_face(face_plane, length):
    flat_face = face_plane.reshape(3, -1)
    if flat_face.shape[1] < length:
        flat_face = jnp.concatenate(
            [flat_face, jnp.zeros((3, length - flat_face.shape[1]), flat_face.dtype)], axis=1
        )
    return flat_face


def unpack_face(flat_face, row_count, col_count):
    return flat_face[:, : row_count * col_count].reshape(3, row_count, col_count)


def level_height(got_height, is_fine):
    return got_height if is_fine else restrict(got_height)


def low_faces(grid_shape, is_fine, flat_field):
    vectors = flat_field.reshape((3,) + grid_shape)
    face_plane = vectors[:, :, :, 0]
    if not is_fine:
        face_plane = enlarge(face_plane)
    return (
        pack_face(vectors[:, :, 0, :], CZ * CY),
        pack_face(vectors[:, 0, :, :], CX * CY),
        face_plane,
    )


def high_faces(grid_shape, is_fine, flat_field):
    vectors = flat_field.reshape((3,) + grid_shape)
    face_plane = vectors[:, :, :, -1]
    if not is_fine:
        face_plane = enlarge(face_plane)
    return (
        pack_face(vectors[:, :, -1, :], CZ * CY),
        pack_face(vectors[:, -1, :, :], CX * CY),
        face_plane,
    )


def advance_magnetic(
    grid_shape, is_fine, does_move, e_flat, h_flat, got_width, got_depth, got_height
):
    if not does_move:
        return h_flat
    deep_cells, wide_cells, tall_cells = grid_shape
    vectors = e_flat.reshape((3,) + grid_shape)
    curl_term = curl_with(
        forward_diff,
        vectors,
        unpack_face(got_depth, wide_cells, tall_cells),
        unpack_face(got_width, deep_cells, tall_cells),
        level_height(got_height, is_fine),
    )
    return (h_flat.reshape((3,) + grid_shape) - courant * curl_term).reshape(3, -1)


def advance_electric(
    grid_shape, is_fine, does_move, e_flat, h_flat, coefficient, got_width, got_depth, got_height
):
    if not does_move:
        return e_flat
    deep_cells, wide_cells, tall_cells = grid_shape
    magnetic = h_flat.reshape((3,) + grid_shape)
    curl_term = curl_with(
        backward_diff,
        magnetic,
        unpack_face(got_depth, wide_cells, tall_cells),
        unpack_face(got_width, deep_cells, tall_cells),
        level_height(got_height, is_fine),
    )
    return (
        e_flat.reshape((3,) + grid_shape) + coefficient.reshape(grid_shape) * curl_term
    ).reshape(3, -1)


def pass_width(face_plane, offset):
    return passed_along(face_plane, "gx", offset)


def pass_depth(face_plane, offset):
    return from_behind(face_plane, "gz", offset)


def pass_height(face_plane, offset):
    return from_behind(face_plane, "gy", offset)


def general_shards(electric, magnetic, material, permittivity):
    cell_count = electric.shape[-1]
    e_flat = electric.reshape(3, cell_count)
    h_flat = magnetic.reshape(3, cell_count)
    coefficient = lookup(material.reshape(cell_count), permittivity)
    is_fine = lax.axis_index("gy") >= lax.axis_size("gy") // 2
    coarse_shape = (CZ, CX, CY)
    fine_shape = (2 * CZ, 2 * CX, CY // 4)
    for substep in range(2):
        coarse_moves = substep == 0
        face_width, face_depth, face_height = lax.cond(
            is_fine,
            partial(low_faces, fine_shape, True),
            partial(low_faces, coarse_shape, False),
            e_flat,
        )
        got_depth = pass_depth(face_depth, -1)
        got_height = pass_height(face_height, -1)
        got_width = pass_width(face_width, -1)
        h_flat = lax.cond(
            is_fine,
            partial(advance_magnetic, fine_shape, True, True),
            partial(advance_magnetic, coarse_shape, False, coarse_moves),
            e_flat,
            h_flat,
            got_width,
            got_depth,
            got_height,
        )
        rim_width, rim_depth, rim_height = lax.cond(
            is_fine,
            partial(high_faces, fine_shape, True),
            partial(high_faces, coarse_shape, False),
            h_flat,
        )
        rim_depth = pass_depth(rim_depth, 1)
        rim_height = pass_height(rim_height, 1)
        rim_width = pass_width(rim_width, 1)
        e_flat = lax.cond(
            is_fine,
            partial(advance_electric, fine_shape, True, True),
            partial(advance_electric, coarse_shape, False, coarse_moves),
            e_flat,
            h_flat,
            coefficient,
            rim_width,
            rim_depth,
            rim_height,
        )
    return (e_flat.reshape(electric.shape), h_flat.reshape(magnetic.shape))


ROWS = 512
HALO = 128
EXT = 1296
LIMIT = 40 * 1024 * 1024
F32 = jnp.float32
VM = pl.BlockSpec(memory_space=pltpu.VMEM)
HBM = pl.BlockSpec(memory_space=pltpu.HBM)
CHUNK = 32
SKEW = 2


class Fine:
    depth, stride, count, own, step, parts, last = 64, 72, 10, 8, 1, 1, 63


class Coarse:
    depth, stride, count, own, step, parts, last = 128, 144, 5, 4, 4, 4, 31


def vmem(*shape, dtype=F32):
    return pltpu.VMEM(shape, dtype)


def held(x):
    return pltpu.with_memory_space_constraint(x, pltpu.VMEM)


def far(x):
    return pltpu.with_memory_space_constraint(x, pltpu.HBM)


def kernel_call(body, out_shape, in_specs, out_specs, scratch=(), aliases=None, cost=None):
    return pl.pallas_call(
        body,
        cost_estimate=cost,
        out_shape=out_shape,
        in_specs=in_specs,
        out_specs=out_specs,
        scratch_shapes=list(scratch),
        input_output_aliases=aliases or {},
        compiler_params=pltpu.CompilerParams(vmem_limit_bytes=LIMIT),
    )


def by_level(body):
    is_fine = lax.axis_index("gy") >= lax.axis_size("gy") // 2
    gz = lax.axis_index("gz")
    pl.when(is_fine)(lambda: body(Fine, gz))
    pl.when(jnp.logical_not(is_fine))(lambda: body(Coarse, gz))


def lanes_of(shape):
    return lax.broadcasted_iota(jnp.int32, shape, len(shape) - 1)


def rows_of(shape):
    return lax.broadcasted_iota(jnp.int32, shape, len(shape) - 2)


def roll_lanes(x, by):
    return pltpu.roll(x, by % 128, 1)


def roll_rows(x, by):
    return pltpu.roll(x, by % x.shape[0], 0)


def layer_row(grid, index):
    return pl.multiple_of(grid.stride * (index + 1), 8)


def own_first(grid, gz):
    return (grid.count - grid.own) * gz


def halo_first(grid, gz):
    return grid.own * (1 - gz)


def clear_pads(grid, ref, *zero_layers):
    for comp in range(3):
        for index in range(grid.count + 2):
            start, size = grid.stride * index, grid.stride
            if index not in zero_layers:
                start, size = start + grid.depth, size - grid.depth
            ref[comp, pl.ds(start, size), :] = jnp.zeros((size, 128), F32)


def own_layers(grid, ref, gz):
    view = ref.reshape(3, EXT // grid.stride, grid.stride, 128)
    return view.at[:, pl.ds(1 + own_first(grid, gz), grid.own), pl.ds(0, grid.depth), :]


def block_layers(grid, ref):
    return ref.reshape(3, grid.own, grid.depth, 128)


def at_lane(tile, lane_from, lane_to, value):
    lane = lanes_of(value.shape)
    return jnp.where(lane == lane_to, roll_lanes(value, lane_to - lane_from), tile)


def average(ref, lead, row, stride):
    steps = (0, 1, stride, stride + 1)
    quad = [ref[lead, pl.ds(row + step, 32, stride=2), :] for step in steps]
    return ((quad[0] + quad[1]) + (quad[2] + quad[3])) * 0.25


def put_column(tile, lane_from, slot, column):
    for block in range(4):
        tile = at_lane(tile, lane_from, 32 * block + slot, column[8 * block : 8 * block + 8])
    return tile


FINE_E = [(0, comp) for comp in range(3)] + [(1, 1), (1, 2)] + [(x, comp) for x in (62, 63) for comp in range(3)]
FINE_H = [(0, comp) for comp in range(3)] + [(62, 1), (62, 2)] + [(63, comp) for comp in range(3)]
FINE_M = [0, 1, 62, 63]
COARSE_E = [(0, 1), (0, 2)] + [(31, comp) for comp in range(3)]
COARSE_H = [(31, 1), (31, 2)]
COARSE_M = [0, 31]
COLUMNS = 192
R_ROW = COLUMNS - 8
FACE = 7 * HALO


def wanted(grid):
    return (FINE_E, FINE_H, FINE_M) if grid is Fine else (COARSE_E, COARSE_H, COARSE_M)


def top_tile(tile, layer, ex, ey, ez, hx, hz):
    tile = put_column(tile, 127, layer, hx + 0.5 * ez)
    tile = put_column(tile, 127, 8 + layer, hz - 0.5 * ex)
    return put_column(tile, 127, 16 + layer, ey)


def edge_tiles(grid, ref):
    view = ref.reshape(grid.own, grid.depth, 128)
    return [view.at[:, pl.ds((grid.depth - 8) * end, 8), :] for end in range(2)]


def material_loads(grid, gz, m_hbm, m_face, m_ends, sems):
    face = pl.ds((1 - gz) * (ROWS - HALO), HALO)
    loads = [pltpu.make_async_copy(m_hbm.at[face], m_face, sems.at[0])]
    for end, tiles in enumerate(edge_tiles(grid, m_hbm)):
        place = m_ends.at[end].reshape(8, 8, 128).at[pl.ds(0, grid.own)]
        loads.append(pltpu.make_async_copy(tiles, place, sems.at[1 + end]))
    return loads


def peek(e_hbm, h_hbm, edge_tile, e_ends, h_ends, sems):
    def body(grid, gz):
        if grid is Fine:
            edge_tile[...] = jnp.zeros((8, 128), F32)
            return
        loads = []
        for end in range(2):
            rows = pl.ds((1 - gz) * (ROWS - HALO) + (HALO - 8) * end, 8)
            place = pl.ds(0, 8)
            loads.append(pltpu.make_async_copy(e_hbm.at[:, rows], e_ends.at[end, :, place], sems.at[2 * end]))
            for slot, comp in enumerate((0, 2)):
                into = h_ends.at[end, comp, place]
                loads.append(pltpu.make_async_copy(h_hbm.at[comp, rows], into, sems.at[4 + 2 * end + slot]))
        for load in loads:
            load.start()
        for load in loads:
            load.wait()
        tile = jnp.zeros((8, 128), F32)
        lane = lanes_of((8, 128))
        for end in range(2):
            rows = pl.ds(0 if end else 3, 8)
            ex, ey, ez = (e_ends[end, comp, rows, :] for comp in range(3))
            hx, hz = h_ends[end, 0, rows, :], h_ends[end, 2, rows, :]
            for kind, value in enumerate((hx + 0.5 * ez, hz - 0.5 * ex, ey)):
                to = 96 * end + 8 * kind + 3 + gz
                tile = jnp.where(lane == to, pltpu.roll(value, to + 1, 1), tile)
        edge_tile[...] = tile

    by_level(body)


def fine_material(m_hbm, after, m_face, m_ends, sems):
    def body(grid, gz):
        if grid is Coarse:
            return
        loads = material_loads(grid, gz, m_hbm, m_face, m_ends, sems)
        for load in loads:
            load.start()
        for load in loads:
            load.wait()

    by_level(body)


def gather(e_own, h_own, m_face, m_ends, zmsg, ytile, columns):
    def body(grid, gz):
        tile = jnp.zeros((8, 128), F32)
        for layer in range(4):
            if grid is Fine:
                row = 2 * grid.depth * layer
                tile = put_column(tile, 0, layer, average(e_own, 0, row, grid.depth))
                tile = put_column(tile, 0, 8 + layer, average(e_own, 2, row, grid.depth))
            else:
                top = pl.ds(grid.depth * layer + 3, 32, stride=4)
                ex, ey, ez = (e_own[comp, top, :] for comp in range(3))
                tile = top_tile(tile, layer, ex, ey, ez, h_own[0, top, :], h_own[2, top, :])
        tile = jnp.where(gz == 1, roll_lanes(tile, 4), tile)
        ytile[...] = tile
        columns[pl.ds(R_ROW, 8), :] = tile
        want_e, want_h, want_m = wanted(grid)
        slot = 0

        def column_rows(x, part):
            return pl.ds(grid.step * x + part, grid.own, stride=grid.depth)

        def put(value):
            nonlocal slot
            columns[pl.ds(slot, grid.own), :] = value
            slot += grid.own

        for x, comp in want_e:
            for part in range(grid.parts):
                put(e_own[comp, column_rows(x, part), :])
        for x, comp in want_h:
            for part in range(grid.parts):
                put(h_own[comp, column_rows(x, part), :])
        for x in want_m if grid is Fine else []:
            for part in range(grid.parts):
                rows = pl.ds(grid.step * x % 8 + part, grid.own, stride=8)
                put(m_ends[int(x > 1), rows, :].astype(F32))
        edge = pl.ds(pl.multiple_of((1 - gz) * (ROWS - HALO), HALO), HALO)
        for comp in range(3):
            zmsg[pl.ds(HALO * comp, HALO), :] = h_own[comp, edge, :]
            zmsg[pl.ds(HALO * (3 + comp), HALO), :] = e_own[comp, edge, :]
        if grid is Fine:
            zmsg[pl.ds(6 * HALO, HALO), :] = m_face[...].astype(F32)
        zmsg[pl.ds(FACE, COLUMNS), :] = columns[...]

    by_level(body)


def join_z(ytile, edge_tile, joined):
    joined[...] = ytile[...] + edge_tile[...]


def up_y(grid, ref, comp, row, f):
    lane = lanes_of(f.shape)
    if grid is Fine:
        return jnp.where(lane == 127, 0.0, roll_lanes(f, -1))
    following = ref[comp, pl.ds(row + 1, f.shape[0]), :]
    following = jnp.where(rows_of(f.shape) % 4 == 3, 0.0, following)
    return roll_lanes(jnp.where(lane == 0, following, f), -1)


def down_y(grid, ref, comp, row, f, ghost):
    lane = lanes_of(f.shape)
    if grid is Fine:
        return roll_lanes(jnp.where(lane == 127, ghost, f), 1)
    previous = ref[comp, pl.ds(row - 1, f.shape[0]), :]
    previous = jnp.where(rows_of(f.shape) % 4 == 0, 0.0, previous)
    return roll_lanes(jnp.where(lane == 127, previous, f), 1)


def half_h(grid, e, h_from, from_row, h_to, row):
    for start in range(0, grid.depth, CHUNK):
        r = row + start
        here = pl.ds(r, CHUNK)
        ex, ey, ez = (e[comp, here, :] for comp in range(3))
        above, beside = pl.ds(r + grid.stride, CHUNK), pl.ds(r + grid.step, CHUNK)
        h0 = [h_from(comp, pl.ds(from_row + start, CHUNK)) for comp in range(3)]
        ez_y, ex_y = up_y(grid, e, 2, r, ez), up_y(grid, e, 0, r, ex)
        h_to[0, here, :] = h0[0] - 0.5 * ((ez_y - ez) - (e[1, above, :] - ey))
        h_to[1, here, :] = h0[1] - 0.5 * ((e[0, above, :] - ex) - (e[2, beside, :] - ez))
        h_to[2, here, :] = h0[2] - 0.5 * ((e[1, beside, :] - ey) - (ex_y - ex))


def half_e(grid, h, e_from, e_to, c_ref, row, ghosts):
    for start in range(0, grid.depth, CHUNK):
        r = row + start
        here = pl.ds(r, CHUNK)
        hx, hy, hz = (h[comp, here, :] for comp in range(3))
        below, beside = pl.ds(r - grid.stride, CHUNK), pl.ds(r - grid.step, CHUNK)
        px, pz = ghosts(start)
        hx_y, hz_y = down_y(grid, h, 0, r, hx, px), down_y(grid, h, 2, r, hz, pz)
        c = c_ref[here, :]
        e_to[0, here, :] = e_from[0, here, :] + c * ((hz - hz_y) - (hy - h[1, below, :]))
        e_to[1, here, :] = e_from[1, here, :] + c * ((hx - h[0, below, :]) - (hz - h[2, beside, :]))
        e_to[2, here, :] = e_from[2, here, :] + c * ((hy - h[1, beside, :]) - (hx - hx_y))


def column_of(tile, block, sub, slot, grid):
    shape = (2 * grid.own, 128)
    row = jnp.broadcast_to(tile[sub : sub + 1, :], shape)
    lane = 32 * block + slot + rows_of(shape) // (2 * grid.own // 8)
    picked = jnp.where(lanes_of(shape) == lane, row, 0.0)
    return jnp.broadcast_to(jnp.sum(picked, axis=1, keepdims=True), shape)


def each(fn, *columns):
    return [fn(*parts) for parts in zip(*columns, strict=True)]


def plus_y(f, ghost=0.0):
    following = f[1:] + [ghost]
    return [
        roll_lanes(jnp.where(lanes_of(p.shape) == 0, nxt, p), -1) - p
        for p, nxt in zip(f, following, strict=True)
    ]


def minus_y(f, ghost=0.0):
    previous = [ghost] + f[:-1]
    return [
        p - roll_lanes(jnp.where(lanes_of(p.shape) == 127, prv, p), 1)
        for p, prv in zip(f, previous, strict=True)
    ]


def plus_z(f):
    return [
        jnp.where(rows_of(p.shape) == p.shape[0] - 1, 0.0, roll_rows(p, -1)) - p for p in f
    ]


def minus_z(f):
    return [p - jnp.where(rows_of(p.shape) == 0, 0.0, roll_rows(p, 1)) for p in f]


def add(a, b):
    return each(lambda p, q: p + q, a, b)


def sub(a, b):
    return each(lambda p, q: p - q, a, b)


def mul(a, b):
    return each(lambda p, q: p * q, a, b)


def scale(by, a):
    return [by * p for p in a]


def read_columns(grid, own, other, gz):
    want_e, want_h, want_m = wanted(grid)
    found, slot = [], 0
    for _ in range(len(want_e) + len(want_h) + len(want_m)):
        col = []
        for _ in range(grid.parts):
            rows = pl.ds(slot, grid.own)
            mine, theirs = own[rows, :], other[pl.ds(FACE + slot, grid.own), :]
            low, high = jnp.where(gz == 0, mine, theirs), jnp.where(gz == 0, theirs, mine)
            col.append(jnp.concatenate([low, high], axis=0))
            slot += grid.own
        found.append(col)
    e_found, found = found[: len(want_e)], found[len(want_e) :]
    h_found, m_found = found[: len(want_h)], found[len(want_h) :]
    return (
        dict(zip(want_e, e_found, strict=True)),
        dict(zip(want_h, h_found, strict=True)),
        dict(zip(want_m, m_found, strict=True)),
    )


def write_planes(ref, columns):
    row = 0
    for col in columns:
        for p in col:
            ref[pl.ds(row, p.shape[0]), :] = p
            row += p.shape[0]


def read_planes(grid, ref, *indices):
    height, parts = 2 * grid.own, grid.parts
    return [
        [ref[pl.ds(height * (parts * i + part), height), :] for part in range(parts)] for i in indices
    ]


MESSAGE = 48
UP = {Fine: [(9, 7)] * 5, Coarse: [(4, 4)] * 2}
DOWN = {Fine: [(10, 6)] + [(9, 7)] * 4, Coarse: [(5, 3)] * 2}


def sent_rows(plane, entry, gz):
    count, begin = entry
    return jnp.where(gz == 0, roll_rows(plane, -begin), plane)[:count]


def places(grid, entries):
    row = 0
    for entry in entries:
        for _ in range(grid.parts):
            yield row, entry
            row += entry[0]


def write_message(grid, ref, entries, columns, gz):
    planes = [p for col in columns for p in col]
    for (row, entry), p in zip(places(grid, entries), planes, strict=True):
        ref[pl.ds(row, entry[0]), :] = sent_rows(p, entry, gz)


def read_message(grid, ref, entries, gz):
    height, planes = 2 * grid.own, []
    for row, (_, begin) in places(grid, entries):
        start = min(row, MESSAGE - height)
        p = ref[pl.ds(start, height), :]
        planes.append(pltpu.roll(p, height + start - row + begin * gz, 0))
    return [planes[i : i + grid.parts] for i in range(0, len(planes), grid.parts)]


def extend(
    e_own,
    h_own,
    m_own,
    zmsg,
    permittivity,
    columns,
    e_ext,
    h_ext,
    c_ext,
    up,
    down,
    to_up,
    to_down,
    c_planes,
    table,
    sems,
):
    def body(grid, gz):
        load = pltpu.make_async_copy(permittivity, table, sems.at[0])
        load.start()
        clear_pads(grid, h_ext, 0)
        clear_pads(grid, e_ext, grid.count + 1)
        for layer in range(grid.own):
            for start in range(0, grid.depth, CHUNK):
                rows = pl.ds(layer_row(grid, own_first(grid, gz) + layer) + start, CHUNK)
                from_rows = pl.ds(grid.depth * layer + start, CHUNK)
                for comp in range(3):
                    e_ext[comp, rows, :] = e_own[comp, from_rows, :]
        halo = halo_first(grid, gz)
        for layer in range(grid.count - grid.own):
            for start in range(0, grid.depth, CHUNK):
                rows = pl.ds(layer_row(grid, halo + layer) + start, CHUNK)
                for comp in range(3):
                    from_rows = pl.ds(HALO * (3 + comp) + grid.depth * layer + start, CHUNK)
                    e_ext[comp, rows, :] = zmsg[from_rows, :]

        def h_halo(comp, rows):
            return zmsg[pl.ds(HALO * comp + rows.start, rows.size), :]

        for layer in range(grid.count - grid.own):
            row = layer_row(grid, halo + layer)
            half_h(grid, e_ext, h_halo, grid.depth * layer, h_ext, row)
        for layer in range(grid.own):
            row = layer_row(grid, own_first(grid, gz) + layer)
            half_h(grid, e_ext, lambda comp, rows: h_own[comp, rows, :], grid.depth * layer, h_ext, row)
        load.wait()
        values = [0.5 / jnp.full((8, 128), table[i], F32) for i in range(MATS)]

        def coef(is_material, rows):
            parts = [jnp.concatenate([value] * (rows // 8), axis=0) for value in values]
            found = parts[MATS - 1]
            for i in range(MATS - 2, -1, -1):
                found = jnp.where(is_material(i), parts[i], found)
            return found

        for start in range(0, HALO if grid is Fine else 0, CHUNK):
            layer, rest = divmod(start, grid.depth)
            material = zmsg[pl.ds(6 * HALO + start, CHUNK), :]
            row = layer_row(grid, halo + layer) + rest
            c_ext[pl.ds(row, CHUNK), :] = coef(lambda i, m=material: m == float(i), CHUNK)
        for start in range(0, ROWS, CHUNK):
            layer, rest = divmod(start, grid.depth)
            material = m_own[pl.ds(start, CHUNK), :]
            row = layer_row(grid, own_first(grid, gz) + layer) + rest
            c_ext[pl.ds(row, CHUNK), :] = coef(lambda i, m=material: m == i, CHUNK)

        e, h, m = read_columns(grid, columns, zmsg, gz)
        if grid is Coarse:
            for x in m:
                rows = [pl.ds(4 * x + part, 4, stride=grid.depth) for part in range(4)]
                own = [m_own[part, :].astype(F32) for part in rows]
                m[x] = [jnp.concatenate([part, part], axis=0) for part in own]
        c = {
            x: [coef(lambda i, q=part: q == float(i), part.shape[0]) for part in col] for x, col in m.items()
        }
        write_planes(c_planes, list(c.values()))
        if grid is Coarse:
            ex, ey, ez = (e[31, comp] for comp in range(3))
            hy = sub(h[31, 1], scale(0.5, add(plus_z(ex), ez)))
            hz = add(h[31, 2], scale(0.5, add(ey, plus_y(ex))))
            sent_up, sent_down = [hy, hz], [e[0, 2], e[0, 1]]
        else:
            ex, ey, ez = (e[0, comp] for comp in range(3))
            hx = sub(h[0, 0], scale(0.5, sub(plus_y(ez), plus_z(ey))))
            hy = sub(h[0, 1], scale(0.5, sub(plus_z(ex), sub(e[1, 2], ez))))
            hz = sub(h[0, 2], scale(0.5, sub(sub(e[1, 1], ey), plus_y(ex))))
            ey_next = add(ey, mul(c[0], sub(minus_z(hx), hz)))
            ez_next = add(ez, mul(c[0], sub(hy, minus_y(hx))))
            sent_down = [ez, ey, ey_next, ez_next, c[0]]
            ex, ey, ez = (e[62, comp] for comp in range(3))
            hy62 = sub(h[62, 1], scale(0.5, sub(plus_z(ex), sub(e[63, 2], ez))))
            hz62 = sub(h[62, 2], scale(0.5, sub(sub(e[63, 1], ey), plus_y(ex))))
            ex, ey, ez = (e[63, comp] for comp in range(3))
            hx = sub(h[63, 0], scale(0.5, sub(plus_y(ez), plus_z(ey))))
            hy = sub(h[63, 1], scale(0.5, add(plus_z(ex), ez)))
            hz = add(h[63, 2], scale(0.5, add(ey, plus_y(ex))))
            ex_next = add(ex, mul(c[63], sub(minus_y(hz), minus_z(hy))))
            ey_next = add(ey, mul(c[63], sub(minus_z(hx), sub(hz, hz62))))
            ez_next = add(ez, mul(c[63], sub(sub(hy, hy62), minus_y(hx))))
            next_y = sub(hy, scale(0.5, add(plus_z(ex_next), ez_next)))
            next_z = add(hz, scale(0.5, add(ey_next, plus_y(ex_next))))
            sent_up = [hy, hz, next_y, next_z, c[63]]
        write_planes(up, sent_up)
        write_planes(down, sent_down)
        write_message(grid, to_up, UP[grid], sent_up, gz)
        write_message(grid, to_down, DOWN[grid], sent_down, gz)

    by_level(body)


def between(top, r):
    lane, row = lanes_of(top.shape), rows_of(top.shape)
    kind = (lane % 32) // 8
    above = jnp.where(lane % 8 == 7, 0.0, roll_lanes(top, -1))
    px = top - 0.5 * roll_lanes(r, -8) + 0.5 * roll_lanes(above - top, -16)
    beside = roll_rows(top, -1)
    beside = jnp.where(row == 7, jnp.where(lane >= 96, 0.0, roll_lanes(beside, -32)), beside)
    pz = top + 0.5 * roll_lanes(r, 8) - 0.5 * roll_lanes(beside - top, -8)
    return jnp.where(kind == 0, px, jnp.where(kind == 1, pz, 0.0))


def join_y(up_in, down_in, c_planes, yzin, r_own, r_other, to_up, to_down):
    def body(grid, gz):
        def patch(ref, entries, index, value):
            row, entry = list(places(grid, entries))[index]
            rows = pl.ds(row, entry[0])
            ref[rows, :] = ref[rows, :] + sent_rows(value, entry, gz)

        top = yzin[...]
        to_up[...] = up_in[...]
        to_down[...] = down_in[...]
        shape = (2 * grid.own, 128)
        if grid is Coarse:
            change = jnp.where(lanes_of(shape) == 127, 0.5 * column_of(top, 3, 7, 0, grid), 0.0)
            patch(to_up, UP[grid], 7, change)
            return
        plane = between(top, r_own[pl.ds(R_ROW, 8), :] + r_other[pl.ds(FACE + R_ROW, 8), :])
        bottom = lanes_of(shape) == 0
        (c0,), (c63,) = read_planes(grid, c_planes, 0, 3)

        patch(to_down, DOWN[grid], 3, jnp.where(bottom, c0 * column_of(plane, 0, 0, 0, grid), 0.0))
        ez_change = jnp.where(bottom, c63 * column_of(plane, 3, 7, 0, grid), 0.0)
        ex_change = jnp.where(bottom, -c63 * column_of(plane, 3, 7, 8, grid), 0.0)
        patch(to_up, UP[grid], 2, -0.5 * (plus_z([ex_change])[0] + ez_change))
        patch(to_up, UP[grid], 3, -0.5 * ex_change)
        to_down[pl.ds(MESSAGE - 1, 1), :] = top[:1]

    by_level(body)


def advance(
    e_ext,
    h_ext,
    c_ext,
    c_planes,
    yin,
    yzin,
    r_own,
    r_other,
    e_out,
    h_out,
    e_edge,
    h_edge,
    patched,
    e_mid,
    h_mid,
    e_last,
    plane,
    sems,
):
    def body(grid, gz):
        first = own_first(grid, gz)
        upper = lanes_of((8, 128)) % 8 >= 4
        tile = jnp.where(upper == (gz == 0), yzin[...], yin[...])
        if grid is Fine:
            top = tile
            tile = between(top, r_own[pl.ds(R_ROW, 8), :] + r_other[pl.ds(FACE + R_ROW, 8), :])
            ((c0,),) = read_planes(grid, c_planes, 0)
            change = jnp.where(lanes_of((16, 128)) == 0, c0 * column_of(tile, 0, 0, 0, grid), 0.0)
            patched[pl.ds(0, 16), :] = change
            patched[pl.ds(16, 16), :] = column_of(top, 0, 0, 16, grid)
        tile = jnp.where(gz == 0, tile, roll_lanes(tile, -3))

        def write(source, target, sem, layer=None):
            source, target = own_layers(grid, source, gz), block_layers(grid, target)
            if layer is not None:
                source, target = source.at[:, layer], target.at[:, layer]
            return pltpu.make_async_copy(source, target, sem)

        def keep_edges(source, target):
            for comp in range(3):
                for layer in range(grid.own):
                    for edge in range(2):
                        row = layer_row(grid, first + layer) + (grid.depth - 8) * edge
                        target[edge, comp, pl.ds(8 * layer, 8), :] = source[comp, pl.ds(row, 8), :]

        clear_pads(grid, h_mid, 0)
        if grid is Fine:
            clear_pads(grid, e_mid, grid.count + 1)
            for kind in range(2):
                for layer in range(5):
                    for block in range(4):
                        value = roll_lanes(tile, 127 - (32 * block + 8 * kind + layer))
                        for step in range(2):
                            rows = pl.ds(64 * layer + 16 * block + step, 8, stride=2)
                            plane[kind, rows, :] = value

            def ghosts(index):
                begin = 64 * (index // 2)

                def of(start):
                    rows = pl.ds(pl.multiple_of(begin + start, 8), CHUNK)
                    return plane[0, rows, :], plane[1, rows, :]

                return of

            def own_write(source, target, sem, layer):
                def start():
                    rows = pl.ds(layer_row(grid, layer), grid.depth)
                    to = block_layers(grid, target).at[:, layer - first]
                    pltpu.make_async_copy(source.at[:, rows], to, sem).start()

                if 2 <= layer < 8:
                    start()
                else:
                    pl.when((layer < 8) == (gz == 0))(start)

            def h1(comp, rows):
                return h_ext[comp, rows, :]

            for step in range(grid.count + 2 * SKEW):
                if step < grid.count:
                    half_e(grid, h_ext, e_ext, e_mid, c_ext, grid.stride * (step + 1), ghosts(step))
                layer = step - SKEW
                if 0 <= layer < grid.count:
                    row = grid.stride * (layer + 1)
                    half_h(grid, e_mid, h1, row, h_mid, row)
                    own_write(h_mid, h_out, sems.at[0], layer)
                layer = step - 2 * SKEW
                if 0 <= layer < grid.count:
                    row = grid.stride * (layer + 1)
                    half_e(grid, h_mid, e_mid, e_last, c_ext, row, ghosts(layer))
                    own_write(e_last, e_out, sems.at[1], layer)
        else:
            for comp in range(3):
                for layer in range(grid.count):
                    rows = pl.ds(layer_row(grid, layer), grid.depth)
                    h_mid[comp, rows, :] = h_ext[comp, rows, :]
            lane = lanes_of((8, 128))
            for layer in range(grid.count):
                for block in range(4):
                    rows = pl.ds(layer_row(grid, layer) + 32 * block + 3, 8, stride=4)
                    rx = roll_lanes(tile, 127 - (32 * block + layer))
                    rz = roll_lanes(tile, 127 - (32 * block + 8 + layer))
                    h_mid[0, rows, :] = h_mid[0, rows, :] - jnp.where(lane == 127, 0.5 * rz, 0.0)
                    h_mid[2, rows, :] = h_mid[2, rows, :] + jnp.where(lane == 127, 0.5 * rx, 0.0)
            write(h_mid, h_out, sems.at[0]).start()
            for layer in range(grid.own):
                row = layer_row(grid, first + layer)
                half_e(grid, h_mid, e_ext, e_last, c_ext, row, lambda start: (0.0, 0.0))
                write(e_last, e_out, sems.at[1], layer).start()
        keep_edges(h_mid, h_edge)
        keep_edges(e_last, e_edge)
        write(h_mid, h_out, sems.at[0]).wait()
        write(e_last, e_out, sems.at[1]).wait()

    by_level(body)


def correct(
    up,
    down,
    c_planes,
    patched,
    from_below,
    from_above,
    e_edge,
    h_edge,
    e_in,
    h_in,
    e_out,
    h_out,
    e_tile,
    h_tile,
    sems,
):
    def body(grid, gz):
        last = grid.last

        def put(ref, edge, comp, x, change):
            for part, p in enumerate(change):
                own = jnp.where(gz == 0, p[: grid.own], p[grid.own :])
                rows = pl.ds(grid.step * x % 8 + part, grid.own, stride=8)
                ref[edge, comp, rows, :] = ref[edge, comp, rows, :] + own

        def finish(edge):
            copies = []
            for slot, (tile, out) in enumerate(((h_tile, h_out), (e_tile, e_out))):
                if grid is Coarse and edge == 0 and slot == 0:
                    continue
                source = tile.at[edge].reshape(3, 8, 8, 128).at[:, pl.ds(0, grid.own)]
                target = block_layers(grid, out).at[:, :, pl.ds((grid.depth - 8) * edge, 8), :]
                copies.append(pltpu.make_async_copy(source, target, sems.at[2 * edge + slot]))
            for copy in copies:
                copy.start()
            return copies

        if grid is Fine:
            zero = [jnp.zeros((16, 128), F32)]
            ez64, ey64, ey64_part, ez64_part, c64 = read_message(grid, from_above, DOWN[grid], gz)
            ey_above = column_of(from_above[pl.ds(MESSAGE - 8, 8), :], 0, 7, 16, grid)
            hy63, hz63 = read_planes(grid, up, 0, 1)
            c0, c1, c62, c63 = read_planes(grid, c_planes, *range(4))
            hy_part, hz_part, next_y, next_z, cm = read_message(grid, from_below, UP[grid], gz)
            ez0, ey0, ey0_part, ez0_part = read_planes(grid, down, *range(4))
            ez0_change, ey_top = read_planes(grid, patched, 0, 1)
            ez0_part = add(ez0_part, ez0_change)
            ghost = -0.5 * ey_top[0]
            dhy, dhz = scale(0.5, ez0), scale(-0.5, ey0)
            hym, hzm = add(hy_part, dhy), add(hz_part, dhz)
            dexm = mul(cm, sub(minus_y(dhz, ghost), minus_z(dhy)))
            dey, dez = mul(c0, hzm), scale(-1.0, mul(c0, hym))
            dhx2 = scale(-0.5, sub(plus_y(dez), plus_z(dey)))
            dhy2 = scale(-0.5, dez)
            dhz2 = scale(0.5, dey)
            change = sub(sub(add(ez0_part, dez), plus_z(dexm)), mul(cm, dhy))
            hym2 = add(add(next_y, dhy), scale(0.5, change))
            change = sub(sub(plus_y(dexm), add(ey0_part, dey)), mul(cm, dhz))
            hzm2 = add(add(next_z, dhz), scale(0.5, change))
            put(h_tile, 0, 0, 0, dhx2)
            put(h_tile, 0, 1, 0, dhy2)
            put(h_tile, 0, 2, 0, dhz2)
            put(e_tile, 0, 0, 0, mul(c0, sub(minus_y(dhz2), minus_z(dhy2))))
            put(e_tile, 0, 1, 0, add(dey, mul(c0, sub(minus_z(dhx2), sub(dhz2, hzm2)))))
            put(e_tile, 0, 2, 0, add(dez, mul(c0, sub(sub(dhy2, hym2), minus_y(dhx2)))))
            put(e_tile, 0, 1, 1, mul(c1, dhz2))
            put(e_tile, 0, 2, 1, scale(-1.0, mul(c1, dhy2)))
            copies = finish(0)

            ghost = -0.5 * ey_above
            dhy, dhz = scale(0.5, ez64), scale(-0.5, ey64)
            dex = mul(c63, sub(minus_y(dhz, ghost), minus_z(dhy)))
            dey = scale(-1.0, mul(c63, dhz))
            dez = mul(c63, dhy)
            dex62 = mul(c62, minus_y(zero, ghost))
            ey64_next = add(ey64_part, mul(c64, add(hz63, dhz)))
            ez64_next = sub(ez64_part, mul(c64, add(hy63, dhy)))
            dhx2 = scale(-0.5, sub(plus_y(dez), plus_z(dey)))
            dhy2 = add(dhy, scale(-0.5, sub(plus_z(dex), sub(ez64_next, dez))))
            dhz2 = add(dhz, scale(-0.5, sub(sub(ey64_next, dey), plus_y(dex))))
            dhy62 = scale(-0.5, sub(plus_z(dex62), dez))
            dhz62 = scale(-0.5, sub(dey, plus_y(dex62)))
            put(h_tile, 1, 0, 63, dhx2)
            put(h_tile, 1, 1, 63, dhy2)
            put(h_tile, 1, 2, 63, dhz2)
            put(h_tile, 1, 1, 62, dhy62)
            put(h_tile, 1, 2, 62, dhz62)
            put(e_tile, 1, 0, 63, add(dex, mul(c63, sub(minus_y(dhz2, ghost), minus_z(dhy2)))))
            put(e_tile, 1, 1, 63, add(dey, mul(c63, sub(minus_z(dhx2), sub(dhz2, dhz62)))))
            put(e_tile, 1, 2, 63, add(dez, mul(c63, sub(sub(dhy2, dhy62), minus_y(dhx2)))))
            put(e_tile, 1, 0, 62, add(dex62, mul(c62, sub(minus_y(dhz62, ghost), minus_z(dhy62)))))
            put(e_tile, 1, 1, 62, scale(-1.0, mul(c62, dhz62)))
            put(e_tile, 1, 2, 62, mul(c62, dhy62))
            copies += finish(1)
        else:
            ez32, ey32 = read_message(grid, from_above, DOWN[grid], gz)
            c0, c31 = read_planes(grid, c_planes, 0, 1)
            dhy, dhz = scale(0.5, ez32), scale(-0.5, ey32)
            put(h_tile, 1, 1, last, dhy)
            put(h_tile, 1, 2, last, dhz)
            put(e_tile, 1, 0, last, mul(c31, sub(minus_y(dhz), minus_z(dhy))))
            put(e_tile, 1, 1, last, scale(-1.0, mul(c31, dhz)))
            put(e_tile, 1, 2, last, mul(c31, dhy))
            copies = finish(1)
            hy_part, hz_part = read_message(grid, from_below, UP[grid], gz)
            ez0, ey0 = read_planes(grid, down, 0, 1)
            put(e_tile, 0, 1, 0, mul(c0, add(hz_part, scale(-0.5, ey0))))
            put(e_tile, 0, 2, 0, scale(-1.0, mul(c0, add(hy_part, scale(0.5, ez0)))))
            copies += finish(0)
        for copy in copies:
            copy.wait()

    by_level(body)


def across(x, dx=0, dy=0, dz=0):
    nx, ny, nz = lax.axis_size("gx"), lax.axis_size("gy"), lax.axis_size("gz")
    pairs = [
        ((i * ny + j) * nz + k, ((i + dx) % nx * ny + (j + dy) % ny) * nz + (k + dz) % nz)
        for i in range(nx)
        for j in range(ny)
        for k in range(nz)
    ]
    return lax.ppermute(x, ("gx", "gy", "gz"), pairs)


def fast_shards(electric, magnetic, material, permittivity):
    e = electric.reshape(3, ROWS, 128)
    h = magnetic.reshape(3, ROWS, 128)
    m = material.reshape(ROWS, 128)
    dma = pltpu.SemaphoreType.DMA
    edge_tile = kernel_call(
        peek,
        vmem(8, 128),
        [HBM] * 2,
        VM,
        [pltpu.VMEM((2, 3, 16, 128), F32)] * 2 + [dma((8,))],
    )(far(e), far(h))
    m_face, m_ends = kernel_call(
        fine_material,
        [vmem(HALO, 128, dtype=jnp.int32), vmem(2, 64, 128, dtype=jnp.int32)],
        [HBM, VM],
        [VM] * 2,
        [dma((3,))],
    )(far(m), held(edge_tile))
    edge_tile = across(edge_tile, dz=1)
    zmsg, ytile, columns = kernel_call(
        gather,
        [vmem(FACE + COLUMNS, 128), vmem(8, 128), vmem(COLUMNS, 128)],
        [VM] * 4,
        [VM] * 3,
    )(held(e), held(h), held(m_face), held(m_ends))
    ytile = kernel_call(
        join_z,
        vmem(8, 128),
        [VM] * 2,
        VM,
        cost=pl.CostEstimate(flops=10**10, bytes_accessed=10**8, transcendentals=0),
    )(held(ytile), held(edge_tile))
    zin = across(zmsg, dz=1)
    yin = across(ytile, dy=1)
    yzin = across(ytile, dy=1, dz=1)
    e_ext, h_ext, c_ext, up, down, up_part, down_part, c_planes = kernel_call(
        extend,
        [
            vmem(3, EXT, 128),
            vmem(3, EXT, 128),
            vmem(EXT, 128),
            vmem(96, 128),
            vmem(96, 128),
            vmem(MESSAGE, 128),
            vmem(MESSAGE, 128),
            vmem(64, 128),
        ],
        [VM] * 4 + [HBM, VM],
        [VM] * 8,
        [pltpu.SMEM((MATS,), F32), dma((1,))],
    )(held(e), held(h), held(m), held(zin), far(permittivity), held(columns))
    to_up, to_down = kernel_call(
        join_y,
        [vmem(MESSAGE, 128), vmem(MESSAGE, 128)],
        [VM] * 6,
        [VM] * 2,
    )(*(held(part) for part in (up_part, down_part, c_planes, yzin, columns, zin)))
    from_below = across(to_up, dx=1, dz=1)
    from_above = across(to_down, dx=-1, dz=1)
    whole = jax.ShapeDtypeStruct((3, ROWS, 128), F32)
    e_out, h_out, e_edge, h_edge, patched = kernel_call(
        advance,
        [whole, whole, vmem(2, 3, 64, 128), vmem(2, 3, 64, 128), vmem(32, 128)],
        [VM] * 8,
        [HBM, HBM, VM, VM, VM],
        [pltpu.VMEM((3, EXT, 128), F32)] * 3 + [pltpu.VMEM((2, 320, 128), F32), dma((2,))],
        cost=pl.CostEstimate(flops=10**10, bytes_accessed=10**8, transcendentals=0),
    )(*(held(part) for part in (e_ext, h_ext, c_ext, c_planes, yin, yzin, columns, zin)))
    e_out, h_out, _, _ = kernel_call(
        correct,
        [whole, whole, vmem(2, 3, 64, 128), vmem(2, 3, 64, 128)],
        [VM] * 8 + [HBM] * 2,
        [HBM] * 2 + [VM] * 2,
        [dma((4,))],
        aliases={8: 0, 9: 1, 6: 2, 7: 3},
    )(
        *(held(part) for part in (up, down, c_planes, patched, from_below, from_above, e_edge, h_edge)),
        e_out,
        h_out,
    )
    return e_out.reshape(electric.shape), h_out.reshape(magnetic.shape)


def solution(mesh):
    placed = (
        P(("parts", "gy"), "gx", "gz", None, None),
        P(("parts", "gy"), "gx", "gz", None, None),
        P(("parts", "gy"), "gx", "gz", None),
        P(),
    )
    fast = mesh.shape["gy"] == 2 and mesh.shape["gz"] == 2
    return jax.shard_map(
        fast_shards if fast else general_shards,
        mesh=mesh,
        in_specs=placed,
        out_specs=(
            P(("parts", "gy"), "gx", "gz", None, None),
            P(("parts", "gy"), "gx", "gz", None, None),
        ),
        check_vma=False,
    )
```

```python
from functools import partial

import jax
import jax.numpy as jnp
from jax import lax
from jax.experimental import pallas as pl
from jax.experimental.pallas import tpu as pltpu
from jax.sharding import PartitionSpec as P

CZ = 4
CX = 32
CY = 512
MATS = 4


courant = 0.5


def passed_along(x, axis, by):
    devices = lax.axis_size(axis)
    return lax.ppermute(x, axis, [(i, (i + by) % devices) for i in range(devices)])


def from_behind(x, axis, by):
    devices = lax.axis_size(axis)
    pairs = [(i, i + by) for i in range(devices) if 0 <= i + by < devices]
    return lax.ppermute(x, axis, pairs)


def forward_diff(values, dim_axis, ghost_plane):
    shifted = jnp.concatenate(
        [
            lax.slice_in_dim(values, 1, values.shape[dim_axis], axis=dim_axis),
            jnp.expand_dims(ghost_plane, dim_axis),
        ],
        axis=dim_axis,
    )
    return shifted - values


def backward_diff(values, dim_axis, ghost_plane):
    shifted = jnp.concatenate(
        [
            jnp.expand_dims(ghost_plane, dim_axis),
            lax.slice_in_dim(values, 0, values.shape[dim_axis] - 1, axis=dim_axis),
        ],
        axis=dim_axis,
    )
    return values - shifted


def curl_with(differ, vectors, ghost_depth, ghost_width, ghost_height):
    ghosts = (ghost_depth, ghost_width, ghost_height)

    def along_axis(component, dim_axis):
        return differ(vectors[component], dim_axis, ghosts[dim_axis][component])

    curl_x = along_axis(2, 2) - along_axis(1, 0)
    curl_y = along_axis(0, 0) - along_axis(2, 1)
    curl_z = along_axis(1, 1) - along_axis(0, 2)
    return jnp.stack([curl_x, curl_y, curl_z])


def restrict(face_plane):
    quads = face_plane.reshape(3, face_plane.shape[1] // 2, 2, face_plane.shape[2] // 2, 2)
    return (
        quads[:, :, 0, :, 0] + quads[:, :, 0, :, 1] + (quads[:, :, 1, :, 0] + quads[:, :, 1, :, 1])
    ) * 0.25


def enlarge(face_plane):
    return jnp.repeat(jnp.repeat(face_plane, 2, axis=1), 2, axis=2)


def lookup(material, permittivity):
    permit_sum = jnp.zeros(material.shape, jnp.float32)
    for material_id in range(MATS):
        permit_sum = permit_sum + jnp.where(material == material_id, permittivity[material_id], 0.0)
    return courant / permit_sum


def pack_face(face_plane, length):
    flat_face = face_plane.reshape(3, -1)
    if flat_face.shape[1] < length:
        flat_face = jnp.concatenate(
            [flat_face, jnp.zeros((3, length - flat_face.shape[1]), flat_face.dtype)], axis=1
        )
    return flat_face


def unpack_face(flat_face, row_count, col_count):
    return flat_face[:, : row_count * col_count].reshape(3, row_count, col_count)


def level_height(got_height, is_fine):
    return got_height if is_fine else restrict(got_height)


def low_faces(grid_shape, is_fine, flat_field):
    vectors = flat_field.reshape((3,) + grid_shape)
    face_plane = vectors[:, :, :, 0]
    if not is_fine:
        face_plane = enlarge(face_plane)
    return (
        pack_face(vectors[:, :, 0, :], CZ * CY),
        pack_face(vectors[:, 0, :, :], CX * CY),
        face_plane,
    )


def high_faces(grid_shape, is_fine, flat_field):
    vectors = flat_field.reshape((3,) + grid_shape)
    face_plane = vectors[:, :, :, -1]
    if not is_fine:
        face_plane = enlarge(face_plane)
    return (
        pack_face(vectors[:, :, -1, :], CZ * CY),
        pack_face(vectors[:, -1, :, :], CX * CY),
        face_plane,
    )


def advance_magnetic(
    grid_shape, is_fine, does_move, e_flat, h_flat, got_width, got_depth, got_height
):
    if not does_move:
        return h_flat
    deep_cells, wide_cells, tall_cells = grid_shape
    vectors = e_flat.reshape((3,) + grid_shape)
    curl_term = curl_with(
        forward_diff,
        vectors,
        unpack_face(got_depth, wide_cells, tall_cells),
        unpack_face(got_width, deep_cells, tall_cells),
        level_height(got_height, is_fine),
    )
    return (h_flat.reshape((3,) + grid_shape) - courant * curl_term).reshape(3, -1)


def advance_electric(
    grid_shape, is_fine, does_move, e_flat, h_flat, coefficient, got_width, got_depth, got_height
):
    if not does_move:
        return e_flat
    deep_cells, wide_cells, tall_cells = grid_shape
    magnetic = h_flat.reshape((3,) + grid_shape)
    curl_term = curl_with(
        backward_diff,
        magnetic,
        unpack_face(got_depth, wide_cells, tall_cells),
        unpack_face(got_width, deep_cells, tall_cells),
        level_height(got_height, is_fine),
    )
    return (
        e_flat.reshape((3,) + grid_shape) + coefficient.reshape(grid_shape) * curl_term
    ).reshape(3, -1)


def pass_width(face_plane, offset):
    return passed_along(face_plane, "gx", offset)


def pass_depth(face_plane, offset):
    return from_behind(face_plane, "gz", offset)


def pass_height(face_plane, offset):
    return from_behind(face_plane, "gy", offset)


def general_shards(electric, magnetic, material, permittivity):
    cell_count = electric.shape[-1]
    e_flat = electric.reshape(3, cell_count)
    h_flat = magnetic.reshape(3, cell_count)
    coefficient = lookup(material.reshape(cell_count), permittivity)
    is_fine = lax.axis_index("gy") >= lax.axis_size("gy") // 2
    coarse_shape = (CZ, CX, CY)
    fine_shape = (2 * CZ, 2 * CX, CY // 4)
    for substep in range(2):
        coarse_moves = substep == 0
        face_width, face_depth, face_height = lax.cond(
            is_fine,
            partial(low_faces, fine_shape, True),
            partial(low_faces, coarse_shape, False),
            e_flat,
        )
        got_depth = pass_depth(face_depth, -1)
        got_height = pass_height(face_height, -1)
        got_width = pass_width(face_width, -1)
        h_flat = lax.cond(
            is_fine,
            partial(advance_magnetic, fine_shape, True, True),
            partial(advance_magnetic, coarse_shape, False, coarse_moves),
            e_flat,
            h_flat,
            got_width,
            got_depth,
            got_height,
        )
        rim_width, rim_depth, rim_height = lax.cond(
            is_fine,
            partial(high_faces, fine_shape, True),
            partial(high_faces, coarse_shape, False),
            h_flat,
        )
        rim_depth = pass_depth(rim_depth, 1)
        rim_height = pass_height(rim_height, 1)
        rim_width = pass_width(rim_width, 1)
        e_flat = lax.cond(
            is_fine,
            partial(advance_electric, fine_shape, True, True),
            partial(advance_electric, coarse_shape, False, coarse_moves),
            e_flat,
            h_flat,
            coefficient,
            rim_width,
            rim_depth,
            rim_height,
        )
    return (e_flat.reshape(electric.shape), h_flat.reshape(magnetic.shape))


ROWS = 512
HALO = 128
EXT = 1296
LIMIT = 40 * 1024 * 1024
F32 = jnp.float32
VM = pl.BlockSpec(memory_space=pltpu.VMEM)
HBM = pl.BlockSpec(memory_space=pltpu.HBM)
CHUNK = 32
SKEW = 2


class Fine:
    depth, stride, count, own, step, parts, last = 64, 72, 10, 8, 1, 1, 63


class Coarse:
    depth, stride, count, own, step, parts, last = 128, 144, 5, 4, 4, 4, 31


def vmem(*shape, dtype=F32):
    return pltpu.VMEM(shape, dtype)


def held(x):
    return pltpu.with_memory_space_constraint(x, pltpu.VMEM)


def far(x):
    return pltpu.with_memory_space_constraint(x, pltpu.HBM)


def kernel_call(body, out_shape, in_specs, out_specs, scratch=(), aliases=None, cost=None):
    return pl.pallas_call(
        body,
        cost_estimate=cost,
        out_shape=out_shape,
        in_specs=in_specs,
        out_specs=out_specs,
        scratch_shapes=list(scratch),
        input_output_aliases=aliases or {},
        compiler_params=pltpu.CompilerParams(vmem_limit_bytes=LIMIT),
    )


def by_level(body):
    is_fine = lax.axis_index("gy") >= lax.axis_size("gy") // 2
    gz = lax.axis_index("gz")
    pl.when(is_fine)(lambda: body(Fine, gz))
    pl.when(jnp.logical_not(is_fine))(lambda: body(Coarse, gz))


def lanes_of(shape):
    return lax.broadcasted_iota(jnp.int32, shape, len(shape) - 1)


def rows_of(shape):
    return lax.broadcasted_iota(jnp.int32, shape, len(shape) - 2)


def roll_lanes(x, by):
    return pltpu.roll(x, by % 128, 1)


def roll_rows(x, by):
    return pltpu.roll(x, by % x.shape[0], 0)


def layer_row(grid, index):
    return pl.multiple_of(grid.stride * (index + 1), 8)


def own_first(grid, gz):
    return (grid.count - grid.own) * gz


def halo_first(grid, gz):
    return grid.own * (1 - gz)


def clear_pads(grid, ref, *zero_layers):
    for comp in range(3):
        for index in range(grid.count + 2):
            start, size = grid.stride * index, grid.stride
            if index not in zero_layers:
                start, size = start + grid.depth, size - grid.depth
            ref[comp, pl.ds(start, size), :] = jnp.zeros((size, 128), F32)


def own_layers(grid, ref, gz):
    view = ref.reshape(3, EXT // grid.stride, grid.stride, 128)
    return view.at[:, pl.ds(1 + own_first(grid, gz), grid.own), pl.ds(0, grid.depth), :]


def block_layers(grid, ref):
    return ref.reshape(3, grid.own, grid.depth, 128)


def at_lane(tile, lane_from, lane_to, value):
    lane = lanes_of(value.shape)
    return jnp.where(lane == lane_to, roll_lanes(value, lane_to - lane_from), tile)


def average(ref, lead, row, stride):
    steps = (0, 1, stride, stride + 1)
    quad = [ref[lead, pl.ds(row + step, 32, stride=2), :] for step in steps]
    return ((quad[0] + quad[1]) + (quad[2] + quad[3])) * 0.25


def put_column(tile, lane_from, slot, column):
    for block in range(4):
        tile = at_lane(tile, lane_from, 32 * block + slot, column[8 * block : 8 * block + 8])
    return tile


FINE_E = [(0, comp) for comp in range(3)] + [(1, 1), (1, 2)] + [(x, comp) for x in (62, 63) for comp in range(3)]
FINE_H = [(0, comp) for comp in range(3)] + [(62, 1), (62, 2)] + [(63, comp) for comp in range(3)]
FINE_M = [0, 1, 62, 63]
COARSE_E = [(0, 1), (0, 2)] + [(31, comp) for comp in range(3)]
COARSE_H = [(31, 1), (31, 2)]
COARSE_M = [0, 31]
COLUMNS = 192
R_ROW = COLUMNS - 8
NEAR = 64
FACE = 6 * HALO + NEAR


def wanted(grid):
    return (FINE_E, FINE_H, FINE_M) if grid is Fine else (COARSE_E, COARSE_H, COARSE_M)


def top_tile(tile, layer, ex, ey, ez, hx, hz):
    tile = put_column(tile, 127, layer, hx + 0.5 * ez)
    tile = put_column(tile, 127, 8 + layer, hz - 0.5 * ex)
    return put_column(tile, 127, 16 + layer, ey)


def edge_tiles(grid, ref):
    view = ref.reshape(grid.own, grid.depth, 128)
    return [view.at[:, pl.ds((grid.depth - 8) * end, 8), :] for end in range(2)]


def material_loads(grid, gz, m_hbm, m_face, m_ends, sems):
    face = pl.ds((1 - gz) * (ROWS - NEAR), NEAR)
    loads = [pltpu.make_async_copy(m_hbm.at[face], m_face, sems.at[0])]
    for end, tiles in enumerate(edge_tiles(grid, m_hbm)):
        place = m_ends.at[end].reshape(8, 8, 128).at[pl.ds(0, grid.own)]
        loads.append(pltpu.make_async_copy(tiles, place, sems.at[1 + end]))
    return loads


def peek(e_hbm, h_hbm, edge_tile, e_ends, h_ends, sems):
    def body(grid, gz):
        if grid is Fine:
            edge_tile[...] = jnp.zeros((8, 128), F32)
            return
        loads = []
        for end in range(2):
            rows = pl.ds((1 - gz) * (ROWS - HALO) + (HALO - 8) * end, 8)
            place = pl.ds(0, 8)
            loads.append(pltpu.make_async_copy(e_hbm.at[:, rows], e_ends.at[end, :, place], sems.at[2 * end]))
            for slot, comp in enumerate((0, 2)):
                into = h_ends.at[end, comp, place]
                loads.append(pltpu.make_async_copy(h_hbm.at[comp, rows], into, sems.at[4 + 2 * end + slot]))
        for load in loads:
            load.start()
        for load in loads:
            load.wait()
        tile = jnp.zeros((8, 128), F32)
        lane = lanes_of((8, 128))
        for end in range(2):
            rows = pl.ds(0 if end else 3, 8)
            ex, ey, ez = (e_ends[end, comp, rows, :] for comp in range(3))
            hx, hz = h_ends[end, 0, rows, :], h_ends[end, 2, rows, :]
            for kind, value in enumerate((hx + 0.5 * ez, hz - 0.5 * ex, ey)):
                to = 96 * end + 8 * kind + 3 + gz
                tile = jnp.where(lane == to, pltpu.roll(value, to + 1, 1), tile)
        edge_tile[...] = tile

    by_level(body)


def fine_material(m_hbm, after, m_face, m_ends, sems):
    def body(grid, gz):
        if grid is Coarse:
            return
        loads = material_loads(grid, gz, m_hbm, m_face, m_ends, sems)
        for load in loads:
            load.start()
        for load in loads:
            load.wait()

    by_level(body)


def gather(e_own, h_own, m_face, m_ends, zmsg, ytile, columns):
    def body(grid, gz):
        tile = jnp.zeros((8, 128), F32)
        for layer in range(4):
            if grid is Fine:
                row = 2 * grid.depth * layer
                tile = put_column(tile, 0, layer, average(e_own, 0, row, grid.depth))
                tile = put_column(tile, 0, 8 + layer, average(e_own, 2, row, grid.depth))
            else:
                top = pl.ds(grid.depth * layer + 3, 32, stride=4)
                ex, ey, ez = (e_own[comp, top, :] for comp in range(3))
                tile = top_tile(tile, layer, ex, ey, ez, h_own[0, top, :], h_own[2, top, :])
        tile = jnp.where(gz == 1, roll_lanes(tile, 4), tile)
        ytile[...] = tile
        columns[pl.ds(R_ROW, 8), :] = tile
        want_e, want_h, want_m = wanted(grid)
        slot = 0

        def column_rows(x, part):
            return pl.ds(grid.step * x + part, grid.own, stride=grid.depth)

        def put(value):
            nonlocal slot
            columns[pl.ds(slot, grid.own), :] = value
            slot += grid.own

        for x, comp in want_e:
            for part in range(grid.parts):
                put(e_own[comp, column_rows(x, part), :])
        for x, comp in want_h:
            for part in range(grid.parts):
                put(h_own[comp, column_rows(x, part), :])
        for x in want_m if grid is Fine else []:
            for part in range(grid.parts):
                rows = pl.ds(grid.step * x % 8 + part, grid.own, stride=8)
                put(m_ends[int(x > 1), rows, :].astype(F32))
        edge = pl.ds(pl.multiple_of((1 - gz) * (ROWS - HALO), HALO), HALO)
        for comp in range(3):
            zmsg[pl.ds(HALO * comp, HALO), :] = h_own[comp, edge, :]
            zmsg[pl.ds(HALO * (3 + comp), HALO), :] = e_own[comp, edge, :]
        if grid is Fine:
            zmsg[pl.ds(6 * HALO, NEAR), :] = m_face[...].astype(F32)
        zmsg[pl.ds(FACE, COLUMNS), :] = columns[...]

    by_level(body)


def join_z(ytile, edge_tile, joined):
    joined[...] = ytile[...] + edge_tile[...]


def up_y(grid, ref, comp, row, f):
    lane = lanes_of(f.shape)
    if grid is Fine:
        return jnp.where(lane == 127, 0.0, roll_lanes(f, -1))
    following = ref[comp, pl.ds(row + 1, f.shape[0]), :]
    following = jnp.where(rows_of(f.shape) % 4 == 3, 0.0, following)
    return roll_lanes(jnp.where(lane == 0, following, f), -1)


def down_y(grid, ref, comp, row, f, ghost):
    lane = lanes_of(f.shape)
    if grid is Fine:
        return roll_lanes(jnp.where(lane == 127, ghost, f), 1)
    previous = ref[comp, pl.ds(row - 1, f.shape[0]), :]
    previous = jnp.where(rows_of(f.shape) % 4 == 0, 0.0, previous)
    return roll_lanes(jnp.where(lane == 127, previous, f), 1)


def half_h(grid, e, h_from, from_row, h_to, row):
    for start in range(0, grid.depth, CHUNK):
        r = row + start
        here = pl.ds(r, CHUNK)
        ex, ey, ez = (e[comp, here, :] for comp in range(3))
        above, beside = pl.ds(r + grid.stride, CHUNK), pl.ds(r + grid.step, CHUNK)
        h0 = [h_from(comp, pl.ds(from_row + start, CHUNK)) for comp in range(3)]
        ez_y, ex_y = up_y(grid, e, 2, r, ez), up_y(grid, e, 0, r, ex)
        h_to[0, here, :] = h0[0] - 0.5 * ((ez_y - ez) - (e[1, above, :] - ey))
        h_to[1, here, :] = h0[1] - 0.5 * ((e[0, above, :] - ex) - (e[2, beside, :] - ez))
        h_to[2, here, :] = h0[2] - 0.5 * ((e[1, beside, :] - ey) - (ex_y - ex))


def half_e(grid, h, e_from, e_to, c_ref, row, ghosts):
    for start in range(0, grid.depth, CHUNK):
        r = row + start
        here = pl.ds(r, CHUNK)
        hx, hy, hz = (h[comp, here, :] for comp in range(3))
        below, beside = pl.ds(r - grid.stride, CHUNK), pl.ds(r - grid.step, CHUNK)
        px, pz = ghosts(start)
        hx_y, hz_y = down_y(grid, h, 0, r, hx, px), down_y(grid, h, 2, r, hz, pz)
        c = c_ref[here, :]
        e_to[0, here, :] = e_from[0, here, :] + c * ((hz - hz_y) - (hy - h[1, below, :]))
        e_to[1, here, :] = e_from[1, here, :] + c * ((hx - h[0, below, :]) - (hz - h[2, beside, :]))
        e_to[2, here, :] = e_from[2, here, :] + c * ((hy - h[1, beside, :]) - (hx - hx_y))


def column_of(tile, block, sub, slot, grid):
    shape = (2 * grid.own, 128)
    row = jnp.broadcast_to(tile[sub : sub + 1, :], shape)
    lane = 32 * block + slot + rows_of(shape) // (2 * grid.own // 8)
    picked = jnp.where(lanes_of(shape) == lane, row, 0.0)
    return jnp.broadcast_to(jnp.sum(picked, axis=1, keepdims=True), shape)


def each(fn, *columns):
    return [fn(*parts) for parts in zip(*columns, strict=True)]


def plus_y(f, ghost=0.0):
    following = f[1:] + [ghost]
    return [
        roll_lanes(jnp.where(lanes_of(p.shape) == 0, nxt, p), -1) - p
        for p, nxt in zip(f, following, strict=True)
    ]


def minus_y(f, ghost=0.0):
    previous = [ghost] + f[:-1]
    return [
        p - roll_lanes(jnp.where(lanes_of(p.shape) == 127, prv, p), 1)
        for p, prv in zip(f, previous, strict=True)
    ]


def plus_z(f):
    return [
        jnp.where(rows_of(p.shape) == p.shape[0] - 1, 0.0, roll_rows(p, -1)) - p for p in f
    ]


def minus_z(f):
    return [p - jnp.where(rows_of(p.shape) == 0, 0.0, roll_rows(p, 1)) for p in f]


def add(a, b):
    return each(lambda p, q: p + q, a, b)


def sub(a, b):
    return each(lambda p, q: p - q, a, b)


def mul(a, b):
    return each(lambda p, q: p * q, a, b)


def scale(by, a):
    return [by * p for p in a]


def read_columns(grid, own, other, gz):
    want_e, want_h, want_m = wanted(grid)
    found, slot = [], 0
    for _ in range(len(want_e) + len(want_h) + len(want_m)):
        col = []
        for _ in range(grid.parts):
            rows = pl.ds(slot, grid.own)
            mine, theirs = own[rows, :], other[pl.ds(FACE + slot, grid.own), :]
            low, high = jnp.where(gz == 0, mine, theirs), jnp.where(gz == 0, theirs, mine)
            col.append(jnp.concatenate([low, high], axis=0))
            slot += grid.own
        found.append(col)
    e_found, found = found[: len(want_e)], found[len(want_e) :]
    h_found, m_found = found[: len(want_h)], found[len(want_h) :]
    return (
        dict(zip(want_e, e_found, strict=True)),
        dict(zip(want_h, h_found, strict=True)),
        dict(zip(want_m, m_found, strict=True)),
    )


def write_planes(ref, columns):
    row = 0
    for col in columns:
        for p in col:
            ref[pl.ds(row, p.shape[0]), :] = p
            row += p.shape[0]


def read_planes(grid, ref, *indices):
    height, parts = 2 * grid.own, grid.parts
    return [
        [ref[pl.ds(height * (parts * i + part), height), :] for part in range(parts)] for i in indices
    ]


MESSAGE = 48
UP = {Fine: [(9, 7)] * 5, Coarse: [(4, 4)] * 2}
DOWN = {Fine: [(10, 6)] + [(9, 7)] * 4, Coarse: [(5, 3)] * 2}


def sent_rows(plane, entry, gz):
    count, begin = entry
    return jnp.where(gz == 0, roll_rows(plane, -begin), plane)[:count]


def places(grid, entries):
    row = 0
    for entry in entries:
        for _ in range(grid.parts):
            yield row, entry
            row += entry[0]


def write_message(grid, ref, entries, columns, gz):
    planes = [p for col in columns for p in col]
    for (row, entry), p in zip(places(grid, entries), planes, strict=True):
        ref[pl.ds(row, entry[0]), :] = sent_rows(p, entry, gz)


def read_message(grid, ref, entries, gz):
    height, planes = 2 * grid.own, []
    for row, (_, begin) in places(grid, entries):
        start = min(row, MESSAGE - height)
        p = ref[pl.ds(start, height), :]
        planes.append(pltpu.roll(p, height + start - row + begin * gz, 0))
    return [planes[i : i + grid.parts] for i in range(0, len(planes), grid.parts)]


def extend(
    e_own,
    h_own,
    m_own,
    zmsg,
    permittivity,
    columns,
    e_ext,
    h_ext,
    c_ext,
    up,
    down,
    to_up,
    to_down,
    c_planes,
    table,
    sems,
):
    def body(grid, gz):
        load = pltpu.make_async_copy(permittivity, table, sems.at[0])
        load.start()
        clear_pads(grid, h_ext, 0)
        clear_pads(grid, e_ext, grid.count + 1)
        for layer in range(grid.own):
            for start in range(0, grid.depth, CHUNK):
                rows = pl.ds(layer_row(grid, own_first(grid, gz) + layer) + start, CHUNK)
                from_rows = pl.ds(grid.depth * layer + start, CHUNK)
                for comp in range(3):
                    e_ext[comp, rows, :] = e_own[comp, from_rows, :]
        halo = halo_first(grid, gz)
        for layer in range(grid.count - grid.own):
            for start in range(0, grid.depth, CHUNK):
                rows = pl.ds(layer_row(grid, halo + layer) + start, CHUNK)
                for comp in range(3):
                    from_rows = pl.ds(HALO * (3 + comp) + grid.depth * layer + start, CHUNK)
                    e_ext[comp, rows, :] = zmsg[from_rows, :]

        def h_halo(comp, rows):
            return zmsg[pl.ds(HALO * comp + rows.start, rows.size), :]

        for layer in range(grid.count - grid.own):
            row = layer_row(grid, halo + layer)
            half_h(grid, e_ext, h_halo, grid.depth * layer, h_ext, row)
        for layer in range(grid.own):
            row = layer_row(grid, own_first(grid, gz) + layer)
            half_h(grid, e_ext, lambda comp, rows: h_own[comp, rows, :], grid.depth * layer, h_ext, row)
        load.wait()
        values = [0.5 / jnp.full((8, 128), table[i], F32) for i in range(MATS)]

        def coef(is_material, rows):
            parts = [jnp.concatenate([value] * (rows // 8), axis=0) for value in values]
            found = parts[MATS - 1]
            for i in range(MATS - 2, -1, -1):
                found = jnp.where(is_material(i), parts[i], found)
            return found

        for start in range(0, NEAR if grid is Fine else 0, CHUNK):
            material = zmsg[pl.ds(6 * HALO + start, CHUNK), :]
            row = layer_row(grid, halo + gz) + start
            c_ext[pl.ds(row, CHUNK), :] = coef(lambda i, m=material: m == float(i), CHUNK)
        for start in range(0, ROWS, CHUNK):
            layer, rest = divmod(start, grid.depth)
            material = m_own[pl.ds(start, CHUNK), :]
            row = layer_row(grid, own_first(grid, gz) + layer) + rest
            c_ext[pl.ds(row, CHUNK), :] = coef(lambda i, m=material: m == i, CHUNK)

        e, h, m = read_columns(grid, columns, zmsg, gz)
        if grid is Coarse:
            for x in m:
                rows = [pl.ds(4 * x + part, 4, stride=grid.depth) for part in range(4)]
                own = [m_own[part, :].astype(F32) for part in rows]
                m[x] = [jnp.concatenate([part, part], axis=0) for part in own]
        c = {
            x: [coef(lambda i, q=part: q == float(i), part.shape[0]) for part in col] for x, col in m.items()
        }
        write_planes(c_planes, list(c.values()))
        if grid is Coarse:
            ex, ey, ez = (e[31, comp] for comp in range(3))
            hy = sub(h[31, 1], scale(0.5, add(plus_z(ex), ez)))
            hz = add(h[31, 2], scale(0.5, add(ey, plus_y(ex))))
            sent_up, sent_down = [hy, hz], [e[0, 2], e[0, 1]]
        else:
            ex, ey, ez = (e[0, comp] for comp in range(3))
            hx = sub(h[0, 0], scale(0.5, sub(plus_y(ez), plus_z(ey))))
            hy = sub(h[0, 1], scale(0.5, sub(plus_z(ex), sub(e[1, 2], ez))))
            hz = sub(h[0, 2], scale(0.5, sub(sub(e[1, 1], ey), plus_y(ex))))
            ey_next = add(ey, mul(c[0], sub(minus_z(hx), hz)))
            ez_next = add(ez, mul(c[0], sub(hy, minus_y(hx))))
            sent_down = [ez, ey, ey_next, ez_next, c[0]]
            ex, ey, ez = (e[62, comp] for comp in range(3))
            hy62 = sub(h[62, 1], scale(0.5, sub(plus_z(ex), sub(e[63, 2], ez))))
            hz62 = sub(h[62, 2], scale(0.5, sub(sub(e[63, 1], ey), plus_y(ex))))
            ex, ey, ez = (e[63, comp] for comp in range(3))
            hx = sub(h[63, 0], scale(0.5, sub(plus_y(ez), plus_z(ey))))
            hy = sub(h[63, 1], scale(0.5, add(plus_z(ex), ez)))
            hz = add(h[63, 2], scale(0.5, add(ey, plus_y(ex))))
            ex_next = add(ex, mul(c[63], sub(minus_y(hz), minus_z(hy))))
            ey_next = add(ey, mul(c[63], sub(minus_z(hx), sub(hz, hz62))))
            ez_next = add(ez, mul(c[63], sub(sub(hy, hy62), minus_y(hx))))
            next_y = sub(hy, scale(0.5, add(plus_z(ex_next), ez_next)))
            next_z = add(hz, scale(0.5, add(ey_next, plus_y(ex_next))))
            sent_up = [hy, hz, next_y, next_z, c[63]]
        write_planes(up, sent_up)
        write_planes(down, sent_down)
        write_message(grid, to_up, UP[grid], sent_up, gz)
        write_message(grid, to_down, DOWN[grid], sent_down, gz)

    by_level(body)


def between(top, r):
    lane, row = lanes_of(top.shape), rows_of(top.shape)
    kind = (lane % 32) // 8
    above = jnp.where(lane % 8 == 7, 0.0, roll_lanes(top, -1))
    px = top - 0.5 * roll_lanes(r, -8) + 0.5 * roll_lanes(above - top, -16)
    beside = roll_rows(top, -1)
    beside = jnp.where(row == 7, jnp.where(lane >= 96, 0.0, roll_lanes(beside, -32)), beside)
    pz = top + 0.5 * roll_lanes(r, 8) - 0.5 * roll_lanes(beside - top, -8)
    return jnp.where(kind == 0, px, jnp.where(kind == 1, pz, 0.0))


def join_y(up_in, down_in, c_planes, yzin, r_own, r_other, to_up, to_down):
    def body(grid, gz):
        def patch(ref, entries, index, value):
            row, entry = list(places(grid, entries))[index]
            rows = pl.ds(row, entry[0])
            ref[rows, :] = ref[rows, :] + sent_rows(value, entry, gz)

        top = yzin[...]
        to_up[...] = up_in[...]
        to_down[...] = down_in[...]
        shape = (2 * grid.own, 128)
        if grid is Coarse:
            change = jnp.where(lanes_of(shape) == 127, 0.5 * column_of(top, 3, 7, 0, grid), 0.0)
            patch(to_up, UP[grid], 7, change)
            return
        plane = between(top, r_own[pl.ds(R_ROW, 8), :] + r_other[pl.ds(FACE + R_ROW, 8), :])
        bottom = lanes_of(shape) == 0
        (c0,), (c63,) = read_planes(grid, c_planes, 0, 3)

        patch(to_down, DOWN[grid], 3, jnp.where(bottom, c0 * column_of(plane, 0, 0, 0, grid), 0.0))
        ez_change = jnp.where(bottom, c63 * column_of(plane, 3, 7, 0, grid), 0.0)
        ex_change = jnp.where(bottom, -c63 * column_of(plane, 3, 7, 8, grid), 0.0)
        patch(to_up, UP[grid], 2, -0.5 * (plus_z([ex_change])[0] + ez_change))
        patch(to_up, UP[grid], 3, -0.5 * ex_change)
        to_down[pl.ds(MESSAGE - 1, 1), :] = top[:1]

    by_level(body)


def advance(
    e_ext,
    h_ext,
    c_ext,
    c_planes,
    yin,
    yzin,
    r_own,
    r_other,
    e_out,
    h_out,
    e_edge,
    h_edge,
    patched,
    e_mid,
    h_mid,
    e_last,
    plane,
    sems,
):
    def body(grid, gz):
        first = own_first(grid, gz)
        upper = lanes_of((8, 128)) % 8 >= 4
        tile = jnp.where(upper == (gz == 0), yzin[...], yin[...])
        if grid is Fine:
            top = tile
            tile = between(top, r_own[pl.ds(R_ROW, 8), :] + r_other[pl.ds(FACE + R_ROW, 8), :])
            ((c0,),) = read_planes(grid, c_planes, 0)
            change = jnp.where(lanes_of((16, 128)) == 0, c0 * column_of(tile, 0, 0, 0, grid), 0.0)
            patched[pl.ds(0, 16), :] = change
            patched[pl.ds(16, 16), :] = column_of(top, 0, 0, 16, grid)
        tile = jnp.where(gz == 0, tile, roll_lanes(tile, -3))

        def write(source, target, sem, layer=None):
            source, target = own_layers(grid, source, gz), block_layers(grid, target)
            if layer is not None:
                source, target = source.at[:, layer], target.at[:, layer]
            return pltpu.make_async_copy(source, target, sem)

        def keep_edges(source, target):
            for comp in range(3):
                for layer in range(grid.own):
                    for edge in range(2):
                        row = layer_row(grid, first + layer) + (grid.depth - 8) * edge
                        target[edge, comp, pl.ds(8 * layer, 8), :] = source[comp, pl.ds(row, 8), :]

        clear_pads(grid, h_mid, 0)
        if grid is Fine:
            clear_pads(grid, e_mid, grid.count + 1)
            for kind in range(2):
                for layer in range(5):
                    for block in range(4):
                        value = roll_lanes(tile, 127 - (32 * block + 8 * kind + layer))
                        for step in range(2):
                            rows = pl.ds(64 * layer + 16 * block + step, 8, stride=2)
                            plane[kind, rows, :] = value

            def ghosts(index):
                begin = 64 * (index // 2)

                def of(start):
                    rows = pl.ds(pl.multiple_of(begin + start, 8), CHUNK)
                    return plane[0, rows, :], plane[1, rows, :]

                return of

            def own_write(source, target, sem, layer):
                def start():
                    rows = pl.ds(layer_row(grid, layer), grid.depth)
                    to = block_layers(grid, target).at[:, layer - first]
                    pltpu.make_async_copy(source.at[:, rows], to, sem).start()

                if 2 <= layer < 8:
                    start()
                else:
                    pl.when((layer < 8) == (gz == 0))(start)

            def h1(comp, rows):
                return h_ext[comp, rows, :]

            for step in range(grid.count + 2 * SKEW):
                if step < grid.count:
                    half_e(grid, h_ext, e_ext, e_mid, c_ext, grid.stride * (step + 1), ghosts(step))
                layer = step - SKEW
                if 0 <= layer < grid.count:
                    row = grid.stride * (layer + 1)
                    half_h(grid, e_mid, h1, row, h_mid, row)
                    own_write(h_mid, h_out, sems.at[0], layer)
                layer = step - 2 * SKEW
                if 0 <= layer < grid.count:
                    row = grid.stride * (layer + 1)
                    half_e(grid, h_mid, e_mid, e_last, c_ext, row, ghosts(layer))
                    own_write(e_last, e_out, sems.at[1], layer)
        else:
            for comp in range(3):
                for layer in range(grid.count):
                    rows = pl.ds(layer_row(grid, layer), grid.depth)
                    h_mid[comp, rows, :] = h_ext[comp, rows, :]
            lane = lanes_of((8, 128))
            for layer in range(grid.count):
                for block in range(4):
                    rows = pl.ds(layer_row(grid, layer) + 32 * block + 3, 8, stride=4)
                    rx = roll_lanes(tile, 127 - (32 * block + layer))
                    rz = roll_lanes(tile, 127 - (32 * block + 8 + layer))
                    h_mid[0, rows, :] = h_mid[0, rows, :] - jnp.where(lane == 127, 0.5 * rz, 0.0)
                    h_mid[2, rows, :] = h_mid[2, rows, :] + jnp.where(lane == 127, 0.5 * rx, 0.0)
            write(h_mid, h_out, sems.at[0]).start()
            for layer in range(grid.own):
                row = layer_row(grid, first + layer)
                half_e(grid, h_mid, e_ext, e_last, c_ext, row, lambda start: (0.0, 0.0))
                write(e_last, e_out, sems.at[1], layer).start()
        keep_edges(h_mid, h_edge)
        keep_edges(e_last, e_edge)
        write(h_mid, h_out, sems.at[0]).wait()
        write(e_last, e_out, sems.at[1]).wait()

    by_level(body)


def correct(
    up,
    down,
    c_planes,
    patched,
    from_below,
    from_above,
    e_edge,
    h_edge,
    e_in,
    h_in,
    e_out,
    h_out,
    e_tile,
    h_tile,
    sems,
):
    def body(grid, gz):
        last = grid.last

        def put(ref, edge, comp, x, change):
            for part, p in enumerate(change):
                own = jnp.where(gz == 0, p[: grid.own], p[grid.own :])
                rows = pl.ds(grid.step * x % 8 + part, grid.own, stride=8)
                ref[edge, comp, rows, :] = ref[edge, comp, rows, :] + own

        def finish(edge):
            copies = []
            for slot, (tile, out) in enumerate(((h_tile, h_out), (e_tile, e_out))):
                if grid is Coarse and edge == 0 and slot == 0:
                    continue
                source = tile.at[edge].reshape(3, 8, 8, 128).at[:, pl.ds(0, grid.own)]
                target = block_layers(grid, out).at[:, :, pl.ds((grid.depth - 8) * edge, 8), :]
                copies.append(pltpu.make_async_copy(source, target, sems.at[2 * edge + slot]))
            for copy in copies:
                copy.start()
            return copies

        if grid is Fine:
            zero = [jnp.zeros((16, 128), F32)]
            ez64, ey64, ey64_part, ez64_part, c64 = read_message(grid, from_above, DOWN[grid], gz)
            ey_above = column_of(from_above[pl.ds(MESSAGE - 8, 8), :], 0, 7, 16, grid)
            hy63, hz63 = read_planes(grid, up, 0, 1)
            c0, c1, c62, c63 = read_planes(grid, c_planes, *range(4))
            hy_part, hz_part, next_y, next_z, cm = read_message(grid, from_below, UP[grid], gz)
            ez0, ey0, ey0_part, ez0_part = read_planes(grid, down, *range(4))
            ez0_change, ey_top = read_planes(grid, patched, 0, 1)
            ez0_part = add(ez0_part, ez0_change)
            ghost = -0.5 * ey_top[0]
            dhy, dhz = scale(0.5, ez0), scale(-0.5, ey0)
            hym, hzm = add(hy_part, dhy), add(hz_part, dhz)
            dexm = mul(cm, sub(minus_y(dhz, ghost), minus_z(dhy)))
            dey, dez = mul(c0, hzm), scale(-1.0, mul(c0, hym))
            dhx2 = scale(-0.5, sub(plus_y(dez), plus_z(dey)))
            dhy2 = scale(-0.5, dez)
            dhz2 = scale(0.5, dey)
            change = sub(sub(add(ez0_part, dez), plus_z(dexm)), mul(cm, dhy))
            hym2 = add(add(next_y, dhy), scale(0.5, change))
            change = sub(sub(plus_y(dexm), add(ey0_part, dey)), mul(cm, dhz))
            hzm2 = add(add(next_z, dhz), scale(0.5, change))
            put(h_tile, 0, 0, 0, dhx2)
            put(h_tile, 0, 1, 0, dhy2)
            put(h_tile, 0, 2, 0, dhz2)
            put(e_tile, 0, 0, 0, mul(c0, sub(minus_y(dhz2), minus_z(dhy2))))
            put(e_tile, 0, 1, 0, add(dey, mul(c0, sub(minus_z(dhx2), sub(dhz2, hzm2)))))
            put(e_tile, 0, 2, 0, add(dez, mul(c0, sub(sub(dhy2, hym2), minus_y(dhx2)))))
            put(e_tile, 0, 1, 1, mul(c1, dhz2))
            put(e_tile, 0, 2, 1, scale(-1.0, mul(c1, dhy2)))
            copies = finish(0)

            ghost = -0.5 * ey_above
            dhy, dhz = scale(0.5, ez64), scale(-0.5, ey64)
            dex = mul(c63, sub(minus_y(dhz, ghost), minus_z(dhy)))
            dey = scale(-1.0, mul(c63, dhz))
            dez = mul(c63, dhy)
            dex62 = mul(c62, minus_y(zero, ghost))
            ey64_next = add(ey64_part, mul(c64, add(hz63, dhz)))
            ez64_next = sub(ez64_part, mul(c64, add(hy63, dhy)))
            dhx2 = scale(-0.5, sub(plus_y(dez), plus_z(dey)))
            dhy2 = add(dhy, scale(-0.5, sub(plus_z(dex), sub(ez64_next, dez))))
            dhz2 = add(dhz, scale(-0.5, sub(sub(ey64_next, dey), plus_y(dex))))
            dhy62 = scale(-0.5, sub(plus_z(dex62), dez))
            dhz62 = scale(-0.5, sub(dey, plus_y(dex62)))
            put(h_tile, 1, 0, 63, dhx2)
            put(h_tile, 1, 1, 63, dhy2)
            put(h_tile, 1, 2, 63, dhz2)
            put(h_tile, 1, 1, 62, dhy62)
            put(h_tile, 1, 2, 62, dhz62)
            put(e_tile, 1, 0, 63, add(dex, mul(c63, sub(minus_y(dhz2, ghost), minus_z(dhy2)))))
            put(e_tile, 1, 1, 63, add(dey, mul(c63, sub(minus_z(dhx2), sub(dhz2, dhz62)))))
            put(e_tile, 1, 2, 63, add(dez, mul(c63, sub(sub(dhy2, dhy62), minus_y(dhx2)))))
            put(e_tile, 1, 0, 62, add(dex62, mul(c62, sub(minus_y(dhz62, ghost), minus_z(dhy62)))))
            put(e_tile, 1, 1, 62, scale(-1.0, mul(c62, dhz62)))
            put(e_tile, 1, 2, 62, mul(c62, dhy62))
            copies += finish(1)
        else:
            ez32, ey32 = read_message(grid, from_above, DOWN[grid], gz)
            c0, c31 = read_planes(grid, c_planes, 0, 1)
            dhy, dhz = scale(0.5, ez32), scale(-0.5, ey32)
            put(h_tile, 1, 1, last, dhy)
            put(h_tile, 1, 2, last, dhz)
            put(e_tile, 1, 0, last, mul(c31, sub(minus_y(dhz), minus_z(dhy))))
            put(e_tile, 1, 1, last, scale(-1.0, mul(c31, dhz)))
            put(e_tile, 1, 2, last, mul(c31, dhy))
            copies = finish(1)
            hy_part, hz_part = read_message(grid, from_below, UP[grid], gz)
            ez0, ey0 = read_planes(grid, down, 0, 1)
            put(e_tile, 0, 1, 0, mul(c0, add(hz_part, scale(-0.5, ey0))))
            put(e_tile, 0, 2, 0, scale(-1.0, mul(c0, add(hy_part, scale(0.5, ez0)))))
            copies += finish(0)
        for copy in copies:
            copy.wait()

    by_level(body)


def across(x, dx=0, dy=0, dz=0):
    nx, ny, nz = lax.axis_size("gx"), lax.axis_size("gy"), lax.axis_size("gz")
    pairs = [
        ((i * ny + j) * nz + k, ((i + dx) % nx * ny + (j + dy) % ny) * nz + (k + dz) % nz)
        for i in range(nx)
        for j in range(ny)
        for k in range(nz)
    ]
    return lax.ppermute(x, ("gx", "gy", "gz"), pairs)


def fast_shards(electric, magnetic, material, permittivity):
    e = electric.reshape(3, ROWS, 128)
    h = magnetic.reshape(3, ROWS, 128)
    m = material.reshape(ROWS, 128)
    dma = pltpu.SemaphoreType.DMA
    edge_tile = kernel_call(
        peek,
        vmem(8, 128),
        [HBM] * 2,
        VM,
        [pltpu.VMEM((2, 3, 16, 128), F32)] * 2 + [dma((8,))],
    )(far(e), far(h))
    m_face, m_ends = kernel_call(
        fine_material,
        [vmem(NEAR, 128, dtype=jnp.int32), vmem(2, 64, 128, dtype=jnp.int32)],
        [HBM, VM],
        [VM] * 2,
        [dma((3,))],
    )(far(m), held(edge_tile))
    edge_tile = across(edge_tile, dz=1)
    zmsg, ytile, columns = kernel_call(
        gather,
        [vmem(FACE + COLUMNS, 128), vmem(8, 128), vmem(COLUMNS, 128)],
        [VM] * 4,
        [VM] * 3,
    )(held(e), held(h), held(m_face), held(m_ends))
    ytile = kernel_call(
        join_z,
        vmem(8, 128),
        [VM] * 2,
        VM,
        cost=pl.CostEstimate(flops=10**10, bytes_accessed=10**8, transcendentals=0),
    )(held(ytile), held(edge_tile))
    zin = across(zmsg, dz=1)
    yin = across(ytile, dy=1)
    yzin = across(ytile, dy=1, dz=1)
    e_ext, h_ext, c_ext, up, down, up_part, down_part, c_planes = kernel_call(
        extend,
        [
            vmem(3, EXT, 128),
            vmem(3, EXT, 128),
            vmem(EXT, 128),
            vmem(96, 128),
            vmem(96, 128),
            vmem(MESSAGE, 128),
            vmem(MESSAGE, 128),
            vmem(64, 128),
        ],
        [VM] * 4 + [HBM, VM],
        [VM] * 8,
        [pltpu.SMEM((MATS,), F32), dma((1,))],
    )(held(e), held(h), held(m), held(zin), far(permittivity), held(columns))
    to_up, to_down = kernel_call(
        join_y,
        [vmem(MESSAGE, 128), vmem(MESSAGE, 128)],
        [VM] * 6,
        [VM] * 2,
    )(*(held(part) for part in (up_part, down_part, c_planes, yzin, columns, zin)))
    from_below = across(to_up, dx=1, dz=1)
    from_above = across(to_down, dx=-1, dz=1)
    whole = jax.ShapeDtypeStruct((3, ROWS, 128), F32)
    e_out, h_out, e_edge, h_edge, patched = kernel_call(
        advance,
        [whole, whole, vmem(2, 3, 64, 128), vmem(2, 3, 64, 128), vmem(32, 128)],
        [VM] * 8,
        [HBM, HBM, VM, VM, VM],
        [pltpu.VMEM((3, EXT, 128), F32)] * 3 + [pltpu.VMEM((2, 320, 128), F32), dma((2,))],
        cost=pl.CostEstimate(flops=10**10, bytes_accessed=10**8, transcendentals=0),
    )(*(held(part) for part in (e_ext, h_ext, c_ext, c_planes, yin, yzin, columns, zin)))
    e_out, h_out, _, _ = kernel_call(
        correct,
        [whole, whole, vmem(2, 3, 64, 128), vmem(2, 3, 64, 128)],
        [VM] * 8 + [HBM] * 2,
        [HBM] * 2 + [VM] * 2,
        [dma((4,))],
        aliases={8: 0, 9: 1, 6: 2, 7: 3},
    )(
        *(held(part) for part in (up, down, c_planes, patched, from_below, from_above, e_edge, h_edge)),
        e_out,
        h_out,
    )
    return e_out.reshape(electric.shape), h_out.reshape(magnetic.shape)


def solution(mesh):
    placed = (
        P(("parts", "gy"), "gx", "gz", None, None),
        P(("parts", "gy"), "gx", "gz", None, None),
        P(("parts", "gy"), "gx", "gz", None),
        P(),
    )
    fast = mesh.shape["gy"] == 2 and mesh.shape["gz"] == 2
    return jax.shard_map(
        fast_shards if fast else general_shards,
        mesh=mesh,
        in_specs=placed,
        out_specs=(
            P(("parts", "gy"), "gx", "gz", None, None),
            P(("parts", "gy"), "gx", "gz", None, None),
        ),
        check_vma=False,
    )
```

```python
from functools import partial

import jax
import jax.numpy as jnp
from jax import lax
from jax.experimental import pallas as pl
from jax.experimental.pallas import tpu as pltpu
from jax.sharding import PartitionSpec as P

CZ = 4
CX = 32
CY = 512
MATS = 4


courant = 0.5


def passed_along(x, axis, by):
    devices = lax.axis_size(axis)
    return lax.ppermute(x, axis, [(i, (i + by) % devices) for i in range(devices)])


def from_behind(x, axis, by):
    devices = lax.axis_size(axis)
    pairs = [(i, i + by) for i in range(devices) if 0 <= i + by < devices]
    return lax.ppermute(x, axis, pairs)


def forward_diff(values, dim_axis, ghost_plane):
    shifted = jnp.concatenate(
        [
            lax.slice_in_dim(values, 1, values.shape[dim_axis], axis=dim_axis),
            jnp.expand_dims(ghost_plane, dim_axis),
        ],
        axis=dim_axis,
    )
    return shifted - values


def backward_diff(values, dim_axis, ghost_plane):
    shifted = jnp.concatenate(
        [
            jnp.expand_dims(ghost_plane, dim_axis),
            lax.slice_in_dim(values, 0, values.shape[dim_axis] - 1, axis=dim_axis),
        ],
        axis=dim_axis,
    )
    return values - shifted


def curl_with(differ, vectors, ghost_depth, ghost_width, ghost_height):
    ghosts = (ghost_depth, ghost_width, ghost_height)

    def along_axis(component, dim_axis):
        return differ(vectors[component], dim_axis, ghosts[dim_axis][component])

    curl_x = along_axis(2, 2) - along_axis(1, 0)
    curl_y = along_axis(0, 0) - along_axis(2, 1)
    curl_z = along_axis(1, 1) - along_axis(0, 2)
    return jnp.stack([curl_x, curl_y, curl_z])


def restrict(face_plane):
    quads = face_plane.reshape(3, face_plane.shape[1] // 2, 2, face_plane.shape[2] // 2, 2)
    return (
        quads[:, :, 0, :, 0] + quads[:, :, 0, :, 1] + (quads[:, :, 1, :, 0] + quads[:, :, 1, :, 1])
    ) * 0.25


def enlarge(face_plane):
    return jnp.repeat(jnp.repeat(face_plane, 2, axis=1), 2, axis=2)


def lookup(material, permittivity):
    permit_sum = jnp.zeros(material.shape, jnp.float32)
    for material_id in range(MATS):
        permit_sum = permit_sum + jnp.where(material == material_id, permittivity[material_id], 0.0)
    return courant / permit_sum


def pack_face(face_plane, length):
    flat_face = face_plane.reshape(3, -1)
    if flat_face.shape[1] < length:
        flat_face = jnp.concatenate(
            [flat_face, jnp.zeros((3, length - flat_face.shape[1]), flat_face.dtype)], axis=1
        )
    return flat_face


def unpack_face(flat_face, row_count, col_count):
    return flat_face[:, : row_count * col_count].reshape(3, row_count, col_count)


def level_height(got_height, is_fine):
    return got_height if is_fine else restrict(got_height)


def low_faces(grid_shape, is_fine, flat_field):
    vectors = flat_field.reshape((3,) + grid_shape)
    face_plane = vectors[:, :, :, 0]
    if not is_fine:
        face_plane = enlarge(face_plane)
    return (
        pack_face(vectors[:, :, 0, :], CZ * CY),
        pack_face(vectors[:, 0, :, :], CX * CY),
        face_plane,
    )


def high_faces(grid_shape, is_fine, flat_field):
    vectors = flat_field.reshape((3,) + grid_shape)
    face_plane = vectors[:, :, :, -1]
    if not is_fine:
        face_plane = enlarge(face_plane)
    return (
        pack_face(vectors[:, :, -1, :], CZ * CY),
        pack_face(vectors[:, -1, :, :], CX * CY),
        face_plane,
    )


def advance_magnetic(
    grid_shape, is_fine, does_move, e_flat, h_flat, got_width, got_depth, got_height
):
    if not does_move:
        return h_flat
    deep_cells, wide_cells, tall_cells = grid_shape
    vectors = e_flat.reshape((3,) + grid_shape)
    curl_term = curl_with(
        forward_diff,
        vectors,
        unpack_face(got_depth, wide_cells, tall_cells),
        unpack_face(got_width, deep_cells, tall_cells),
        level_height(got_height, is_fine),
    )
    return (h_flat.reshape((3,) + grid_shape) - courant * curl_term).reshape(3, -1)


def advance_electric(
    grid_shape, is_fine, does_move, e_flat, h_flat, coefficient, got_width, got_depth, got_height
):
    if not does_move:
        return e_flat
    deep_cells, wide_cells, tall_cells = grid_shape
    magnetic = h_flat.reshape((3,) + grid_shape)
    curl_term = curl_with(
        backward_diff,
        magnetic,
        unpack_face(got_depth, wide_cells, tall_cells),
        unpack_face(got_width, deep_cells, tall_cells),
        level_height(got_height, is_fine),
    )
    return (
        e_flat.reshape((3,) + grid_shape) + coefficient.reshape(grid_shape) * curl_term
    ).reshape(3, -1)


def pass_width(face_plane, offset):
    return passed_along(face_plane, "gx", offset)


def pass_depth(face_plane, offset):
    return from_behind(face_plane, "gz", offset)


def pass_height(face_plane, offset):
    return from_behind(face_plane, "gy", offset)


def general_shards(electric, magnetic, material, permittivity):
    cell_count = electric.shape[-1]
    e_flat = electric.reshape(3, cell_count)
    h_flat = magnetic.reshape(3, cell_count)
    coefficient = lookup(material.reshape(cell_count), permittivity)
    is_fine = lax.axis_index("gy") >= lax.axis_size("gy") // 2
    coarse_shape = (CZ, CX, CY)
    fine_shape = (2 * CZ, 2 * CX, CY // 4)
    for substep in range(2):
        coarse_moves = substep == 0
        face_width, face_depth, face_height = lax.cond(
            is_fine,
            partial(low_faces, fine_shape, True),
            partial(low_faces, coarse_shape, False),
            e_flat,
        )
        got_depth = pass_depth(face_depth, -1)
        got_height = pass_height(face_height, -1)
        got_width = pass_width(face_width, -1)
        h_flat = lax.cond(
            is_fine,
            partial(advance_magnetic, fine_shape, True, True),
            partial(advance_magnetic, coarse_shape, False, coarse_moves),
            e_flat,
            h_flat,
            got_width,
            got_depth,
            got_height,
        )
        rim_width, rim_depth, rim_height = lax.cond(
            is_fine,
            partial(high_faces, fine_shape, True),
            partial(high_faces, coarse_shape, False),
            h_flat,
        )
        rim_depth = pass_depth(rim_depth, 1)
        rim_height = pass_height(rim_height, 1)
        rim_width = pass_width(rim_width, 1)
        e_flat = lax.cond(
            is_fine,
            partial(advance_electric, fine_shape, True, True),
            partial(advance_electric, coarse_shape, False, coarse_moves),
            e_flat,
            h_flat,
            coefficient,
            rim_width,
            rim_depth,
            rim_height,
        )
    return (e_flat.reshape(electric.shape), h_flat.reshape(magnetic.shape))


ROWS = 512
HALO = 128
EXT = 1296
LIMIT = 40 * 1024 * 1024
F32 = jnp.float32
VM = pl.BlockSpec(memory_space=pltpu.VMEM)
HBM = pl.BlockSpec(memory_space=pltpu.HBM)
CHUNK = 32
SKEW = 3


class Fine:
    depth, stride, count, own, step, parts, last = 64, 72, 10, 8, 1, 1, 63


class Coarse:
    depth, stride, count, own, step, parts, last = 128, 144, 5, 4, 4, 4, 31


def vmem(*shape, dtype=F32):
    return pltpu.VMEM(shape, dtype)


def held(x):
    return pltpu.with_memory_space_constraint(x, pltpu.VMEM)


def far(x):
    return pltpu.with_memory_space_constraint(x, pltpu.HBM)


def kernel_call(body, out_shape, in_specs, out_specs, scratch=(), aliases=None, cost=None):
    return pl.pallas_call(
        body,
        cost_estimate=cost,
        out_shape=out_shape,
        in_specs=in_specs,
        out_specs=out_specs,
        scratch_shapes=list(scratch),
        input_output_aliases=aliases or {},
        compiler_params=pltpu.CompilerParams(vmem_limit_bytes=LIMIT),
    )


def by_level(body):
    is_fine = lax.axis_index("gy") >= lax.axis_size("gy") // 2
    gz = lax.axis_index("gz")
    pl.when(is_fine)(lambda: body(Fine, gz))
    pl.when(jnp.logical_not(is_fine))(lambda: body(Coarse, gz))


def lanes_of(shape):
    return lax.broadcasted_iota(jnp.int32, shape, len(shape) - 1)


def rows_of(shape):
    return lax.broadcasted_iota(jnp.int32, shape, len(shape) - 2)


def roll_lanes(x, by):
    return pltpu.roll(x, by % 128, 1)


def roll_rows(x, by):
    return pltpu.roll(x, by % x.shape[0], 0)


def layer_row(grid, index):
    return pl.multiple_of(grid.stride * (index + 1), 8)


def own_first(grid, gz):
    return (grid.count - grid.own) * gz


def halo_first(grid, gz):
    return grid.own * (1 - gz)


def clear_pads(grid, ref, *zero_layers):
    for comp in range(3):
        for index in range(grid.count + 2):
            start, size = grid.stride * index, grid.stride
            if index not in zero_layers:
                start, size = start + grid.depth, size - grid.depth
            ref[comp, pl.ds(start, size), :] = jnp.zeros((size, 128), F32)


def own_layers(grid, ref, gz):
    view = ref.reshape(3, EXT // grid.stride, grid.stride, 128)
    return view.at[:, pl.ds(1 + own_first(grid, gz), grid.own), pl.ds(0, grid.depth), :]


def block_layers(grid, ref):
    return ref.reshape(3, grid.own, grid.depth, 128)


def at_lane(tile, lane_from, lane_to, value):
    lane = lanes_of(value.shape)
    return jnp.where(lane == lane_to, roll_lanes(value, lane_to - lane_from), tile)


def average(ref, lead, row, stride):
    steps = (0, 1, stride, stride + 1)
    quad = [ref[lead, pl.ds(row + step, 32, stride=2), :] for step in steps]
    return ((quad[0] + quad[1]) + (quad[2] + quad[3])) * 0.25


def put_column(tile, lane_from, slot, column):
    for block in range(4):
        tile = at_lane(tile, lane_from, 32 * block + slot, column[8 * block : 8 * block + 8])
    return tile


FINE_E = [(0, comp) for comp in range(3)] + [(1, 1), (1, 2)] + [(x, comp) for x in (62, 63) for comp in range(3)]
FINE_H = [(0, comp) for comp in range(3)] + [(62, 1), (62, 2)] + [(63, comp) for comp in range(3)]
FINE_M = [0, 1, 62, 63]
COARSE_E = [(0, 1), (0, 2)] + [(31, comp) for comp in range(3)]
COARSE_H = [(31, 1), (31, 2)]
COARSE_M = [0, 31]
COLUMNS = 192
R_ROW = COLUMNS - 8
NEAR = 64
FACE = 6 * HALO + NEAR


def wanted(grid):
    return (FINE_E, FINE_H, FINE_M) if grid is Fine else (COARSE_E, COARSE_H, COARSE_M)


def top_tile(tile, layer, ex, ey, ez, hx, hz):
    tile = put_column(tile, 127, layer, hx + 0.5 * ez)
    tile = put_column(tile, 127, 8 + layer, hz - 0.5 * ex)
    return put_column(tile, 127, 16 + layer, ey)


def edge_tiles(grid, ref):
    view = ref.reshape(grid.own, grid.depth, 128)
    return [view.at[:, pl.ds((grid.depth - 8) * end, 8), :] for end in range(2)]


def material_loads(grid, gz, m_hbm, m_face, m_ends, sems):
    face = pl.ds((1 - gz) * (ROWS - NEAR), NEAR)
    loads = [pltpu.make_async_copy(m_hbm.at[face], m_face, sems.at[0])]
    for end, tiles in enumerate(edge_tiles(grid, m_hbm)):
        place = m_ends.at[end].reshape(8, 8, 128).at[pl.ds(0, grid.own)]
        loads.append(pltpu.make_async_copy(tiles, place, sems.at[1 + end]))
    return loads


def peek(e_hbm, h_hbm, edge_tile, e_ends, h_ends, sems):
    def body(grid, gz):
        if grid is Fine:
            edge_tile[...] = jnp.zeros((8, 128), F32)
            return
        loads = []
        for end in range(2):
            rows = pl.ds((1 - gz) * (ROWS - HALO) + (HALO - 8) * end, 8)
            place = pl.ds(0, 8)
            loads.append(pltpu.make_async_copy(e_hbm.at[:, rows], e_ends.at[end, :, place], sems.at[2 * end]))
            for slot, comp in enumerate((0, 2)):
                into = h_ends.at[end, comp, place]
                loads.append(pltpu.make_async_copy(h_hbm.at[comp, rows], into, sems.at[4 + 2 * end + slot]))
        for load in loads:
            load.start()
        for load in loads:
            load.wait()
        tile = jnp.zeros((8, 128), F32)
        lane = lanes_of((8, 128))
        for end in range(2):
            rows = pl.ds(0 if end else 3, 8)
            ex, ey, ez = (e_ends[end, comp, rows, :] for comp in range(3))
            hx, hz = h_ends[end, 0, rows, :], h_ends[end, 2, rows, :]
            for kind, value in enumerate((hx + 0.5 * ez, hz - 0.5 * ex, ey)):
                to = 96 * end + 8 * kind + 3 + gz
                tile = jnp.where(lane == to, pltpu.roll(value, to + 1, 1), tile)
        edge_tile[...] = tile

    by_level(body)


def fine_material(m_hbm, after, m_face, m_ends, sems):
    def body(grid, gz):
        if grid is Coarse:
            return
        loads = material_loads(grid, gz, m_hbm, m_face, m_ends, sems)
        for load in loads:
            load.start()
        for load in loads:
            load.wait()

    by_level(body)


def gather(e_own, h_own, m_face, m_ends, zmsg, ytile, columns):
    def body(grid, gz):
        tile = jnp.zeros((8, 128), F32)
        for layer in range(4):
            if grid is Fine:
                row = 2 * grid.depth * layer
                tile = put_column(tile, 0, layer, average(e_own, 0, row, grid.depth))
                tile = put_column(tile, 0, 8 + layer, average(e_own, 2, row, grid.depth))
            else:
                top = pl.ds(grid.depth * layer + 3, 32, stride=4)
                ex, ey, ez = (e_own[comp, top, :] for comp in range(3))
                tile = top_tile(tile, layer, ex, ey, ez, h_own[0, top, :], h_own[2, top, :])
        tile = jnp.where(gz == 1, roll_lanes(tile, 4), tile)
        ytile[...] = tile
        columns[pl.ds(R_ROW, 8), :] = tile
        want_e, want_h, want_m = wanted(grid)
        slot = 0

        def column_rows(x, part):
            return pl.ds(grid.step * x + part, grid.own, stride=grid.depth)

        def put(value):
            nonlocal slot
            columns[pl.ds(slot, grid.own), :] = value
            slot += grid.own

        for x, comp in want_e:
            for part in range(grid.parts):
                put(e_own[comp, column_rows(x, part), :])
        for x, comp in want_h:
            for part in range(grid.parts):
                put(h_own[comp, column_rows(x, part), :])
        for x in want_m if grid is Fine else []:
            for part in range(grid.parts):
                rows = pl.ds(grid.step * x % 8 + part, grid.own, stride=8)
                put(m_ends[int(x > 1), rows, :].astype(F32))
        edge = pl.ds(pl.multiple_of((1 - gz) * (ROWS - HALO), HALO), HALO)
        for comp in range(3):
            zmsg[pl.ds(HALO * comp, HALO), :] = h_own[comp, edge, :]
            zmsg[pl.ds(HALO * (3 + comp), HALO), :] = e_own[comp, edge, :]
        if grid is Fine:
            zmsg[pl.ds(6 * HALO, NEAR), :] = m_face[...].astype(F32)
        zmsg[pl.ds(FACE, COLUMNS), :] = columns[...]

    by_level(body)


def join_z(ytile, edge_tile, joined):
    joined[...] = ytile[...] + edge_tile[...]


def up_y(grid, ref, comp, row, f):
    lane = lanes_of(f.shape)
    if grid is Fine:
        return jnp.where(lane == 127, 0.0, roll_lanes(f, -1))
    following = ref[comp, pl.ds(row + 1, f.shape[0]), :]
    following = jnp.where(rows_of(f.shape) % 4 == 3, 0.0, following)
    return roll_lanes(jnp.where(lane == 0, following, f), -1)


def down_y(grid, ref, comp, row, f, ghost):
    lane = lanes_of(f.shape)
    if grid is Fine:
        return roll_lanes(jnp.where(lane == 127, ghost, f), 1)
    previous = ref[comp, pl.ds(row - 1, f.shape[0]), :]
    previous = jnp.where(rows_of(f.shape) % 4 == 0, 0.0, previous)
    return roll_lanes(jnp.where(lane == 127, previous, f), 1)


def half_h(grid, e, h_from, from_row, h_to, row):
    for start in range(0, grid.depth, CHUNK):
        r = row + start
        here = pl.ds(r, CHUNK)
        ex, ey, ez = (e[comp, here, :] for comp in range(3))
        above, beside = pl.ds(r + grid.stride, CHUNK), pl.ds(r + grid.step, CHUNK)
        h0 = [h_from(comp, pl.ds(from_row + start, CHUNK)) for comp in range(3)]
        ez_y, ex_y = up_y(grid, e, 2, r, ez), up_y(grid, e, 0, r, ex)
        h_to[0, here, :] = h0[0] - 0.5 * ((ez_y - ez) - (e[1, above, :] - ey))
        h_to[1, here, :] = h0[1] - 0.5 * ((e[0, above, :] - ex) - (e[2, beside, :] - ez))
        h_to[2, here, :] = h0[2] - 0.5 * ((e[1, beside, :] - ey) - (ex_y - ex))


def half_e(grid, h, e_from, e_to, c_ref, row, ghosts):
    for start in range(0, grid.depth, CHUNK):
        r = row + start
        here = pl.ds(r, CHUNK)
        hx, hy, hz = (h[comp, here, :] for comp in range(3))
        below, beside = pl.ds(r - grid.stride, CHUNK), pl.ds(r - grid.step, CHUNK)
        px, pz = ghosts(start)
        hx_y, hz_y = down_y(grid, h, 0, r, hx, px), down_y(grid, h, 2, r, hz, pz)
        c = c_ref[here, :]
        e_to[0, here, :] = e_from[0, here, :] + c * ((hz - hz_y) - (hy - h[1, below, :]))
        e_to[1, here, :] = e_from[1, here, :] + c * ((hx - h[0, below, :]) - (hz - h[2, beside, :]))
        e_to[2, here, :] = e_from[2, here, :] + c * ((hy - h[1, beside, :]) - (hx - hx_y))


def column_of(tile, block, sub, slot, grid):
    shape = (2 * grid.own, 128)
    row = jnp.broadcast_to(tile[sub : sub + 1, :], shape)
    lane = 32 * block + slot + rows_of(shape) // (2 * grid.own // 8)
    picked = jnp.where(lanes_of(shape) == lane, row, 0.0)
    return jnp.broadcast_to(jnp.sum(picked, axis=1, keepdims=True), shape)


def each(fn, *columns):
    return [fn(*parts) for parts in zip(*columns, strict=True)]


def plus_y(f, ghost=0.0):
    following = f[1:] + [ghost]
    return [
        roll_lanes(jnp.where(lanes_of(p.shape) == 0, nxt, p), -1) - p
        for p, nxt in zip(f, following, strict=True)
    ]


def minus_y(f, ghost=0.0):
    previous = [ghost] + f[:-1]
    return [
        p - roll_lanes(jnp.where(lanes_of(p.shape) == 127, prv, p), 1)
        for p, prv in zip(f, previous, strict=True)
    ]


def plus_z(f):
    return [
        jnp.where(rows_of(p.shape) == p.shape[0] - 1, 0.0, roll_rows(p, -1)) - p for p in f
    ]


def minus_z(f):
    return [p - jnp.where(rows_of(p.shape) == 0, 0.0, roll_rows(p, 1)) for p in f]


def add(a, b):
    return each(lambda p, q: p + q, a, b)


def sub(a, b):
    return each(lambda p, q: p - q, a, b)


def mul(a, b):
    return each(lambda p, q: p * q, a, b)


def scale(by, a):
    return [by * p for p in a]


def read_columns(grid, own, other, gz):
    want_e, want_h, want_m = wanted(grid)
    found, slot = [], 0
    for _ in range(len(want_e) + len(want_h) + len(want_m)):
        col = []
        for _ in range(grid.parts):
            rows = pl.ds(slot, grid.own)
            mine, theirs = own[rows, :], other[pl.ds(FACE + slot, grid.own), :]
            low, high = jnp.where(gz == 0, mine, theirs), jnp.where(gz == 0, theirs, mine)
            col.append(jnp.concatenate([low, high], axis=0))
            slot += grid.own
        found.append(col)
    e_found, found = found[: len(want_e)], found[len(want_e) :]
    h_found, m_found = found[: len(want_h)], found[len(want_h) :]
    return (
        dict(zip(want_e, e_found, strict=True)),
        dict(zip(want_h, h_found, strict=True)),
        dict(zip(want_m, m_found, strict=True)),
    )


def write_planes(ref, columns):
    row = 0
    for col in columns:
        for p in col:
            ref[pl.ds(row, p.shape[0]), :] = p
            row += p.shape[0]


def read_planes(grid, ref, *indices):
    height, parts = 2 * grid.own, grid.parts
    return [
        [ref[pl.ds(height * (parts * i + part), height), :] for part in range(parts)] for i in indices
    ]


MESSAGE = 48
UP = {Fine: [(9, 7)] * 5, Coarse: [(4, 4)] * 2}
DOWN = {Fine: [(10, 6)] + [(9, 7)] * 4, Coarse: [(5, 3)] * 2}


def sent_rows(plane, entry, gz):
    count, begin = entry
    return jnp.where(gz == 0, roll_rows(plane, -begin), plane)[:count]


def places(grid, entries):
    row = 0
    for entry in entries:
        for _ in range(grid.parts):
            yield row, entry
            row += entry[0]


def write_message(grid, ref, entries, columns, gz):
    planes = [p for col in columns for p in col]
    for (row, entry), p in zip(places(grid, entries), planes, strict=True):
        ref[pl.ds(row, entry[0]), :] = sent_rows(p, entry, gz)


def read_message(grid, ref, entries, gz):
    height, planes = 2 * grid.own, []
    for row, (_, begin) in places(grid, entries):
        start = min(row, MESSAGE - height)
        p = ref[pl.ds(start, height), :]
        planes.append(pltpu.roll(p, height + start - row + begin * gz, 0))
    return [planes[i : i + grid.parts] for i in range(0, len(planes), grid.parts)]


def extend(
    e_own,
    h_own,
    m_own,
    zmsg,
    permittivity,
    columns,
    e_ext,
    h_ext,
    c_ext,
    up,
    down,
    to_up,
    to_down,
    c_planes,
    table,
    sems,
):
    def body(grid, gz):
        load = pltpu.make_async_copy(permittivity, table, sems.at[0])
        load.start()
        clear_pads(grid, h_ext, 0)
        clear_pads(grid, e_ext, grid.count + 1)
        for layer in range(grid.own):
            for start in range(0, grid.depth, CHUNK):
                rows = pl.ds(layer_row(grid, own_first(grid, gz) + layer) + start, CHUNK)
                from_rows = pl.ds(grid.depth * layer + start, CHUNK)
                for comp in range(3):
                    e_ext[comp, rows, :] = e_own[comp, from_rows, :]
        halo = halo_first(grid, gz)
        for layer in range(grid.count - grid.own):
            for start in range(0, grid.depth, CHUNK):
                rows = pl.ds(layer_row(grid, halo + layer) + start, CHUNK)
                for comp in range(3):
                    from_rows = pl.ds(HALO * (3 + comp) + grid.depth * layer + start, CHUNK)
                    e_ext[comp, rows, :] = zmsg[from_rows, :]

        def h_halo(comp, rows):
            return zmsg[pl.ds(HALO * comp + rows.start, rows.size), :]

        for layer in range(grid.count - grid.own):
            row = layer_row(grid, halo + layer)
            half_h(grid, e_ext, h_halo, grid.depth * layer, h_ext, row)
        for layer in range(grid.own):
            row = layer_row(grid, own_first(grid, gz) + layer)
            half_h(grid, e_ext, lambda comp, rows: h_own[comp, rows, :], grid.depth * layer, h_ext, row)
        load.wait()
        values = [0.5 / jnp.full((8, 128), table[i], F32) for i in range(MATS)]

        def coef(is_material, rows):
            parts = [jnp.concatenate([value] * (rows // 8), axis=0) for value in values]
            found = parts[MATS - 1]
            for i in range(MATS - 2, -1, -1):
                found = jnp.where(is_material(i), parts[i], found)
            return found

        for start in range(0, NEAR if grid is Fine else 0, CHUNK):
            material = zmsg[pl.ds(6 * HALO + start, CHUNK), :]
            row = layer_row(grid, halo + gz) + start
            c_ext[pl.ds(row, CHUNK), :] = coef(lambda i, m=material: m == float(i), CHUNK)
        for start in range(0, ROWS, CHUNK):
            layer, rest = divmod(start, grid.depth)
            material = m_own[pl.ds(start, CHUNK), :]
            row = layer_row(grid, own_first(grid, gz) + layer) + rest
            c_ext[pl.ds(row, CHUNK), :] = coef(lambda i, m=material: m == i, CHUNK)

        e, h, m = read_columns(grid, columns, zmsg, gz)
        if grid is Coarse:
            for x in m:
                rows = [pl.ds(4 * x + part, 4, stride=grid.depth) for part in range(4)]
                own = [m_own[part, :].astype(F32) for part in rows]
                m[x] = [jnp.concatenate([part, part], axis=0) for part in own]
        c = {
            x: [coef(lambda i, q=part: q == float(i), part.shape[0]) for part in col] for x, col in m.items()
        }
        write_planes(c_planes, list(c.values()))
        if grid is Coarse:
            ex, ey, ez = (e[31, comp] for comp in range(3))
            hy = sub(h[31, 1], scale(0.5, add(plus_z(ex), ez)))
            hz = add(h[31, 2], scale(0.5, add(ey, plus_y(ex))))
            sent_up, sent_down = [hy, hz], [e[0, 2], e[0, 1]]
        else:
            ex, ey, ez = (e[0, comp] for comp in range(3))
            hx = sub(h[0, 0], scale(0.5, sub(plus_y(ez), plus_z(ey))))
            hy = sub(h[0, 1], scale(0.5, sub(plus_z(ex), sub(e[1, 2], ez))))
            hz = sub(h[0, 2], scale(0.5, sub(sub(e[1, 1], ey), plus_y(ex))))
            ey_next = add(ey, mul(c[0], sub(minus_z(hx), hz)))
            ez_next = add(ez, mul(c[0], sub(hy, minus_y(hx))))
            sent_down = [ez, ey, ey_next, ez_next, c[0]]
            ex, ey, ez = (e[62, comp] for comp in range(3))
            hy62 = sub(h[62, 1], scale(0.5, sub(plus_z(ex), sub(e[63, 2], ez))))
            hz62 = sub(h[62, 2], scale(0.5, sub(sub(e[63, 1], ey), plus_y(ex))))
            ex, ey, ez = (e[63, comp] for comp in range(3))
            hx = sub(h[63, 0], scale(0.5, sub(plus_y(ez), plus_z(ey))))
            hy = sub(h[63, 1], scale(0.5, add(plus_z(ex), ez)))
            hz = add(h[63, 2], scale(0.5, add(ey, plus_y(ex))))
            ex_next = add(ex, mul(c[63], sub(minus_y(hz), minus_z(hy))))
            ey_next = add(ey, mul(c[63], sub(minus_z(hx), sub(hz, hz62))))
            ez_next = add(ez, mul(c[63], sub(sub(hy, hy62), minus_y(hx))))
            next_y = sub(hy, scale(0.5, add(plus_z(ex_next), ez_next)))
            next_z = add(hz, scale(0.5, add(ey_next, plus_y(ex_next))))
            sent_up = [hy, hz, next_y, next_z, c[63]]
        write_planes(up, sent_up)
        write_planes(down, sent_down)
        write_message(grid, to_up, UP[grid], sent_up, gz)
        write_message(grid, to_down, DOWN[grid], sent_down, gz)

    by_level(body)


def between(top, r):
    lane, row = lanes_of(top.shape), rows_of(top.shape)
    kind = (lane % 32) // 8
    above = jnp.where(lane % 8 == 7, 0.0, roll_lanes(top, -1))
    px = top - 0.5 * roll_lanes(r, -8) + 0.5 * roll_lanes(above - top, -16)
    beside = roll_rows(top, -1)
    beside = jnp.where(row == 7, jnp.where(lane >= 96, 0.0, roll_lanes(beside, -32)), beside)
    pz = top + 0.5 * roll_lanes(r, 8) - 0.5 * roll_lanes(beside - top, -8)
    return jnp.where(kind == 0, px, jnp.where(kind == 1, pz, 0.0))


def join_y(up_in, down_in, c_planes, yzin, r_own, r_other, to_up, to_down):
    def body(grid, gz):
        def patch(ref, entries, index, value):
            row, entry = list(places(grid, entries))[index]
            rows = pl.ds(row, entry[0])
            ref[rows, :] = ref[rows, :] + sent_rows(value, entry, gz)

        top = yzin[...]
        to_up[...] = up_in[...]
        to_down[...] = down_in[...]
        shape = (2 * grid.own, 128)
        if grid is Coarse:
            change = jnp.where(lanes_of(shape) == 127, 0.5 * column_of(top, 3, 7, 0, grid), 0.0)
            patch(to_up, UP[grid], 7, change)
            return
        plane = between(top, r_own[pl.ds(R_ROW, 8), :] + r_other[pl.ds(FACE + R_ROW, 8), :])
        bottom = lanes_of(shape) == 0
        (c0,), (c63,) = read_planes(grid, c_planes, 0, 3)

        patch(to_down, DOWN[grid], 3, jnp.where(bottom, c0 * column_of(plane, 0, 0, 0, grid), 0.0))
        ez_change = jnp.where(bottom, c63 * column_of(plane, 3, 7, 0, grid), 0.0)
        ex_change = jnp.where(bottom, -c63 * column_of(plane, 3, 7, 8, grid), 0.0)
        patch(to_up, UP[grid], 2, -0.5 * (plus_z([ex_change])[0] + ez_change))
        patch(to_up, UP[grid], 3, -0.5 * ex_change)
        to_down[pl.ds(MESSAGE - 1, 1), :] = top[:1]

    by_level(body)


def advance(
    e_ext,
    h_ext,
    c_ext,
    c_planes,
    yin,
    yzin,
    r_own,
    r_other,
    e_out,
    h_out,
    e_edge,
    h_edge,
    patched,
    e_mid,
    h_mid,
    e_last,
    plane,
    sems,
):
    def body(grid, gz):
        first = own_first(grid, gz)
        upper = lanes_of((8, 128)) % 8 >= 4
        tile = jnp.where(upper == (gz == 0), yzin[...], yin[...])
        if grid is Fine:
            top = tile
            tile = between(top, r_own[pl.ds(R_ROW, 8), :] + r_other[pl.ds(FACE + R_ROW, 8), :])
            ((c0,),) = read_planes(grid, c_planes, 0)
            change = jnp.where(lanes_of((16, 128)) == 0, c0 * column_of(tile, 0, 0, 0, grid), 0.0)
            patched[pl.ds(0, 16), :] = change
            patched[pl.ds(16, 16), :] = column_of(top, 0, 0, 16, grid)
        tile = jnp.where(gz == 0, tile, roll_lanes(tile, -3))

        def write(source, target, sem, layer=None):
            source, target = own_layers(grid, source, gz), block_layers(grid, target)
            if layer is not None:
                source, target = source.at[:, layer], target.at[:, layer]
            return pltpu.make_async_copy(source, target, sem)

        def keep_edges(source, target):
            for comp in range(3):
                for layer in range(grid.own):
                    for edge in range(2):
                        row = layer_row(grid, first + layer) + (grid.depth - 8) * edge
                        target[edge, comp, pl.ds(8 * layer, 8), :] = source[comp, pl.ds(row, 8), :]

        clear_pads(grid, h_mid, 0)
        if grid is Fine:
            clear_pads(grid, e_mid, grid.count + 1)
            for kind in range(2):
                for layer in range(5):
                    for block in range(4):
                        value = roll_lanes(tile, 127 - (32 * block + 8 * kind + layer))
                        for step in range(2):
                            rows = pl.ds(64 * layer + 16 * block + step, 8, stride=2)
                            plane[kind, rows, :] = value

            def ghosts(index):
                begin = 64 * (index // 2)

                def of(start):
                    rows = pl.ds(pl.multiple_of(begin + start, 8), CHUNK)
                    return plane[0, rows, :], plane[1, rows, :]

                return of

            def own_write(source, target, sem, layer):
                def start():
                    rows = pl.ds(layer_row(grid, layer), grid.depth)
                    to = block_layers(grid, target).at[:, layer - first]
                    pltpu.make_async_copy(source.at[:, rows], to, sem).start()

                if 2 <= layer < 8:
                    start()
                else:
                    pl.when((layer < 8) == (gz == 0))(start)

            def h1(comp, rows):
                return h_ext[comp, rows, :]

            for step in range(grid.count + 2 * SKEW):
                if step < grid.count:
                    half_e(grid, h_ext, e_ext, e_mid, c_ext, grid.stride * (step + 1), ghosts(step))
                layer = step - SKEW
                if 0 <= layer < grid.count:
                    row = grid.stride * (layer + 1)
                    half_h(grid, e_mid, h1, row, h_mid, row)
                    own_write(h_mid, h_out, sems.at[0], layer)
                layer = step - 2 * SKEW
                if 0 <= layer < grid.count:
                    row = grid.stride * (layer + 1)
                    half_e(grid, h_mid, e_mid, e_last, c_ext, row, ghosts(layer))
                    own_write(e_last, e_out, sems.at[1], layer)
        else:
            for comp in range(3):
                for layer in range(grid.count):
                    rows = pl.ds(layer_row(grid, layer), grid.depth)
                    h_mid[comp, rows, :] = h_ext[comp, rows, :]
            lane = lanes_of((8, 128))
            for layer in range(grid.count):
                for block in range(4):
                    rows = pl.ds(layer_row(grid, layer) + 32 * block + 3, 8, stride=4)
                    rx = roll_lanes(tile, 127 - (32 * block + layer))
                    rz = roll_lanes(tile, 127 - (32 * block + 8 + layer))
                    h_mid[0, rows, :] = h_mid[0, rows, :] - jnp.where(lane == 127, 0.5 * rz, 0.0)
                    h_mid[2, rows, :] = h_mid[2, rows, :] + jnp.where(lane == 127, 0.5 * rx, 0.0)
            write(h_mid, h_out, sems.at[0]).start()
            for layer in range(grid.own):
                row = layer_row(grid, first + layer)
                half_e(grid, h_mid, e_ext, e_last, c_ext, row, lambda start: (0.0, 0.0))
                write(e_last, e_out, sems.at[1], layer).start()
        keep_edges(h_mid, h_edge)
        keep_edges(e_last, e_edge)
        write(h_mid, h_out, sems.at[0]).wait()
        write(e_last, e_out, sems.at[1]).wait()

    by_level(body)


def correct(
    up,
    down,
    c_planes,
    patched,
    from_below,
    from_above,
    e_edge,
    h_edge,
    e_in,
    h_in,
    e_out,
    h_out,
    e_tile,
    h_tile,
    sems,
):
    def body(grid, gz):
        last = grid.last

        def put(ref, edge, comp, x, change):
            for part, p in enumerate(change):
                own = jnp.where(gz == 0, p[: grid.own], p[grid.own :])
                rows = pl.ds(grid.step * x % 8 + part, grid.own, stride=8)
                ref[edge, comp, rows, :] = ref[edge, comp, rows, :] + own

        def finish(edge):
            copies = []
            for slot, (tile, out) in enumerate(((h_tile, h_out), (e_tile, e_out))):
                if grid is Coarse and edge == 0 and slot == 0:
                    continue
                source = tile.at[edge].reshape(3, 8, 8, 128).at[:, pl.ds(0, grid.own)]
                target = block_layers(grid, out).at[:, :, pl.ds((grid.depth - 8) * edge, 8), :]
                copies.append(pltpu.make_async_copy(source, target, sems.at[2 * edge + slot]))
            for copy in copies:
                copy.start()
            return copies

        if grid is Fine:
            zero = [jnp.zeros((16, 128), F32)]
            ez64, ey64, ey64_part, ez64_part, c64 = read_message(grid, from_above, DOWN[grid], gz)
            ey_above = column_of(from_above[pl.ds(MESSAGE - 8, 8), :], 0, 7, 16, grid)
            hy63, hz63 = read_planes(grid, up, 0, 1)
            c0, c1, c62, c63 = read_planes(grid, c_planes, *range(4))
            hy_part, hz_part, next_y, next_z, cm = read_message(grid, from_below, UP[grid], gz)
            ez0, ey0, ey0_part, ez0_part = read_planes(grid, down, *range(4))
            ez0_change, ey_top = read_planes(grid, patched, 0, 1)
            ez0_part = add(ez0_part, ez0_change)
            ghost = -0.5 * ey_top[0]
            dhy, dhz = scale(0.5, ez0), scale(-0.5, ey0)
            hym, hzm = add(hy_part, dhy), add(hz_part, dhz)
            dexm = mul(cm, sub(minus_y(dhz, ghost), minus_z(dhy)))
            dey, dez = mul(c0, hzm), scale(-1.0, mul(c0, hym))
            dhx2 = scale(-0.5, sub(plus_y(dez), plus_z(dey)))
            dhy2 = scale(-0.5, dez)
            dhz2 = scale(0.5, dey)
            change = sub(sub(add(ez0_part, dez), plus_z(dexm)), mul(cm, dhy))
            hym2 = add(add(next_y, dhy), scale(0.5, change))
            change = sub(sub(plus_y(dexm), add(ey0_part, dey)), mul(cm, dhz))
            hzm2 = add(add(next_z, dhz), scale(0.5, change))
            put(h_tile, 0, 0, 0, dhx2)
            put(h_tile, 0, 1, 0, dhy2)
            put(h_tile, 0, 2, 0, dhz2)
            put(e_tile, 0, 0, 0, mul(c0, sub(minus_y(dhz2), minus_z(dhy2))))
            put(e_tile, 0, 1, 0, add(dey, mul(c0, sub(minus_z(dhx2), sub(dhz2, hzm2)))))
            put(e_tile, 0, 2, 0, add(dez, mul(c0, sub(sub(dhy2, hym2), minus_y(dhx2)))))
            put(e_tile, 0, 1, 1, mul(c1, dhz2))
            put(e_tile, 0, 2, 1, scale(-1.0, mul(c1, dhy2)))
            copies = finish(0)

            ghost = -0.5 * ey_above
            dhy, dhz = scale(0.5, ez64), scale(-0.5, ey64)
            dex = mul(c63, sub(minus_y(dhz, ghost), minus_z(dhy)))
            dey = scale(-1.0, mul(c63, dhz))
            dez = mul(c63, dhy)
            dex62 = mul(c62, minus_y(zero, ghost))
            ey64_next = add(ey64_part, mul(c64, add(hz63, dhz)))
            ez64_next = sub(ez64_part, mul(c64, add(hy63, dhy)))
            dhx2 = scale(-0.5, sub(plus_y(dez), plus_z(dey)))
            dhy2 = add(dhy, scale(-0.5, sub(plus_z(dex), sub(ez64_next, dez))))
            dhz2 = add(dhz, scale(-0.5, sub(sub(ey64_next, dey), plus_y(dex))))
            dhy62 = scale(-0.5, sub(plus_z(dex62), dez))
            dhz62 = scale(-0.5, sub(dey, plus_y(dex62)))
            put(h_tile, 1, 0, 63, dhx2)
            put(h_tile, 1, 1, 63, dhy2)
            put(h_tile, 1, 2, 63, dhz2)
            put(h_tile, 1, 1, 62, dhy62)
            put(h_tile, 1, 2, 62, dhz62)
            put(e_tile, 1, 0, 63, add(dex, mul(c63, sub(minus_y(dhz2, ghost), minus_z(dhy2)))))
            put(e_tile, 1, 1, 63, add(dey, mul(c63, sub(minus_z(dhx2), sub(dhz2, dhz62)))))
            put(e_tile, 1, 2, 63, add(dez, mul(c63, sub(sub(dhy2, dhy62), minus_y(dhx2)))))
            put(e_tile, 1, 0, 62, add(dex62, mul(c62, sub(minus_y(dhz62, ghost), minus_z(dhy62)))))
            put(e_tile, 1, 1, 62, scale(-1.0, mul(c62, dhz62)))
            put(e_tile, 1, 2, 62, mul(c62, dhy62))
            copies += finish(1)
        else:
            ez32, ey32 = read_message(grid, from_above, DOWN[grid], gz)
            c0, c31 = read_planes(grid, c_planes, 0, 1)
            dhy, dhz = scale(0.5, ez32), scale(-0.5, ey32)
            put(h_tile, 1, 1, last, dhy)
            put(h_tile, 1, 2, last, dhz)
            put(e_tile, 1, 0, last, mul(c31, sub(minus_y(dhz), minus_z(dhy))))
            put(e_tile, 1, 1, last, scale(-1.0, mul(c31, dhz)))
            put(e_tile, 1, 2, last, mul(c31, dhy))
            copies = finish(1)
            hy_part, hz_part = read_message(grid, from_below, UP[grid], gz)
            ez0, ey0 = read_planes(grid, down, 0, 1)
            put(e_tile, 0, 1, 0, mul(c0, add(hz_part, scale(-0.5, ey0))))
            put(e_tile, 0, 2, 0, scale(-1.0, mul(c0, add(hy_part, scale(0.5, ez0)))))
            copies += finish(0)
        for copy in copies:
            copy.wait()

    by_level(body)


def across(x, dx=0, dy=0, dz=0):
    nx, ny, nz = lax.axis_size("gx"), lax.axis_size("gy"), lax.axis_size("gz")
    pairs = [
        ((i * ny + j) * nz + k, ((i + dx) % nx * ny + (j + dy) % ny) * nz + (k + dz) % nz)
        for i in range(nx)
        for j in range(ny)
        for k in range(nz)
    ]
    return lax.ppermute(x, ("gx", "gy", "gz"), pairs)


def fast_shards(electric, magnetic, material, permittivity):
    e = electric.reshape(3, ROWS, 128)
    h = magnetic.reshape(3, ROWS, 128)
    m = material.reshape(ROWS, 128)
    dma = pltpu.SemaphoreType.DMA
    edge_tile = kernel_call(
        peek,
        vmem(8, 128),
        [HBM] * 2,
        VM,
        [pltpu.VMEM((2, 3, 16, 128), F32)] * 2 + [dma((8,))],
    )(far(e), far(h))
    m_face, m_ends = kernel_call(
        fine_material,
        [vmem(NEAR, 128, dtype=jnp.int32), vmem(2, 64, 128, dtype=jnp.int32)],
        [HBM, VM],
        [VM] * 2,
        [dma((3,))],
    )(far(m), held(edge_tile))
    edge_tile = across(edge_tile, dz=1)
    zmsg, ytile, columns = kernel_call(
        gather,
        [vmem(FACE + COLUMNS, 128), vmem(8, 128), vmem(COLUMNS, 128)],
        [VM] * 4,
        [VM] * 3,
    )(held(e), held(h), held(m_face), held(m_ends))
    ytile = kernel_call(
        join_z,
        vmem(8, 128),
        [VM] * 2,
        VM,
        cost=pl.CostEstimate(flops=10**10, bytes_accessed=10**8, transcendentals=0),
    )(held(ytile), held(edge_tile))
    zin = across(zmsg, dz=1)
    yin = across(ytile, dy=1)
    yzin = across(ytile, dy=1, dz=1)
    e_ext, h_ext, c_ext, up, down, up_part, down_part, c_planes = kernel_call(
        extend,
        [
            vmem(3, EXT, 128),
            vmem(3, EXT, 128),
            vmem(EXT, 128),
            vmem(96, 128),
            vmem(96, 128),
            vmem(MESSAGE, 128),
            vmem(MESSAGE, 128),
            vmem(64, 128),
        ],
        [VM] * 4 + [HBM, VM],
        [VM] * 8,
        [pltpu.SMEM((MATS,), F32), dma((1,))],
    )(held(e), held(h), held(m), held(zin), far(permittivity), held(columns))
    to_up, to_down = kernel_call(
        join_y,
        [vmem(MESSAGE, 128), vmem(MESSAGE, 128)],
        [VM] * 6,
        [VM] * 2,
    )(*(held(part) for part in (up_part, down_part, c_planes, yzin, columns, zin)))
    from_below = across(to_up, dx=1, dz=1)
    from_above = across(to_down, dx=-1, dz=1)
    whole = jax.ShapeDtypeStruct((3, ROWS, 128), F32)
    e_out, h_out, e_edge, h_edge, patched = kernel_call(
        advance,
        [whole, whole, vmem(2, 3, 64, 128), vmem(2, 3, 64, 128), vmem(32, 128)],
        [VM] * 8,
        [HBM, HBM, VM, VM, VM],
        [pltpu.VMEM((3, EXT, 128), F32)] * 3 + [pltpu.VMEM((2, 320, 128), F32), dma((2,))],
        cost=pl.CostEstimate(flops=10**10, bytes_accessed=10**8, transcendentals=0),
    )(*(held(part) for part in (e_ext, h_ext, c_ext, c_planes, yin, yzin, columns, zin)))
    e_out, h_out, _, _ = kernel_call(
        correct,
        [whole, whole, vmem(2, 3, 64, 128), vmem(2, 3, 64, 128)],
        [VM] * 8 + [HBM] * 2,
        [HBM] * 2 + [VM] * 2,
        [dma((4,))],
        aliases={8: 0, 9: 1, 6: 2, 7: 3},
    )(
        *(held(part) for part in (up, down, c_planes, patched, from_below, from_above, e_edge, h_edge)),
        e_out,
        h_out,
    )
    return e_out.reshape(electric.shape), h_out.reshape(magnetic.shape)


def solution(mesh):
    placed = (
        P(("parts", "gy"), "gx", "gz", None, None),
        P(("parts", "gy"), "gx", "gz", None, None),
        P(("parts", "gy"), "gx", "gz", None),
        P(),
    )
    fast = mesh.shape["gy"] == 2 and mesh.shape["gz"] == 2
    return jax.shard_map(
        fast_shards if fast else general_shards,
        mesh=mesh,
        in_specs=placed,
        out_specs=(
            P(("parts", "gy"), "gx", "gz", None, None),
            P(("parts", "gy"), "gx", "gz", None, None),
        ),
        check_vma=False,
    )
```
